32 devices in a mesh: plane: 8 (over z, x), span: 4 (over y, core).
Axes of the slice: x: 2, y: 2, z: 4, core: 2. Of those that a mesh axis runs over, the one named last changes fastest.
Arguments:
- pressure_source: float32 [512, 32, 1024], P('span', 'plane'), may hold values from -24 to 24
- solid_mask: int32 [32, 1024], P('plane'), may hold values from 0 to 1, as said below
Outputs:
- pressure: float32 [512, 32, 1024], P('span', 'plane')
The draws below stay inside these ranges and needn't reach their ends.
Inputs may be any that keep to these rules, and one draw needn't show every extreme that they name: `solid_mask`: 1 where a plane cell lies inside a tube of a staggered bank of tubes, else 0.
All inputs are finite; a program needn't handle non-finite values.
Results may differ from the reference program's by a relative error of at most 0.0001.
Values sent between devices are 32-bit elements; how exact they have to be, the bound alone decides.
No kernel may reach another device: no remote copies, remote signals or barrier semaphores. Data moves between devices by JAX's collectives and lax.ppermute only.
A program may use at most 64 MiB of HBM per device.

```python
import jax
import jax.numpy as jnp
from jax import lax

NS = 512
NY = 1024
NX = 32


def draw_solid_mask(key, part):
    pitch = max(NY // 40, 4)
    key_offset, key_radius = jax.random.split(jax.random.fold_in(key, 7))
    offset = jax.random.randint(key_offset, (), 0, pitch)
    row_tubes = NX // pitch + 3
    column_tubes = NY // pitch + 2
    radii = jax.random.randint(key_radius, (row_tubes, column_tubes), pitch // 4, pitch // 2 + 1)
    row_pos = jnp.broadcast_to(jnp.arange(NX, dtype=jnp.int32)[:, None], (NX, NY))
    column_pos = jnp.broadcast_to(jnp.arange(NY, dtype=jnp.int32)[None, :], (NX, NY))
    column_tube = column_pos // pitch
    row_shift = column_tube % 2 * (pitch // 2) + offset
    row_tube = (row_pos - row_shift) // pitch
    center_row = row_tube * pitch + row_shift + pitch // 2
    center_column = column_tube * pitch + pitch // 2
    tube_radius = radii[jnp.clip(row_tube + 1, 0, row_tubes - 1), column_tube]
    row_gap = row_pos - center_row
    column_gap = column_pos - center_column
    inside = row_gap * row_gap + column_gap * column_gap <= tube_radius * tube_radius
    return inside.astype(jnp.int32)


def block_levels(own_key, extent, cuts, smallest, high):
    level = 1.0
    for axis_at, parts in cuts:
        steps = jax.random.uniform(jax.random.fold_in(jax.random.fold_in(own_key, 6), axis_at), (parts,), jnp.float32, smallest / len(cuts), high / len(cuts))
        level = level * jnp.repeat(jnp.exp(steps), extent[axis_at] // parts).reshape((-1,) + (1,) * (len(extent) - 1 - axis_at))
    return level


def bell_draw(key, extent, spread, reach, cuts=(), kind=jnp.bfloat16):
    result = jax.random.normal(key, extent, jnp.float32) * spread
    if len(cuts) > 0:
        result = block_levels(key, extent, cuts, -0.22, 0.18) * result
    return jnp.clip(result, min=-reach, max=reach).astype(kind)


def setup_inputs(seed: int = 0) -> dict:
    key_of = jax.random.split(jax.random.key(seed), 3)
    return {
        "pressure_source": bell_draw(key_of[0], (NS, NX, NY), 4.0, 24.0, ((0, 4), (1, 8)), jnp.float32),
        "solid_mask": draw_solid_mask(jax.random.fold_in(key_of[2], 71), 0),
    }


PENALTY = 12.0


def tables(length):
    nyquist = length // 2
    modes = jnp.arange(length, dtype=jnp.int32)
    wavenumber = jnp.where(modes <= nyquist, modes, modes - nyquist).astype(jnp.int32)
    points = jnp.arange(length, dtype=jnp.int32)
    phases = (points[:, None] * wavenumber[None, :]) % length
    angles = phases.astype(jnp.float32) * jnp.float32(2.0 * jnp.pi / length)
    cosine_mode = modes <= nyquist
    forward = jnp.where(cosine_mode[None, :], jnp.cos(angles), jnp.sin(angles))
    weight = jnp.where(cosine_mode & ((wavenumber == 0) | (wavenumber == nyquist)), jnp.float32(1.0), jnp.float32(2.0)) / jnp.float32(length)
    inverse = (forward * weight[None, :]).T
    eigen_values = 2.0 - 2.0 * jnp.cos(wavenumber.astype(jnp.float32) * jnp.float32(2.0 * jnp.pi / length))
    kept = jnp.where(3 * wavenumber <= length, jnp.float32(1.0), jnp.float32(0.0))
    return forward * kept[None, :], inverse, eigen_values


def reference(pressure_source, solid_mask):
    forward, inverse, eigen_values = tables(NS)
    penalty = solid_mask.astype(jnp.float32) * PENALTY
    block_size = min(64, NS)
    block_count = NS // block_size
    forward_blocks = forward.reshape(NS, block_count, block_size).transpose(1, 0, 2)
    inverse_blocks = inverse.reshape(block_count, block_size, NS)
    eigen_blocks = eigen_values.reshape(block_count, block_size)

    def sweep_block(running, block_tables):
        forward_part, inverse_part, eigen_part = block_tables
        spectrum = jnp.einsum("sm,sxy->mxy", forward_part, pressure_source, precision=lax.Precision.HIGHEST)
        diagonal = 4.0 + eigen_part[:, None, None] + penalty[None]
        sweep_one = spectrum / diagonal
        padded = jnp.pad(sweep_one, ((0, 0), (1, 1), (1, 1)))
        beside_all = padded[:, :-2, 1:-1] + padded[:, 2:, 1:-1] + padded[:, 1:-1, :-2] + padded[:, 1:-1, 2:]
        sweep_two = (spectrum + beside_all) / diagonal
        running = running + jnp.einsum("ms,mxy->sxy", inverse_part, sweep_two, precision=lax.Precision.HIGHEST)
        return running, None

    start_field = jnp.zeros(pressure_source.shape, jnp.float32)
    pressure, _ = lax.scan(sweep_block, start_field, (forward_blocks, inverse_blocks, eigen_blocks))
    return pressure
```

```python
import functools

import jax
import jax.numpy as jnp
import ml_dtypes
import numpy as np
from jax import lax
from jax.experimental import pallas as pl
from jax.experimental.pallas import tpu as pltpu
from jax.sharding import PartitionSpec as P

PENALTY = 12.0
LANES = 128
VMEM = pl.BlockSpec(memory_space=pltpu.VMEM)
PARAMS = pltpu.CompilerParams(vmem_limit_bytes=32 * 1024 * 1024)


def split(values):
    high = values.astype(ml_dtypes.bfloat16)
    low = (values - high.astype(np.float64)).astype(ml_dtypes.bfloat16)
    return high, low


def tables(length, cells):
    half = length // 2
    points = np.arange(half)
    groups = []
    for parity in (0, 1):
        kept = [k for k in range(length // 2 + 1) if 3 * k <= length and k % 2 == parity]
        modes = [(k, False) for k in kept] + [(k, True) for k in kept if 0 < k < length // 2]
        groups.append(modes)
    padded = -(-max(len(modes) for modes in groups) // 16) * 16
    forward = np.zeros((2, padded, half))
    inverse = np.zeros((2, half, padded))
    fluid = np.zeros((2 * padded, 1))
    solid = np.zeros((2 * padded, 1))
    for parity, modes in enumerate(groups):
        for at, (k, sine) in enumerate(modes):
            angles = (points * k % length) * (2.0 * np.pi / length)
            wave = np.sin(angles) if sine else np.cos(angles)
            weight = 1.0 if k in (0, length // 2) else 2.0
            eigen = 2.0 - 2.0 * np.cos(2.0 * np.pi * k / length)
            forward[parity, at] = wave
            inverse[parity, :, at] = wave * weight / length
            fluid[parity * padded + at] = 1.0 / (4.0 + eigen)
            solid[parity * padded + at] = 1.0 / (4.0 + eigen + PENALTY)
    blocks = half // cells
    high, low = split(forward.reshape(2, padded, blocks, cells).transpose(0, 2, 1, 3))
    forward = np.concatenate([high, low, high], axis=3)
    high, low = split(inverse.reshape(2, blocks, cells, padded))
    inverse = np.concatenate([high, low, high], axis=3)
    return forward, inverse, fluid.astype(np.float32), solid.astype(np.float32)


def thirds(values, axis):
    high = values.astype(jnp.bfloat16)
    low = (values - high.astype(jnp.float32)).astype(jnp.bfloat16)
    return jnp.concatenate([high, high, low], axis=axis)


def pack_kernel(rows, row_count, count, cells, width, x_ref, *outs):
    me = lax.axis_index("span")
    tiles = width // LANES
    stride = count * tiles * row_count
    lane = lax.broadcasted_iota(jnp.int32, (cells, LANES), 1)
    sides = jnp.zeros((cells, LANES), jnp.float32)
    for d in range(count):
        target = jnp.bitwise_xor(me, d)
        for i, row in enumerate(rows):
            for tile in range(tiles):
                outs[d][i * cells : (i + 1) * cells, tile * LANES : (tile + 1) * LANES] = x_ref[
                    pl.ds((target * tiles + tile) * row_count + row, cells, stride=stride), :
                ]
            before = jnp.maximum(target * tiles - 1, 0)
            after = jnp.minimum((target + 1) * tiles, count * tiles - 1)
            for side, (tile, source) in enumerate(((before, LANES - 1), (after, 0))):
                at = d * 8 + i * 2 + side
                column = x_ref[pl.ds(tile * row_count + row, cells, stride=stride), :]
                column = pltpu.roll(column, (at - source) % LANES, 1)
                sides = jnp.where(lane == at, column, sides)
    if cells < LANES:
        sides = jnp.concatenate([sides, jnp.zeros((LANES - cells, LANES), jnp.float32)], axis=0)
    turned = sides.T
    for d in range(count):
        if width > LANES:
            outs[d][len(rows) * cells :, :] = jnp.zeros((8, width), jnp.float32)
        outs[d][len(rows) * cells :, :LANES] = turned[d * 8 : (d + 1) * 8]


def transform(rows, count, cells, blocks, forward_ref):
    me = lax.axis_index("span")
    half = count // 2
    spectra = []
    for i in range(rows + 1):
        parts = []
        for parity in (0, 1):
            total = None
            for d in range(half):
                table = forward_ref[parity, jnp.bitwise_and(jnp.bitwise_xor(me, d), half - 1)]
                if i < rows:
                    near = blocks[d][i * cells : (i + 1) * cells, :]
                    far = blocks[d + half][i * cells : (i + 1) * cells, :]
                else:
                    near = blocks[d][rows * cells :, :cells]
                    far = blocks[d + half][rows * cells :, :cells]
                value = near + far if parity == 0 else near - far
                if i < rows:
                    term = jnp.dot(table, thirds(value, 0), preferred_element_type=jnp.float32)
                else:
                    value = jnp.concatenate([value, jnp.zeros_like(value)], axis=0)
                    term = lax.dot_general(
                        table, thirds(value, 1), (((1,), (1,)), ((), ())), preferred_element_type=jnp.float32
                    )
                total = term if total is None else total + term
            parts.append(total)
        spectra.append(jnp.concatenate(parts, axis=0))
    return spectra[:-1], spectra[-1]


def inverse_rows(sweeps, count, cells, inverse_ref, outs):
    me = lax.axis_index("span")
    half = count // 2
    padded = sweeps[0].shape[0] // 2
    for i, sweep in enumerate(sweeps):
        even = thirds(sweep[:padded], 0)
        odd = thirds(sweep[padded:], 0)
        for d in range(half):
            place = jnp.bitwise_and(jnp.bitwise_xor(me, d), half - 1)
            first = jnp.dot(inverse_ref[0, place], even, preferred_element_type=jnp.float32)
            second = jnp.dot(inverse_ref[1, place], odd, preferred_element_type=jnp.float32)
            outs[d][i * cells : (i + 1) * cells, :] = first + second
            outs[d + half][i * cells : (i + 1) * cells, :] = first - second


def second_sweep(spectrum, one, above, below, sides, at, inverse_diagonal):
    width = one.shape[1]
    lane = lax.broadcasted_iota(jnp.int32, one.shape, 1)
    left = jnp.where(lane == 0, sides[:, at : at + 1], pltpu.roll(one, 1, 1))
    right = jnp.where(lane == width - 1, sides[:, at + 1 : at + 2], pltpu.roll(one, width - 1, 1))
    return (spectrum + above + below + left + right) * inverse_diagonal


def edge_kernel(count, cells, *refs):
    blocks, (forward_ref, fluid_ref, solid_ref, mask_ref, side_ref), outs = refs[:count], refs[count : count + 5], refs[count + 5 :]
    spectrum_ref, first_ref, last_ref, sides_ref = outs
    spectra, sides = transform(2, count, cells, blocks, forward_ref)
    fluid, solid = fluid_ref[...], solid_ref[...]
    for i, one_ref in enumerate((first_ref, last_ref)):
        spectrum_ref[i] = spectra[i]
        one_ref[...] = spectra[i] * jnp.where(mask_ref[i : i + 1, :] != 0, solid, fluid)
    sides_ref[...] = sides * side_factor(side_ref, fluid, solid)


def side_factor(side_ref, fluid, solid):
    kind = side_ref[0:1, :16]
    return jnp.where(kind == 0, fluid, jnp.where(kind == 1, solid, 0.0))


def inner_kernel(rows, count, cells, *refs):
    blocks, rest = refs[:count], refs[count:]
    forward_ref, inverse_ref, fluid_ref, solid_ref, mask_ref, side_ref, first_ref, last_ref = rest[:8]
    outs, ones_ref = rest[8 : 8 + count], rest[8 + count]
    spectra, sides = transform(rows, count, cells, blocks, forward_ref)
    fluid, solid = fluid_ref[...], solid_ref[...]
    sides = sides * side_factor(side_ref, fluid, solid)
    diagonals = [jnp.where(mask_ref[i : i + 1, :] != 0, solid, fluid) for i in range(rows)]
    ones = [spectra[i] * diagonals[i] for i in range(rows)]
    ones_ref[0] = ones[0]
    ones_ref[1] = ones[-1]
    around = [first_ref[...]] + ones + [last_ref[...]]
    sweeps = [
        second_sweep(spectra[i], ones[i], around[i], around[i + 2], sides, 2 * i, diagonals[i]) for i in range(rows)
    ]
    inverse_rows(sweeps, count, cells, inverse_ref, outs)


def rim_kernel(count, cells, *refs):
    spectrum_ref, first_ref, last_ref, sides_ref, ones_ref, low_ref, high_ref = refs[:7]
    inverse_ref, fluid_ref, solid_ref, mask_ref = refs[7:11]
    outs = refs[11:]
    fluid, solid = fluid_ref[...], solid_ref[...]
    sides = sides_ref[...]
    sweeps = []
    for i, (one, above, below) in enumerate(
        ((first_ref, low_ref, ones_ref.at[0]), (last_ref, ones_ref.at[1], high_ref))
    ):
        diagonal = jnp.where(mask_ref[i : i + 1, :] != 0, solid, fluid)
        sweeps.append(second_sweep(spectrum_ref[i], one[...], above[...], below[...], sides, 2 * i, diagonal))
    inverse_rows(sweeps, count, cells, inverse_ref, outs)


def unpack_kernel(row_groups, row_count, count, cells, width, *refs):
    me = lax.axis_index("span")
    tiles = width // LANES
    stride = count * tiles * row_count
    out_ref = refs[-1]
    for g, rows in enumerate(row_groups):
        for d in range(count):
            block = refs[g * count + d]
            source = jnp.bitwise_xor(me, d)
            for i, row in enumerate(rows):
                for tile in range(tiles):
                    out_ref[pl.ds((source * tiles + tile) * row_count + row, cells, stride=stride), :] = block[
                        i * cells : (i + 1) * cells, tile * LANES : (tile + 1) * LANES
                    ]


def call(kernel, outs, *args):
    shapes = [jax.ShapeDtypeStruct(shape, jnp.float32) for shape in outs]
    return pl.pallas_call(
        kernel,
        out_shape=shapes,
        in_specs=[VMEM] * len(args),
        out_specs=[VMEM] * len(outs),
        compiler_params=PARAMS,
    )(*args)


def exchange(blocks):
    count = len(blocks)
    return [blocks[0]] + [
        lax.ppermute(blocks[d], "span", [(i, i ^ d) for i in range(count)]) for d in range(1, count)
    ]


def local(pressure_source, solid_mask):
    count = lax.axis_size("span")
    plane_count = lax.axis_size("plane")
    cells, row_count, columns = pressure_source.shape
    width = columns // count
    tiles = columns // LANES
    inner = tuple(range(1, row_count - 1))
    edges = (0, row_count - 1)
    forward, inverse, fluid, solid = tables(cells * count, cells)
    modes = fluid.shape[0]
    forward, inverse, fluid, solid = map(jnp.asarray, (forward, inverse, fluid, solid))

    source = pressure_source.reshape(cells, row_count, tiles, LANES).transpose(0, 2, 1, 3).reshape(-1, LANES)

    me = lax.axis_index("span")
    mask = lax.dynamic_slice_in_dim(solid_mask, me * width, width, axis=1)
    outside = jnp.full((row_count, 1), 2, jnp.int32)
    framed = jnp.concatenate([outside, solid_mask, outside], axis=1)
    before = lax.dynamic_slice_in_dim(framed, me * width, 1, axis=1)
    after = lax.dynamic_slice_in_dim(framed, me * width + width + 1, 1, axis=1)
    beside = jnp.concatenate([before, after], axis=1)

    def picked(rows):
        kinds = jnp.concatenate([beside[row] for row in rows])
        kinds = jnp.pad(kinds, (0, LANES - kinds.shape[0]), constant_values=2)
        return jnp.stack([mask[row] for row in rows]), kinds[None, :]

    edge_mask, edge_sides = picked(edges)
    inner_mask, inner_sides = picked(inner)

    def pack(rows):
        return call(
            functools.partial(pack_kernel, rows, row_count, count, cells, width),
            [(len(rows) * cells + 8, width)] * count,
            source,
        )

    edge_blocks = exchange(pack(edges))
    inner_blocks = exchange(pack(inner))
    spectrum, first, last, sides = call(
        functools.partial(edge_kernel, count, cells),
        [(2, modes, width), (modes, width), (modes, width), (modes, 16)],
        *edge_blocks, forward, fluid, solid, edge_mask, edge_sides,
    )
    up = [(i, i + 1) for i in range(plane_count - 1)]
    down = [(i + 1, i) for i in range(plane_count - 1)]
    low = lax.ppermute(last, "plane", up)
    high = lax.ppermute(first, "plane", down)
    *inner_out, ones = call(
        functools.partial(inner_kernel, len(inner), count, cells),
        [(len(inner) * cells, width)] * count + [(2, modes, width)],
        *inner_blocks, forward, inverse, fluid, solid, inner_mask, inner_sides, first, last,
    )
    inner_got = exchange(inner_out)
    edge_out = call(
        functools.partial(rim_kernel, count, cells),
        [(2 * cells, width)] * count,
        spectrum, first, last, sides, ones, low, high, inverse, fluid, solid, edge_mask,
    )
    edge_got = exchange(edge_out)
    (result,) = call(
        functools.partial(unpack_kernel, (inner, edges), row_count, count, cells, width),
        [(cells * tiles * row_count, LANES)],
        *inner_got, *edge_got,
    )
    return result.reshape(cells, tiles, row_count, LANES).transpose(0, 2, 1, 3).reshape(cells, row_count, columns)


def solution(mesh):
    placed = (P("span", "plane", None), P("plane", None))
    return jax.shard_map(
        local, mesh=mesh, in_specs=placed, out_specs=P("span", "plane", None), check_vma=False
    )
```

```python
import functools

import jax
import jax.numpy as jnp
import ml_dtypes
import numpy as np
from jax import lax
from jax.experimental import pallas as pl
from jax.experimental.pallas import tpu as pltpu
from jax.sharding import PartitionSpec as P

PENALTY = 12.0
LANES = 128
VMEM = pl.BlockSpec(memory_space=pltpu.VMEM)
PARAMS = pltpu.CompilerParams(vmem_limit_bytes=32 * 1024 * 1024)


def split(values):
    high = values.astype(ml_dtypes.bfloat16)
    low = (values - high.astype(np.float64)).astype(ml_dtypes.bfloat16)
    return high, low


def tables(length, cells):
    half = length // 2
    points = np.arange(half)
    groups = []
    for parity in (0, 1):
        kept = [k for k in range(length // 2 + 1) if 3 * k <= length and k % 2 == parity]
        modes = [(k, False) for k in kept] + [(k, True) for k in kept if 0 < k < length // 2]
        groups.append(modes)
    padded = -(-max(len(modes) for modes in groups) // 16) * 16
    forward = np.zeros((2, padded, half))
    inverse = np.zeros((2, half, padded))
    fluid = np.zeros((2 * padded, 1))
    solid = np.zeros((2 * padded, 1))
    for parity, modes in enumerate(groups):
        for at, (k, sine) in enumerate(modes):
            angles = (points * k % length) * (2.0 * np.pi / length)
            wave = np.sin(angles) if sine else np.cos(angles)
            weight = 1.0 if k in (0, length // 2) else 2.0
            eigen = 2.0 - 2.0 * np.cos(2.0 * np.pi * k / length)
            forward[parity, at] = wave
            inverse[parity, :, at] = wave * weight / length
            fluid[parity * padded + at] = 1.0 / (4.0 + eigen)
            solid[parity * padded + at] = 1.0 / (4.0 + eigen + PENALTY)
    blocks = half // cells
    high, low = split(forward.reshape(2, padded, blocks, cells).transpose(0, 2, 1, 3))
    forward = np.concatenate([high, low, high], axis=3)
    high, low = split(inverse.reshape(2, blocks, cells, padded))
    inverse = np.concatenate([high, low, high], axis=3)
    return forward, inverse, fluid.astype(np.float32), solid.astype(np.float32)


def thirds(values, axis):
    high = values.astype(jnp.bfloat16)
    low = (values - high.astype(jnp.float32)).astype(jnp.bfloat16)
    return jnp.concatenate([high, high, low], axis=axis)


def pack_kernel(jobs, row_count, count, cells, width, tiles, split_at, x_ref, *refs):
    outs, (held, arrived) = refs[:-2], refs[-2:]
    me = lax.axis_index("span")
    lines = x_ref.shape[1]
    pitch = held.shape[0] // cells
    some = cells // split_at
    copies = [
        pltpu.make_async_copy(
            x_ref.at[pl.ds(part * some, some)],
            held.reshape(cells, pitch, LANES).at[pl.ds(part * some, some), pl.ds(0, lines)],
            arrived.at[part],
        )
        for part in range(split_at)
    ]
    for copy in copies:
        copy.start()
    lane = lax.broadcasted_iota(jnp.int32, (some, LANES), 1)
    sides = []
    for part, copy in enumerate(copies):
        copy.wait()
        beside = jnp.zeros((some, LANES), jnp.float32)

        def line(tile, row):
            return held[pl.ds(part * some * pitch + tile * row_count + row, some, stride=pitch), :]

        for job, (out, place, d, column) in enumerate(jobs):
            first = (column * count + jnp.bitwise_xor(me, d)) * tiles
            base = place * (row_count * cells + 8) + part * some
            for row in range(row_count):
                for tile in range(tiles):
                    outs[out][base + row * cells : base + row * cells + some, tile * LANES : (tile + 1) * LANES] = line(
                        first + tile, row
                    )
                before = jnp.maximum(first - 1, 0)
                after = jnp.minimum(first + tiles, lines // row_count - 1)
                for side, (tile, source) in enumerate(((before, LANES - 1), (after, 0))):
                    at = job * 8 + row * 2 + side
                    beside = jnp.where(lane == at, pltpu.roll(line(tile, row), (at - source) % LANES, 1), beside)
        sides.append(beside)
    if cells < LANES:
        sides.append(jnp.zeros((LANES - cells, LANES), jnp.float32))
    turned = jnp.concatenate(sides, axis=0).T
    for job, (out, place, _, _) in enumerate(jobs):
        base = place * (row_count * cells + 8) + row_count * cells
        outs[out][base : base + 8, :LANES] = turned[job * 8 : (job + 1) * 8]
        if width > LANES:
            outs[out][base : base + 8, LANES:] = jnp.zeros((8, width - LANES), jnp.float32)


def transform(rows, count, cells, blocks, forward_ref):
    me = lax.axis_index("span")
    half = count // 2
    spectra = []
    for i in range(rows + 1):
        parts = []
        for parity in (0, 1):
            total = None
            for d in range(half):
                table = forward_ref[parity, jnp.bitwise_and(jnp.bitwise_xor(me, d), half - 1)]
                if i < rows:
                    near = blocks[d][i * cells : (i + 1) * cells, :]
                    far = blocks[d + half][i * cells : (i + 1) * cells, :]
                else:
                    near = blocks[d][rows * cells :, :cells]
                    far = blocks[d + half][rows * cells :, :cells]
                value = near + far if parity == 0 else near - far
                if i < rows:
                    term = jnp.dot(table, thirds(value, 0), preferred_element_type=jnp.float32)
                else:
                    value = jnp.concatenate([value, jnp.zeros_like(value)], axis=0)
                    term = lax.dot_general(
                        table, thirds(value, 1), (((1,), (1,)), ((), ())), preferred_element_type=jnp.float32
                    )
                total = term if total is None else total + term
            parts.append(total)
        spectra.append(jnp.concatenate(parts, axis=0))
    return spectra[:-1], spectra[-1]


def inverse_rows(sweeps, count, cells, inverse_ref, outs):
    me = lax.axis_index("span")
    half = count // 2
    padded = sweeps[0].shape[0] // 2
    for i, sweep in enumerate(sweeps):
        even = thirds(sweep[:padded], 0)
        odd = thirds(sweep[padded:], 0)
        for d in range(half):
            place = jnp.bitwise_and(jnp.bitwise_xor(me, d), half - 1)
            first = jnp.dot(inverse_ref[0, place], even, preferred_element_type=jnp.float32)
            second = jnp.dot(inverse_ref[1, place], odd, preferred_element_type=jnp.float32)
            outs[d][i * cells : (i + 1) * cells, :] = first + second
            outs[d + half][i * cells : (i + 1) * cells, :] = first - second


def second_sweep(spectrum, one, above, below, sides, at, inverse_diagonal):
    width = one.shape[1]
    lane = lax.broadcasted_iota(jnp.int32, one.shape, 1)
    left = jnp.where(lane == 0, sides[:, at : at + 1], pltpu.roll(one, 1, 1))
    right = jnp.where(lane == width - 1, sides[:, at + 1 : at + 2], pltpu.roll(one, width - 1, 1))
    return (spectrum + above + below + left + right) * inverse_diagonal


def side_factor(side_ref, fluid, solid):
    kind = side_ref[0:1, :16]
    return jnp.where(kind == 0, fluid, jnp.where(kind == 1, solid, 0.0))


def forward_kernel(rows, count, cells, column, *refs):
    blocks, (forward_ref, fluid_ref, solid_ref, mask_ref, side_ref), outs = refs[:count], refs[count : count + 5], refs[count + 5 :]
    spectrum_ref, first_ref, last_ref, sides_ref = outs
    size = rows * cells + 8
    blocks = [ref.at[column * size : (column + 1) * size] if ref.shape[0] > size else ref for ref in blocks]
    spectra, sides = transform(rows, count, cells, blocks, forward_ref)
    fluid, solid = fluid_ref[...], solid_ref[...]
    for row in range(rows):
        spectrum_ref[row] = spectra[row]
    first_ref[...] = spectra[0] * jnp.where(mask_ref[0:1, :] != 0, solid, fluid)
    last_ref[...] = spectra[-1] * jnp.where(mask_ref[rows - 1 : rows, :] != 0, solid, fluid)
    sides_ref[...] = sides * side_factor(side_ref, fluid, solid)


def sweep_kernel(wanted, rows, count, cells, *refs):
    spectrum_ref, sides_ref, low_ref, high_ref, inverse_ref, fluid_ref, solid_ref, mask_ref = refs[:8]
    outs = refs[8:]
    fluid, solid = fluid_ref[...], solid_ref[...]
    sides = sides_ref[...]
    needed = sorted({at for row in wanted for at in (row - 1, row, row + 1) if 0 <= at < rows})
    diagonal = {at: jnp.where(mask_ref[at : at + 1, :] != 0, solid, fluid) for at in needed}
    one = {at: spectrum_ref[at] * diagonal[at] for at in needed}
    if 0 in wanted:
        one[-1] = low_ref[...]
    if rows - 1 in wanted:
        one[rows] = high_ref[...]
    sweeps = [
        second_sweep(spectrum_ref[row], one[row], one[row - 1], one[row + 1], sides, 2 * row, diagonal[row])
        for row in wanted
    ]
    inverse_rows(sweeps, count, cells, inverse_ref, outs)


def unpack_kernel(row_groups, row_count, count, cells, tiles, column, *refs):
    me = lax.axis_index("span")
    blocks = refs[: len(row_groups) * count]
    out_ref, held, done = refs[-3:]
    pitch = held.shape[0] // cells
    lines = count * tiles * row_count
    for g, rows in enumerate(row_groups):
        for d in range(count):
            source = jnp.bitwise_xor(me, d)
            for i, row in enumerate(rows):
                for tile in range(tiles):
                    held[pl.ds((source * tiles + tile) * row_count + row, cells, stride=pitch), :] = blocks[g * count + d][
                        i * cells : (i + 1) * cells, tile * LANES : (tile + 1) * LANES
                    ]
    copy = pltpu.make_async_copy(
        held.reshape(cells, pitch, LANES).at[:, pl.ds(0, lines)], out_ref.at[:, pl.ds(column * lines, lines)], done
    )
    copy.start()
    copy.wait()


def call(kernel, outs, *args):
    shapes = [jax.ShapeDtypeStruct(shape, jnp.float32) for shape in outs]
    return pl.pallas_call(
        kernel,
        out_shape=shapes,
        in_specs=[VMEM] * len(args),
        out_specs=[VMEM] * len(outs),
        compiler_params=PARAMS,
    )(*args)


def local(pressure_source, solid_mask):
    count = lax.axis_size("span")
    plane_count = lax.axis_size("plane")
    cells, rows, columns = pressure_source.shape
    half = count // 2
    parts = 2 if columns // count >= 2 * LANES else 1
    width = columns // count // parts
    tiles = width // LANES
    lines = columns // LANES * rows
    inner = tuple(range(1, rows - 1))
    edges = (0, rows - 1)
    forward, inverse, fluid, solid = tables(cells * count, cells)
    modes = fluid.shape[0]
    forward, inverse, fluid, solid = map(jnp.asarray, (forward, inverse, fluid, solid))

    source = pressure_source.reshape(cells, rows, columns // LANES, LANES).transpose(0, 2, 1, 3).reshape(cells, lines, LANES)
    me = lax.axis_index("span")
    outside = jnp.full((rows, 1), 2, jnp.int32)
    framed = jnp.concatenate([outside, solid_mask, outside], axis=1)

    def masks(part):
        start = (part * count + me) * width
        mask = lax.dynamic_slice_in_dim(solid_mask, start, width, axis=1)
        before = lax.dynamic_slice_in_dim(framed, start, 1, axis=1)
        after = lax.dynamic_slice_in_dim(framed, start + width + 1, 1, axis=1)
        kinds = jnp.concatenate([before, after], axis=1).reshape(1, 2 * rows)
        return mask, jnp.pad(kinds, ((0, 0), (0, LANES - 2 * rows)), constant_values=2)

    size = rows * cells + 8

    def pack(jobs, sizes, limit):
        return pl.pallas_call(
            functools.partial(pack_kernel, jobs, rows, count, cells, width, tiles, 4),
            out_shape=[jax.ShapeDtypeStruct((places * size, width), jnp.float32) for places in sizes],
            in_specs=[pl.BlockSpec(memory_space=pl.ANY)],
            out_specs=[VMEM] * len(sizes),
            scratch_shapes=[
                pltpu.VMEM((cells * (lines + 8), LANES), jnp.float32),
                pltpu.SemaphoreType.DMA((4,)),
            ],
            compiler_params=pltpu.CompilerParams(vmem_limit_bytes=limit * 1024 * 1024),
        )(source)

    def swap(block, d):
        return lax.ppermute(block, "span", [(i, i ^ d) for i in range(count)])

    far = range(half, count)
    packed = pack([(d - half, 0, d, 0) for d in far], [1] * half, 56)
    got = {(0, d): swap(block, d) for d, block in zip(far, packed)}
    source = lax.optimization_barrier((source, *packed))[0]
    jobs = [(at, part, d, part) for at, d in enumerate(range(half)) for part in range(parts)]
    sizes = [parts] * half
    for part in range(1, parts):
        for d in far:
            jobs.append((len(sizes), 0, d, part))
            sizes.append(1)
    packed = pack(jobs, sizes, 32)
    near = [packed[0]] + [swap(packed[d], d) for d in range(1, half)]
    at = half
    for part in range(1, parts):
        for d in far:
            got[part, d] = swap(packed[at], d)
            at += 1

    up = [(i, i + 1) for i in range(plane_count - 1)]
    down = [(i + 1, i) for i in range(plane_count - 1)]
    state, inner_got, edge_got = [], [], []

    def sweep(wanted, part, low, high):
        spectrum, sides, mask = state[part][0], state[part][1], state[part][2]
        blocks = call(
            functools.partial(sweep_kernel, wanted, rows, count, cells),
            [(len(wanted) * cells, width)] * count,
            spectrum, sides, low, high, inverse, fluid, solid, mask,
        )
        return [blocks[0]] + [swap(blocks[d], d) for d in range(1, count)]

    for part in range(parts):
        mask, kinds = masks(part)
        spectrum, first, last, sides = call(
            functools.partial(forward_kernel, rows, count, cells, part),
            [(rows, modes, width), (modes, width), (modes, width), (modes, 16)],
            *near, *[got[part, d] for d in far], forward, fluid, solid, mask, kinds,
        )
        low = lax.ppermute(last, "plane", up)
        high = lax.ppermute(first, "plane", down)
        state.append((spectrum, sides, mask, low, high))
        inner_got.append(sweep(inner, part, first, last))
    for part in range(parts):
        edge_got.append(sweep(edges, part, state[part][3], state[part][4]))

    result = None
    for part in range(parts):
        blocks = inner_got[part] + edge_got[part]
        held = count * tiles * rows + 8
        result = pl.pallas_call(
            functools.partial(unpack_kernel, (inner, edges), rows, count, cells, tiles, part),
            out_shape=jax.ShapeDtypeStruct((cells, lines, LANES), jnp.float32),
            in_specs=[VMEM] * len(blocks) + [pl.BlockSpec(memory_space=pl.ANY)] * (result is not None),
            out_specs=pl.BlockSpec(memory_space=pl.ANY),
            scratch_shapes=[pltpu.VMEM((cells * held, LANES), jnp.float32), pltpu.SemaphoreType.DMA],
            input_output_aliases={} if result is None else {len(blocks): 0},
            compiler_params=PARAMS,
        )(*blocks, *([] if result is None else [result]))
    return result.reshape(cells, columns // LANES, rows, LANES).transpose(0, 2, 1, 3).reshape(cells, rows, columns)


def solution(mesh):
    placed = (P("span", "plane", None), P("plane", None))
    return jax.shard_map(
        local, mesh=mesh, in_specs=placed, out_specs=P("span", "plane", None), check_vma=False
    )
```

```python
import functools

import jax
import jax.numpy as jnp
import ml_dtypes
import numpy as np
from jax import lax
from jax.experimental import pallas as pl
from jax.experimental.pallas import tpu as pltpu
from jax.sharding import PartitionSpec as P

PENALTY = 12.0
LANES = 128
VMEM = pl.BlockSpec(memory_space=pltpu.VMEM)
ANY = pl.BlockSpec(memory_space=pl.ANY)
PARAMS = pltpu.CompilerParams(vmem_limit_bytes=16 * 1024 * 1024)
COST = pl.CostEstimate(flops=1024, bytes_accessed=1024, transcendentals=0)


def split(values):
    high = values.astype(ml_dtypes.bfloat16)
    low = (values - high.astype(np.float64)).astype(ml_dtypes.bfloat16)
    return high, low


def tables(length, cells):
    half = length // 2
    points = np.arange(half)
    groups = []
    for parity in (0, 1):
        kept = [k for k in range(length // 2 + 1) if 3 * k <= length and k % 2 == parity]
        modes = [(k, False) for k in kept] + [(k, True) for k in kept if 0 < k < length // 2]
        groups.append(modes)
    padded = -(-max(len(modes) for modes in groups) // 16) * 16
    forward = np.zeros((2, padded, half))
    inverse = np.zeros((2, half, padded))
    fluid = np.zeros((2 * padded, 1))
    solid = np.zeros((2 * padded, 1))
    for parity, modes in enumerate(groups):
        for at, (k, sine) in enumerate(modes):
            angles = (points * k % length) * (2.0 * np.pi / length)
            wave = np.sin(angles) if sine else np.cos(angles)
            weight = 1.0 if k in (0, length // 2) else 2.0
            eigen = 2.0 - 2.0 * np.cos(2.0 * np.pi * k / length)
            forward[parity, at] = wave
            inverse[parity, :, at] = wave * weight / length
            fluid[parity * padded + at] = 1.0 / (4.0 + eigen)
            solid[parity * padded + at] = 1.0 / (4.0 + eigen + PENALTY)
    blocks = half // cells
    high, low = split(forward.reshape(2, padded, blocks, cells).transpose(0, 2, 1, 3))
    forward = np.concatenate([high, low, high], axis=3)
    high, low = split(inverse.reshape(2, blocks, cells, padded))
    inverse = np.concatenate([high, low, high], axis=3)
    return forward, inverse, fluid.astype(np.float32), solid.astype(np.float32)


def thirds(values, axis):
    high = values.astype(jnp.bfloat16)
    low = (values - high.astype(jnp.float32)).astype(jnp.bfloat16)
    return jnp.concatenate([high, high, low], axis=axis)


def pack_kernel(jobs, earlier, row_count, count, cells, width, tiles, split_at, x_ref, *refs):
    outs, (held, arrived) = refs[earlier:-2], refs[-2:]
    me = lax.axis_index("span")
    lines = x_ref.shape[1]
    pitch = held.shape[0] // cells
    some = cells // split_at
    copies = [
        pltpu.make_async_copy(
            x_ref.at[pl.ds(part * some, some)],
            held.reshape(cells, pitch, LANES).at[pl.ds(part * some, some), pl.ds(0, lines)],
            arrived.at[part],
        )
        for part in range(split_at)
    ]
    for copy in copies:
        copy.start()
    lane = lax.broadcasted_iota(jnp.int32, (some, LANES), 1)
    sides = []
    for part, copy in enumerate(copies):
        copy.wait()
        beside = jnp.zeros((some, LANES), jnp.float32)

        def line(tile, row):
            return held[pl.ds(part * some * pitch + tile * row_count + row, some, stride=pitch), :]

        for job, (out, place, d, column) in enumerate(jobs):
            first = (column * count + jnp.bitwise_xor(me, d)) * tiles
            base = place * (row_count * cells + 8) + part * some
            for row in range(row_count):
                for tile in range(tiles):
                    outs[out][base + row * cells : base + row * cells + some, tile * LANES : (tile + 1) * LANES] = line(
                        first + tile, row
                    )
                before = jnp.maximum(first - 1, 0)
                after = jnp.minimum(first + tiles, lines // row_count - 1)
                for side, (tile, source) in enumerate(((before, LANES - 1), (after, 0))):
                    at = job * 8 + row * 2 + side
                    beside = jnp.where(lane == at, pltpu.roll(line(tile, row), (at - source) % LANES, 1), beside)
        sides.append(beside)
    if cells < LANES:
        sides.append(jnp.zeros((LANES - cells, LANES), jnp.float32))
    turned = jnp.concatenate(sides, axis=0).T
    for job, (out, place, _, _) in enumerate(jobs):
        base = place * (row_count * cells + 8) + row_count * cells
        outs[out][base : base + 8, :LANES] = turned[job * 8 : (job + 1) * 8]
        if width > LANES:
            outs[out][base : base + 8, LANES:] = jnp.zeros((8, width - LANES), jnp.float32)


def transform(rows, count, cells, blocks, forward_ref):
    me = lax.axis_index("span")
    half = count // 2
    spectra = []
    for i in range(rows + 1):
        parts = []
        for parity in (0, 1):
            total = None
            for d in range(half):
                table = forward_ref[parity, jnp.bitwise_and(jnp.bitwise_xor(me, d), half - 1)]
                if i < rows:
                    near = blocks[d][i * cells : (i + 1) * cells, :]
                    far = blocks[d + half][i * cells : (i + 1) * cells, :]
                else:
                    near = blocks[d][rows * cells :, :cells]
                    far = blocks[d + half][rows * cells :, :cells]
                value = near + far if parity == 0 else near - far
                if i < rows:
                    term = jnp.dot(table, thirds(value, 0), preferred_element_type=jnp.float32)
                else:
                    value = jnp.concatenate([value, jnp.zeros_like(value)], axis=0)
                    term = lax.dot_general(
                        table, thirds(value, 1), (((1,), (1,)), ((), ())), preferred_element_type=jnp.float32
                    )
                total = term if total is None else total + term
            parts.append(total)
        spectra.append(jnp.concatenate(parts, axis=0))
    return spectra[:-1], spectra[-1]


def inverse_rows(sweeps, count, cells, inverse_ref, outs):
    me = lax.axis_index("span")
    half = count // 2
    padded = sweeps[0].shape[0] // 2
    for i, sweep in enumerate(sweeps):
        even = thirds(sweep[:padded], 0)
        odd = thirds(sweep[padded:], 0)
        for d in range(half):
            place = jnp.bitwise_and(jnp.bitwise_xor(me, d), half - 1)
            first = jnp.dot(inverse_ref[0, place], even, preferred_element_type=jnp.float32)
            second = jnp.dot(inverse_ref[1, place], odd, preferred_element_type=jnp.float32)
            outs[d][i * cells : (i + 1) * cells, :] = first + second
            outs[d + half][i * cells : (i + 1) * cells, :] = first - second


def second_sweep(spectrum, one, above, below, sides, at, inverse_diagonal):
    width = one.shape[1]
    lane = lax.broadcasted_iota(jnp.int32, one.shape, 1)
    left = jnp.where(lane == 0, sides[:, at : at + 1], pltpu.roll(one, 1, 1))
    right = jnp.where(lane == width - 1, sides[:, at + 1 : at + 2], pltpu.roll(one, width - 1, 1))
    return (spectrum + above + below + left + right) * inverse_diagonal


def side_factor(side_ref, fluid, solid):
    kind = side_ref[0:1, :16]
    return jnp.where(kind == 0, fluid, jnp.where(kind == 1, solid, 0.0))


def forward_kernel(rows, count, cells, column, *refs):
    blocks, (forward_ref, fluid_ref, solid_ref, mask_ref, side_ref) = refs[:count], refs[count : count + 5]
    spectrum_ref, first_ref, last_ref, sides_ref = refs[-4:]
    size = rows * cells + 8
    blocks = [ref.at[column * size : (column + 1) * size] if ref.shape[0] > size else ref for ref in blocks]
    spectra, sides = transform(rows, count, cells, blocks, forward_ref)
    fluid, solid = fluid_ref[...], solid_ref[...]
    for row in range(rows):
        spectrum_ref[row] = spectra[row]
    first_ref[...] = spectra[0] * jnp.where(mask_ref[0:1, :] != 0, solid, fluid)
    last_ref[...] = spectra[-1] * jnp.where(mask_ref[rows - 1 : rows, :] != 0, solid, fluid)
    sides_ref[...] = sides * side_factor(side_ref, fluid, solid)


def sweep_rows(wanted, rows, refs):
    spectrum_ref, sides_ref, low_ref, high_ref, fluid_ref, solid_ref, mask_ref = refs
    fluid, solid = fluid_ref[...], solid_ref[...]
    sides = sides_ref[...]
    needed = sorted({at for row in wanted for at in (row - 1, row, row + 1) if 0 <= at < rows})
    diagonal = {at: jnp.where(mask_ref[at : at + 1, :] != 0, solid, fluid) for at in needed}
    one = {at: spectrum_ref[at] * diagonal[at] for at in needed}
    if 0 in wanted:
        one[-1] = low_ref[...]
    if rows - 1 in wanted:
        one[rows] = high_ref[...]
    return [
        second_sweep(spectrum_ref[row], one[row], one[row - 1], one[row + 1], sides, 2 * row, diagonal[row])
        for row in wanted
    ]


def inner_kernel(rows, count, cells, *refs):
    sweeps = sweep_rows(range(1, rows - 1), rows, refs[:7])
    inverse_rows(sweeps, count, cells, refs[7], refs[-count:])


def edge_kernel(rows, count, cells, *refs):
    half = count // 2
    inner, outs = refs[8 : 8 + half], refs[-count:]
    sweeps = sweep_rows((0, rows - 1), rows, refs[:7])
    for d in range(half):
        outs[d][2 * cells :, :] = inner[d][...]
    inverse_rows(sweeps, count, cells, refs[7], outs)


def unpack_kernel(row_groups, row_count, count, cells, tiles, column, *refs):
    me = lax.axis_index("span")
    out_ref, held, done = refs[-3:]
    pitch = held.shape[0] // cells
    lines = count * tiles * row_count
    for at, (d, rows) in enumerate(row_groups):
        source = jnp.bitwise_xor(me, d)
        for i, row in enumerate(rows):
            for tile in range(tiles):
                held[pl.ds((source * tiles + tile) * row_count + row, cells, stride=pitch), :] = refs[at][
                    i * cells : (i + 1) * cells, tile * LANES : (tile + 1) * LANES
                ]
    copy = pltpu.make_async_copy(
        held.reshape(cells, pitch, LANES).at[:, pl.ds(0, lines)], out_ref.at[:, pl.ds(column * lines, lines)], done
    )
    copy.start()
    copy.wait()


def call(kernel, outs, args, earlier=()):
    shapes = [jax.ShapeDtypeStruct(shape, jnp.float32) for shape in outs]
    return pl.pallas_call(
        kernel,
        out_shape=shapes,
        in_specs=[VMEM] * len(args) + [ANY] * len(earlier),
        out_specs=[VMEM] * len(outs),
        compiler_params=PARAMS,
        cost_estimate=COST,
    )(*args, *earlier)


def local(pressure_source, solid_mask):
    count = lax.axis_size("span")
    plane_count = lax.axis_size("plane")
    cells, rows, columns = pressure_source.shape
    half = count // 2
    parts = 2 if columns // count >= 2 * LANES else 1
    width = columns // count // parts
    tiles = width // LANES
    lines = columns // LANES * rows
    inner = tuple(range(1, rows - 1))
    edges = (0, rows - 1)
    forward, inverse, fluid, solid = tables(cells * count, cells)
    modes = fluid.shape[0]
    forward, inverse, fluid, solid = map(jnp.asarray, (forward, inverse, fluid, solid))

    source = pressure_source.reshape(cells, rows, columns // LANES, LANES).transpose(0, 2, 1, 3).reshape(cells, lines, LANES)
    me = lax.axis_index("span")
    outside = jnp.full((rows, 1), 2, jnp.int32)
    framed = jnp.concatenate([outside, solid_mask, outside], axis=1)

    def masks(part):
        start = (part * count + me) * width
        mask = lax.dynamic_slice_in_dim(solid_mask, start, width, axis=1)
        before = lax.dynamic_slice_in_dim(framed, start, 1, axis=1)
        after = lax.dynamic_slice_in_dim(framed, start + width + 1, 1, axis=1)
        kinds = jnp.concatenate([before, after], axis=1).reshape(1, 2 * rows)
        return mask, jnp.pad(kinds, ((0, 0), (0, LANES - 2 * rows)), constant_values=2)

    size = rows * cells + 8

    def pack(jobs, sizes, earlier):
        return pl.pallas_call(
            functools.partial(pack_kernel, jobs, len(earlier), rows, count, cells, width, tiles, 4),
            out_shape=[jax.ShapeDtypeStruct((places * size, width), jnp.float32) for places in sizes],
            in_specs=[ANY] * (1 + len(earlier)),
            out_specs=[VMEM] * len(sizes),
            scratch_shapes=[
                pltpu.VMEM((cells * (lines + 8), LANES), jnp.float32),
                pltpu.SemaphoreType.DMA((4,)),
            ],
            compiler_params=PARAMS,
            cost_estimate=COST,
        )(source, *earlier)

    def swap(block, d):
        return lax.ppermute(block, "span", [(i, i ^ d) for i in range(count)])

    far = range(half, count)
    first_packed = pack([(d - half, 0, d, 0) for d in far], [1] * half, ())
    got = {(0, d): swap(block, d) for d, block in zip(far, first_packed)}
    jobs = [(at, part, d, part) for at, d in enumerate(range(half)) for part in range(parts)]
    sizes = [parts] * half
    for part in range(1, parts):
        for d in far:
            jobs.append((len(sizes), 0, d, part))
            sizes.append(1)
    packed = pack(jobs, sizes, (first_packed[-1],))
    near = [packed[0]] + [swap(packed[d], d) for d in range(1, half)]
    at = half
    for part in range(1, parts):
        for d in far:
            got[part, d] = swap(packed[at], d)
            at += 1

    up = [(i, i + 1) for i in range(plane_count - 1)]
    down = [(i + 1, i) for i in range(plane_count - 1)]
    state, blocks, groups, earlier = [], [], [], ()
    for part in range(parts):
        mask, kinds = masks(part)
        spectrum, first, last, sides = call(
            functools.partial(forward_kernel, rows, count, cells, part),
            [(rows, modes, width), (modes, width), (modes, width), (modes, 16)],
            [*near, *[got[part, d] for d in far], forward, fluid, solid, mask, kinds],
            earlier,
        )
        low = lax.ppermute(last, "plane", up)
        high = lax.ppermute(first, "plane", down)
        state.append((spectrum, sides, low, high, fluid, solid, mask))
        inner_out = call(
            functools.partial(inner_kernel, rows, count, cells),
            [(len(inner) * cells, width)] * count,
            [spectrum, sides, first, last, fluid, solid, mask, inverse],
        )
        blocks.append(inner_out)
        earlier = (inner_out[-1],)
    sent = [[swap(block[d], d) for d in far] for block in blocks]
    result = None
    for part in range(parts):
        edge_out = call(
            functools.partial(edge_kernel, rows, count, cells),
            [(rows * cells, width)] * half + [(2 * cells, width)] * half,
            [*state[part], inverse, *blocks[part][:half]],
            earlier,
        )
        earlier = (edge_out[-1],)
        pieces = [(0, edges + inner, edge_out[0])]
        pieces += [(d, inner, block) for d, block in zip(far, sent[part])]
        pieces += [(d, edges, swap(edge_out[d], d)) for d in far]
        pieces += [(d, edges + inner, swap(edge_out[d], d)) for d in range(1, half)]
        previous = () if result is None else (result,)
        result = pl.pallas_call(
            functools.partial(
                unpack_kernel, [piece[:2] for piece in pieces], rows, count, cells, tiles, part
            ),
            out_shape=jax.ShapeDtypeStruct((cells, lines, LANES), jnp.float32),
            in_specs=[VMEM] * len(pieces) + [ANY] * len(previous),
            out_specs=ANY,
            scratch_shapes=[
                pltpu.VMEM((cells * (count * tiles * rows + 8), LANES), jnp.float32),
                pltpu.SemaphoreType.DMA,
            ],
            input_output_aliases={len(pieces): 0} if previous else {},
            compiler_params=PARAMS,
            cost_estimate=COST,
        )(*[piece[2] for piece in pieces], *previous)
    return result.reshape(cells, columns // LANES, rows, LANES).transpose(0, 2, 1, 3).reshape(cells, rows, columns)


def solution(mesh):
    placed = (P("span", "plane", None), P("plane", None))
    return jax.shard_map(
        local, mesh=mesh, in_specs=placed, out_specs=P("span", "plane", None), check_vma=False
    )
```

```python
import functools

import jax
import jax.numpy as jnp
import ml_dtypes
import numpy as np
from jax import lax
from jax.experimental import pallas as pl
from jax.experimental.pallas import tpu as pltpu
from jax.sharding import PartitionSpec as P

PENALTY = 12.0
LANES = 128
VMEM = pl.BlockSpec(memory_space=pltpu.VMEM)
ANY = pl.BlockSpec(memory_space=pl.ANY)
PARAMS = pltpu.CompilerParams(vmem_limit_bytes=16 * 1024 * 1024)
COST = pl.CostEstimate(flops=1024, bytes_accessed=1024, transcendentals=0)


def split(values):
    high = values.astype(ml_dtypes.bfloat16)
    low = (values - high.astype(np.float64)).astype(ml_dtypes.bfloat16)
    return high, low


def tables(length, cells):
    half = length // 2
    points = np.arange(half)
    groups = []
    for parity in (0, 1):
        kept = [k for k in range(length // 2 + 1) if 3 * k <= length and k % 2 == parity]
        modes = [(k, False) for k in kept] + [(k, True) for k in kept if 0 < k < length // 2]
        groups.append(modes)
    padded = -(-max(len(modes) for modes in groups) // 16) * 16
    forward = np.zeros((2, padded, half))
    inverse = np.zeros((2, half, padded))
    fluid = np.zeros((2 * padded, 1))
    solid = np.zeros((2 * padded, 1))
    for parity, modes in enumerate(groups):
        for at, (k, sine) in enumerate(modes):
            angles = (points * k % length) * (2.0 * np.pi / length)
            wave = np.sin(angles) if sine else np.cos(angles)
            weight = 1.0 if k in (0, length // 2) else 2.0
            eigen = 2.0 - 2.0 * np.cos(2.0 * np.pi * k / length)
            forward[parity, at] = wave
            inverse[parity, :, at] = wave * weight / length
            fluid[parity * padded + at] = 1.0 / (4.0 + eigen)
            solid[parity * padded + at] = 1.0 / (4.0 + eigen + PENALTY)
    blocks = half // cells
    high, low = split(forward.reshape(2, padded, blocks, cells).transpose(0, 2, 1, 3))
    forward = np.concatenate([high, low, high], axis=3)
    high, low = split(inverse.reshape(2, blocks, cells, padded))
    inverse = np.concatenate([high, low, high], axis=3)
    return forward, inverse, fluid.astype(np.float32), solid.astype(np.float32)


def thirds(values, axis):
    high = values.astype(jnp.bfloat16)
    low = (values - high.astype(jnp.float32)).astype(jnp.bfloat16)
    return jnp.concatenate([high, high, low], axis=axis)


def pack_kernel(jobs, earlier, row_count, count, cells, width, tiles, split_at, x_ref, *refs):
    outs, (held, arrived) = refs[earlier:-2], refs[-2:]
    me = lax.axis_index("span")
    lines = x_ref.shape[1]
    pitch = held.shape[0] // cells
    some = cells // split_at
    copies = [
        pltpu.make_async_copy(
            x_ref.at[pl.ds(part * some, some)],
            held.reshape(cells, pitch, LANES).at[pl.ds(part * some, some), pl.ds(0, lines)],
            arrived.at[part],
        )
        for part in range(split_at)
    ]
    for copy in copies:
        copy.start()
    lane = lax.broadcasted_iota(jnp.int32, (some, LANES), 1)
    sides = []
    for part, copy in enumerate(copies):
        copy.wait()
        beside = jnp.zeros((some, LANES), jnp.float32)

        def line(tile, row):
            return held[pl.ds(part * some * pitch + tile * row_count + row, some, stride=pitch), :]

        for job, (out, place, d, column) in enumerate(jobs):
            first = (column * count + jnp.bitwise_xor(me, d)) * tiles
            base = place * (row_count * cells + 8) + part * some
            for row in range(row_count):
                for tile in range(tiles):
                    outs[out][base + row * cells : base + row * cells + some, tile * LANES : (tile + 1) * LANES] = line(
                        first + tile, row
                    )
                before = jnp.maximum(first - 1, 0)
                after = jnp.minimum(first + tiles, lines // row_count - 1)
                for side, (tile, source) in enumerate(((before, LANES - 1), (after, 0))):
                    at = job * 8 + row * 2 + side
                    beside = jnp.where(lane == at, pltpu.roll(line(tile, row), (at - source) % LANES, 1), beside)
        sides.append(beside)
    if cells < LANES:
        sides.append(jnp.zeros((LANES - cells, LANES), jnp.float32))
    turned = jnp.concatenate(sides, axis=0).T
    for job, (out, place, _, _) in enumerate(jobs):
        base = place * (row_count * cells + 8) + row_count * cells
        outs[out][base : base + 8, :LANES] = turned[job * 8 : (job + 1) * 8]
        if width > LANES:
            outs[out][base : base + 8, LANES:] = jnp.zeros((8, width - LANES), jnp.float32)


def transform(rows, count, cells, blocks, forward_ref):
    me = lax.axis_index("span")
    half = count // 2
    spectra = []
    for i in range(rows + 1):
        parts = []
        for parity in (0, 1):
            total = None
            for d in range(half):
                table = forward_ref[parity, jnp.bitwise_and(jnp.bitwise_xor(me, d), half - 1)]
                if i < rows:
                    near = blocks[d][i * cells : (i + 1) * cells, :]
                    far = blocks[d + half][i * cells : (i + 1) * cells, :]
                else:
                    near = blocks[d][rows * cells :, :cells]
                    far = blocks[d + half][rows * cells :, :cells]
                value = near + far if parity == 0 else near - far
                if i < rows:
                    term = jnp.dot(table, thirds(value, 0), preferred_element_type=jnp.float32)
                else:
                    value = jnp.concatenate([value, jnp.zeros_like(value)], axis=0)
                    term = lax.dot_general(
                        table, thirds(value, 1), (((1,), (1,)), ((), ())), preferred_element_type=jnp.float32
                    )
                total = term if total is None else total + term
            parts.append(total)
        spectra.append(jnp.concatenate(parts, axis=0))
    return spectra[:-1], spectra[-1]


def inverse_rows(sweeps, count, cells, inverse_ref, outs):
    me = lax.axis_index("span")
    half = count // 2
    padded = sweeps[0].shape[0] // 2
    for i, sweep in enumerate(sweeps):
        even = thirds(sweep[:padded], 0)
        odd = thirds(sweep[padded:], 0)
        for d in range(half):
            place = jnp.bitwise_and(jnp.bitwise_xor(me, d), half - 1)
            first = jnp.dot(inverse_ref[0, place], even, preferred_element_type=jnp.float32)
            second = jnp.dot(inverse_ref[1, place], odd, preferred_element_type=jnp.float32)
            outs[d][i * cells : (i + 1) * cells, :] = first + second
            outs[d + half][i * cells : (i + 1) * cells, :] = first - second


def second_sweep(spectrum, one, above, below, sides, at, inverse_diagonal):
    width = one.shape[1]
    lane = lax.broadcasted_iota(jnp.int32, one.shape, 1)
    left = jnp.where(lane == 0, sides[:, at : at + 1], pltpu.roll(one, 1, 1))
    right = jnp.where(lane == width - 1, sides[:, at + 1 : at + 2], pltpu.roll(one, width - 1, 1))
    return (spectrum + above + below + left + right) * inverse_diagonal


def side_factor(side_ref, fluid, solid):
    kind = side_ref[0:1, :16]
    return jnp.where(kind == 0, fluid, jnp.where(kind == 1, solid, 0.0))


def forward_kernel(rows, count, cells, bases, *refs):
    size = rows * cells + 8
    blocks = [ref.at[base : base + size] for ref, base in zip(refs, bases)]
    forward_ref, fluid_ref, solid_ref, mask_ref, side_ref = refs[count : count + 5]
    spectrum_ref, first_ref, last_ref, sides_ref = refs[-4:]
    spectra, sides = transform(rows, count, cells, blocks, forward_ref)
    fluid, solid = fluid_ref[...], solid_ref[...]
    for row in range(rows):
        spectrum_ref[row] = spectra[row]
    first_ref[...] = spectra[0] * jnp.where(mask_ref[0:1, :] != 0, solid, fluid)
    last_ref[...] = spectra[-1] * jnp.where(mask_ref[rows - 1 : rows, :] != 0, solid, fluid)
    sides_ref[...] = sides * side_factor(side_ref, fluid, solid)


def sweep_rows(wanted, rows, refs):
    spectrum_ref, sides_ref, low_ref, high_ref, fluid_ref, solid_ref, mask_ref = refs
    fluid, solid = fluid_ref[...], solid_ref[...]
    sides = sides_ref[...]
    needed = sorted({at for row in wanted for at in (row - 1, row, row + 1) if 0 <= at < rows})
    diagonal = {at: jnp.where(mask_ref[at : at + 1, :] != 0, solid, fluid) for at in needed}
    one = {at: spectrum_ref[at] * diagonal[at] for at in needed}
    if 0 in wanted:
        one[-1] = low_ref[...]
    if rows - 1 in wanted:
        one[rows] = high_ref[...]
    return [
        second_sweep(spectrum_ref[row], one[row], one[row - 1], one[row + 1], sides, 2 * row, diagonal[row])
        for row in wanted
    ]


def far_views(outs, half, size):
    if len(outs) == half:
        return list(outs)
    return [outs[0].at[e * size : (e + 1) * size] for e in range(half)]


def inner_kernel(rows, count, cells, outputs, *refs):
    half = count // 2
    outs = refs[-outputs:]
    sweeps = sweep_rows(range(1, rows - 1), rows, refs[:7])
    inverse_rows(sweeps, count, cells, refs[7], [*outs[:half], *far_views(outs[half:], half, (rows - 2) * cells)])


def edge_kernel(rows, count, cells, outputs, *refs):
    half = count // 2
    inner, outs = refs[8 : 8 + half], refs[-outputs:]
    sweeps = sweep_rows((0, rows - 1), rows, refs[:7])
    for d in range(half):
        outs[d][2 * cells :, :] = inner[d][...]
    inverse_rows(sweeps, count, cells, refs[7], [*outs[:half], *far_views(outs[half:], half, 2 * cells)])


def unpack_kernel(row_groups, row_count, count, cells, tiles, column, *refs):
    me = lax.axis_index("span")
    out_ref, held, done = refs[-3:]
    pitch = held.shape[0] // cells
    lines = count * tiles * row_count
    for at, (d, base, rows) in enumerate(row_groups):
        source = jnp.bitwise_xor(me, d)
        for i, row in enumerate(rows):
            for tile in range(tiles):
                held[pl.ds((source * tiles + tile) * row_count + row, cells, stride=pitch), :] = refs[at][
                    base + i * cells : base + (i + 1) * cells, tile * LANES : (tile + 1) * LANES
                ]
    copy = pltpu.make_async_copy(
        held.reshape(cells, pitch, LANES).at[:, pl.ds(0, lines)], out_ref.at[:, pl.ds(column * lines, lines)], done
    )
    copy.start()
    copy.wait()


def call(kernel, outs, args, earlier=()):
    shapes = [jax.ShapeDtypeStruct(shape, jnp.float32) for shape in outs]
    return pl.pallas_call(
        kernel,
        out_shape=shapes,
        in_specs=[VMEM] * len(args) + [ANY] * len(earlier),
        out_specs=[VMEM] * len(outs),
        compiler_params=PARAMS,
        cost_estimate=COST,
    )(*args, *earlier)


def local(pressure_source, solid_mask):
    count = lax.axis_size("span")
    plane_count = lax.axis_size("plane")
    cells, rows, columns = pressure_source.shape
    half = count // 2
    parts = 2 if columns // count >= 2 * LANES else 1
    width = columns // count // parts
    tiles = width // LANES
    lines = columns // LANES * rows
    inner = tuple(range(1, rows - 1))
    edges = (0, rows - 1)
    forward, inverse, fluid, solid = tables(cells * count, cells)
    modes = fluid.shape[0]
    forward, inverse, fluid, solid = map(jnp.asarray, (forward, inverse, fluid, solid))

    source = pressure_source.reshape(cells, rows, columns // LANES, LANES).transpose(0, 2, 1, 3).reshape(cells, lines, LANES)
    me = lax.axis_index("span")
    outside = jnp.full((rows, 1), 2, jnp.int32)
    framed = jnp.concatenate([outside, solid_mask, outside], axis=1)

    def masks(part):
        start = (part * count + me) * width
        mask = lax.dynamic_slice_in_dim(solid_mask, start, width, axis=1)
        before = lax.dynamic_slice_in_dim(framed, start, 1, axis=1)
        after = lax.dynamic_slice_in_dim(framed, start + width + 1, 1, axis=1)
        kinds = jnp.concatenate([before, after], axis=1).reshape(1, 2 * rows)
        return mask, jnp.pad(kinds, ((0, 0), (0, LANES - 2 * rows)), constant_values=2)

    size = rows * cells + 8

    def pack(jobs, sizes, earlier):
        return pl.pallas_call(
            functools.partial(pack_kernel, jobs, len(earlier), rows, count, cells, width, tiles, 4),
            out_shape=[jax.ShapeDtypeStruct((places * size, width), jnp.float32) for places in sizes],
            in_specs=[ANY] * (1 + len(earlier)),
            out_specs=[VMEM] * len(sizes),
            scratch_shapes=[
                pltpu.VMEM((cells * (lines + 8), LANES), jnp.float32),
                pltpu.SemaphoreType.DMA((4,)),
            ],
            compiler_params=PARAMS,
            cost_estimate=COST,
        )(source, *earlier)

    def swap(block, d):
        return lax.ppermute(block, "span", [(i, i ^ d) for i in range(count)])

    far = range(half, count)

    def relay(block, size):
        arrived = swap(block, half)
        return [(arrived, 0)] + [(swap(arrived[e * size : (e + 1) * size], e), 0) for e in range(1, half)]

    (first_packed,) = pack([(0, d - half, d, 0) for d in far], [half], ())
    got = [relay(first_packed, size)]
    jobs = [(part * half + d, 0, d, part) for part in range(parts) for d in range(half)]
    sizes = [1] * (parts * half)
    for part in range(1, parts):
        jobs += [(len(sizes), d - half, d, part) for d in far]
        sizes.append(half)
    packed = pack(jobs, sizes, (first_packed,))
    near = [
        [(packed[part * half], 0)] + [(swap(packed[part * half + d], d), 0) for d in range(1, half)]
        for part in range(parts)
    ]
    got += [relay(block, size) for block in packed[parts * half :]]

    up = [(i, i + 1) for i in range(plane_count - 1)]
    down = [(i + 1, i) for i in range(plane_count - 1)]
    result, earlier = None, ()
    for part in range(parts):
        last_part = part == parts - 1
        mask, kinds = masks(part)
        blocks = near[part] + got[part]
        spectrum, first, last, sides = call(
            functools.partial(forward_kernel, rows, count, cells, [base for _, base in blocks]),
            [(rows, modes, width), (modes, width), (modes, width), (modes, 16)],
            [*[block for block, _ in blocks], forward, fluid, solid, mask, kinds],
            earlier,
        )
        low = lax.ppermute(last, "plane", up)
        high = lax.ppermute(first, "plane", down)

        def outputs(near_rows, far_rows):
            far_shapes = [(far_rows * cells, width)] * half if last_part else [(half * far_rows * cells, width)]
            return [(near_rows * cells, width)] * half + far_shapes

        def send(blocks, size):
            if last_part:
                return [(swap(block, d), 0) for d, block in zip(far, blocks)]
            return relay(blocks[0], size)

        shapes = outputs(len(inner), len(inner))
        inner_out = call(
            functools.partial(inner_kernel, rows, count, cells, len(shapes)),
            shapes,
            [spectrum, sides, first, last, fluid, solid, mask, inverse],
        )
        inner_got = send(inner_out[half:], len(inner) * cells)
        shapes = outputs(rows, 2)
        edge_out = call(
            functools.partial(edge_kernel, rows, count, cells, len(shapes)),
            shapes,
            [spectrum, sides, low, high, fluid, solid, mask, inverse, *inner_out[:half]],
            (inner_out[-1],) if result is None else (result,),
        )
        earlier = (edge_out[-1],)
        edge_got = send(edge_out[half:], 2 * cells)
        pieces = [(0, 0, edges + inner, edge_out[0])]
        pieces += [(d, base, inner, block) for d, (block, base) in zip(far, inner_got)]
        pieces += [(d, base, edges, block) for d, (block, base) in zip(far, edge_got)]
        pieces += [(d, 0, edges + inner, swap(edge_out[d], d)) for d in range(1, half)]
        previous = () if result is None else (result,)
        result = pl.pallas_call(
            functools.partial(unpack_kernel, [piece[:3] for piece in pieces], rows, count, cells, tiles, part),
            out_shape=jax.ShapeDtypeStruct((cells, lines, LANES), jnp.float32),
            in_specs=[VMEM] * len(pieces) + [ANY] * len(previous),
            out_specs=ANY,
            scratch_shapes=[
                pltpu.VMEM((cells * (count * tiles * rows + 8), LANES), jnp.float32),
                pltpu.SemaphoreType.DMA,
            ],
            input_output_aliases={len(pieces): 0} if previous else {},
            compiler_params=PARAMS,
            cost_estimate=COST,
        )(*[piece[3] for piece in pieces], *previous)
    return result.reshape(cells, columns // LANES, rows, LANES).transpose(0, 2, 1, 3).reshape(cells, rows, columns)


def solution(mesh):
    placed = (P("span", "plane", None), P("plane", None))
    return jax.shard_map(
        local, mesh=mesh, in_specs=placed, out_specs=P("span", "plane", None), check_vma=False
    )
```

```python
import functools

import jax
import jax.numpy as jnp
import ml_dtypes
import numpy as np
from jax import lax
from jax.experimental import pallas as pl
from jax.experimental.pallas import tpu as pltpu
from jax.sharding import PartitionSpec as P

PENALTY = 12.0
LANES = 128
VMEM = pl.BlockSpec(memory_space=pltpu.VMEM)
ANY = pl.BlockSpec(memory_space=pl.ANY)
PARAMS = pltpu.CompilerParams(vmem_limit_bytes=16 * 1024 * 1024)
COST = pl.CostEstimate(flops=1024, bytes_accessed=1024, transcendentals=0)


def split(values):
    high = values.astype(ml_dtypes.bfloat16)
    low = (values - high.astype(np.float64)).astype(ml_dtypes.bfloat16)
    return high, low


def tables(length, cells):
    half = length // 2
    points = np.arange(half)
    groups = []
    for parity in (0, 1):
        kept = [k for k in range(length // 2 + 1) if 3 * k <= length and k % 2 == parity]
        modes = [(k, False) for k in kept] + [(k, True) for k in kept if 0 < k < length // 2]
        groups.append(modes)
    padded = -(-max(len(modes) for modes in groups) // 16) * 16
    forward = np.zeros((2, padded, half))
    inverse = np.zeros((2, half, padded))
    fluid = np.zeros((2 * padded, 1))
    solid = np.zeros((2 * padded, 1))
    for parity, modes in enumerate(groups):
        for at, (k, sine) in enumerate(modes):
            angles = (points * k % length) * (2.0 * np.pi / length)
            wave = np.sin(angles) if sine else np.cos(angles)
            weight = 1.0 if k in (0, length // 2) else 2.0
            eigen = 2.0 - 2.0 * np.cos(2.0 * np.pi * k / length)
            forward[parity, at] = wave
            inverse[parity, :, at] = wave * weight / length
            fluid[parity * padded + at] = 1.0 / (4.0 + eigen)
            solid[parity * padded + at] = 1.0 / (4.0 + eigen + PENALTY)
    blocks = half // cells
    high, low = split(forward.reshape(2, padded, blocks, cells).transpose(0, 2, 1, 3))
    forward = np.concatenate([high, low, high], axis=3)
    high, low = split(inverse.reshape(2, blocks, cells, padded))
    inverse = np.concatenate([high, low, high], axis=3)
    return forward, inverse, fluid.astype(np.float32), solid.astype(np.float32)


def thirds(values, axis):
    high = values.astype(jnp.bfloat16)
    low = (values - high.astype(jnp.float32)).astype(jnp.bfloat16)
    return jnp.concatenate([high, high, low], axis=axis)


def pack_kernel(jobs, earlier, row_count, count, cells, width, tiles, split_at, x_ref, *refs):
    outs, (held, arrived) = refs[earlier:-2], refs[-2:]
    outs[-1][...] = jnp.zeros((8, LANES), jnp.float32)
    me = lax.axis_index("span")
    lines = x_ref.shape[1]
    pitch = held.shape[0] // cells
    some = cells // split_at
    copies = [
        pltpu.make_async_copy(
            x_ref.at[pl.ds(part * some, some)],
            held.reshape(cells, pitch, LANES).at[pl.ds(part * some, some), pl.ds(0, lines)],
            arrived.at[part],
        )
        for part in range(split_at)
    ]
    for copy in copies:
        copy.start()
    lane = lax.broadcasted_iota(jnp.int32, (some, LANES), 1)
    sides = []
    for part, copy in enumerate(copies):
        copy.wait()
        beside = jnp.zeros((some, LANES), jnp.float32)

        def line(tile, row):
            return held[pl.ds(part * some * pitch + tile * row_count + row, some, stride=pitch), :]

        for job, (out, place, d, column) in enumerate(jobs):
            first = (column * count + jnp.bitwise_xor(me, d)) * tiles
            base = place * (row_count * cells + 8) + part * some
            for row in range(row_count):
                for tile in range(tiles if d else 0):
                    outs[out][base + row * cells : base + row * cells + some, tile * LANES : (tile + 1) * LANES] = line(
                        first + tile, row
                    )
                before = jnp.maximum(first - 1, 0)
                after = jnp.minimum(first + tiles, lines // row_count - 1)
                for side, (tile, source) in enumerate(((before, LANES - 1), (after, 0))):
                    at = job * 8 + row * 2 + side
                    beside = jnp.where(lane == at, pltpu.roll(line(tile, row), (at - source) % LANES, 1), beside)
        sides.append(beside)
    if cells < LANES:
        sides.append(jnp.zeros((LANES - cells, LANES), jnp.float32))
    turned = jnp.concatenate(sides, axis=0).T
    for job, (out, place, d, _) in enumerate(jobs):
        base = place * (row_count * cells + 8) + (row_count * cells if d else 0)
        outs[out][base : base + 8, :LANES] = turned[job * 8 : (job + 1) * 8]
        if width > LANES:
            outs[out][base : base + 8, LANES:] = jnp.zeros((8, width - LANES), jnp.float32)


def transform(rows, count, cells, blocks, forward_ref):
    me = lax.axis_index("span")
    half = count // 2
    spectra = []
    for i in range(rows + 1):
        parts = []
        for parity in (0, 1):
            total = None
            for d in range(half):
                table = forward_ref[parity, jnp.bitwise_and(jnp.bitwise_xor(me, d), half - 1)]
                if i < rows:
                    near = blocks[d][i * cells : (i + 1) * cells, :]
                    far = blocks[d + half][i * cells : (i + 1) * cells, :]
                else:
                    near = blocks[d][rows * cells :, :cells]
                    far = blocks[d + half][rows * cells :, :cells]
                value = near + far if parity == 0 else near - far
                if i < rows:
                    term = jnp.dot(table, thirds(value, 0), preferred_element_type=jnp.float32)
                else:
                    value = jnp.concatenate([value, jnp.zeros_like(value)], axis=0)
                    term = lax.dot_general(
                        table, thirds(value, 1), (((1,), (1,)), ((), ())), preferred_element_type=jnp.float32
                    )
                total = term if total is None else total + term
            parts.append(total)
        spectra.append(jnp.concatenate(parts, axis=0))
    return spectra[:-1], spectra[-1]


def inverse_rows(sweeps, count, cells, inverse_ref, outs):
    me = lax.axis_index("span")
    half = count // 2
    padded = sweeps[0].shape[0] // 2
    for i, sweep in enumerate(sweeps):
        even = thirds(sweep[:padded], 0)
        odd = thirds(sweep[padded:], 0)
        for d in range(half):
            place = jnp.bitwise_and(jnp.bitwise_xor(me, d), half - 1)
            first = jnp.dot(inverse_ref[0, place], even, preferred_element_type=jnp.float32)
            second = jnp.dot(inverse_ref[1, place], odd, preferred_element_type=jnp.float32)
            outs[d][i * cells : (i + 1) * cells, :] = first + second
            outs[d + half][i * cells : (i + 1) * cells, :] = first - second


def second_sweep(spectrum, one, above, below, sides, at, inverse_diagonal):
    width = one.shape[1]
    lane = lax.broadcasted_iota(jnp.int32, one.shape, 1)
    left = jnp.where(lane == 0, sides[:, at : at + 1], pltpu.roll(one, 1, 1))
    right = jnp.where(lane == width - 1, sides[:, at + 1 : at + 2], pltpu.roll(one, width - 1, 1))
    return (spectrum + above + below + left + right) * inverse_diagonal


def side_factor(side_ref, fluid, solid):
    kind = side_ref[0:1, :16]
    return jnp.where(kind == 0, fluid, jnp.where(kind == 1, solid, 0.0))


def forward_kernel(rows, count, cells, column, *refs):
    source_ref, beside_ref, blocks = refs[0], refs[1], list(refs[2 : count + 1])
    forward_ref, fluid_ref, solid_ref, mask_ref, side_ref = refs[count + 1 : count + 6]
    spectrum_ref, first_ref, last_ref, sides_ref, token_ref = refs[-5:]
    width = mask_ref.shape[1]
    tiles = width // LANES
    first = (column * count + lax.axis_index("span")) * tiles
    stride = source_ref.shape[0] // cells
    own = [
        jnp.concatenate(
            [source_ref[pl.ds((first + tile) * rows + row, cells, stride=stride), :] for tile in range(tiles)], axis=1
        )
        for row in range(rows)
    ]
    own = jnp.concatenate([*own, beside_ref[...]], axis=0)
    spectra, sides = transform(rows, count, cells, [own, *blocks], forward_ref)
    fluid, solid = fluid_ref[...], solid_ref[...]
    for row in range(rows):
        spectrum_ref[row] = spectra[row]
    first_ref[...] = spectra[0] * jnp.where(mask_ref[0:1, :] != 0, solid, fluid)
    last_ref[...] = spectra[-1] * jnp.where(mask_ref[rows - 1 : rows, :] != 0, solid, fluid)
    sides_ref[...] = sides * side_factor(side_ref, fluid, solid)
    token_ref[...] = jnp.zeros((8, LANES), jnp.float32)


def sweep_rows(wanted, rows, refs):
    spectrum_ref, sides_ref, low_ref, high_ref, fluid_ref, solid_ref, mask_ref = refs
    fluid, solid = fluid_ref[...], solid_ref[...]
    sides = sides_ref[...]
    needed = sorted({at for row in wanted for at in (row - 1, row, row + 1) if 0 <= at < rows})
    diagonal = {at: jnp.where(mask_ref[at : at + 1, :] != 0, solid, fluid) for at in needed}
    one = {at: spectrum_ref[at] * diagonal[at] for at in needed}
    if 0 in wanted:
        one[-1] = low_ref[...]
    if rows - 1 in wanted:
        one[rows] = high_ref[...]
    return [
        second_sweep(spectrum_ref[row], one[row], one[row - 1], one[row + 1], sides, 2 * row, diagonal[row])
        for row in wanted
    ]


def output_kernel(wanted, rows, count, cells, taken, outputs, *refs):
    half = count // 2
    outs, token_ref = refs[-outputs - 1 : -1], refs[-1]
    sweeps = sweep_rows(wanted, rows, refs[:7])
    size = len(wanted) * cells
    if taken:
        for d in range(half):
            outs[d][size:, :] = refs[8 + d][...]
    far = outs[half:]
    if outputs < count:
        far = [far[0].at[e * size : (e + 1) * size] for e in range(half)]
    inverse_rows(sweeps, count, cells, refs[7], [*outs[:half], *far])
    token_ref[...] = jnp.zeros((8, LANES), jnp.float32)


def unpack_kernel(row_groups, row_count, count, cells, tiles, column, *refs):
    me = lax.axis_index("span")
    out_ref, held, done = refs[-3:]
    pitch = held.shape[0] // cells
    lines = count * tiles * row_count
    for at, (d, rows) in enumerate(row_groups):
        source = jnp.bitwise_xor(me, d)
        for i, row in enumerate(rows):
            for tile in range(tiles):
                held[pl.ds((source * tiles + tile) * row_count + row, cells, stride=pitch), :] = refs[at][
                    i * cells : (i + 1) * cells, tile * LANES : (tile + 1) * LANES
                ]
    copy = pltpu.make_async_copy(
        held.reshape(cells, pitch, LANES).at[:, pl.ds(0, lines)], out_ref.at[:, pl.ds(column * lines, lines)], done
    )
    copy.start()
    copy.wait()


def call(kernel, outs, args, earlier=()):
    shapes = [jax.ShapeDtypeStruct(shape, jnp.float32) for shape in (*outs, (8, LANES))]
    return pl.pallas_call(
        kernel,
        out_shape=shapes,
        in_specs=[VMEM] * len(args) + [ANY] * len(earlier),
        out_specs=[VMEM] * len(shapes),
        compiler_params=PARAMS,
        cost_estimate=COST,
    )(*args, *earlier)


def local(pressure_source, solid_mask):
    count = lax.axis_size("span")
    plane_count = lax.axis_size("plane")
    cells, rows, columns = pressure_source.shape
    half = count // 2
    parts = 2 if columns // count >= 2 * LANES else 1
    width = columns // count // parts
    tiles = width // LANES
    lines = columns // LANES * rows
    inner = tuple(range(1, rows - 1))
    edges = (0, rows - 1)
    forward, inverse, fluid, solid = tables(cells * count, cells)
    modes = fluid.shape[0]
    forward, inverse, fluid, solid = map(jnp.asarray, (forward, inverse, fluid, solid))

    source = pressure_source.reshape(cells, rows, columns // LANES, LANES).transpose(0, 2, 1, 3).reshape(cells, lines, LANES)
    me = lax.axis_index("span")
    outside = jnp.full((rows, 1), 2, jnp.int32)
    framed = jnp.concatenate([outside, solid_mask, outside], axis=1)

    def masks(part):
        start = (part * count + me) * width
        mask = lax.dynamic_slice_in_dim(solid_mask, start, width, axis=1)
        before = lax.dynamic_slice_in_dim(framed, start, 1, axis=1)
        after = lax.dynamic_slice_in_dim(framed, start + width + 1, 1, axis=1)
        kinds = jnp.concatenate([before, after], axis=1).reshape(1, 2 * rows)
        return mask, jnp.pad(kinds, ((0, 0), (0, LANES - 2 * rows)), constant_values=2)

    size = rows * cells + 8

    def pack(jobs, sizes, earlier):
        shapes = [*[(length, width) for length in sizes], (8, LANES)]
        return pl.pallas_call(
            functools.partial(pack_kernel, jobs, len(earlier), rows, count, cells, width, tiles, 4),
            out_shape=[jax.ShapeDtypeStruct(shape, jnp.float32) for shape in shapes],
            in_specs=[ANY] * (1 + len(earlier)),
            out_specs=[VMEM] * len(shapes),
            scratch_shapes=[
                pltpu.VMEM((cells * (lines + 8), LANES), jnp.float32),
                pltpu.SemaphoreType.DMA((4,)),
            ],
            compiler_params=PARAMS,
            cost_estimate=COST,
        )(source, *earlier)

    def swap(block, d):
        return lax.ppermute(block, "span", [(i, i ^ d) for i in range(count)])

    near, far = range(1, half), range(half, count)

    def relay(block, size):
        arrived = swap(block, half)
        return [arrived] + [swap(arrived[e * size : (e + 1) * size], e) for e in near]

    got, earlier = [], ()
    for part in range(parts):
        *packed, token = pack([(d, 0, d, part) for d in range(count)], [8] + [size] * (count - 1), earlier)
        earlier = (token,)
        got.append([packed[0]] + [swap(packed[d], d) for d in range(1, count)])

    up = [(i, i + 1) for i in range(plane_count - 1)]
    down = [(i + 1, i) for i in range(plane_count - 1)]
    flat = source.reshape(cells * lines, LANES)
    everywhere = tuple(range(rows))
    states, inners, earlier = [], [], ()
    for part in range(parts):
        mask, kinds = masks(part)
        spectrum, first, last, sides, token = call(
            functools.partial(forward_kernel, rows, count, cells, part),
            [(rows, modes, width), (modes, width), (modes, width), (modes, 16)],
            [flat, *got[part], forward, fluid, solid, mask, kinds],
            earlier,
        )
        earlier = (token,)
        low = lax.ppermute(last, "plane", up)
        high = lax.ppermute(first, "plane", down)
        states.append([spectrum, sides, low, high, fluid, solid, mask, inverse])
        if part < parts - 1:
            length = len(inner) * cells
            *inner_out, token = call(
                functools.partial(output_kernel, inner, rows, count, cells, False, half + 1),
                [(length, width)] * half + [(half * length, width)],
                [spectrum, sides, first, last, fluid, solid, mask, inverse],
                earlier,
            )
            earlier = (token,)
            inners.append((inner_out[:half], relay(inner_out[half], length)))

    pieces = []
    for part in range(parts - 1):
        length = len(edges) * cells
        *edge_out, token = call(
            functools.partial(output_kernel, edges, rows, count, cells, True, half + 1),
            [(rows * cells, width)] * half + [(half * length, width)],
            [*states[part], *inners[part][0]],
            earlier,
        )
        earlier = (token, inners[part][1][-1])
        edge_got = relay(edge_out[half], length)
        pieces.append(
            [(0, edges + inner, edge_out[0])]
            + [(d, inner, block) for d, block in zip(far, inners[part][1])]
            + [(d, edges, block) for d, block in zip(far, edge_got)]
            + [(d, edges + inner, swap(edge_out[d], d)) for d in near]
        )
    *last_out, token = call(
        functools.partial(output_kernel, everywhere, rows, count, cells, False, count),
        [(rows * cells, width)] * count,
        states[-1],
        earlier,
    )
    pieces.append(
        [(0, everywhere, last_out[0])] + [(d, everywhere, swap(last_out[d], d)) for d in (*far, *near)]
    )

    result = None
    for part in range(parts):
        previous = () if result is None else (result,)
        result = pl.pallas_call(
            functools.partial(unpack_kernel, [piece[:2] for piece in pieces[part]], rows, count, cells, tiles, part),
            out_shape=jax.ShapeDtypeStruct((cells, lines, LANES), jnp.float32),
            in_specs=[VMEM] * len(pieces[part]) + [ANY] * len(previous),
            out_specs=ANY,
            scratch_shapes=[
                pltpu.VMEM((cells * (count * tiles * rows + 8), LANES), jnp.float32),
                pltpu.SemaphoreType.DMA,
            ],
            input_output_aliases={len(pieces[part]): 0} if previous else {},
            compiler_params=PARAMS,
            cost_estimate=COST,
        )(*[piece[2] for piece in pieces[part]], *previous)
    return result.reshape(cells, columns // LANES, rows, LANES).transpose(0, 2, 1, 3).reshape(cells, rows, columns)


def solution(mesh):
    placed = (P("span", "plane", None), P("plane", None))
    return jax.shard_map(
        local, mesh=mesh, in_specs=placed, out_specs=P("span", "plane", None), check_vma=False
    )
```

```python
import functools

import jax
import jax.numpy as jnp
import ml_dtypes
import numpy as np
from jax import lax
from jax.experimental import pallas as pl
from jax.experimental.pallas import tpu as pltpu
from jax.sharding import PartitionSpec as P

PENALTY = 12.0
LANES = 128
VMEM = pl.BlockSpec(memory_space=pltpu.VMEM)
ANY = pl.BlockSpec(memory_space=pl.ANY)
PARAMS = pltpu.CompilerParams(vmem_limit_bytes=24 * 1024 * 1024)
COST = pl.CostEstimate(flops=0, bytes_accessed=200_000_000, transcendentals=0)
SPLIT = 4


def split(values):
    high = values.astype(ml_dtypes.bfloat16)
    low = (values - high.astype(np.float64)).astype(ml_dtypes.bfloat16)
    return high, low


def tables(length, cells):
    half = length // 2
    points = np.arange(half)
    groups = []
    for parity in (0, 1):
        kept = [k for k in range(length // 2 + 1) if 3 * k <= length and k % 2 == parity]
        modes = [(k, False) for k in kept] + [(k, True) for k in kept if 0 < k < length // 2]
        groups.append(modes)
    padded = -(-max(len(modes) for modes in groups) // 16) * 16
    forward = np.zeros((2, padded, half))
    inverse = np.zeros((2, half, padded))
    fluid = np.zeros((2 * padded, 1))
    solid = np.zeros((2 * padded, 1))
    for parity, modes in enumerate(groups):
        for at, (k, sine) in enumerate(modes):
            angles = (points * k % length) * (2.0 * np.pi / length)
            wave = np.sin(angles) if sine else np.cos(angles)
            weight = 1.0 if k in (0, length // 2) else 2.0
            eigen = 2.0 - 2.0 * np.cos(2.0 * np.pi * k / length)
            forward[parity, at] = wave
            inverse[parity, :, at] = wave * weight / length
            fluid[parity * padded + at] = 1.0 / (4.0 + eigen)
            solid[parity * padded + at] = 1.0 / (4.0 + eigen + PENALTY)
    blocks = half // cells
    high, low = split(forward.reshape(2, padded, blocks, cells).transpose(0, 2, 1, 3))
    forward = np.concatenate([high, low, high], axis=3)
    high, low = split(inverse.reshape(2, blocks, cells, padded))
    inverse = np.concatenate([high, low, high], axis=3)
    return forward, inverse, fluid.astype(np.float32), solid.astype(np.float32)


def thirds(values, axis):
    high = values.astype(jnp.bfloat16)
    low = (values - high.astype(jnp.float32)).astype(jnp.bfloat16)
    return jnp.concatenate([high, high, low], axis=axis)


def pack_kernel(rows, row_count, count, cells, width, earlier, x_ref, *refs):
    outs, (held, arrived) = refs[earlier:-2], refs[-2:]
    me = lax.axis_index("span")
    tiles = width // LANES
    lines = x_ref.shape[1]
    pitch = held.shape[0] // cells
    some = cells // SPLIT
    copies = [
        pltpu.make_async_copy(
            x_ref.at[pl.ds(part * some, some)],
            held.reshape(cells, pitch, LANES).at[pl.ds(part * some, some), pl.ds(0, lines)],
            arrived.at[part],
        )
        for part in range(SPLIT)
    ]
    for copy in copies:
        copy.start()
    lane = lax.broadcasted_iota(jnp.int32, (some, LANES), 1)
    sides = []
    for part, copy in enumerate(copies):
        copy.wait()
        beside = jnp.zeros((some, LANES), jnp.float32)

        def line(tile, row):
            return held[pl.ds(part * some * pitch + tile * row_count + row, some, stride=pitch), :]

        for d in range(count):
            first = jnp.bitwise_xor(me, d) * tiles
            for i, row in enumerate(rows):
                base = i * cells + part * some
                for tile in range(tiles):
                    outs[d][base : base + some, tile * LANES : (tile + 1) * LANES] = line(first + tile, row)
                before = jnp.maximum(first - 1, 0)
                after = jnp.minimum(first + tiles, count * tiles - 1)
                for side, (tile, source) in enumerate(((before, LANES - 1), (after, 0))):
                    at = d * 8 + i * 2 + side
                    beside = jnp.where(lane == at, pltpu.roll(line(tile, row), (at - source) % LANES, 1), beside)
        sides.append(beside)
    if cells < LANES:
        sides.append(jnp.zeros((LANES - cells, LANES), jnp.float32))
    turned = jnp.concatenate(sides, axis=0).T
    for d in range(count):
        if width > LANES:
            outs[d][len(rows) * cells :, :] = jnp.zeros((8, width), jnp.float32)
        outs[d][len(rows) * cells :, :LANES] = turned[d * 8 : (d + 1) * 8]


def transform(rows, count, cells, blocks, forward_ref):
    me = lax.axis_index("span")
    half = count // 2
    spectra = []
    for i in range(rows + 1):
        parts = []
        for parity in (0, 1):
            total = None
            for d in range(half):
                table = forward_ref[parity, jnp.bitwise_and(jnp.bitwise_xor(me, d), half - 1)]
                if i < rows:
                    near = blocks[d][i * cells : (i + 1) * cells, :]
                    far = blocks[d + half][i * cells : (i + 1) * cells, :]
                else:
                    near = blocks[d][rows * cells :, :cells]
                    far = blocks[d + half][rows * cells :, :cells]
                value = near + far if parity == 0 else near - far
                if i < rows:
                    term = jnp.dot(table, thirds(value, 0), preferred_element_type=jnp.float32)
                else:
                    value = jnp.concatenate([value, jnp.zeros_like(value)], axis=0)
                    term = lax.dot_general(
                        table, thirds(value, 1), (((1,), (1,)), ((), ())), preferred_element_type=jnp.float32
                    )
                total = term if total is None else total + term
            parts.append(total)
        spectra.append(jnp.concatenate(parts, axis=0))
    return spectra[:-1], spectra[-1]


def inverse_rows(sweeps, count, cells, inverse_ref, outs):
    me = lax.axis_index("span")
    half = count // 2
    padded = sweeps[0].shape[0] // 2
    for i, sweep in enumerate(sweeps):
        even = thirds(sweep[:padded], 0)
        odd = thirds(sweep[padded:], 0)
        for d in range(half):
            place = jnp.bitwise_and(jnp.bitwise_xor(me, d), half - 1)
            first = jnp.dot(inverse_ref[0, place], even, preferred_element_type=jnp.float32)
            second = jnp.dot(inverse_ref[1, place], odd, preferred_element_type=jnp.float32)
            outs[d][i * cells : (i + 1) * cells, :] = first + second
            outs[d + half][i * cells : (i + 1) * cells, :] = first - second


def second_sweep(spectrum, one, above, below, sides, at, inverse_diagonal):
    width = one.shape[1]
    lane = lax.broadcasted_iota(jnp.int32, one.shape, 1)
    left = jnp.where(lane == 0, sides[:, at : at + 1], pltpu.roll(one, 1, 1))
    right = jnp.where(lane == width - 1, sides[:, at + 1 : at + 2], pltpu.roll(one, width - 1, 1))
    return (spectrum + above + below + left + right) * inverse_diagonal


def edge_kernel(count, cells, *refs):
    blocks, (forward_ref, fluid_ref, solid_ref, mask_ref, side_ref), outs = refs[:count], refs[count : count + 5], refs[count + 5 :]
    spectrum_ref, first_ref, last_ref, sides_ref = outs
    spectra, sides = transform(2, count, cells, blocks, forward_ref)
    fluid, solid = fluid_ref[...], solid_ref[...]
    for i, one_ref in enumerate((first_ref, last_ref)):
        spectrum_ref[i] = spectra[i]
        one_ref[...] = spectra[i] * jnp.where(mask_ref[i : i + 1, :] != 0, solid, fluid)
    sides_ref[...] = sides * side_factor(side_ref, fluid, solid)


def side_factor(side_ref, fluid, solid):
    kind = side_ref[0:1, :16]
    return jnp.where(kind == 0, fluid, jnp.where(kind == 1, solid, 0.0))


def inner_kernel(rows, count, cells, *refs):
    blocks, rest = refs[:count], refs[count:]
    forward_ref, inverse_ref, fluid_ref, solid_ref, mask_ref, side_ref, first_ref, last_ref = rest[:8]
    outs, ones_ref = rest[8 : 8 + count], rest[8 + count]
    spectra, sides = transform(rows, count, cells, blocks, forward_ref)
    fluid, solid = fluid_ref[...], solid_ref[...]
    sides = sides * side_factor(side_ref, fluid, solid)
    diagonals = [jnp.where(mask_ref[i : i + 1, :] != 0, solid, fluid) for i in range(rows)]
    ones = [spectra[i] * diagonals[i] for i in range(rows)]
    ones_ref[0] = ones[0]
    ones_ref[1] = ones[-1]
    around = [first_ref[...]] + ones + [last_ref[...]]
    sweeps = [
        second_sweep(spectra[i], ones[i], around[i], around[i + 2], sides, 2 * i, diagonals[i]) for i in range(rows)
    ]
    inverse_rows(sweeps, count, cells, inverse_ref, outs)


def rim_kernel(count, cells, *refs):
    spectrum_ref, first_ref, last_ref, sides_ref, ones_ref, low_ref, high_ref = refs[:7]
    inverse_ref, fluid_ref, solid_ref, mask_ref = refs[7:11]
    outs = refs[11:]
    fluid, solid = fluid_ref[...], solid_ref[...]
    sides = sides_ref[...]
    sweeps = []
    for i, (one, above, below) in enumerate(
        ((first_ref, low_ref, ones_ref.at[0]), (last_ref, ones_ref.at[1], high_ref))
    ):
        diagonal = jnp.where(mask_ref[i : i + 1, :] != 0, solid, fluid)
        sweeps.append(second_sweep(spectrum_ref[i], one[...], above[...], below[...], sides, 2 * i, diagonal))
    inverse_rows(sweeps, count, cells, inverse_ref, outs)


def unpack_kernel(row_groups, row_count, count, cells, width, *refs):
    me = lax.axis_index("span")
    tiles = width // LANES
    blocks, (out_ref, held, done) = refs[:-3], refs[-3:]
    pitch = held.shape[0] // cells
    lines = out_ref.shape[1]
    some = cells // SPLIT
    copies = []
    for part in range(SPLIT):
        for g, rows in enumerate(row_groups):
            for d in range(count):
                source = jnp.bitwise_xor(me, d)
                for i, row in enumerate(rows):
                    base = i * cells + part * some
                    for tile in range(tiles):
                        at = part * some * pitch + (source * tiles + tile) * row_count + row
                        held[pl.ds(at, some, stride=pitch), :] = blocks[g * count + d][
                            base : base + some, tile * LANES : (tile + 1) * LANES
                        ]
        copies.append(
            pltpu.make_async_copy(
                held.reshape(cells, pitch, LANES).at[pl.ds(part * some, some), pl.ds(0, lines)],
                out_ref.at[pl.ds(part * some, some)],
                done.at[part],
            )
        )
        copies[-1].start()
    for copy in copies:
        copy.wait()


def call(kernel, outs, *args):
    shapes = [jax.ShapeDtypeStruct(shape, jnp.float32) for shape in outs]
    return pl.pallas_call(
        kernel,
        out_shape=shapes,
        in_specs=[VMEM] * len(args),
        out_specs=[VMEM] * len(outs),
        compiler_params=PARAMS,
        cost_estimate=COST,
    )(*args)


def exchange(blocks):
    count = len(blocks)
    return [blocks[0]] + [
        lax.ppermute(blocks[d], "span", [(i, i ^ d) for i in range(count)]) for d in range(1, count)
    ]


def local(pressure_source, solid_mask):
    count = lax.axis_size("span")
    plane_count = lax.axis_size("plane")
    cells, row_count, columns = pressure_source.shape
    width = columns // count
    tiles = columns // LANES
    inner = tuple(range(1, row_count - 1))
    edges = (0, row_count - 1)
    forward, inverse, fluid, solid = tables(cells * count, cells)
    modes = fluid.shape[0]
    forward, inverse, fluid, solid = map(jnp.asarray, (forward, inverse, fluid, solid))

    source = pressure_source.reshape(cells, row_count, tiles, LANES).transpose(0, 2, 1, 3)
    source = source.reshape(cells, tiles * row_count, LANES)

    me = lax.axis_index("span")
    mask = lax.dynamic_slice_in_dim(solid_mask, me * width, width, axis=1)
    outside = jnp.full((row_count, 1), 2, jnp.int32)
    framed = jnp.concatenate([outside, solid_mask, outside], axis=1)
    before = lax.dynamic_slice_in_dim(framed, me * width, 1, axis=1)
    after = lax.dynamic_slice_in_dim(framed, me * width + width + 1, 1, axis=1)
    beside = jnp.concatenate([before, after], axis=1)

    def picked(rows):
        kinds = jnp.concatenate([beside[row] for row in rows])
        kinds = jnp.pad(kinds, (0, LANES - kinds.shape[0]), constant_values=2)
        return jnp.stack([mask[row] for row in rows]), kinds[None, :]

    edge_mask, edge_sides = picked(edges)
    inner_mask, inner_sides = picked(inner)

    lines = tiles * row_count
    scratch = [pltpu.VMEM((cells * (lines + 8), LANES), jnp.float32), pltpu.SemaphoreType.DMA((SPLIT,))]

    def pack(rows, *earlier):
        return pl.pallas_call(
            functools.partial(pack_kernel, rows, row_count, count, cells, width, len(earlier)),
            out_shape=[jax.ShapeDtypeStruct((len(rows) * cells + 8, width), jnp.float32)] * count,
            in_specs=[ANY] * (1 + len(earlier)),
            out_specs=[VMEM] * count,
            scratch_shapes=scratch,
            compiler_params=PARAMS,
            cost_estimate=COST,
        )(source, *earlier)

    edge_blocks = exchange(pack(edges))
    inner_blocks = exchange(pack(inner, edge_blocks[1]))
    spectrum, first, last, sides = call(
        functools.partial(edge_kernel, count, cells),
        [(2, modes, width), (modes, width), (modes, width), (modes, 16)],
        *edge_blocks, forward, fluid, solid, edge_mask, edge_sides,
    )
    up = [(i, i + 1) for i in range(plane_count - 1)]
    down = [(i + 1, i) for i in range(plane_count - 1)]
    low = lax.ppermute(last, "plane", up)
    high = lax.ppermute(first, "plane", down)
    *inner_out, ones = call(
        functools.partial(inner_kernel, len(inner), count, cells),
        [(len(inner) * cells, width)] * count + [(2, modes, width)],
        *inner_blocks, forward, inverse, fluid, solid, inner_mask, inner_sides, first, last,
    )
    inner_got = exchange(inner_out)
    edge_out = call(
        functools.partial(rim_kernel, count, cells),
        [(2 * cells, width)] * count,
        spectrum, first, last, sides, ones, low, high, inverse, fluid, solid, edge_mask,
    )
    edge_got = exchange(edge_out)
    blocks = [*inner_got, *edge_got]
    result = pl.pallas_call(
        functools.partial(unpack_kernel, (inner, edges), row_count, count, cells, width),
        out_shape=jax.ShapeDtypeStruct((cells, lines, LANES), jnp.float32),
        in_specs=[VMEM] * len(blocks),
        out_specs=ANY,
        scratch_shapes=scratch,
        compiler_params=PARAMS,
        cost_estimate=COST,
    )(*blocks)
    return result.reshape(cells, tiles, row_count, LANES).transpose(0, 2, 1, 3).reshape(cells, row_count, columns)


def solution(mesh):
    placed = (P("span", "plane", None), P("plane", None))
    return jax.shard_map(
        local, mesh=mesh, in_specs=placed, out_specs=P("span", "plane", None), check_vma=False
    )
```

```python
import functools

import jax
import jax.numpy as jnp
import ml_dtypes
import numpy as np
from jax import lax
from jax.experimental import pallas as pl
from jax.experimental.pallas import tpu as pltpu
from jax.sharding import PartitionSpec as P

PENALTY = 12.0
LANES = 128
VMEM = pl.BlockSpec(memory_space=pltpu.VMEM)
ANY = pl.BlockSpec(memory_space=pl.ANY)
PARAMS = pltpu.CompilerParams(vmem_limit_bytes=24 * 1024 * 1024)
LONG = pl.CostEstimate(flops=0, bytes_accessed=200_000_000, transcendentals=0)
SHORT = pl.CostEstimate(flops=0, bytes_accessed=1024, transcendentals=0)
SPLIT = 4
HEAD_LIMIT = 24


def split(values):
    high = values.astype(ml_dtypes.bfloat16)
    low = (values - high.astype(np.float64)).astype(ml_dtypes.bfloat16)
    return high, low


def tables(length, cells):
    half = length // 2
    points = np.arange(half)
    groups = []
    for parity in (0, 1):
        kept = [k for k in range(length // 2 + 1) if 3 * k <= length and k % 2 == parity]
        modes = [(k, False) for k in kept] + [(k, True) for k in kept if 0 < k < length // 2]
        groups.append(modes)
    padded = -(-max(len(modes) for modes in groups) // 16) * 16
    forward = np.zeros((2, padded, half))
    inverse = np.zeros((2, half, padded))
    fluid = np.zeros((2 * padded, 1))
    solid = np.zeros((2 * padded, 1))
    for parity, modes in enumerate(groups):
        for at, (k, sine) in enumerate(modes):
            angles = (points * k % length) * (2.0 * np.pi / length)
            wave = np.sin(angles) if sine else np.cos(angles)
            weight = 1.0 if k in (0, length // 2) else 2.0
            eigen = 2.0 - 2.0 * np.cos(2.0 * np.pi * k / length)
            forward[parity, at] = wave
            inverse[parity, :, at] = wave * weight / length
            fluid[parity * padded + at] = 1.0 / (4.0 + eigen)
            solid[parity * padded + at] = 1.0 / (4.0 + eigen + PENALTY)
    columns = np.zeros((8, -(-2 * padded // LANES) * LANES), np.float32)
    columns[0, : 2 * padded] = fluid[:, 0]
    columns[1, : 2 * padded] = solid[:, 0]
    blocks = half // cells
    high, low = split(forward.reshape(2, padded, blocks, cells).transpose(0, 2, 1, 3))
    forward = np.concatenate([high, low, high], axis=3)
    high, low = split(inverse.reshape(2, blocks, cells, padded))
    inverse = np.concatenate([high, low, high], axis=3)
    return forward, inverse, columns


def thirds(values, axis):
    high = values.astype(jnp.bfloat16)
    low = (values - high.astype(jnp.float32)).astype(jnp.bfloat16)
    return jnp.concatenate([high, high, low], axis=axis)


def pack_kernel(jobs, row_count, cells, earlier, x_ref, *refs):
    outs, (held, arrived) = refs[earlier:-2], refs[-2:]
    me = lax.axis_index("span")
    lines = x_ref.shape[1]
    all_tiles = lines // row_count
    own_tiles = all_tiles // lax.axis_size("span")
    pitch = held.shape[0] // cells
    some = cells // SPLIT
    copies = [
        pltpu.make_async_copy(
            x_ref.at[pl.ds(part * some, some)],
            held.reshape(cells, pitch, LANES).at[pl.ds(part * some, some), pl.ds(0, lines)],
            arrived.at[part],
        )
        for part in range(SPLIT)
    ]
    for copy in copies:
        copy.start()
    lane = lax.broadcasted_iota(jnp.int32, (some, LANES), 1)
    sides = []
    for part, copy in enumerate(copies):
        copy.wait()
        beside = jnp.zeros((some, LANES), jnp.float32)

        def line(tile, row):
            return held[pl.ds(part * some * pitch + tile * row_count + row, some, stride=pitch), :]

        for job, (out, base, d, rows, offset, tiles) in enumerate(jobs):
            first = jnp.bitwise_xor(me, d) * own_tiles + offset
            for i, row in enumerate(rows):
                at = base + i * cells + part * some
                for tile in range(tiles):
                    outs[out][at : at + some, tile * LANES : (tile + 1) * LANES] = line(first + tile, row)
                before = jnp.maximum(first - 1, 0)
                after = jnp.minimum(first + tiles, all_tiles - 1)
                for side, (tile, source) in enumerate(((before, LANES - 1), (after, 0))):
                    at = job * 8 + i * 2 + side
                    beside = jnp.where(lane == at, pltpu.roll(line(tile, row), (at - source) % LANES, 1), beside)
        sides.append(beside)
    if cells < LANES:
        sides.append(jnp.zeros((LANES - cells, LANES), jnp.float32))
    turned = jnp.concatenate(sides, axis=0).T
    for job, (out, base, _, rows, _, tiles) in enumerate(jobs):
        at = base + len(rows) * cells
        outs[out][at : at + 8, :LANES] = turned[job * 8 : (job + 1) * 8]
        if tiles > 1:
            outs[out][at : at + 8, LANES:] = jnp.zeros((8, (tiles - 1) * LANES), jnp.float32)


def transform(rows, count, cells, blocks, forward_ref):
    me = lax.axis_index("span")
    half = count // 2
    spectra = []
    for i in range(rows + 1):
        parts = []
        for parity in (0, 1):
            total = None
            for d in range(half):
                table = forward_ref[parity, jnp.bitwise_and(jnp.bitwise_xor(me, d), half - 1)]
                if i < rows:
                    near = blocks[d][i * cells : (i + 1) * cells, :]
                    far = blocks[d + half][i * cells : (i + 1) * cells, :]
                else:
                    near = blocks[d][rows * cells :, :cells]
                    far = blocks[d + half][rows * cells :, :cells]
                value = near + far if parity == 0 else near - far
                if i < rows:
                    term = jnp.dot(table, thirds(value, 0), preferred_element_type=jnp.float32)
                else:
                    value = jnp.concatenate([value, jnp.zeros_like(value)], axis=0)
                    term = lax.dot_general(
                        table, thirds(value, 1), (((1,), (1,)), ((), ())), preferred_element_type=jnp.float32
                    )
                total = term if total is None else total + term
            parts.append(total)
        spectra.append(jnp.concatenate(parts, axis=0))
    return spectra[:-1], spectra[-1]


def inverse_rows(sweeps, count, cells, inverse_ref, outs):
    me = lax.axis_index("span")
    half = count // 2
    padded = sweeps[0].shape[0] // 2
    for i, sweep in enumerate(sweeps):
        even = thirds(sweep[:padded], 0)
        odd = thirds(sweep[padded:], 0)
        for d in range(half):
            place = jnp.bitwise_and(jnp.bitwise_xor(me, d), half - 1)
            first = jnp.dot(inverse_ref[0, place], even, preferred_element_type=jnp.float32)
            second = jnp.dot(inverse_ref[1, place], odd, preferred_element_type=jnp.float32)
            outs[d][i * cells : (i + 1) * cells, :] = first + second
            outs[d + half][i * cells : (i + 1) * cells, :] = first - second


def second_sweep(spectrum, one, above, below, sides, at, inverse_diagonal):
    width = one.shape[1]
    lane = lax.broadcasted_iota(jnp.int32, one.shape, 1)
    left = jnp.where(lane == 0, sides[:, at : at + 1], pltpu.roll(one, 1, 1))
    right = jnp.where(lane == width - 1, sides[:, at + 1 : at + 2], pltpu.roll(one, width - 1, 1))
    return (spectrum + above + below + left + right) * inverse_diagonal


def reciprocals(mask_ref, columns_ref, modes, rows, offset, width):
    turned = columns_ref[...].T
    fluid, solid = turned[:modes, 0:1], turned[:modes, 1:2]
    own = mask_ref.shape[1] // lax.axis_size("span")
    start = pl.multiple_of(lax.axis_index("span") * own + offset, LANES)
    last = mask_ref.shape[1] - LANES
    before = mask_ref[:, pl.ds(pl.multiple_of(jnp.maximum(start - LANES, 0), LANES), LANES)][:, LANES - 1 :]
    after = mask_ref[:, pl.ds(pl.multiple_of(jnp.minimum(start + width, last), LANES), LANES)][:, :1]
    before = jnp.where(start == 0, 2, before)
    after = jnp.where(start + width == mask_ref.shape[1], 2, after)
    lane = lax.broadcasted_iota(jnp.int32, (1, 16), 1)
    kinds = jnp.full((1, 16), 2, jnp.int32)
    diagonals = []
    for i, row in enumerate(rows):
        kinds = jnp.where(lane == 2 * i, before[row : row + 1], kinds)
        kinds = jnp.where(lane == 2 * i + 1, after[row : row + 1], kinds)
        mask = mask_ref[row : row + 1, pl.ds(start, width)]
        diagonals.append(jnp.where(mask != 0, solid, fluid))
    return diagonals, jnp.where(kinds == 0, fluid, jnp.where(kinds == 1, solid, 0.0))


def views(refs, places, size):
    return [ref.at[base : base + size] for ref, base in zip(refs, places)]


def edge_kernel(rows, count, cells, *refs):
    blocks, (forward_ref, columns_ref, mask_ref) = refs[:count], refs[count : count + 3]
    spectrum_ref, first_ref, last_ref, sides_ref = refs[count + 3 :]
    spectra, sides = transform(len(rows), count, cells, blocks, forward_ref)
    modes, width = spectra[0].shape
    diagonals, beside = reciprocals(mask_ref, columns_ref, modes, rows, 0, width)
    for i, one_ref in enumerate((first_ref, last_ref)):
        spectrum_ref[i] = spectra[i]
        one_ref[...] = spectra[i] * diagonals[i]
    sides_ref[...] = sides * beside


def inner_kernel(rows, count, cells, offset, width, places, *refs):
    half = count // 2
    blocks = views(refs, places, len(rows) * cells + 8)
    forward_ref, inverse_ref, columns_ref, mask_ref, first_ref, last_ref = refs[count : count + 6]
    outs, far_ref, ones_ref = refs[-2 - half : -2], refs[-2], refs[-1]
    spectra, sides = transform(len(rows), count, cells, blocks, forward_ref)
    diagonals, beside = reciprocals(mask_ref, columns_ref, spectra[0].shape[0], rows, offset, width)
    sides = sides * beside
    ones = [spectrum * diagonal for spectrum, diagonal in zip(spectra, diagonals)]
    ones_ref[0] = ones[0]
    ones_ref[1] = ones[-1]
    around = [first_ref[:, offset : offset + width], *ones, last_ref[:, offset : offset + width]]
    sweeps = [
        second_sweep(spectra[i], ones[i], around[i], around[i + 2], sides, 2 * i, diagonals[i])
        for i in range(len(rows))
    ]
    size = len(rows) * cells
    inverse_rows(sweeps, count, cells, inverse_ref, [*outs, *views([far_ref] * half, range(0, half * size, size), size)])


def rim_kernel(rows, parts, count, cells, *refs):
    spectrum_ref, first_ref, last_ref, sides_ref, low_ref, high_ref, inverse_ref, columns_ref, mask_ref = refs[:9]
    ones, outs = refs[9 : 9 + parts], refs[-count:]
    modes, width = first_ref.shape
    diagonals, _ = reciprocals(mask_ref, columns_ref, modes, rows, 0, width)
    sides = sides_ref[...]
    inner = [jnp.concatenate([one[i] for one in ones], axis=1) for i in (0, 1)]
    sweeps = [
        second_sweep(spectrum_ref[0], first_ref[...], low_ref[...], inner[0], sides, 0, diagonals[0]),
        second_sweep(spectrum_ref[1], last_ref[...], inner[1], high_ref[...], sides, 2, diagonals[1]),
    ]
    inverse_rows(sweeps, count, cells, inverse_ref, outs)


def unpack_kernel(pieces, row_count, cells, *refs):
    me = lax.axis_index("span")
    blocks, (out_ref, held, done) = refs[:-3], refs[-3:]
    pitch = held.shape[0] // cells
    lines = out_ref.shape[1]
    own_tiles = lines // row_count // lax.axis_size("span")
    some = cells // SPLIT
    copies = []
    for part in range(SPLIT):
        for block, (d, base, rows, offset, tiles) in zip(blocks, pieces):
            first = jnp.bitwise_xor(me, d) * own_tiles + offset
            for i, row in enumerate(rows):
                line = base + i * cells + part * some
                for tile in range(tiles):
                    at = part * some * pitch + (first + tile) * row_count + row
                    held[pl.ds(at, some, stride=pitch), :] = block[line : line + some, tile * LANES : (tile + 1) * LANES]
        copies.append(
            pltpu.make_async_copy(
                held.reshape(cells, pitch, LANES).at[pl.ds(part * some, some), pl.ds(0, lines)],
                out_ref.at[pl.ds(part * some, some)],
                done.at[part],
            )
        )
        copies[-1].start()
    for copy in copies:
        copy.wait()


def call(kernel, outs, *args, cost=LONG, earlier=()):
    shapes = [jax.ShapeDtypeStruct(shape, jnp.float32) for shape in outs]
    return pl.pallas_call(
        kernel,
        out_shape=shapes,
        in_specs=[VMEM] * len(args) + [ANY] * len(earlier),
        out_specs=[VMEM] * len(outs),
        compiler_params=PARAMS,
        cost_estimate=cost,
    )(*args, *earlier)


def swap(block, d):
    return lax.ppermute(block, "span", [(i, i ^ d) for i in range(lax.axis_size("span"))])


def local(pressure_source, solid_mask):
    count = lax.axis_size("span")
    half = count // 2
    plane_count = lax.axis_size("plane")
    cells, row_count, columns = pressure_source.shape
    width = columns // count
    tiles = width // LANES
    parts = 2 if tiles % 2 == 0 else 1
    part_tiles, part_width = tiles // parts, width // parts
    inner = tuple(range(1, row_count - 1))
    edges = (0, row_count - 1)
    near, far = range(1, half), range(half, count)
    forward, inverse, one_over = map(jnp.asarray, tables(cells * count, cells))
    modes = 2 * forward.shape[2]

    lines = columns // LANES * row_count
    source = pressure_source.reshape(cells, row_count, columns // LANES, LANES).transpose(0, 2, 1, 3)
    source = source.reshape(cells, lines, LANES)
    scratch = [pltpu.VMEM((cells * (lines + 8), LANES), jnp.float32), pltpu.SemaphoreType.DMA((SPLIT,))]

    def pack(jobs, shapes, limit, *earlier):
        return pl.pallas_call(
            functools.partial(pack_kernel, jobs, row_count, cells, len(earlier)),
            out_shape=[jax.ShapeDtypeStruct(shape, jnp.float32) for shape in shapes],
            in_specs=[ANY] * (1 + len(earlier)),
            out_specs=[VMEM] * len(shapes),
            scratch_shapes=scratch,
            compiler_params=pltpu.CompilerParams(vmem_limit_bytes=limit * 1024 * 1024),
            cost_estimate=LONG,
        )(source, *earlier)

    edge_size, size = len(edges) * cells + 8, len(inner) * cells + 8
    jobs = [(d - 1, 0, d, edges, 0, tiles) for d in range(1, count)]
    packed = pack(jobs, [(edge_size, width)] * (count - 1), HEAD_LIMIT)
    edge_blocks = [swap(block, d) for d, block in enumerate(packed, 1)]
    jobs, shapes = [(0, 0, 0, edges, 0, tiles)], [(edge_size, width)]

    def add(d, wanted):
        jobs.extend(
            (len(shapes), at * size, d, inner, part * part_tiles, part_tiles) for at, part in enumerate(wanted)
        )
        shapes.append((len(wanted) * size, part_width))

    for d in range(half):
        add(d, range(parts))
    for part in range(parts):
        for d in far:
            add(d, [part])
    packed = pack(jobs, shapes, 24, *edge_blocks[: half - 1])
    edge_blocks = [packed[0], *edge_blocks]
    near_blocks = [packed[1]] + [swap(packed[1 + d], d) for d in near]
    far_blocks = []
    for part in range(parts):
        mine = packed[1 + half * (part + 1) : 1 + half * (part + 2)]
        message = [mine[0]] + [swap(mine[d], d) for d in near]
        far_blocks.append(swap(jnp.concatenate(message), half))

    spectrum, first, last, sides = call(
        functools.partial(edge_kernel, edges, count, cells),
        [(2, modes, width), (modes, width), (modes, width), (modes, 16)],
        *edge_blocks, forward, one_over, solid_mask,
    )
    up = [(i, i + 1) for i in range(plane_count - 1)]
    down = [(i + 1, i) for i in range(plane_count - 1)]
    low = lax.ppermute(last, "plane", up)
    high = lax.ppermute(first, "plane", down)

    ones, made, arrived, pieces, earlier = [], [], [], [], ()
    size = len(inner) * cells
    for part in range(parts):
        blocks = [(block, part * (size + 8)) for block in near_blocks]
        blocks += [(far_blocks[part], e * (size + 8)) for e in range(half)]
        offset = part * part_width
        *outs, one = call(
            functools.partial(
                inner_kernel, inner, count, cells, offset, part_width, [base for _, base in blocks]
            ),
            [(size, part_width)] * half + [(half * size, part_width), (2, modes, part_width)],
            *[block for block, _ in blocks], forward, inverse, one_over, solid_mask, first, last,
            cost=SHORT, earlier=earlier,
        )
        ones.append(one)
        earlier = (one,)
        made.append(outs[:half])
        arrived.append(swap(outs[half], half))

    def place(part):
        return inner, part * part_tiles, part_tiles

    def onward(part, d):
        return arrived[part][d * size : (d + 1) * size]

    earlier = list(arrived[:-1])
    for part in range(parts):
        pieces += [(made[part][0], 0, 0, *place(part)), (arrived[part], half, 0, *place(part))]
        for d in near:
            if part < parts - 1:
                message = swap(jnp.concatenate([onward(part, d), made[part][d]]), d)
                pieces += [(message, half + d, 0, *place(part)), (message, d, size, *place(part))]
            else:
                earlier.append(swap(made[part][d], d))
                pieces += [(earlier[-1], d, 0, *place(part))]
                pieces += [(swap(onward(part, d), d), half + d, 0, *place(part))]
    outs = call(
        functools.partial(rim_kernel, edges, parts, count, cells),
        [(len(edges) * cells, width)] * count,
        spectrum, first, last, sides, low, high, inverse, one_over, solid_mask, *ones, earlier=tuple(earlier),
    )
    pieces.append((outs[0], 0, 0, edges, 0, tiles))
    pieces += [(swap(outs[d], d), d, 0, edges, 0, tiles) for d in (*far, *near)]
    result = pl.pallas_call(
        functools.partial(unpack_kernel, [piece[1:] for piece in pieces], row_count, cells),
        out_shape=jax.ShapeDtypeStruct((cells, lines, LANES), jnp.float32),
        in_specs=[VMEM] * len(pieces),
        out_specs=ANY,
        scratch_shapes=scratch,
        compiler_params=PARAMS,
        cost_estimate=LONG,
    )(*[piece[0] for piece in pieces])
    result = result.reshape(cells, columns // LANES, row_count, LANES).transpose(0, 2, 1, 3)
    return result.reshape(cells, row_count, columns)


def solution(mesh):
    placed = (P("span", "plane", None), P("plane", None))
    return jax.shard_map(
        local, mesh=mesh, in_specs=placed, out_specs=P("span", "plane", None), check_vma=False
    )
```

```python
import functools

import jax
import jax.numpy as jnp
import ml_dtypes
import numpy as np
from jax import lax
from jax.experimental import pallas as pl
from jax.experimental.pallas import tpu as pltpu
from jax.sharding import PartitionSpec as P

PENALTY = 12.0
LANES = 128
VMEM = pl.BlockSpec(memory_space=pltpu.VMEM)
ANY = pl.BlockSpec(memory_space=pl.ANY)
PARAMS = pltpu.CompilerParams(vmem_limit_bytes=24 * 1024 * 1024)
LONG = pl.CostEstimate(flops=0, bytes_accessed=200_000_000, transcendentals=0)
SHORT = pl.CostEstimate(flops=0, bytes_accessed=1024, transcendentals=0)
SPLIT = 4


def split(values):
    high = values.astype(ml_dtypes.bfloat16)
    low = (values - high.astype(np.float64)).astype(ml_dtypes.bfloat16)
    return high, low


def tables(length, cells):
    half = length // 2
    points = np.arange(half)
    groups = []
    for parity in (0, 1):
        kept = [k for k in range(length // 2 + 1) if 3 * k <= length and k % 2 == parity]
        modes = [(k, False) for k in kept] + [(k, True) for k in kept if 0 < k < length // 2]
        groups.append(modes)
    padded = -(-max(len(modes) for modes in groups) // 16) * 16
    forward = np.zeros((2, padded, half))
    inverse = np.zeros((2, half, padded))
    fluid = np.zeros((2 * padded, 1))
    solid = np.zeros((2 * padded, 1))
    for parity, modes in enumerate(groups):
        for at, (k, sine) in enumerate(modes):
            angles = (points * k % length) * (2.0 * np.pi / length)
            wave = np.sin(angles) if sine else np.cos(angles)
            weight = 1.0 if k in (0, length // 2) else 2.0
            eigen = 2.0 - 2.0 * np.cos(2.0 * np.pi * k / length)
            forward[parity, at] = wave
            inverse[parity, :, at] = wave * weight / length
            fluid[parity * padded + at] = 1.0 / (4.0 + eigen)
            solid[parity * padded + at] = 1.0 / (4.0 + eigen + PENALTY)
    columns = np.zeros((8, -(-2 * padded // LANES) * LANES), np.float32)
    columns[0, : 2 * padded] = fluid[:, 0]
    columns[1, : 2 * padded] = solid[:, 0]
    blocks = half // cells
    high, low = split(forward.reshape(2, padded, blocks, cells).transpose(0, 2, 1, 3))
    forward = np.concatenate([high, low, high], axis=3)
    high, low = split(inverse.reshape(2, blocks, cells, padded))
    inverse = np.concatenate([high, low, high], axis=3)
    return forward, inverse, columns


def thirds(values, axis):
    high = values.astype(jnp.bfloat16)
    low = (values - high.astype(jnp.float32)).astype(jnp.bfloat16)
    return jnp.concatenate([high, high, low], axis=axis)


def pack_kernel(jobs, row_count, cells, x_ref, *refs):
    outs, (held, arrived) = refs[:-2], refs[-2:]
    me = lax.axis_index("span")
    lines = x_ref.shape[1]
    all_tiles = lines // row_count
    own_tiles = all_tiles // lax.axis_size("span")
    pitch = held.shape[0] // cells
    some = cells // SPLIT
    copies = [
        pltpu.make_async_copy(
            x_ref.at[pl.ds(part * some, some)],
            held.reshape(cells, pitch, LANES).at[pl.ds(part * some, some), pl.ds(0, lines)],
            arrived.at[part],
        )
        for part in range(SPLIT)
    ]
    for copy in copies:
        copy.start()
    lane = lax.broadcasted_iota(jnp.int32, (some, LANES), 1)
    sides = []
    for part, copy in enumerate(copies):
        copy.wait()
        beside = jnp.zeros((some, LANES), jnp.float32)

        def line(tile, row):
            return held[pl.ds(part * some * pitch + tile * row_count + row, some, stride=pitch), :]

        for job, (out, base, d, rows, offset, tiles) in enumerate(jobs):
            first = jnp.bitwise_xor(me, d) * own_tiles + offset
            for i, row in enumerate(rows):
                at = base + i * cells + part * some
                for tile in range(tiles):
                    outs[out][at : at + some, tile * LANES : (tile + 1) * LANES] = line(first + tile, row)
                before = jnp.maximum(first - 1, 0)
                after = jnp.minimum(first + tiles, all_tiles - 1)
                for side, (tile, source) in enumerate(((before, LANES - 1), (after, 0))):
                    at = job * 8 + i * 2 + side
                    beside = jnp.where(lane == at, pltpu.roll(line(tile, row), (at - source) % LANES, 1), beside)
        sides.append(beside)
    if cells < LANES:
        sides.append(jnp.zeros((LANES - cells, LANES), jnp.float32))
    turned = jnp.concatenate(sides, axis=0).T
    for job, (out, base, _, rows, _, tiles) in enumerate(jobs):
        at = base + len(rows) * cells
        outs[out][at : at + 8, :LANES] = turned[job * 8 : (job + 1) * 8]
        if tiles > 1:
            outs[out][at : at + 8, LANES:] = jnp.zeros((8, (tiles - 1) * LANES), jnp.float32)


def transform(rows, count, cells, blocks, forward_ref):
    me = lax.axis_index("span")
    half = count // 2
    spectra = []
    for i in range(rows + 1):
        parts = []
        for parity in (0, 1):
            total = None
            for d in range(half):
                table = forward_ref[parity, jnp.bitwise_and(jnp.bitwise_xor(me, d), half - 1)]
                if i < rows:
                    near = blocks[d][i * cells : (i + 1) * cells, :]
                    far = blocks[d + half][i * cells : (i + 1) * cells, :]
                else:
                    near = blocks[d][rows * cells :, :cells]
                    far = blocks[d + half][rows * cells :, :cells]
                value = near + far if parity == 0 else near - far
                if i < rows:
                    term = jnp.dot(table, thirds(value, 0), preferred_element_type=jnp.float32)
                else:
                    value = jnp.concatenate([value, jnp.zeros_like(value)], axis=0)
                    term = lax.dot_general(
                        table, thirds(value, 1), (((1,), (1,)), ((), ())), preferred_element_type=jnp.float32
                    )
                total = term if total is None else total + term
            parts.append(total)
        spectra.append(jnp.concatenate(parts, axis=0))
    return spectra[:-1], spectra[-1]


def inverse_rows(sweeps, count, cells, inverse_ref, outs):
    me = lax.axis_index("span")
    half = count // 2
    padded = sweeps[0].shape[0] // 2
    for i, sweep in enumerate(sweeps):
        even = thirds(sweep[:padded], 0)
        odd = thirds(sweep[padded:], 0)
        for d in range(half):
            place = jnp.bitwise_and(jnp.bitwise_xor(me, d), half - 1)
            first = jnp.dot(inverse_ref[0, place], even, preferred_element_type=jnp.float32)
            second = jnp.dot(inverse_ref[1, place], odd, preferred_element_type=jnp.float32)
            outs[d][i * cells : (i + 1) * cells, :] = first + second
            outs[d + half][i * cells : (i + 1) * cells, :] = first - second


def second_sweep(spectrum, one, above, below, sides, at, inverse_diagonal):
    width = one.shape[1]
    lane = lax.broadcasted_iota(jnp.int32, one.shape, 1)
    left = jnp.where(lane == 0, sides[:, at : at + 1], pltpu.roll(one, 1, 1))
    right = jnp.where(lane == width - 1, sides[:, at + 1 : at + 2], pltpu.roll(one, width - 1, 1))
    return (spectrum + above + below + left + right) * inverse_diagonal


def reciprocals(mask_ref, columns_ref, modes, rows, offset, width):
    turned = columns_ref[...].T
    fluid, solid = turned[:modes, 0:1], turned[:modes, 1:2]
    own = mask_ref.shape[1] // lax.axis_size("span")
    start = pl.multiple_of(lax.axis_index("span") * own + offset, LANES)
    last = mask_ref.shape[1] - LANES
    before = mask_ref[:, pl.ds(pl.multiple_of(jnp.maximum(start - LANES, 0), LANES), LANES)][:, LANES - 1 :]
    after = mask_ref[:, pl.ds(pl.multiple_of(jnp.minimum(start + width, last), LANES), LANES)][:, :1]
    before = jnp.where(start == 0, 2, before)
    after = jnp.where(start + width == mask_ref.shape[1], 2, after)
    lane = lax.broadcasted_iota(jnp.int32, (1, 16), 1)
    kinds = jnp.full((1, 16), 2, jnp.int32)
    diagonals = []
    for i, row in enumerate(rows):
        kinds = jnp.where(lane == 2 * i, before[row : row + 1], kinds)
        kinds = jnp.where(lane == 2 * i + 1, after[row : row + 1], kinds)
        mask = mask_ref[row : row + 1, pl.ds(start, width)]
        diagonals.append(jnp.where(mask != 0, solid, fluid))
    return diagonals, jnp.where(kinds == 0, fluid, jnp.where(kinds == 1, solid, 0.0))


def views(refs, places, size):
    return [ref.at[base : base + size] for ref, base in zip(refs, places)]


def edge_kernel(rows, count, cells, *refs):
    blocks, (forward_ref, columns_ref, mask_ref) = refs[:count], refs[count : count + 3]
    spectrum_ref, first_ref, last_ref, sides_ref = refs[count + 3 :]
    spectra, sides = transform(len(rows), count, cells, blocks, forward_ref)
    modes, width = spectra[0].shape
    diagonals, beside = reciprocals(mask_ref, columns_ref, modes, rows, 0, width)
    for i, one_ref in enumerate((first_ref, last_ref)):
        spectrum_ref[i] = spectra[i]
        one_ref[...] = spectra[i] * diagonals[i]
    sides_ref[...] = sides * beside


def inner_kernel(rows, count, cells, offset, width, places, *refs):
    half = count // 2
    blocks = views(refs, places, len(rows) * cells + 8)
    forward_ref, inverse_ref, columns_ref, mask_ref, first_ref, last_ref = refs[count : count + 6]
    outs, far_ref, ones_ref = refs[-2 - half : -2], refs[-2], refs[-1]
    spectra, sides = transform(len(rows), count, cells, blocks, forward_ref)
    diagonals, beside = reciprocals(mask_ref, columns_ref, spectra[0].shape[0], rows, offset, width)
    sides = sides * beside
    ones = [spectrum * diagonal for spectrum, diagonal in zip(spectra, diagonals)]
    ones_ref[0] = ones[0]
    ones_ref[1] = ones[-1]
    around = [first_ref[:, offset : offset + width], *ones, last_ref[:, offset : offset + width]]
    sweeps = [
        second_sweep(spectra[i], ones[i], around[i], around[i + 2], sides, 2 * i, diagonals[i])
        for i in range(len(rows))
    ]
    size = len(rows) * cells
    inverse_rows(sweeps, count, cells, inverse_ref, [*outs, *views([far_ref] * half, range(0, half * size, size), size)])


def rim_kernel(rows, parts, count, cells, *refs):
    spectrum_ref, first_ref, last_ref, sides_ref, low_ref, high_ref, inverse_ref, columns_ref, mask_ref = refs[:9]
    ones, outs = refs[9 : 9 + parts], refs[-count:]
    modes, width = first_ref.shape
    diagonals, _ = reciprocals(mask_ref, columns_ref, modes, rows, 0, width)
    sides = sides_ref[...]
    inner = [jnp.concatenate([one[i] for one in ones], axis=1) for i in (0, 1)]
    sweeps = [
        second_sweep(spectrum_ref[0], first_ref[...], low_ref[...], inner[0], sides, 0, diagonals[0]),
        second_sweep(spectrum_ref[1], last_ref[...], inner[1], high_ref[...], sides, 2, diagonals[1]),
    ]
    inverse_rows(sweeps, count, cells, inverse_ref, outs)


def join_kernel(groups, *refs):
    refs, outs = refs[:-groups], refs[-groups:]
    size = len(refs) // groups
    for group, out_ref in enumerate(outs):
        at = 0
        for ref in refs[group * size : (group + 1) * size]:
            out_ref[at : at + ref.shape[0], :] = ref[...]
            at += ref.shape[0]


def unpack_kernel(pieces, row_count, cells, *refs):
    me = lax.axis_index("span")
    blocks, (out_ref, held, done) = refs[:-3], refs[-3:]
    pitch = held.shape[0] // cells
    lines = out_ref.shape[1]
    own_tiles = lines // row_count // lax.axis_size("span")
    some = cells // SPLIT
    copies = []
    for part in range(SPLIT):
        for block, (d, base, rows, offset, tiles) in zip(blocks, pieces):
            first = jnp.bitwise_xor(me, d) * own_tiles + offset
            for i, row in enumerate(rows):
                line = base + i * cells + part * some
                for tile in range(tiles):
                    at = part * some * pitch + (first + tile) * row_count + row
                    held[pl.ds(at, some, stride=pitch), :] = block[line : line + some, tile * LANES : (tile + 1) * LANES]
        copies.append(
            pltpu.make_async_copy(
                held.reshape(cells, pitch, LANES).at[pl.ds(part * some, some), pl.ds(0, lines)],
                out_ref.at[pl.ds(part * some, some)],
                done.at[part],
            )
        )
        copies[-1].start()
    for copy in copies:
        copy.wait()


def call(kernel, outs, *args, cost=LONG, earlier=()):
    shapes = [jax.ShapeDtypeStruct(shape, jnp.float32) for shape in outs]
    return pl.pallas_call(
        kernel,
        out_shape=shapes,
        in_specs=[VMEM] * len(args) + [ANY] * len(earlier),
        out_specs=[VMEM] * len(outs),
        compiler_params=PARAMS,
        cost_estimate=cost,
    )(*args, *earlier)


def join(*groups):
    shapes = [(sum(block.shape[0] for block in group), group[0].shape[1]) for group in groups]
    blocks = [block for group in groups for block in group]
    return call(functools.partial(join_kernel, len(groups)), shapes, *blocks, cost=SHORT)


def swap(block, d):
    return lax.ppermute(block, "span", [(i, i ^ d) for i in range(lax.axis_size("span"))])


def local(pressure_source, solid_mask):
    count = lax.axis_size("span")
    half = count // 2
    plane_count = lax.axis_size("plane")
    cells, row_count, columns = pressure_source.shape
    width = columns // count
    tiles = width // LANES
    parts = 2 if tiles % 2 == 0 else 1
    part_tiles, part_width = tiles // parts, width // parts
    inner = tuple(range(1, row_count - 1))
    edges = (0, row_count - 1)
    near, far = range(1, half), range(half, count)
    forward, inverse, one_over = map(jnp.asarray, tables(cells * count, cells))
    modes = 2 * forward.shape[2]

    lines = columns // LANES * row_count
    source = pressure_source.reshape(cells, row_count, columns // LANES, LANES).transpose(0, 2, 1, 3)
    source = source.reshape(cells, lines, LANES)
    scratch = [pltpu.VMEM((cells * (lines + 8), LANES), jnp.float32), pltpu.SemaphoreType.DMA((SPLIT,))]

    edge_size, size = len(edges) * cells + 8, len(inner) * cells + 8
    jobs = [(d, 0, d, edges, 0, tiles) for d in range(count)]
    shapes = [(edge_size, width)] * count

    def add(d, wanted):
        jobs.extend(
            (len(shapes), at * size, d, inner, part * part_tiles, part_tiles) for at, part in enumerate(wanted)
        )
        shapes.append((len(wanted) * size, part_width))

    for d in range(half):
        add(d, range(parts))
    for part in range(parts):
        for d in far:
            add(d, [part])
    packed = pl.pallas_call(
        functools.partial(pack_kernel, jobs, row_count, cells),
        out_shape=[jax.ShapeDtypeStruct(shape, jnp.float32) for shape in shapes],
        in_specs=[ANY],
        out_specs=[VMEM] * len(shapes),
        scratch_shapes=scratch,
        compiler_params=PARAMS,
        cost_estimate=LONG,
    )(source)
    edge_blocks = [packed[0]] + [swap(packed[d], d) for d in range(1, count)]
    near_blocks = [packed[count]] + [swap(packed[count + d], d) for d in near]
    messages = []
    for part in range(parts):
        mine = packed[count + half * (part + 1) : count + half * (part + 2)]
        messages.append([mine[0]] + [swap(mine[d], d) for d in near])
    far_blocks = [swap(message, half) for message in join(*messages)]

    spectrum, first, last, sides = call(
        functools.partial(edge_kernel, edges, count, cells),
        [(2, modes, width), (modes, width), (modes, width), (modes, 16)],
        *edge_blocks, forward, one_over, solid_mask,
    )
    up = [(i, i + 1) for i in range(plane_count - 1)]
    down = [(i + 1, i) for i in range(plane_count - 1)]
    low = lax.ppermute(last, "plane", up)
    high = lax.ppermute(first, "plane", down)

    ones, made, arrived, pieces, earlier = [], [], [], [], ()
    size = len(inner) * cells
    for part in range(parts):
        blocks = [(block, part * (size + 8)) for block in near_blocks]
        blocks += [(far_blocks[part], e * (size + 8)) for e in range(half)]
        offset = part * part_width
        *outs, one = call(
            functools.partial(
                inner_kernel, inner, count, cells, offset, part_width, [base for _, base in blocks]
            ),
            [(size, part_width)] * half + [(half * size, part_width), (2, modes, part_width)],
            *[block for block, _ in blocks], forward, inverse, one_over, solid_mask, first, last,
            cost=SHORT, earlier=earlier,
        )
        ones.append(one)
        earlier = (one,)
        made.append(outs[:half])
        arrived.append(swap(outs[half], half))

    def place(part):
        return inner, part * part_tiles, part_tiles

    def onward(part, d):
        return arrived[part][d * size : (d + 1) * size]

    earlier = list(arrived[:-1])
    for part in range(parts):
        pieces += [(made[part][0], 0, 0, *place(part)), (arrived[part], half, 0, *place(part))]
        for d in near:
            if part < parts - 1:
                message = swap(join([onward(part, d), made[part][d]])[0], d)
                pieces += [(message, half + d, 0, *place(part)), (message, d, size, *place(part))]
            else:
                earlier.append(swap(made[part][d], d))
                pieces += [(earlier[-1], d, 0, *place(part))]
                pieces += [(swap(onward(part, d), d), half + d, 0, *place(part))]
    outs = call(
        functools.partial(rim_kernel, edges, parts, count, cells),
        [(len(edges) * cells, width)] * count,
        spectrum, first, last, sides, low, high, inverse, one_over, solid_mask, *ones, earlier=tuple(earlier),
    )
    pieces.append((outs[0], 0, 0, edges, 0, tiles))
    pieces += [(swap(outs[d], d), d, 0, edges, 0, tiles) for d in (*far, *near)]
    result = pl.pallas_call(
        functools.partial(unpack_kernel, [piece[1:] for piece in pieces], row_count, cells),
        out_shape=jax.ShapeDtypeStruct((cells, lines, LANES), jnp.float32),
        in_specs=[VMEM] * len(pieces),
        out_specs=ANY,
        scratch_shapes=scratch,
        compiler_params=PARAMS,
        cost_estimate=LONG,
    )(*[piece[0] for piece in pieces])
    result = result.reshape(cells, columns // LANES, row_count, LANES).transpose(0, 2, 1, 3)
    return result.reshape(cells, row_count, columns)


def solution(mesh):
    placed = (P("span", "plane", None), P("plane", None))
    return jax.shard_map(
        local, mesh=mesh, in_specs=placed, out_specs=P("span", "plane", None), check_vma=False
    )
```

```python
import functools

import jax
import jax.numpy as jnp
import ml_dtypes
import numpy as np
from jax import lax
from jax.experimental import pallas as pl
from jax.experimental.pallas import tpu as pltpu
from jax.sharding import PartitionSpec as P

PENALTY = 12.0
LANES = 128
VMEM = pl.BlockSpec(memory_space=pltpu.VMEM)
ANY = pl.BlockSpec(memory_space=pl.ANY)
PARAMS = pltpu.CompilerParams(vmem_limit_bytes=24 * 1024 * 1024)
LONG = pl.CostEstimate(flops=0, bytes_accessed=200_000_000, transcendentals=0)
SHORT = pl.CostEstimate(flops=0, bytes_accessed=1024, transcendentals=0)
SPLIT = 4


def split(values):
    high = values.astype(ml_dtypes.bfloat16)
    low = (values - high.astype(np.float64)).astype(ml_dtypes.bfloat16)
    return high, low


def tables(length, cells):
    half = length // 2
    points = np.arange(half)
    groups = []
    for parity in (0, 1):
        kept = [k for k in range(length // 2 + 1) if 3 * k <= length and k % 2 == parity]
        modes = [(k, False) for k in kept] + [(k, True) for k in kept if 0 < k < length // 2]
        groups.append(modes)
    padded = -(-max(len(modes) for modes in groups) // 16) * 16
    forward = np.zeros((2, padded, half))
    inverse = np.zeros((2, half, padded))
    fluid = np.zeros((2 * padded, 1))
    solid = np.zeros((2 * padded, 1))
    for parity, modes in enumerate(groups):
        for at, (k, sine) in enumerate(modes):
            angles = (points * k % length) * (2.0 * np.pi / length)
            wave = np.sin(angles) if sine else np.cos(angles)
            weight = 1.0 if k in (0, length // 2) else 2.0
            eigen = 2.0 - 2.0 * np.cos(2.0 * np.pi * k / length)
            forward[parity, at] = wave
            inverse[parity, :, at] = wave * weight / length
            fluid[parity * padded + at] = 1.0 / (4.0 + eigen)
            solid[parity * padded + at] = 1.0 / (4.0 + eigen + PENALTY)
    columns = np.zeros((8, -(-2 * padded // LANES) * LANES), np.float32)
    columns[0, : 2 * padded] = fluid[:, 0]
    columns[1, : 2 * padded] = solid[:, 0]
    blocks = half // cells
    high, low = split(forward.reshape(2, padded, blocks, cells).transpose(0, 2, 1, 3))
    forward = np.concatenate([high, low, high], axis=3)
    high, low = split(inverse.reshape(2, blocks, cells, padded))
    inverse = np.concatenate([high, low, high], axis=3)
    return forward, inverse, columns


def thirds(values, axis):
    high = values.astype(jnp.bfloat16)
    low = (values - high.astype(jnp.float32)).astype(jnp.bfloat16)
    return jnp.concatenate([high, high, low], axis=axis)


def pack_kernel(jobs, row_count, cells, earlier, x_ref, *refs):
    outs, (held, arrived) = refs[earlier:-2], refs[-2:]
    me = lax.axis_index("span")
    lines = x_ref.shape[1]
    all_tiles = lines // row_count
    own_tiles = all_tiles // lax.axis_size("span")
    pitch = held.shape[0] // cells
    some = cells // SPLIT
    copies = [
        pltpu.make_async_copy(
            x_ref.at[pl.ds(part * some, some)],
            held.reshape(cells, pitch, LANES).at[pl.ds(part * some, some), pl.ds(0, lines)],
            arrived.at[part],
        )
        for part in range(SPLIT)
    ]
    for copy in copies:
        copy.start()
    lane = lax.broadcasted_iota(jnp.int32, (some, LANES), 1)
    sides = []
    for part, copy in enumerate(copies):
        copy.wait()
        beside = jnp.zeros((some, LANES), jnp.float32)

        def line(tile, row):
            return held[pl.ds(part * some * pitch + tile * row_count + row, some, stride=pitch), :]

        for job, (out, base, d, rows, offset, tiles) in enumerate(jobs):
            first = jnp.bitwise_xor(me, d) * own_tiles + offset
            for i, row in enumerate(rows):
                at = base + i * cells + part * some
                for tile in range(tiles):
                    outs[out][at : at + some, tile * LANES : (tile + 1) * LANES] = line(first + tile, row)
                before = jnp.maximum(first - 1, 0)
                after = jnp.minimum(first + tiles, all_tiles - 1)
                for side, (tile, source) in enumerate(((before, LANES - 1), (after, 0))):
                    at = job * 8 + i * 2 + side
                    beside = jnp.where(lane == at, pltpu.roll(line(tile, row), (at - source) % LANES, 1), beside)
        sides.append(beside)
    if cells < LANES:
        sides.append(jnp.zeros((LANES - cells, LANES), jnp.float32))
    turned = jnp.concatenate(sides, axis=0).T
    for job, (out, base, _, rows, _, tiles) in enumerate(jobs):
        at = base + len(rows) * cells
        outs[out][at : at + 8, :LANES] = turned[job * 8 : (job + 1) * 8]
        if tiles > 1:
            outs[out][at : at + 8, LANES:] = jnp.zeros((8, (tiles - 1) * LANES), jnp.float32)


def transform(rows, count, cells, blocks, forward_ref):
    me = lax.axis_index("span")
    half = count // 2
    spectra = []
    for i in range(rows + 1):
        parts = []
        for parity in (0, 1):
            total = None
            for d in range(half):
                table = forward_ref[parity, jnp.bitwise_and(jnp.bitwise_xor(me, d), half - 1)]
                if i < rows:
                    near = blocks[d][i * cells : (i + 1) * cells, :]
                    far = blocks[d + half][i * cells : (i + 1) * cells, :]
                else:
                    near = blocks[d][rows * cells :, :cells]
                    far = blocks[d + half][rows * cells :, :cells]
                value = near + far if parity == 0 else near - far
                if i < rows:
                    term = jnp.dot(table, thirds(value, 0), preferred_element_type=jnp.float32)
                else:
                    value = jnp.concatenate([value, jnp.zeros_like(value)], axis=0)
                    term = lax.dot_general(
                        table, thirds(value, 1), (((1,), (1,)), ((), ())), preferred_element_type=jnp.float32
                    )
                total = term if total is None else total + term
            parts.append(total)
        spectra.append(jnp.concatenate(parts, axis=0))
    return spectra[:-1], spectra[-1]


def inverse_rows(sweeps, count, cells, inverse_ref, outs):
    me = lax.axis_index("span")
    half = count // 2
    padded = sweeps[0].shape[0] // 2
    for i, sweep in enumerate(sweeps):
        even = thirds(sweep[:padded], 0)
        odd = thirds(sweep[padded:], 0)
        for d in range(half):
            place = jnp.bitwise_and(jnp.bitwise_xor(me, d), half - 1)
            first = jnp.dot(inverse_ref[0, place], even, preferred_element_type=jnp.float32)
            second = jnp.dot(inverse_ref[1, place], odd, preferred_element_type=jnp.float32)
            outs[d][i * cells : (i + 1) * cells, :] = first + second
            outs[d + half][i * cells : (i + 1) * cells, :] = first - second


def second_sweep(spectrum, one, above, below, sides, at, inverse_diagonal):
    width = one.shape[1]
    lane = lax.broadcasted_iota(jnp.int32, one.shape, 1)
    left = jnp.where(lane == 0, sides[:, at : at + 1], pltpu.roll(one, 1, 1))
    right = jnp.where(lane == width - 1, sides[:, at + 1 : at + 2], pltpu.roll(one, width - 1, 1))
    return (spectrum + above + below + left + right) * inverse_diagonal


def reciprocals(mask_ref, columns_ref, modes, rows, offset, width):
    turned = columns_ref[...].T
    fluid, solid = turned[:modes, 0:1], turned[:modes, 1:2]
    own = mask_ref.shape[1] // lax.axis_size("span")
    start = pl.multiple_of(lax.axis_index("span") * own + offset, LANES)
    last = mask_ref.shape[1] - LANES
    before = mask_ref[:, pl.ds(pl.multiple_of(jnp.maximum(start - LANES, 0), LANES), LANES)][:, LANES - 1 :]
    after = mask_ref[:, pl.ds(pl.multiple_of(jnp.minimum(start + width, last), LANES), LANES)][:, :1]
    before = jnp.where(start == 0, 2, before)
    after = jnp.where(start + width == mask_ref.shape[1], 2, after)
    lane = lax.broadcasted_iota(jnp.int32, (1, 16), 1)
    kinds = jnp.full((1, 16), 2, jnp.int32)
    diagonals = []
    for i, row in enumerate(rows):
        kinds = jnp.where(lane == 2 * i, before[row : row + 1], kinds)
        kinds = jnp.where(lane == 2 * i + 1, after[row : row + 1], kinds)
        mask = mask_ref[row : row + 1, pl.ds(start, width)]
        diagonals.append(jnp.where(mask != 0, solid, fluid))
    return diagonals, jnp.where(kinds == 0, fluid, jnp.where(kinds == 1, solid, 0.0))


def views(refs, places, size):
    return [ref.at[base : base + size] for ref, base in zip(refs, places)]


def edge_kernel(rows, count, cells, *refs):
    blocks, (forward_ref, columns_ref, mask_ref) = refs[:count], refs[count : count + 3]
    spectrum_ref, first_ref, last_ref, sides_ref = refs[count + 3 :]
    spectra, sides = transform(len(rows), count, cells, blocks, forward_ref)
    modes, width = spectra[0].shape
    diagonals, beside = reciprocals(mask_ref, columns_ref, modes, rows, 0, width)
    for i, one_ref in enumerate((first_ref, last_ref)):
        spectrum_ref[i] = spectra[i]
        one_ref[...] = spectra[i] * diagonals[i]
    sides_ref[...] = sides * beside


def inner_kernel(rows, count, cells, offset, width, places, *refs):
    half = count // 2
    blocks = views(refs, places, len(rows) * cells + 8)
    forward_ref, inverse_ref, columns_ref, mask_ref, first_ref, last_ref = refs[count : count + 6]
    outs, far_ref, ones_ref = refs[-2 - half : -2], refs[-2], refs[-1]
    spectra, sides = transform(len(rows), count, cells, blocks, forward_ref)
    diagonals, beside = reciprocals(mask_ref, columns_ref, spectra[0].shape[0], rows, offset, width)
    sides = sides * beside
    ones = [spectrum * diagonal for spectrum, diagonal in zip(spectra, diagonals)]
    ones_ref[0] = ones[0]
    ones_ref[1] = ones[-1]
    around = [first_ref[:, offset : offset + width], *ones, last_ref[:, offset : offset + width]]
    sweeps = [
        second_sweep(spectra[i], ones[i], around[i], around[i + 2], sides, 2 * i, diagonals[i])
        for i in range(len(rows))
    ]
    size = len(rows) * cells
    inverse_rows(sweeps, count, cells, inverse_ref, [*outs, *views([far_ref] * half, range(0, half * size, size), size)])


def rim_kernel(rows, parts, count, cells, *refs):
    spectrum_ref, first_ref, last_ref, sides_ref, low_ref, high_ref, inverse_ref, columns_ref, mask_ref = refs[:9]
    ones, outs = refs[9 : 9 + parts], refs[-count:]
    modes, width = first_ref.shape
    diagonals, _ = reciprocals(mask_ref, columns_ref, modes, rows, 0, width)
    sides = sides_ref[...]
    inner = [jnp.concatenate([one[i] for one in ones], axis=1) for i in (0, 1)]
    sweeps = [
        second_sweep(spectrum_ref[0], first_ref[...], low_ref[...], inner[0], sides, 0, diagonals[0]),
        second_sweep(spectrum_ref[1], last_ref[...], inner[1], high_ref[...], sides, 2, diagonals[1]),
    ]
    inverse_rows(sweeps, count, cells, inverse_ref, outs)


def join_kernel(groups, size, *refs):
    outs = refs[-groups:]
    for group, out_ref in enumerate(outs):
        at = 0
        for ref in refs[group * size : (group + 1) * size]:
            out_ref[at : at + ref.shape[0], :] = ref[...]
            at += ref.shape[0]


def unpack_kernel(pieces, row_count, cells, *refs):
    me = lax.axis_index("span")
    blocks, (out_ref, held, done) = refs[:-3], refs[-3:]
    pitch = held.shape[0] // cells
    lines = out_ref.shape[1]
    own_tiles = lines // row_count // lax.axis_size("span")
    some = cells // SPLIT
    copies = []
    for part in range(SPLIT):
        for block, (d, base, rows, offset, tiles) in zip(blocks, pieces):
            first = jnp.bitwise_xor(me, d) * own_tiles + offset
            for i, row in enumerate(rows):
                line = base + i * cells + part * some
                for tile in range(tiles):
                    at = part * some * pitch + (first + tile) * row_count + row
                    held[pl.ds(at, some, stride=pitch), :] = block[line : line + some, tile * LANES : (tile + 1) * LANES]
        copies.append(
            pltpu.make_async_copy(
                held.reshape(cells, pitch, LANES).at[pl.ds(part * some, some), pl.ds(0, lines)],
                out_ref.at[pl.ds(part * some, some)],
                done.at[part],
            )
        )
        copies[-1].start()
    for copy in copies:
        copy.wait()


def call(kernel, outs, *args, cost=LONG, earlier=()):
    shapes = [jax.ShapeDtypeStruct(shape, jnp.float32) for shape in outs]
    return pl.pallas_call(
        kernel,
        out_shape=shapes,
        in_specs=[VMEM] * len(args) + [ANY] * len(earlier),
        out_specs=[VMEM] * len(outs),
        compiler_params=PARAMS,
        cost_estimate=cost,
    )(*args, *earlier)


def join(*groups, earlier=()):
    shapes = [(sum(block.shape[0] for block in group), group[0].shape[1]) for group in groups]
    blocks = [block for group in groups for block in group]
    return call(functools.partial(join_kernel, len(groups), len(groups[0])), shapes, *blocks, cost=SHORT, earlier=earlier)


def swap(block, d):
    return lax.ppermute(block, "span", [(i, i ^ d) for i in range(lax.axis_size("span"))])


def local(pressure_source, solid_mask):
    count = lax.axis_size("span")
    half = count // 2
    plane_count = lax.axis_size("plane")
    cells, row_count, columns = pressure_source.shape
    width = columns // count
    tiles = width // LANES
    parts = 2 if tiles % 2 == 0 else 1
    part_tiles, part_width = tiles // parts, width // parts
    inner = tuple(range(1, row_count - 1))
    edges = (0, row_count - 1)
    near, far = range(1, half), range(half, count)
    forward, inverse, one_over = map(jnp.asarray, tables(cells * count, cells))
    modes = 2 * forward.shape[2]

    lines = columns // LANES * row_count
    source = pressure_source.reshape(cells, row_count, columns // LANES, LANES).transpose(0, 2, 1, 3)
    source = source.reshape(cells, lines, LANES)
    scratch = [pltpu.VMEM((cells * (lines + 8), LANES), jnp.float32), pltpu.SemaphoreType.DMA((SPLIT,))]

    def pack(jobs, shapes, *earlier):
        return pl.pallas_call(
            functools.partial(pack_kernel, jobs, row_count, cells, len(earlier)),
            out_shape=[jax.ShapeDtypeStruct(shape, jnp.float32) for shape in shapes],
            in_specs=[ANY] * (1 + len(earlier)),
            out_specs=[VMEM] * len(shapes),
            scratch_shapes=scratch,
            compiler_params=PARAMS,
            cost_estimate=LONG,
        )(source, *earlier)

    edge_size, size = len(edges) * cells + 8, len(inner) * cells + 8
    jobs = [(d - 1, 0, d, edges, 0, tiles) for d in range(1, count)]
    edge_blocks = [swap(block, d) for d, block in enumerate(pack(jobs, [(edge_size, width)] * (count - 1)), 1)]
    jobs, shapes = [(0, 0, 0, edges, 0, tiles)], [(edge_size, width)]

    def add(d, wanted):
        jobs.extend(
            (len(shapes), at * size, d, inner, part * part_tiles, part_tiles) for at, part in enumerate(wanted)
        )
        shapes.append((len(wanted) * size, part_width))

    for d in range(half):
        add(d, range(parts))
    for part in range(parts):
        for d in far:
            add(d, [part])
    packed = pack(jobs, shapes, *edge_blocks[: half - 1])
    edge_blocks = [packed[0], *edge_blocks]
    near_blocks = [packed[1]] + [swap(packed[1 + d], d) for d in near]
    messages = []
    for part in range(parts):
        mine = packed[1 + half * (part + 1) : 1 + half * (part + 2)]
        messages.append([mine[0]] + [swap(mine[d], d) for d in near])
    far_blocks = [swap(message, half) for message in join(*messages, earlier=(edge_blocks[half],))]

    spectrum, first, last, sides = call(
        functools.partial(edge_kernel, edges, count, cells),
        [(2, modes, width), (modes, width), (modes, width), (modes, 16)],
        *edge_blocks, forward, one_over, solid_mask,
    )
    up = [(i, i + 1) for i in range(plane_count - 1)]
    down = [(i + 1, i) for i in range(plane_count - 1)]
    low = lax.ppermute(last, "plane", up)
    high = lax.ppermute(first, "plane", down)

    ones, made, arrived, pieces, earlier = [], [], [], [], ()
    size = len(inner) * cells
    for part in range(parts):
        blocks = [(block, part * (size + 8)) for block in near_blocks]
        blocks += [(far_blocks[part], e * (size + 8)) for e in range(half)]
        offset = part * part_width
        *outs, one = call(
            functools.partial(
                inner_kernel, inner, count, cells, offset, part_width, [base for _, base in blocks]
            ),
            [(size, part_width)] * half + [(half * size, part_width), (2, modes, part_width)],
            *[block for block, _ in blocks], forward, inverse, one_over, solid_mask, first, last,
            cost=SHORT, earlier=earlier,
        )
        ones.append(one)
        earlier = (one,)
        made.append(outs[:half])
        arrived.append(swap(outs[half], half))

    def place(part):
        return inner, part * part_tiles, part_tiles

    def onward(part, d):
        return arrived[part][d * size : (d + 1) * size]

    earlier = list(arrived[:-1])
    for part in range(parts):
        pieces += [(made[part][0], 0, 0, *place(part)), (arrived[part], half, 0, *place(part))]
        for d in near:
            if part < parts - 1:
                message = swap(join([onward(part, d), made[part][d]])[0], d)
                pieces += [(message, half + d, 0, *place(part)), (message, d, size, *place(part))]
            else:
                earlier.append(swap(made[part][d], d))
                pieces += [(earlier[-1], d, 0, *place(part))]
                pieces += [(swap(onward(part, d), d), half + d, 0, *place(part))]
    outs = call(
        functools.partial(rim_kernel, edges, parts, count, cells),
        [(len(edges) * cells, width)] * count,
        spectrum, first, last, sides, low, high, inverse, one_over, solid_mask, *ones, earlier=tuple(earlier),
    )
    pieces.append((outs[0], 0, 0, edges, 0, tiles))
    pieces += [(swap(outs[d], d), d, 0, edges, 0, tiles) for d in (*far, *near)]
    result = pl.pallas_call(
        functools.partial(unpack_kernel, [piece[1:] for piece in pieces], row_count, cells),
        out_shape=jax.ShapeDtypeStruct((cells, lines, LANES), jnp.float32),
        in_specs=[VMEM] * len(pieces),
        out_specs=ANY,
        scratch_shapes=scratch,
        compiler_params=PARAMS,
        cost_estimate=LONG,
    )(*[piece[0] for piece in pieces])
    result = result.reshape(cells, columns // LANES, row_count, LANES).transpose(0, 2, 1, 3)
    return result.reshape(cells, row_count, columns)


def solution(mesh):
    placed = (P("span", "plane", None), P("plane", None))
    return jax.shard_map(
        local, mesh=mesh, in_specs=placed, out_specs=P("span", "plane", None), check_vma=False
    )
```

```python
import functools

import jax
import jax.numpy as jnp
import ml_dtypes
import numpy as np
from jax import lax
from jax.experimental import pallas as pl
from jax.experimental.pallas import tpu as pltpu
from jax.sharding import PartitionSpec as P

PENALTY = 12.0
LANES = 128
VMEM = pl.BlockSpec(memory_space=pltpu.VMEM)
ANY = pl.BlockSpec(memory_space=pl.ANY)
PARAMS = pltpu.CompilerParams(vmem_limit_bytes=24 * 1024 * 1024)
LONG = pl.CostEstimate(flops=0, bytes_accessed=200_000_000, transcendentals=0)
SHORT = pl.CostEstimate(flops=0, bytes_accessed=1024, transcendentals=0)
SPLIT = 4


def split(values):
    high = values.astype(ml_dtypes.bfloat16)
    low = (values - high.astype(np.float64)).astype(ml_dtypes.bfloat16)
    return high, low


def tables(length, cells):
    half = length // 2
    points = np.arange(half)
    groups = []
    for parity in (0, 1):
        kept = [k for k in range(length // 2 + 1) if 3 * k <= length and k % 2 == parity]
        modes = [(k, False) for k in kept] + [(k, True) for k in kept if 0 < k < length // 2]
        groups.append(modes)
    padded = -(-max(len(modes) for modes in groups) // 16) * 16
    forward = np.zeros((2, padded, half))
    inverse = np.zeros((2, half, padded))
    fluid = np.zeros((2 * padded, 1))
    solid = np.zeros((2 * padded, 1))
    for parity, modes in enumerate(groups):
        for at, (k, sine) in enumerate(modes):
            angles = (points * k % length) * (2.0 * np.pi / length)
            wave = np.sin(angles) if sine else np.cos(angles)
            weight = 1.0 if k in (0, length // 2) else 2.0
            eigen = 2.0 - 2.0 * np.cos(2.0 * np.pi * k / length)
            forward[parity, at] = wave
            inverse[parity, :, at] = wave * weight / length
            fluid[parity * padded + at] = 1.0 / (4.0 + eigen)
            solid[parity * padded + at] = 1.0 / (4.0 + eigen + PENALTY)
    columns = np.zeros((8, -(-2 * padded // LANES) * LANES), np.float32)
    columns[0, : 2 * padded] = fluid[:, 0]
    columns[1, : 2 * padded] = solid[:, 0]
    blocks = half // cells
    high, low = split(forward.reshape(2, padded, blocks, cells).transpose(0, 2, 1, 3))
    forward = np.concatenate([high, low, high], axis=3)
    high, low = split(inverse.reshape(2, blocks, cells, padded))
    inverse = np.concatenate([high, low, high], axis=3)
    return forward, inverse, columns


def thirds(values, axis):
    high = values.astype(jnp.bfloat16)
    low = (values - high.astype(jnp.float32)).astype(jnp.bfloat16)
    return jnp.concatenate([high, high, low], axis=axis)


def pack_kernel(jobs, row_count, cells, earlier, x_ref, *refs):
    outs, (held, arrived) = refs[earlier:-2], refs[-2:]
    me = lax.axis_index("span")
    lines = x_ref.shape[1]
    all_tiles = lines // row_count
    own_tiles = all_tiles // lax.axis_size("span")
    pitch = held.shape[0] // cells
    some = cells // SPLIT
    copies = [
        pltpu.make_async_copy(
            x_ref.at[pl.ds(part * some, some)],
            held.reshape(cells, pitch, LANES).at[pl.ds(part * some, some), pl.ds(0, lines)],
            arrived.at[part],
        )
        for part in range(SPLIT)
    ]
    for copy in copies:
        copy.start()
    lane = lax.broadcasted_iota(jnp.int32, (some, LANES), 1)
    sides = []
    for part, copy in enumerate(copies):
        copy.wait()
        beside = jnp.zeros((some, LANES), jnp.float32)

        def line(tile, row):
            return held[pl.ds(part * some * pitch + tile * row_count + row, some, stride=pitch), :]

        for job, (out, base, d, rows, offset, tiles) in enumerate(jobs):
            first = jnp.bitwise_xor(me, d) * own_tiles + offset
            for i, row in enumerate(rows):
                at = base + i * cells + part * some
                for tile in range(tiles):
                    outs[out][at : at + some, tile * LANES : (tile + 1) * LANES] = line(first + tile, row)
                before = jnp.maximum(first - 1, 0)
                after = jnp.minimum(first + tiles, all_tiles - 1)
                for side, (tile, source) in enumerate(((before, LANES - 1), (after, 0))):
                    at = job * 8 + i * 2 + side
                    beside = jnp.where(lane == at, pltpu.roll(line(tile, row), (at - source) % LANES, 1), beside)
        sides.append(beside)
    if cells < LANES:
        sides.append(jnp.zeros((LANES - cells, LANES), jnp.float32))
    turned = jnp.concatenate(sides, axis=0).T
    for job, (out, base, _, rows, _, tiles) in enumerate(jobs):
        at = base + len(rows) * cells
        outs[out][at : at + 8, :LANES] = turned[job * 8 : (job + 1) * 8]
        if tiles > 1:
            outs[out][at : at + 8, LANES:] = jnp.zeros((8, (tiles - 1) * LANES), jnp.float32)


def transform(rows, count, cells, blocks, forward_ref):
    me = lax.axis_index("span")
    half = count // 2
    spectra = []
    for i in range(rows + 1):
        parts = []
        for parity in (0, 1):
            total = None
            for d in range(half):
                table = forward_ref[parity, jnp.bitwise_and(jnp.bitwise_xor(me, d), half - 1)]
                if i < rows:
                    near = blocks[d][i * cells : (i + 1) * cells, :]
                    far = blocks[d + half][i * cells : (i + 1) * cells, :]
                else:
                    near = blocks[d][rows * cells :, :cells]
                    far = blocks[d + half][rows * cells :, :cells]
                value = near + far if parity == 0 else near - far
                if i < rows:
                    term = jnp.dot(table, thirds(value, 0), preferred_element_type=jnp.float32)
                else:
                    value = jnp.concatenate([value, jnp.zeros_like(value)], axis=0)
                    term = lax.dot_general(
                        table, thirds(value, 1), (((1,), (1,)), ((), ())), preferred_element_type=jnp.float32
                    )
                total = term if total is None else total + term
            parts.append(total)
        spectra.append(jnp.concatenate(parts, axis=0))
    return spectra[:-1], spectra[-1]


def inverse_rows(sweeps, count, cells, inverse_ref, outs):
    me = lax.axis_index("span")
    half = count // 2
    padded = sweeps[0].shape[0] // 2
    for i, sweep in enumerate(sweeps):
        even = thirds(sweep[:padded], 0)
        odd = thirds(sweep[padded:], 0)
        for d in range(half):
            place = jnp.bitwise_and(jnp.bitwise_xor(me, d), half - 1)
            first = jnp.dot(inverse_ref[0, place], even, preferred_element_type=jnp.float32)
            second = jnp.dot(inverse_ref[1, place], odd, preferred_element_type=jnp.float32)
            outs[d][i * cells : (i + 1) * cells, :] = first + second
            outs[d + half][i * cells : (i + 1) * cells, :] = first - second


def second_sweep(spectrum, one, above, below, sides, at, inverse_diagonal):
    width = one.shape[1]
    lane = lax.broadcasted_iota(jnp.int32, one.shape, 1)
    left = jnp.where(lane == 0, sides[:, at : at + 1], pltpu.roll(one, 1, 1))
    right = jnp.where(lane == width - 1, sides[:, at + 1 : at + 2], pltpu.roll(one, width - 1, 1))
    return (spectrum + above + below + left + right) * inverse_diagonal


def reciprocals(mask_ref, columns_ref, modes, rows, offset, width):
    turned = columns_ref[...].T
    fluid, solid = turned[:modes, 0:1], turned[:modes, 1:2]
    own = mask_ref.shape[1] // lax.axis_size("span")
    start = pl.multiple_of(lax.axis_index("span") * own + offset, LANES)
    last = mask_ref.shape[1] - LANES
    before = mask_ref[:, pl.ds(pl.multiple_of(jnp.maximum(start - LANES, 0), LANES), LANES)][:, LANES - 1 :]
    after = mask_ref[:, pl.ds(pl.multiple_of(jnp.minimum(start + width, last), LANES), LANES)][:, :1]
    before = jnp.where(start == 0, 2, before)
    after = jnp.where(start + width == mask_ref.shape[1], 2, after)
    lane = lax.broadcasted_iota(jnp.int32, (1, 16), 1)
    kinds = jnp.full((1, 16), 2, jnp.int32)
    diagonals = []
    for i, row in enumerate(rows):
        kinds = jnp.where(lane == 2 * i, before[row : row + 1], kinds)
        kinds = jnp.where(lane == 2 * i + 1, after[row : row + 1], kinds)
        mask = mask_ref[row : row + 1, pl.ds(start, width)]
        diagonals.append(jnp.where(mask != 0, solid, fluid))
    return diagonals, jnp.where(kinds == 0, fluid, jnp.where(kinds == 1, solid, 0.0))


def views(refs, places, size):
    return [ref.at[base : base + size] for ref, base in zip(refs, places)]


def edge_kernel(rows, count, cells, *refs):
    blocks, (forward_ref, columns_ref, mask_ref) = refs[:count], refs[count : count + 3]
    spectrum_ref, first_ref, last_ref, sides_ref = refs[count + 3 :]
    spectra, sides = transform(len(rows), count, cells, blocks, forward_ref)
    modes, width = spectra[0].shape
    diagonals, beside = reciprocals(mask_ref, columns_ref, modes, rows, 0, width)
    for i, one_ref in enumerate((first_ref, last_ref)):
        spectrum_ref[i] = spectra[i]
        one_ref[...] = spectra[i] * diagonals[i]
    sides_ref[...] = sides * beside


def inner_kernel(rows, count, cells, offset, width, places, *refs):
    half = count // 2
    blocks = views(refs, places, len(rows) * cells + 8)
    forward_ref, inverse_ref, columns_ref, mask_ref, first_ref, last_ref = refs[count : count + 6]
    outs, far_ref, ones_ref = refs[-2 - half : -2], refs[-2], refs[-1]
    spectra, sides = transform(len(rows), count, cells, blocks, forward_ref)
    diagonals, beside = reciprocals(mask_ref, columns_ref, spectra[0].shape[0], rows, offset, width)
    sides = sides * beside
    ones = [spectrum * diagonal for spectrum, diagonal in zip(spectra, diagonals)]
    ones_ref[0] = ones[0]
    ones_ref[1] = ones[-1]
    around = [first_ref[:, offset : offset + width], *ones, last_ref[:, offset : offset + width]]
    sweeps = [
        second_sweep(spectra[i], ones[i], around[i], around[i + 2], sides, 2 * i, diagonals[i])
        for i in range(len(rows))
    ]
    size = len(rows) * cells
    inverse_rows(sweeps, count, cells, inverse_ref, [*outs, *views([far_ref] * half, range(0, half * size, size), size)])


def rim_kernel(rows, parts, count, cells, *refs):
    spectrum_ref, first_ref, last_ref, sides_ref, low_ref, high_ref, inverse_ref, columns_ref, mask_ref = refs[:9]
    ones, outs = refs[9 : 9 + parts], refs[-count:]
    modes, width = first_ref.shape
    diagonals, _ = reciprocals(mask_ref, columns_ref, modes, rows, 0, width)
    sides = sides_ref[...]
    inner = [jnp.concatenate([one[i] for one in ones], axis=1) for i in (0, 1)]
    sweeps = [
        second_sweep(spectrum_ref[0], first_ref[...], low_ref[...], inner[0], sides, 0, diagonals[0]),
        second_sweep(spectrum_ref[1], last_ref[...], inner[1], high_ref[...], sides, 2, diagonals[1]),
    ]
    inverse_rows(sweeps, count, cells, inverse_ref, outs)


def join_kernel(groups, size, *refs):
    outs = refs[-groups:]
    for group, out_ref in enumerate(outs):
        at = 0
        for ref in refs[group * size : (group + 1) * size]:
            out_ref[at : at + ref.shape[0], :] = ref[...]
            at += ref.shape[0]


def unpack_kernel(pieces, devices, row_count, cells, *refs):
    me = lax.axis_index("span")
    blocks, (out_ref, held, done) = refs[: len(pieces)], refs[-3:]
    pitch = held.shape[0] // cells
    own_lines = out_ref.shape[1] // lax.axis_size("span")
    some = cells // SPLIT
    copies = []
    for part in range(SPLIT):
        for block, (d, base, rows, offset, tiles) in zip(blocks, pieces):
            for i, row in enumerate(rows):
                line = base + i * cells + part * some
                for tile in range(tiles):
                    at = part * some * pitch + devices.index(d) * own_lines + (offset + tile) * row_count + row
                    held[pl.ds(at, some, stride=pitch), :] = block[line : line + some, tile * LANES : (tile + 1) * LANES]
        for at, d in enumerate(devices):
            first = pl.multiple_of(jnp.bitwise_xor(me, d) * own_lines, own_lines)
            copies.append(
                pltpu.make_async_copy(
                    held.reshape(cells, pitch, LANES).at[pl.ds(part * some, some), pl.ds(at * own_lines, own_lines)],
                    out_ref.at[pl.ds(part * some, some), pl.ds(first, own_lines)],
                    done.at[part, at],
                )
            )
            copies[-1].start()
    for copy in copies:
        copy.wait()


def call(kernel, outs, *args, cost=LONG, earlier=()):
    shapes = [jax.ShapeDtypeStruct(shape, jnp.float32) for shape in outs]
    return pl.pallas_call(
        kernel,
        out_shape=shapes,
        in_specs=[VMEM] * len(args) + [ANY] * len(earlier),
        out_specs=[VMEM] * len(outs),
        compiler_params=PARAMS,
        cost_estimate=cost,
    )(*args, *earlier)


def join(*groups, earlier=()):
    shapes = [(sum(block.shape[0] for block in group), group[0].shape[1]) for group in groups]
    blocks = [block for group in groups for block in group]
    return call(functools.partial(join_kernel, len(groups), len(groups[0])), shapes, *blocks, cost=SHORT, earlier=earlier)


def swap(block, d):
    return lax.ppermute(block, "span", [(i, i ^ d) for i in range(lax.axis_size("span"))])


def local(pressure_source, solid_mask):
    count = lax.axis_size("span")
    half = count // 2
    plane_count = lax.axis_size("plane")
    cells, row_count, columns = pressure_source.shape
    width = columns // count
    tiles = width // LANES
    parts = 2 if tiles % 2 == 0 else 1
    part_tiles, part_width = tiles // parts, width // parts
    inner = tuple(range(1, row_count - 1))
    edges = (0, row_count - 1)
    near, far = range(1, half), range(half, count)
    forward, inverse, one_over = map(jnp.asarray, tables(cells * count, cells))
    modes = 2 * forward.shape[2]

    lines = columns // LANES * row_count
    source = pressure_source.reshape(cells, row_count, columns // LANES, LANES).transpose(0, 2, 1, 3)
    source = source.reshape(cells, lines, LANES)
    scratch = [pltpu.VMEM((cells * (lines + 8), LANES), jnp.float32), pltpu.SemaphoreType.DMA((SPLIT,))]

    def pack(jobs, shapes, *earlier):
        return pl.pallas_call(
            functools.partial(pack_kernel, jobs, row_count, cells, len(earlier)),
            out_shape=[jax.ShapeDtypeStruct(shape, jnp.float32) for shape in shapes],
            in_specs=[ANY] * (1 + len(earlier)),
            out_specs=[VMEM] * len(shapes),
            scratch_shapes=scratch,
            compiler_params=PARAMS,
            cost_estimate=LONG,
        )(source, *earlier)

    edge_size, size = len(edges) * cells + 8, len(inner) * cells + 8
    jobs = [(d - 1, 0, d, edges, 0, tiles) for d in range(1, count)]
    edge_blocks = [swap(block, d) for d, block in enumerate(pack(jobs, [(edge_size, width)] * (count - 1)), 1)]
    jobs, shapes = [(0, 0, 0, edges, 0, tiles)], [(edge_size, width)]

    def add(d, wanted):
        jobs.extend(
            (len(shapes), at * size, d, inner, part * part_tiles, part_tiles) for at, part in enumerate(wanted)
        )
        shapes.append((len(wanted) * size, part_width))

    for d in range(half):
        add(d, range(parts))
    for part in range(parts):
        for d in far:
            add(d, [part])
    packed = pack(jobs, shapes, *edge_blocks[: half - 1])
    edge_blocks = [packed[0], *edge_blocks]
    near_blocks = [packed[1]] + [swap(packed[1 + d], d) for d in near]
    messages = []
    for part in range(parts):
        mine = packed[1 + half * (part + 1) : 1 + half * (part + 2)]
        messages.append([mine[0]] + [swap(mine[d], d) for d in near])
    far_blocks = [swap(message, half) for message in join(*messages, earlier=(edge_blocks[half],))]

    spectrum, first, last, sides = call(
        functools.partial(edge_kernel, edges, count, cells),
        [(2, modes, width), (modes, width), (modes, width), (modes, 16)],
        *edge_blocks, forward, one_over, solid_mask,
    )
    up = [(i, i + 1) for i in range(plane_count - 1)]
    down = [(i + 1, i) for i in range(plane_count - 1)]
    low = lax.ppermute(last, "plane", up)
    high = lax.ppermute(first, "plane", down)

    ones, made, arrived, pieces, earlier = [], [], [], [], ()
    size = len(inner) * cells
    for part in range(parts):
        blocks = [(block, part * (size + 8)) for block in near_blocks]
        blocks += [(far_blocks[part], e * (size + 8)) for e in range(half)]
        offset = part * part_width
        *outs, one = call(
            functools.partial(
                inner_kernel, inner, count, cells, offset, part_width, [base for _, base in blocks]
            ),
            [(size, part_width)] * half + [(half * size, part_width), (2, modes, part_width)],
            *[block for block, _ in blocks], forward, inverse, one_over, solid_mask, first, last,
            cost=SHORT, earlier=earlier,
        )
        ones.append(one)
        earlier = (one,)
        made.append(outs[:half])
        arrived.append(swap(outs[half], half))

    def place(part):
        return inner, part * part_tiles, part_tiles

    def onward(part, d):
        return arrived[part][d * size : (d + 1) * size]

    earlier = list(arrived[:-1])
    for part in range(parts):
        pieces += [(made[part][0], 0, 0, *place(part)), (arrived[part], half, 0, *place(part))]
        for d in near:
            if part < parts - 1:
                message = swap(join([onward(part, d), made[part][d]])[0], d)
                pieces += [(message, half + d, 0, *place(part)), (message, d, size, *place(part))]
            else:
                earlier.append(swap(made[part][d], d))
                pieces += [(earlier[-1], d, 0, *place(part))]
                pieces += [(swap(onward(part, d), d), half + d, 0, *place(part))]
    outs = call(
        functools.partial(rim_kernel, edges, parts, count, cells),
        [(len(edges) * cells, width)] * count,
        spectrum, first, last, sides, low, high, inverse, one_over, solid_mask, *ones, earlier=tuple(earlier),
    )
    pieces.append((outs[0], 0, 0, edges, 0, tiles))
    pieces += [(swap(outs[d], d), d, 0, edges, 0, tiles) for d in (*far, *near)]
    result = None
    own_lines = tiles * row_count
    for devices in (range(count - 1), [count - 1]) if own_lines % 8 == 0 else (range(count),):
        chosen = [piece for piece in pieces if piece[1] in devices]
        previous = () if result is None else (result,)
        result = pl.pallas_call(
            functools.partial(unpack_kernel, [piece[1:] for piece in chosen], list(devices), row_count, cells),
            out_shape=jax.ShapeDtypeStruct((cells, lines, LANES), jnp.float32),
            in_specs=[VMEM] * len(chosen) + [ANY] * len(previous),
            out_specs=ANY,
            scratch_shapes=[
                pltpu.VMEM((cells * (len(devices) * own_lines + 8), LANES), jnp.float32),
                pltpu.SemaphoreType.DMA((SPLIT, len(devices))),
            ],
            input_output_aliases={len(chosen): 0} if previous else {},
            compiler_params=PARAMS,
            cost_estimate=SHORT if previous else LONG,
        )(*[piece[0] for piece in chosen], *previous)
    result = result.reshape(cells, columns // LANES, row_count, LANES).transpose(0, 2, 1, 3)
    return result.reshape(cells, row_count, columns)


def solution(mesh):
    placed = (P("span", "plane", None), P("plane", None))
    return jax.shard_map(
        local, mesh=mesh, in_specs=placed, out_specs=P("span", "plane", None), check_vma=False
    )
```

```python
import functools

import jax
import jax.numpy as jnp
import ml_dtypes
import numpy as np
from jax import lax
from jax.experimental import pallas as pl
from jax.experimental.pallas import tpu as pltpu
from jax.sharding import PartitionSpec as P

PENALTY = 12.0
LANES = 128
VMEM = pl.BlockSpec(memory_space=pltpu.VMEM)
ANY = pl.BlockSpec(memory_space=pl.ANY)
PARAMS = pltpu.CompilerParams(vmem_limit_bytes=24 * 1024 * 1024)
LONG = pl.CostEstimate(flops=0, bytes_accessed=200_000_000, transcendentals=0)
SHORT = pl.CostEstimate(flops=0, bytes_accessed=1024, transcendentals=0)
SPLIT = 4


def split(values):
    high = values.astype(ml_dtypes.bfloat16)
    low = (values - high.astype(np.float64)).astype(ml_dtypes.bfloat16)
    return high, low


def tables(length, cells):
    half = length // 2
    points = np.arange(half)
    groups = []
    for parity in (0, 1):
        kept = [k for k in range(length // 2 + 1) if 3 * k <= length and k % 2 == parity]
        modes = [(k, False) for k in kept] + [(k, True) for k in kept if 0 < k < length // 2]
        groups.append(modes)
    padded = -(-max(len(modes) for modes in groups) // 16) * 16
    forward = np.zeros((2, padded, half))
    inverse = np.zeros((2, half, padded))
    fluid = np.zeros((2 * padded, 1))
    solid = np.zeros((2 * padded, 1))
    for parity, modes in enumerate(groups):
        for at, (k, sine) in enumerate(modes):
            angles = (points * k % length) * (2.0 * np.pi / length)
            wave = np.sin(angles) if sine else np.cos(angles)
            weight = 1.0 if k in (0, length // 2) else 2.0
            eigen = 2.0 - 2.0 * np.cos(2.0 * np.pi * k / length)
            forward[parity, at] = wave
            inverse[parity, :, at] = wave * weight / length
            fluid[parity * padded + at] = 1.0 / (4.0 + eigen)
            solid[parity * padded + at] = 1.0 / (4.0 + eigen + PENALTY)
    columns = np.zeros((8, -(-2 * padded // LANES) * LANES), np.float32)
    columns[0, : 2 * padded] = fluid[:, 0]
    columns[1, : 2 * padded] = solid[:, 0]
    blocks = half // cells
    high, low = split(forward.reshape(2, padded, blocks, cells).transpose(0, 2, 1, 3))
    forward = np.concatenate([high, low, high], axis=3)
    high, low = split(inverse.reshape(2, blocks, cells, padded))
    inverse = np.concatenate([high, low, high], axis=3)
    return forward, inverse, columns


def thirds(values, axis):
    high = values.astype(jnp.bfloat16)
    low = (values - high.astype(jnp.float32)).astype(jnp.bfloat16)
    return jnp.concatenate([high, high, low], axis=axis)


def pack_kernel(jobs, row_count, cells, earlier, x_ref, *refs):
    outs, (held, arrived) = refs[earlier:-2], refs[-2:]
    me = lax.axis_index("span")
    lines = x_ref.shape[1]
    all_tiles = lines // row_count
    own_tiles = all_tiles // lax.axis_size("span")
    pitch = held.shape[0] // cells
    some = cells // SPLIT
    copies = [
        pltpu.make_async_copy(
            x_ref.at[pl.ds(part * some, some)],
            held.reshape(cells, pitch, LANES).at[pl.ds(part * some, some), pl.ds(0, lines)],
            arrived.at[part],
        )
        for part in range(SPLIT)
    ]
    for copy in copies:
        copy.start()
    lane = lax.broadcasted_iota(jnp.int32, (some, LANES), 1)
    sides = []
    for part, copy in enumerate(copies):
        copy.wait()
        beside = jnp.zeros((some, LANES), jnp.float32)

        def line(tile, row):
            return held[pl.ds(part * some * pitch + tile * row_count + row, some, stride=pitch), :]

        for job, (out, base, d, rows, offset, tiles) in enumerate(jobs):
            first = jnp.bitwise_xor(me, d) * own_tiles + offset
            for i, row in enumerate(rows):
                at = base + i * cells + part * some
                for tile in range(tiles):
                    outs[out][at : at + some, tile * LANES : (tile + 1) * LANES] = line(first + tile, row)
                before = jnp.maximum(first - 1, 0)
                after = jnp.minimum(first + tiles, all_tiles - 1)
                for side, (tile, source) in enumerate(((before, LANES - 1), (after, 0))):
                    at = job * 8 + i * 2 + side
                    beside = jnp.where(lane == at, pltpu.roll(line(tile, row), (at - source) % LANES, 1), beside)
        sides.append(beside)
    if cells < LANES:
        sides.append(jnp.zeros((LANES - cells, LANES), jnp.float32))
    turned = jnp.concatenate(sides, axis=0).T
    for job, (out, base, _, rows, _, tiles) in enumerate(jobs):
        at = base + len(rows) * cells
        outs[out][at : at + 8, :LANES] = turned[job * 8 : (job + 1) * 8]
        if tiles > 1:
            outs[out][at : at + 8, LANES:] = jnp.zeros((8, (tiles - 1) * LANES), jnp.float32)


def transform(rows, count, cells, blocks, forward_ref):
    me = lax.axis_index("span")
    half = count // 2
    spectra = []
    for i in range(rows + 1):
        parts = []
        for parity in (0, 1):
            total = None
            for d in range(half):
                table = forward_ref[parity, jnp.bitwise_and(jnp.bitwise_xor(me, d), half - 1)]
                if i < rows:
                    near = blocks[d][i * cells : (i + 1) * cells, :]
                    far = blocks[d + half][i * cells : (i + 1) * cells, :]
                else:
                    near = blocks[d][rows * cells :, :cells]
                    far = blocks[d + half][rows * cells :, :cells]
                value = near + far if parity == 0 else near - far
                if i < rows:
                    term = jnp.dot(table, thirds(value, 0), preferred_element_type=jnp.float32)
                else:
                    value = jnp.concatenate([value, jnp.zeros_like(value)], axis=0)
                    term = lax.dot_general(
                        table, thirds(value, 1), (((1,), (1,)), ((), ())), preferred_element_type=jnp.float32
                    )
                total = term if total is None else total + term
            parts.append(total)
        spectra.append(jnp.concatenate(parts, axis=0))
    return spectra[:-1], spectra[-1]


def inverse_rows(sweeps, count, cells, inverse_ref, outs):
    me = lax.axis_index("span")
    half = count // 2
    padded = sweeps[0].shape[0] // 2
    for i, sweep in enumerate(sweeps):
        even = thirds(sweep[:padded], 0)
        odd = thirds(sweep[padded:], 0)
        for d in range(half):
            place = jnp.bitwise_and(jnp.bitwise_xor(me, d), half - 1)
            first = jnp.dot(inverse_ref[0, place], even, preferred_element_type=jnp.float32)
            second = jnp.dot(inverse_ref[1, place], odd, preferred_element_type=jnp.float32)
            outs[d][i * cells : (i + 1) * cells, :] = first + second
            outs[d + half][i * cells : (i + 1) * cells, :] = first - second


def second_sweep(spectrum, one, above, below, sides, at, inverse_diagonal):
    width = one.shape[1]
    lane = lax.broadcasted_iota(jnp.int32, one.shape, 1)
    left = jnp.where(lane == 0, sides[:, at : at + 1], pltpu.roll(one, 1, 1))
    right = jnp.where(lane == width - 1, sides[:, at + 1 : at + 2], pltpu.roll(one, width - 1, 1))
    return (spectrum + above + below + left + right) * inverse_diagonal


def reciprocals(mask_ref, columns_ref, modes, rows, offset, width):
    turned = columns_ref[...].T
    fluid, solid = turned[:modes, 0:1], turned[:modes, 1:2]
    own = mask_ref.shape[1] // lax.axis_size("span")
    start = pl.multiple_of(lax.axis_index("span") * own + offset, LANES)
    last = mask_ref.shape[1] - LANES
    before = mask_ref[:, pl.ds(pl.multiple_of(jnp.maximum(start - LANES, 0), LANES), LANES)][:, LANES - 1 :]
    after = mask_ref[:, pl.ds(pl.multiple_of(jnp.minimum(start + width, last), LANES), LANES)][:, :1]
    before = jnp.where(start == 0, 2, before)
    after = jnp.where(start + width == mask_ref.shape[1], 2, after)
    lane = lax.broadcasted_iota(jnp.int32, (1, 16), 1)
    kinds = jnp.full((1, 16), 2, jnp.int32)
    diagonals = []
    for i, row in enumerate(rows):
        kinds = jnp.where(lane == 2 * i, before[row : row + 1], kinds)
        kinds = jnp.where(lane == 2 * i + 1, after[row : row + 1], kinds)
        mask = mask_ref[row : row + 1, pl.ds(start, width)]
        diagonals.append(jnp.where(mask != 0, solid, fluid))
    return diagonals, jnp.where(kinds == 0, fluid, jnp.where(kinds == 1, solid, 0.0))


def views(refs, places, size):
    return [ref.at[base : base + size] for ref, base in zip(refs, places)]


def edge_kernel(rows, count, cells, *refs):
    blocks, (forward_ref, columns_ref, mask_ref) = refs[:count], refs[count : count + 3]
    spectrum_ref, first_ref, last_ref, sides_ref = refs[count + 3 :]
    spectra, sides = transform(len(rows), count, cells, blocks, forward_ref)
    modes, width = spectra[0].shape
    diagonals, beside = reciprocals(mask_ref, columns_ref, modes, rows, 0, width)
    for i, one_ref in enumerate((first_ref, last_ref)):
        spectrum_ref[i] = spectra[i]
        one_ref[...] = spectra[i] * diagonals[i]
    sides_ref[...] = sides * beside


def inner_kernel(rows, count, cells, offset, width, places, *refs):
    half = count // 2
    blocks = views(refs, places, len(rows) * cells + 8)
    forward_ref, inverse_ref, columns_ref, mask_ref, first_ref, last_ref = refs[count : count + 6]
    outs, far_ref, ones_ref = refs[-2 - half : -2], refs[-2], refs[-1]
    spectra, sides = transform(len(rows), count, cells, blocks, forward_ref)
    diagonals, beside = reciprocals(mask_ref, columns_ref, spectra[0].shape[0], rows, offset, width)
    sides = sides * beside
    ones = [spectrum * diagonal for spectrum, diagonal in zip(spectra, diagonals)]
    ones_ref[0] = ones[0]
    ones_ref[1] = ones[-1]
    around = [first_ref[:, offset : offset + width], *ones, last_ref[:, offset : offset + width]]
    sweeps = [
        second_sweep(spectra[i], ones[i], around[i], around[i + 2], sides, 2 * i, diagonals[i])
        for i in range(len(rows))
    ]
    size = len(rows) * cells
    inverse_rows(sweeps, count, cells, inverse_ref, [*outs, *views([far_ref] * half, range(0, half * size, size), size)])


def rim_kernel(rows, parts, count, cells, *refs):
    spectrum_ref, first_ref, last_ref, sides_ref, low_ref, high_ref, inverse_ref, columns_ref, mask_ref = refs[:9]
    ones, outs = refs[9 : 9 + parts], refs[-count:]
    modes, width = first_ref.shape
    diagonals, _ = reciprocals(mask_ref, columns_ref, modes, rows, 0, width)
    sides = sides_ref[...]
    inner = [jnp.concatenate([one[i] for one in ones], axis=1) for i in (0, 1)]
    sweeps = [
        second_sweep(spectrum_ref[0], first_ref[...], low_ref[...], inner[0], sides, 0, diagonals[0]),
        second_sweep(spectrum_ref[1], last_ref[...], inner[1], high_ref[...], sides, 2, diagonals[1]),
    ]
    inverse_rows(sweeps, count, cells, inverse_ref, outs)


def join_kernel(groups, size, *refs):
    outs = refs[-groups:]
    for group, out_ref in enumerate(outs):
        at = 0
        for ref in refs[group * size : (group + 1) * size]:
            out_ref[at : at + ref.shape[0], :] = ref[...]
            at += ref.shape[0]


def unpack_kernel(pieces, devices, row_count, cells, *refs):
    me = lax.axis_index("span")
    blocks, (out_ref, held, done) = refs[: len(pieces)], refs[-3:]
    pitch = held.shape[0] // cells
    own_lines = out_ref.shape[1] // lax.axis_size("span")
    some = cells // SPLIT
    copies = []
    for part in range(SPLIT):
        for block, (d, base, rows, offset, tiles) in zip(blocks, pieces):
            for i, row in enumerate(rows):
                line = base + i * cells + part * some
                for tile in range(tiles):
                    at = part * some * pitch + devices.index(d) * own_lines + (offset + tile) * row_count + row
                    held[pl.ds(at, some, stride=pitch), :] = block[line : line + some, tile * LANES : (tile + 1) * LANES]
        for at, d in enumerate(devices):
            first = pl.multiple_of(jnp.bitwise_xor(me, d) * own_lines, own_lines)
            copies.append(
                pltpu.make_async_copy(
                    held.reshape(cells, pitch, LANES).at[pl.ds(part * some, some), pl.ds(at * own_lines, own_lines)],
                    out_ref.at[pl.ds(part * some, some), pl.ds(first, own_lines)],
                    done.at[part, at],
                )
            )
            copies[-1].start()
    for copy in copies:
        copy.wait()


def call(kernel, outs, *args, cost=LONG, earlier=()):
    shapes = [jax.ShapeDtypeStruct(shape, jnp.float32) for shape in outs]
    return pl.pallas_call(
        kernel,
        out_shape=shapes,
        in_specs=[VMEM] * len(args) + [ANY] * len(earlier),
        out_specs=[VMEM] * len(outs),
        compiler_params=PARAMS,
        cost_estimate=cost,
    )(*args, *earlier)


def join(*groups, earlier=()):
    shapes = [(sum(block.shape[0] for block in group), group[0].shape[1]) for group in groups]
    blocks = [block for group in groups for block in group]
    return call(functools.partial(join_kernel, len(groups), len(groups[0])), shapes, *blocks, cost=SHORT, earlier=earlier)


def swap(block, d):
    return lax.ppermute(block, "span", [(i, i ^ d) for i in range(lax.axis_size("span"))])


def local(pressure_source, solid_mask):
    count = lax.axis_size("span")
    half = count // 2
    plane_count = lax.axis_size("plane")
    cells, row_count, columns = pressure_source.shape
    width = columns // count
    tiles = width // LANES
    parts = 2 if tiles % 2 == 0 else 1
    part_tiles, part_width = tiles // parts, width // parts
    inner = tuple(range(1, row_count - 1))
    edges = (0, row_count - 1)
    near, far = range(1, half), range(half, count)
    forward, inverse, one_over = map(jnp.asarray, tables(cells * count, cells))
    modes = 2 * forward.shape[2]

    lines = columns // LANES * row_count
    source = pressure_source.reshape(cells, row_count, columns // LANES, LANES).transpose(0, 2, 1, 3)
    source = source.reshape(cells, lines, LANES)
    scratch = [pltpu.VMEM((cells * (lines + 8), LANES), jnp.float32), pltpu.SemaphoreType.DMA((SPLIT,))]

    def pack(source, jobs, shapes, *earlier):
        return pl.pallas_call(
            functools.partial(pack_kernel, jobs, row_count, cells, len(earlier)),
            out_shape=[jax.ShapeDtypeStruct(shape, jnp.float32) for shape in shapes],
            in_specs=[ANY] * (1 + len(earlier)),
            out_specs=[VMEM] * len(shapes),
            scratch_shapes=scratch,
            compiler_params=PARAMS,
            cost_estimate=LONG,
        )(source, *earlier)

    edge_size, size = len(edges) * cells + 8, len(inner) * cells + 8
    jobs = [(d - 1, 0, d, edges, 0, tiles) for d in range(1, count)]
    packed = pack(pltpu.with_memory_space_constraint(source, pltpu.HBM), jobs, [(edge_size, width)] * (count - 1))
    edge_blocks = [swap(block, d) for d, block in enumerate(packed, 1)]
    jobs, shapes = [(0, 0, 0, edges, 0, tiles)], [(edge_size, width)]

    def add(d, wanted):
        jobs.extend(
            (len(shapes), at * size, d, inner, part * part_tiles, part_tiles) for at, part in enumerate(wanted)
        )
        shapes.append((len(wanted) * size, part_width))

    for d in range(half):
        add(d, range(parts))
    for part in range(parts):
        for d in far:
            add(d, [part])
    packed = pack(source, jobs, shapes, packed[half - 1])
    edge_blocks = [packed[0], *edge_blocks]
    near_blocks = [packed[1]] + [swap(packed[1 + d], d) for d in near]
    messages = []
    for part in range(parts):
        mine = packed[1 + half * (part + 1) : 1 + half * (part + 2)]
        messages.append([mine[0]] + [swap(mine[d], d) for d in near])
    far_blocks = [swap(message, half) for message in join(*messages, earlier=(edge_blocks[half],))]

    spectrum, first, last, sides = call(
        functools.partial(edge_kernel, edges, count, cells),
        [(2, modes, width), (modes, width), (modes, width), (modes, 16)],
        *edge_blocks, forward, one_over, solid_mask,
    )
    up = [(i, i + 1) for i in range(plane_count - 1)]
    down = [(i + 1, i) for i in range(plane_count - 1)]
    low = lax.ppermute(last, "plane", up)
    high = lax.ppermute(first, "plane", down)

    ones, made, arrived, pieces, earlier = [], [], [], [], ()
    size = len(inner) * cells
    for part in range(parts):
        blocks = [(block, part * (size + 8)) for block in near_blocks]
        blocks += [(far_blocks[part], e * (size + 8)) for e in range(half)]
        offset = part * part_width
        *outs, one = call(
            functools.partial(
                inner_kernel, inner, count, cells, offset, part_width, [base for _, base in blocks]
            ),
            [(size, part_width)] * half + [(half * size, part_width), (2, modes, part_width)],
            *[block for block, _ in blocks], forward, inverse, one_over, solid_mask, first, last,
            cost=SHORT, earlier=earlier,
        )
        ones.append(one)
        earlier = (one,)
        made.append(outs[:half])
        arrived.append(swap(outs[half], half))

    def place(part):
        return inner, part * part_tiles, part_tiles

    def onward(part, d):
        return arrived[part][d * size : (d + 1) * size]

    earlier = list(arrived[:-1])
    for part in range(parts):
        pieces += [(made[part][0], 0, 0, *place(part)), (arrived[part], half, 0, *place(part))]
        for d in near:
            if part < parts - 1:
                message = swap(join([onward(part, d), made[part][d]])[0], d)
                pieces += [(message, half + d, 0, *place(part)), (message, d, size, *place(part))]
            else:
                earlier.append(swap(made[part][d], d))
                pieces += [(earlier[-1], d, 0, *place(part))]
                pieces += [(swap(onward(part, d), d), half + d, 0, *place(part))]
    outs = call(
        functools.partial(rim_kernel, edges, parts, count, cells),
        [(len(edges) * cells, width)] * count,
        spectrum, first, last, sides, low, high, inverse, one_over, solid_mask, *ones, earlier=tuple(earlier),
    )
    pieces.append((outs[0], 0, 0, edges, 0, tiles))
    pieces += [(swap(outs[d], d), d, 0, edges, 0, tiles) for d in (*far, *near)]
    result = None
    own_lines = tiles * row_count
    for devices in (range(count - 1), [count - 1]) if own_lines % 8 == 0 else (range(count),):
        chosen = [piece for piece in pieces if piece[1] in devices]
        previous = () if result is None else (result,)
        result = pl.pallas_call(
            functools.partial(unpack_kernel, [piece[1:] for piece in chosen], list(devices), row_count, cells),
            out_shape=jax.ShapeDtypeStruct((cells, lines, LANES), jnp.float32),
            in_specs=[VMEM] * len(chosen) + [ANY] * len(previous),
            out_specs=ANY,
            scratch_shapes=[
                pltpu.VMEM((cells * (len(devices) * own_lines + 8), LANES), jnp.float32),
                pltpu.SemaphoreType.DMA((SPLIT, len(devices))),
            ],
            input_output_aliases={len(chosen): 0} if previous else {},
            compiler_params=PARAMS,
            cost_estimate=SHORT if previous else LONG,
        )(*[piece[0] for piece in chosen], *previous)
    result = result.reshape(cells, columns // LANES, row_count, LANES).transpose(0, 2, 1, 3)
    return result.reshape(cells, row_count, columns)


def solution(mesh):
    placed = (P("span", "plane", None), P("plane", None))
    return jax.shard_map(
        local, mesh=mesh, in_specs=placed, out_specs=P("span", "plane", None), check_vma=False
    )
```

```python
import functools

import jax
import jax.numpy as jnp
import ml_dtypes
import numpy as np
from jax import lax
from jax.experimental import pallas as pl
from jax.experimental.pallas import tpu as pltpu
from jax.sharding import PartitionSpec as P

PENALTY = 12.0
LANES = 128
VMEM = pl.BlockSpec(memory_space=pltpu.VMEM)
ANY = pl.BlockSpec(memory_space=pl.ANY)
PARAMS = pltpu.CompilerParams(vmem_limit_bytes=24 * 1024 * 1024)
LONG = pl.CostEstimate(flops=0, bytes_accessed=200_000_000, transcendentals=0)
SHORT = pl.CostEstimate(flops=0, bytes_accessed=1024, transcendentals=0)
SPLIT = 4


def split(values):
    high = values.astype(ml_dtypes.bfloat16)
    low = (values - high.astype(np.float64)).astype(ml_dtypes.bfloat16)
    return high, low


def tables(length, cells):
    half = length // 2
    points = np.arange(half)
    groups = []
    for parity in (0, 1):
        kept = [k for k in range(length // 2 + 1) if 3 * k <= length and k % 2 == parity]
        modes = [(k, False) for k in kept] + [(k, True) for k in kept if 0 < k < length // 2]
        groups.append(modes)
    padded = -(-max(len(modes) for modes in groups) // 16) * 16
    forward = np.zeros((2, padded, half))
    inverse = np.zeros((2, half, padded))
    fluid = np.zeros((2 * padded, 1))
    solid = np.zeros((2 * padded, 1))
    for parity, modes in enumerate(groups):
        for at, (k, sine) in enumerate(modes):
            angles = (points * k % length) * (2.0 * np.pi / length)
            wave = np.sin(angles) if sine else np.cos(angles)
            weight = 1.0 if k in (0, length // 2) else 2.0
            eigen = 2.0 - 2.0 * np.cos(2.0 * np.pi * k / length)
            forward[parity, at] = wave
            inverse[parity, :, at] = wave * weight / length
            fluid[parity * padded + at] = 1.0 / (4.0 + eigen)
            solid[parity * padded + at] = 1.0 / (4.0 + eigen + PENALTY)
    columns = np.zeros((8, -(-2 * padded // LANES) * LANES), np.float32)
    columns[0, : 2 * padded] = fluid[:, 0]
    columns[1, : 2 * padded] = solid[:, 0]
    blocks = half // cells
    high, low = split(forward.reshape(2, padded, blocks, cells).transpose(0, 2, 1, 3))
    forward = np.concatenate([high, low, high], axis=3)
    high, low = split(inverse.reshape(2, blocks, cells, padded))
    inverse = np.concatenate([high, low, high], axis=3)
    return forward, inverse, columns


def thirds(values, axis):
    high = values.astype(jnp.bfloat16)
    low = (values - high.astype(jnp.float32)).astype(jnp.bfloat16)
    return jnp.concatenate([high, high, low], axis=axis)


def pack_kernel(jobs, row_count, cells, earlier, x_ref, *refs):
    outs, (held, arrived) = refs[earlier:-2], refs[-2:]
    me = lax.axis_index("span")
    lines = x_ref.shape[1]
    all_tiles = lines // row_count
    own_tiles = all_tiles // lax.axis_size("span")
    pitch = held.shape[0] // cells
    some = cells // SPLIT
    copies = [
        pltpu.make_async_copy(
            x_ref.at[pl.ds(part * some, some)],
            held.reshape(cells, pitch, LANES).at[pl.ds(part * some, some), pl.ds(0, lines)],
            arrived.at[part],
        )
        for part in range(SPLIT)
    ]
    for copy in copies:
        copy.start()
    lane = lax.broadcasted_iota(jnp.int32, (some, LANES), 1)
    sides = []
    for part, copy in enumerate(copies):
        copy.wait()
        beside = jnp.zeros((some, LANES), jnp.float32)

        def line(tile, row):
            return held[pl.ds(part * some * pitch + tile * row_count + row, some, stride=pitch), :]

        for job, (out, base, d, rows, offset, tiles) in enumerate(jobs):
            first = jnp.bitwise_xor(me, d) * own_tiles + offset
            for i, row in enumerate(rows):
                at = base + i * cells + part * some
                for tile in range(tiles):
                    outs[out][at : at + some, tile * LANES : (tile + 1) * LANES] = line(first + tile, row)
                before = jnp.maximum(first - 1, 0)
                after = jnp.minimum(first + tiles, all_tiles - 1)
                for side, (tile, source) in enumerate(((before, LANES - 1), (after, 0))):
                    at = job * 8 + i * 2 + side
                    beside = jnp.where(lane == at, pltpu.roll(line(tile, row), (at - source) % LANES, 1), beside)
        sides.append(beside)
    if cells < LANES:
        sides.append(jnp.zeros((LANES - cells, LANES), jnp.float32))
    turned = jnp.concatenate(sides, axis=0).T
    for job, (out, base, _, rows, _, tiles) in enumerate(jobs):
        at = base + len(rows) * cells
        outs[out][at : at + 8, :LANES] = turned[job * 8 : (job + 1) * 8]
        if tiles > 1:
            outs[out][at : at + 8, LANES:] = jnp.zeros((8, (tiles - 1) * LANES), jnp.float32)


def transform(rows, count, cells, blocks, forward_ref):
    me = lax.axis_index("span")
    half = count // 2
    spectra = []
    for i in range(rows + 1):
        parts = []
        for parity in (0, 1):
            total = None
            for d in range(half):
                table = forward_ref[parity, jnp.bitwise_and(jnp.bitwise_xor(me, d), half - 1)]
                if i < rows:
                    near = blocks[d][i * cells : (i + 1) * cells, :]
                    far = blocks[d + half][i * cells : (i + 1) * cells, :]
                else:
                    near = blocks[d][rows * cells :, :cells]
                    far = blocks[d + half][rows * cells :, :cells]
                value = near + far if parity == 0 else near - far
                if i < rows:
                    term = jnp.dot(table, thirds(value, 0), preferred_element_type=jnp.float32)
                else:
                    value = jnp.concatenate([value, jnp.zeros_like(value)], axis=0)
                    term = lax.dot_general(
                        table, thirds(value, 1), (((1,), (1,)), ((), ())), preferred_element_type=jnp.float32
                    )
                total = term if total is None else total + term
            parts.append(total)
        spectra.append(jnp.concatenate(parts, axis=0))
    return spectra[:-1], spectra[-1]


def inverse_rows(sweeps, count, cells, inverse_ref, outs):
    me = lax.axis_index("span")
    half = count // 2
    padded = sweeps[0].shape[0] // 2
    for i, sweep in enumerate(sweeps):
        even = thirds(sweep[:padded], 0)
        odd = thirds(sweep[padded:], 0)
        for d in range(half):
            place = jnp.bitwise_and(jnp.bitwise_xor(me, d), half - 1)
            first = jnp.dot(inverse_ref[0, place], even, preferred_element_type=jnp.float32)
            second = jnp.dot(inverse_ref[1, place], odd, preferred_element_type=jnp.float32)
            outs[d][i * cells : (i + 1) * cells, :] = first + second
            outs[d + half][i * cells : (i + 1) * cells, :] = first - second


def second_sweep(spectrum, one, above, below, sides, at, inverse_diagonal):
    width = one.shape[1]
    lane = lax.broadcasted_iota(jnp.int32, one.shape, 1)
    left = jnp.where(lane == 0, sides[:, at : at + 1], pltpu.roll(one, 1, 1))
    right = jnp.where(lane == width - 1, sides[:, at + 1 : at + 2], pltpu.roll(one, width - 1, 1))
    return (spectrum + above + below + left + right) * inverse_diagonal


def reciprocals(mask_ref, columns_ref, modes, rows, offset, width):
    turned = columns_ref[...].T
    fluid, solid = turned[:modes, 0:1], turned[:modes, 1:2]
    own = mask_ref.shape[1] // lax.axis_size("span")
    start = pl.multiple_of(lax.axis_index("span") * own + offset, LANES)
    last = mask_ref.shape[1] - LANES
    before = mask_ref[:, pl.ds(pl.multiple_of(jnp.maximum(start - LANES, 0), LANES), LANES)][:, LANES - 1 :]
    after = mask_ref[:, pl.ds(pl.multiple_of(jnp.minimum(start + width, last), LANES), LANES)][:, :1]
    before = jnp.where(start == 0, 2, before)
    after = jnp.where(start + width == mask_ref.shape[1], 2, after)
    lane = lax.broadcasted_iota(jnp.int32, (1, 16), 1)
    kinds = jnp.full((1, 16), 2, jnp.int32)
    diagonals = []
    for i, row in enumerate(rows):
        kinds = jnp.where(lane == 2 * i, before[row : row + 1], kinds)
        kinds = jnp.where(lane == 2 * i + 1, after[row : row + 1], kinds)
        mask = mask_ref[row : row + 1, pl.ds(start, width)]
        diagonals.append(jnp.where(mask != 0, solid, fluid))
    return diagonals, jnp.where(kinds == 0, fluid, jnp.where(kinds == 1, solid, 0.0))


def views(refs, places, size):
    return [ref.at[base : base + size] for ref, base in zip(refs, places)]


def paired_edge():
    return lax.rem(lax.axis_index("plane") + 1, 2)


def edge_kernel(rows, count, cells, *refs):
    blocks, (forward_ref, columns_ref, mask_ref) = refs[:count], refs[count : count + 3]
    spectrum_ref, ones_ref, paired_ref, other_ref, sides_ref = refs[count + 3 :]
    spectra, sides = transform(len(rows), count, cells, blocks, forward_ref)
    modes, width = spectra[0].shape
    diagonals, beside = reciprocals(mask_ref, columns_ref, modes, rows, 0, width)
    ones = [spectrum * diagonal for spectrum, diagonal in zip(spectra, diagonals)]
    for i in (0, 1):
        spectrum_ref[i] = spectra[i]
        ones_ref[i] = ones[i]
    last = paired_edge() == 1
    paired_ref[...] = jnp.where(last, ones[1], ones[0])
    other_ref[...] = jnp.where(last, ones[0], ones[1])
    sides_ref[...] = sides * beside


def inner_kernel(rows, count, cells, offset, width, places, *refs):
    half = count // 2
    blocks = views(refs, places, len(rows) * cells + 8)
    forward_ref, inverse_ref, columns_ref, mask_ref, edges_ref = refs[count : count + 5]
    outs, far_ref, ones_ref = refs[-2 - half : -2], refs[-2], refs[-1]
    spectra, sides = transform(len(rows), count, cells, blocks, forward_ref)
    diagonals, beside = reciprocals(mask_ref, columns_ref, spectra[0].shape[0], rows, offset, width)
    sides = sides * beside
    ones = [spectrum * diagonal for spectrum, diagonal in zip(spectra, diagonals)]
    ones_ref[0] = ones[0]
    ones_ref[1] = ones[-1]
    around = [edges_ref[0, :, offset : offset + width], *ones, edges_ref[1, :, offset : offset + width]]
    sweeps = [
        second_sweep(spectra[i], ones[i], around[i], around[i + 2], sides, 2 * i, diagonals[i])
        for i in range(len(rows))
    ]
    size = len(rows) * cells
    inverse_rows(sweeps, count, cells, inverse_ref, [*outs, *views([far_ref] * half, range(0, half * size, size), size)])


def rim_kernel(rows, order, parts, count, cells, *refs):
    spectrum_ref, edges_ref, sides_ref, halo_ref, inverse_ref, columns_ref, mask_ref = refs[:7]
    ones, outs = refs[7 : 7 + parts], refs[-count:]
    _, modes, width = edges_ref.shape
    edge = paired_edge() if order == 0 else 1 - paired_edge()
    diagonals, _ = reciprocals(mask_ref, columns_ref, modes, rows, 0, width)
    sides = jnp.where(edge == 0, sides_ref[:, 0:2], sides_ref[:, 2:4])
    beneath = jnp.concatenate([one[edge] for one in ones], axis=1)
    diagonal = jnp.where(edge == 0, diagonals[0], diagonals[1])
    sweep = second_sweep(spectrum_ref[edge], edges_ref[edge], halo_ref[...], beneath, sides, 0, diagonal)
    inverse_rows([sweep], count, cells, inverse_ref, outs)


def join_kernel(groups, size, *refs):
    outs = refs[-groups:]
    for group, out_ref in enumerate(outs):
        at = 0
        for ref in refs[group * size : (group + 1) * size]:
            out_ref[at : at + ref.shape[0], :] = ref[...]
            at += ref.shape[0]


def unpack_kernel(pieces, devices, row_count, cells, *refs):
    me = lax.axis_index("span")
    blocks, (out_ref, held, done) = refs[: len(pieces)], refs[-3:]
    pitch = held.shape[0] // cells
    own_lines = out_ref.shape[1] // lax.axis_size("span")
    some = cells // SPLIT
    edge_rows = {"near": paired_edge() * (row_count - 1), "far": (1 - paired_edge()) * (row_count - 1)}
    copies = []
    for part in range(SPLIT):
        for block, (d, base, rows, offset, tiles) in zip(blocks, pieces):
            for i, row in enumerate(rows):
                if row in edge_rows:
                    row = edge_rows[row]
                line = base + i * cells + part * some
                for tile in range(tiles):
                    at = part * some * pitch + devices.index(d) * own_lines + (offset + tile) * row_count + row
                    held[pl.ds(at, some, stride=pitch), :] = block[line : line + some, tile * LANES : (tile + 1) * LANES]
        for at, d in enumerate(devices):
            first = pl.multiple_of(jnp.bitwise_xor(me, d) * own_lines, own_lines)
            copies.append(
                pltpu.make_async_copy(
                    held.reshape(cells, pitch, LANES).at[pl.ds(part * some, some), pl.ds(at * own_lines, own_lines)],
                    out_ref.at[pl.ds(part * some, some), pl.ds(first, own_lines)],
                    done.at[part, at],
                )
            )
            copies[-1].start()
    for copy in copies:
        copy.wait()


def call(kernel, outs, *args, cost=LONG, earlier=()):
    shapes = [jax.ShapeDtypeStruct(shape, jnp.float32) for shape in outs]
    return pl.pallas_call(
        kernel,
        out_shape=shapes,
        in_specs=[VMEM] * len(args) + [ANY] * len(earlier),
        out_specs=[VMEM] * len(outs),
        compiler_params=PARAMS,
        cost_estimate=cost,
    )(*args, *earlier)


def join(*groups, earlier=()):
    shapes = [(sum(block.shape[0] for block in group), group[0].shape[1]) for group in groups]
    blocks = [block for group in groups for block in group]
    return call(functools.partial(join_kernel, len(groups), len(groups[0])), shapes, *blocks, cost=SHORT, earlier=earlier)


def swap(block, d):
    return lax.ppermute(block, "span", [(i, i ^ d) for i in range(lax.axis_size("span"))])


def local(pressure_source, solid_mask):
    count = lax.axis_size("span")
    half = count // 2
    plane_count = lax.axis_size("plane")
    cells, row_count, columns = pressure_source.shape
    width = columns // count
    tiles = width // LANES
    parts = 2 if tiles % 2 == 0 else 1
    part_tiles, part_width = tiles // parts, width // parts
    inner = tuple(range(1, row_count - 1))
    edges = (0, row_count - 1)
    near, far = range(1, half), range(half, count)
    forward, inverse, one_over = map(jnp.asarray, tables(cells * count, cells))
    modes = 2 * forward.shape[2]

    lines = columns // LANES * row_count
    source = pressure_source.reshape(cells, row_count, columns // LANES, LANES).transpose(0, 2, 1, 3)
    source = source.reshape(cells, lines, LANES)
    scratch = [pltpu.VMEM((cells * (lines + 8), LANES), jnp.float32), pltpu.SemaphoreType.DMA((SPLIT,))]

    def pack(source, jobs, shapes, *earlier):
        return pl.pallas_call(
            functools.partial(pack_kernel, jobs, row_count, cells, len(earlier)),
            out_shape=[jax.ShapeDtypeStruct(shape, jnp.float32) for shape in shapes],
            in_specs=[ANY] * (1 + len(earlier)),
            out_specs=[VMEM] * len(shapes),
            scratch_shapes=scratch,
            compiler_params=PARAMS,
            cost_estimate=LONG,
        )(source, *earlier)

    edge_size, size = len(edges) * cells + 8, len(inner) * cells + 8
    jobs = [(d - 1, 0, d, edges, 0, tiles) for d in range(1, count)]
    packed = pack(pltpu.with_memory_space_constraint(source, pltpu.HBM), jobs, [(edge_size, width)] * (count - 1))
    edge_blocks = [swap(block, d) for d, block in enumerate(packed, 1)]
    jobs, shapes = [(0, 0, 0, edges, 0, tiles)], [(edge_size, width)]

    def add(d, wanted):
        jobs.extend(
            (len(shapes), at * size, d, inner, part * part_tiles, part_tiles) for at, part in enumerate(wanted)
        )
        shapes.append((len(wanted) * size, part_width))

    for d in range(half):
        add(d, range(parts))
    for part in range(parts):
        for d in far:
            add(d, [part])
    packed = pack(source, jobs, shapes, packed[half - 1])
    edge_blocks = [packed[0], *edge_blocks]
    near_blocks = [packed[1]] + [swap(packed[1 + d], d) for d in near]
    messages = []
    for part in range(parts):
        mine = packed[1 + half * (part + 1) : 1 + half * (part + 2)]
        messages.append([mine[0]] + [swap(mine[d], d) for d in near])
    far_blocks = [swap(message, half) for message in join(*messages, earlier=(edge_blocks[half],))]

    spectrum, edge_ones, paired, other, sides = call(
        functools.partial(edge_kernel, edges, count, cells),
        [(2, modes, width), (2, modes, width), (modes, width), (modes, width), (modes, 16)],
        *edge_blocks, forward, one_over, solid_mask,
    )
    pairs = [[(i, i ^ 1) for i in range(plane_count)], [(i, ((i + 1) ^ 1) - 1) for i in range(plane_count)]]
    halos = [
        lax.ppermute(row, "plane", [(i, j) for i, j in pair if 0 <= j < plane_count])
        for row, pair in zip((paired, other), pairs)
    ]

    ones, made, arrived, pieces, earlier = [], [], [], [], ()
    size = len(inner) * cells
    for part in range(parts):
        blocks = [(block, part * (size + 8)) for block in near_blocks]
        blocks += [(far_blocks[part], e * (size + 8)) for e in range(half)]
        offset = part * part_width
        *outs, one = call(
            functools.partial(
                inner_kernel, inner, count, cells, offset, part_width, [base for _, base in blocks]
            ),
            [(size, part_width)] * half + [(half * size, part_width), (2, modes, part_width)],
            *[block for block, _ in blocks], forward, inverse, one_over, solid_mask, edge_ones,
            cost=SHORT, earlier=earlier,
        )
        ones.append(one)
        earlier = (one,)
        made.append(outs[:half])
        arrived.append(swap(outs[half], half))

    def place(part):
        return inner, part * part_tiles, part_tiles

    def onward(part, d):
        return arrived[part][d * size : (d + 1) * size]

    earlier = list(arrived[:-1])
    for part in range(parts):
        pieces += [(made[part][0], 0, 0, *place(part)), (arrived[part], half, 0, *place(part))]
        for d in near:
            if part < parts - 1:
                message = swap(join([onward(part, d), made[part][d]])[0], d)
                pieces += [(message, half + d, 0, *place(part)), (message, d, size, *place(part))]
            else:
                earlier.append(swap(made[part][d], d))
                pieces += [(earlier[-1], d, 0, *place(part))]
                pieces += [(swap(onward(part, d), d), half + d, 0, *place(part))]
    before = ()
    for order, name in enumerate(("near", "far")):
        outs = call(
            functools.partial(rim_kernel, edges, order, parts, count, cells),
            [(cells, width)] * count,
            spectrum, edge_ones, sides, halos[order], inverse, one_over, solid_mask, *ones,
            cost=LONG if order else SHORT, earlier=(*before, *earlier) if order else (),
        )
        before = (outs[-1],)
        pieces.append((outs[0], 0, 0, (name,), 0, tiles))
        pieces += [(swap(outs[d], d), d, 0, (name,), 0, tiles) for d in (*far, *near)]
    result = None
    own_lines = tiles * row_count
    for devices in (range(count - 1), [count - 1]) if own_lines % 8 == 0 else (range(count),):
        chosen = [piece for piece in pieces if piece[1] in devices]
        previous = () if result is None else (result,)
        result = pl.pallas_call(
            functools.partial(unpack_kernel, [piece[1:] for piece in chosen], list(devices), row_count, cells),
            out_shape=jax.ShapeDtypeStruct((cells, lines, LANES), jnp.float32),
            in_specs=[VMEM] * len(chosen) + [ANY] * len(previous),
            out_specs=ANY,
            scratch_shapes=[
                pltpu.VMEM((cells * (len(devices) * own_lines + 8), LANES), jnp.float32),
                pltpu.SemaphoreType.DMA((SPLIT, len(devices))),
            ],
            input_output_aliases={len(chosen): 0} if previous else {},
            compiler_params=PARAMS,
            cost_estimate=SHORT if previous else LONG,
        )(*[piece[0] for piece in chosen], *previous)
    result = result.reshape(cells, columns // LANES, row_count, LANES).transpose(0, 2, 1, 3)
    return result.reshape(cells, row_count, columns)


def solution(mesh):
    placed = (P("span", "plane", None), P("plane", None))
    return jax.shard_map(
        local, mesh=mesh, in_specs=placed, out_specs=P("span", "plane", None), check_vma=False
    )
```

```python
import functools

import jax
import jax.numpy as jnp
import ml_dtypes
import numpy as np
from jax import lax
from jax.experimental import pallas as pl
from jax.experimental.pallas import tpu as pltpu
from jax.sharding import PartitionSpec as P

PENALTY = 12.0
LANES = 128
VMEM = pl.BlockSpec(memory_space=pltpu.VMEM)
ANY = pl.BlockSpec(memory_space=pl.ANY)
PARAMS = pltpu.CompilerParams(vmem_limit_bytes=24 * 1024 * 1024)
LONG = pl.CostEstimate(flops=0, bytes_accessed=200_000_000, transcendentals=0)
SHORT = pl.CostEstimate(flops=0, bytes_accessed=1024, transcendentals=0)
SPLIT = 4


def split(values):
    high = values.astype(ml_dtypes.bfloat16)
    low = (values - high.astype(np.float64)).astype(ml_dtypes.bfloat16)
    return np.concatenate([high, low, high], axis=-1)


def table_modes(length, wanted):
    modes = [(k, False) for k in range(length // 2 + 1) if wanted(k)]
    return modes + [(k, True) for k in range(1, length // 2) if wanted(k)]


def wave(length, points, k, sine):
    angles = (points * k % length) * (2.0 * np.pi / length)
    return np.sin(angles) if sine else np.cos(angles)


def fill(length, modes, forward, inverse, fluid, solid):
    points = np.arange(length // 2)
    for at, (k, sine) in enumerate(modes):
        forward[at] = wave(length, points, k, sine)
        inverse[:, at] = forward[at] * (1.0 if k in (0, length // 2) else 2.0) / length
        eigen = 2.0 - 2.0 * np.cos(2.0 * np.pi * k / length)
        fluid[at] = 1.0 / (4.0 + eigen)
        solid[at] = 1.0 / (4.0 + eigen + PENALTY)


def up_to(number, step):
    return -(-number // step) * step


def tables(length, cells):
    half = length // 2
    blocks = half // cells
    kept = [table_modes(length, lambda k: 3 * k <= length and k % 2 == parity) for parity in (0, 1)]
    padded = up_to(max(len(modes) for modes in kept), 16)
    left = table_modes(length, lambda k: 3 * k > length)
    rest = up_to(len(left), 16)
    columns = np.zeros((8, up_to(max(2 * padded, rest), LANES)))
    forward, inverse = np.zeros((2, padded, half)), np.zeros((2, half, padded))
    for parity, modes in enumerate(kept):
        part = slice(parity * padded, (parity + 1) * padded)
        fill(length, modes, forward[parity], inverse[parity], columns[0, part], columns[1, part])
    powers = 8
    send, take = np.zeros((rest + 6 * powers, half)), np.zeros((half, up_to(rest + powers, 16)))
    fill(length, left, send[:rest], take[:, :rest], columns[2, :rest], columns[3, :rest])
    take[:, : len(left)] *= [-1.0 if k % 2 == 0 else 1.0 for k, _ in left]
    ends = (np.arange(half), half - 1.0 - np.arange(half))
    for side in (0, 1):
        x, y = ends[side], ends[1 - side] + 1.0
        first = rest + 4 * side
        for solid, diagonal in enumerate((6.0, 6.0 + PENALTY)):
            rho = diagonal / 2.0 - np.sqrt(diagonal * diagonal / 4.0 - 1.0)
            at = first + 2 * solid
            take[:, at], take[:, at + 1] = rho**x, x * rho**x
            single = rho / (1.0 - rho**2) * rho**y
            double = rho**2 / (1.0 - rho**2) ** 2
            send[at + powers * solid] = single
            send[at + powers * (2 + solid)] = (double * (1.0 + rho**2) / (1.0 - rho**2) + double * y) * rho**y
            send[at + 1 + powers * (2 + solid)] = double * rho**y
            send[at + powers * 4] = single / PENALTY * (1.0 if solid == 0 else -1.0)
    forward = split(forward.reshape(2, padded, blocks, cells).transpose(0, 2, 1, 3))
    inverse = split(inverse.reshape(2, blocks, cells, padded))
    send = split(send.reshape(-1, blocks, cells).transpose(1, 0, 2))
    take = split(take.reshape(blocks, cells, -1))
    return forward, inverse, send, take, columns.astype(np.float32), 2 * padded, rest


def thirds(values, axis):
    high = values.astype(jnp.bfloat16)
    low = (values - high.astype(jnp.float32)).astype(jnp.bfloat16)
    return jnp.concatenate([high, high, low], axis=axis)


def pack_kernel(jobs, row_count, cells, earlier, x_ref, *refs):
    outs, (held, arrived) = refs[earlier:-2], refs[-2:]
    me = lax.axis_index("span")
    lines = x_ref.shape[1]
    all_tiles = lines // row_count
    own_tiles = all_tiles // lax.axis_size("span")
    pitch = held.shape[0] // cells
    some = cells // SPLIT
    copies = [
        pltpu.make_async_copy(
            x_ref.at[pl.ds(part * some, some)],
            held.reshape(cells, pitch, LANES).at[pl.ds(part * some, some), pl.ds(0, lines)],
            arrived.at[part],
        )
        for part in range(SPLIT)
    ]
    for copy in copies:
        copy.start()
    lane = lax.broadcasted_iota(jnp.int32, (some, LANES), 1)
    sides = []
    for part, copy in enumerate(copies):
        copy.wait()
        beside = jnp.zeros((some, LANES), jnp.float32)

        def line(tile, row):
            return held[pl.ds(part * some * pitch + tile * row_count + row, some, stride=pitch), :]

        for job, (out, base, d, rows, offset, tiles) in enumerate(jobs):
            first = jnp.bitwise_xor(me, d) * own_tiles + offset
            for i, row in enumerate(rows):
                at = base + i * cells + part * some
                for tile in range(tiles):
                    outs[out][at : at + some, tile * LANES : (tile + 1) * LANES] = line(first + tile, row)
                before = jnp.maximum(first - 1, 0)
                after = jnp.minimum(first + tiles, all_tiles - 1)
                for side, (tile, source) in enumerate(((before, LANES - 1), (after, 0))):
                    at = job * 8 + i * 2 + side
                    beside = jnp.where(lane == at, pltpu.roll(line(tile, row), (at - source) % LANES, 1), beside)
        sides.append(beside)
    if cells < LANES:
        sides.append(jnp.zeros((LANES - cells, LANES), jnp.float32))
    turned = jnp.concatenate(sides, axis=0).T
    for job, (out, base, _, rows, _, tiles) in enumerate(jobs):
        at = base + len(rows) * cells
        outs[out][at : at + 8, :LANES] = turned[job * 8 : (job + 1) * 8]
        if tiles > 1:
            outs[out][at : at + 8, LANES:] = jnp.zeros((8, (tiles - 1) * LANES), jnp.float32)


def place(d):
    half = lax.axis_size("span") // 2
    return jnp.bitwise_and(jnp.bitwise_xor(lax.axis_index("span"), d), half - 1)


def row_product(table, value):
    return jnp.dot(table, thirds(value, 0), preferred_element_type=jnp.float32)


def side_product(table, value):
    value = thirds(jnp.concatenate([value, jnp.zeros_like(value)], axis=0), 1)
    return lax.dot_general(table, value, (((1,), (1,)), ((), ())), preferred_element_type=jnp.float32)


def transform(rows, cells, near, far, forward_ref):
    def spectrum(lines, lanes, product):
        halves = []
        for parity in (0, 1):
            total = 0.0
            for d, block in enumerate(near):
                value = block[lines, lanes]
                if far:
                    other = far[d][lines, lanes]
                    value = value + other if parity == 0 else value - other
                total = total + product(forward_ref[parity, place(d)], value)
            halves.append(total)
        return jnp.concatenate(halves, axis=0)

    spectra = [spectrum(slice(i * cells, (i + 1) * cells), slice(None), row_product) for i in range(rows)]
    return spectra, spectrum(slice(rows * cells, rows * cells + 8), slice(0, cells), side_product)


def inverse_rows(sweeps, cells, inverse_ref, near, far=()):
    padded = sweeps[0].shape[0] // 2
    for i, sweep in enumerate(sweeps):
        even = thirds(sweep[:padded], 0)
        odd = thirds(sweep[padded:], 0)
        for d, out in enumerate(near):
            first = jnp.dot(inverse_ref[0, place(d)], even, preferred_element_type=jnp.float32)
            second = jnp.dot(inverse_ref[1, place(d)], odd, preferred_element_type=jnp.float32)
            out[i * cells : (i + 1) * cells, :] = first + second
            if far:
                far[d][i * cells : (i + 1) * cells, :] = first - second


def second_sweep(spectrum, one, above, below, sides, at, inverse_diagonal):
    width = one.shape[1]
    lane = lax.broadcasted_iota(jnp.int32, one.shape, 1)
    left = jnp.where(lane == 0, sides[:, at : at + 1], pltpu.roll(one, 1, 1))
    right = jnp.where(lane == width - 1, sides[:, at + 1 : at + 2], pltpu.roll(one, width - 1, 1))
    return (spectrum + above + below + left + right) * inverse_diagonal


def masks(mask_ref, rows, d, width):
    start = pl.multiple_of(jnp.bitwise_xor(lax.axis_index("span"), d) * width, LANES)
    last = mask_ref.shape[1] - LANES
    before = mask_ref[:, pl.ds(pl.multiple_of(jnp.maximum(start - LANES, 0), LANES), LANES)][:, LANES - 1 :]
    after = mask_ref[:, pl.ds(pl.multiple_of(jnp.minimum(start + width, last), LANES), LANES)][:, :1]
    before = jnp.where(start == 0, 2, before)
    after = jnp.where(start + width == mask_ref.shape[1], 2, after)
    lane = lax.broadcasted_iota(jnp.int32, (1, 16), 1)
    kinds = jnp.full((1, 16), 2, jnp.int32)
    for i, row in enumerate(rows):
        kinds = jnp.where(lane == 2 * i, before[row : row + 1], kinds)
        kinds = jnp.where(lane == 2 * i + 1, after[row : row + 1], kinds)
    return [mask_ref[row : row + 1, pl.ds(start, width)] for row in range(mask_ref.shape[0])], kinds


def pick(kind, fluid, solid):
    return jnp.where(kind == 0, fluid, jnp.where(kind == 1, solid, 0.0))


def one_over(columns_ref, first, modes):
    turned = columns_ref[...].T
    return turned[:modes, first : first + 1], turned[:modes, first + 1 : first + 2]


def paired_edge():
    return lax.rem(lax.axis_index("plane") + 1, 2)


def edge_kernel(rows, count, cells, *refs):
    near, far = refs[: count // 2], refs[count // 2 : count]
    forward_ref, columns_ref, mask_ref = refs[count : count + 3]
    spectrum_ref, ones_ref, paired_ref, other_ref, sides_ref = refs[-5:]
    spectra, sides = transform(len(rows), cells, near, far, forward_ref)
    modes, width = spectra[0].shape
    mask, kinds = masks(mask_ref, rows, 0, width)
    fluid, solid = one_over(columns_ref, 0, modes)
    ones = [spectrum * pick(mask[row], fluid, solid) for spectrum, row in zip(spectra, rows)]
    for i in (0, 1):
        spectrum_ref[i] = spectra[i]
        ones_ref[i] = ones[i]
    last = paired_edge() == 1
    paired_ref[...] = jnp.where(last, ones[1], ones[0])
    other_ref[...] = jnp.where(last, ones[0], ones[1])
    sides_ref[...] = sides * pick(kinds, fluid, solid)


def inner_sweeps(spectra, sides, rows, mask, kinds, fluid, solid, edges):
    diagonals = [pick(mask[row], fluid, solid) for row in rows]
    ones = [spectrum * diagonal for spectrum, diagonal in zip(spectra, diagonals)]
    around = [edges[0], *ones, edges[1]]
    sides = sides * pick(kinds, fluid, solid)
    return ones, [
        second_sweep(spectra[i], ones[i], around[i], around[i + 2], sides, 2 * i, diagonals[i])
        for i in range(len(rows))
    ]


def inner_kernel(rows, count, cells, *refs):
    half = count // 2
    far_ref, forward_ref, inverse_ref, columns_ref, mask_ref, edges_ref = refs[half : half + 6]
    outs, ones_ref = refs[-1 - half : -1], refs[-1]
    size = len(rows) * cells + 8
    far = [far_ref.at[e * size : (e + 1) * size] for e in range(half)]
    spectra, sides = transform(len(rows), cells, refs[:half], far, forward_ref)
    modes, width = spectra[0].shape
    mask, kinds = masks(mask_ref, rows, 0, width)
    fluid, solid = one_over(columns_ref, 0, modes)
    ones, sweeps = inner_sweeps(spectra, sides, rows, mask, kinds, fluid, solid, (edges_ref[0], edges_ref[1]))
    ones_ref[0] = ones[0]
    ones_ref[1] = ones[-1]
    inverse_rows(sweeps, cells, inverse_ref, outs)


def local_kernel(rows, edge_rows, count, cells, *refs):
    half = count // 2
    message_ref, edges = refs[0], refs[1 : 1 + half]
    forward_ref, inverse_ref, columns_ref, mask_ref = refs[1 + half : 5 + half]
    out_ref = refs[-1]
    size = len(rows) * cells + 8
    near = [message_ref.at[d * size : (d + 1) * size] for d in range(half)]
    spectra, sides = transform(len(rows), cells, near, (), forward_ref)
    edge_spectra, _ = transform(len(edge_rows), cells, edges, (), forward_ref)
    modes, width = spectra[0].shape
    mask, kinds = masks(mask_ref, rows, half, width)
    fluid, solid = one_over(columns_ref, 0, modes)
    around = [spectrum * pick(mask[row], fluid, solid) for spectrum, row in zip(edge_spectra, edge_rows)]
    _, sweeps = inner_sweeps(spectra, sides, rows, mask, kinds, fluid, solid, around)
    size = len(rows) * cells
    inverse_rows(sweeps, cells, inverse_ref, [out_ref.at[d * size : (d + 1) * size] for d in range(half)])


def send_kernel(rows, edge_rows, rest, count, cells, *refs):
    half = count // 2
    inner, edges = refs[:half], refs[half : 2 * half]
    send_ref, columns_ref, mask_ref, out_ref = refs[2 * half :]

    def product(blocks, lines, lanes, kind):
        return sum(kind(send_ref[place(d)], block[lines, lanes]) for d, block in enumerate(blocks))

    def whole(blocks, i):
        return product(blocks, slice(i * cells, (i + 1) * cells), slice(None), row_product)

    spectra = [whole(inner, i) for i in range(len(rows))]
    around = [whole(edges, i) for i in range(len(edge_rows))]
    sides = product(inner, slice(len(rows) * cells, len(rows) * cells + 8), slice(0, cells), side_product)
    mask, kinds = masks(mask_ref, rows, 0, inner[0].shape[1])
    fluid, solid = one_over(columns_ref, 2, rest)
    outer = [values[:rest] * pick(mask[row], fluid, solid) for values, row in zip(around, edge_rows)]
    _, sweeps = inner_sweeps([v[:rest] for v in spectra], sides[:rest], rows, mask, kinds, fluid, solid, outer)

    def power(values, at):
        return values[rest + 8 * at : rest + 8 * at + 8]

    numbers = []
    for target in (0, 1):

        def beside(values, kind):
            same, cross = power(values, 2 + target), power(values, 4)
            return pick(kind, same, cross) if target == 0 else pick(kind, cross, same)

        own = [beside(values, mask[row]) for values, row in zip(spectra, rows)]
        edge = [beside(values, mask[row]) for values, row in zip(around, edge_rows)]
        column = [edge[0], *own, edge[1]]
        outside = beside(sides, kinds)
        numbers.append(
            [
                second_sweep(power(spectra[i], target), own[i], column[i], column[i + 2], outside, 2 * i, 1.0)
                for i in range(len(rows))
            ]
        )
    for i, row in enumerate(rows):
        base = i * (rest + 8)
        out_ref[base : base + rest, :] = sweeps[i]
        out_ref[base + rest : base + rest + 8, :] = jnp.where(mask[row] == 0, numbers[0][i], numbers[1][i])


def take_kernel(rows, count, cells, *refs):
    half = count // 2
    message_ref, local_ref, take_ref = refs[:3]
    outs = refs[-half:]
    lines = message_ref.shape[0] // len(rows)
    short = take_ref.shape[2] // 3 - lines
    for i in range(len(rows)):
        values = message_ref[i * lines : (i + 1) * lines, :]
        if short:
            values = jnp.concatenate([values, jnp.zeros((short, values.shape[1]), jnp.float32)], axis=0)
        values = thirds(values, 0)
        for d, out in enumerate(outs):
            base = (d * len(rows) + i) * cells
            out[i * cells : (i + 1) * cells, :] = local_ref[base : base + cells, :] + jnp.dot(
                take_ref[place(d)], values, preferred_element_type=jnp.float32
            )


def rim_kernel(rows, order, count, cells, *refs):
    spectrum_ref, edges_ref, sides_ref, halo_ref, ones_ref, inverse_ref, columns_ref, mask_ref = refs[:8]
    outs = refs[-count:]
    _, modes, width = edges_ref.shape
    edge = paired_edge() if order == 0 else 1 - paired_edge()
    mask, _ = masks(mask_ref, rows, 0, width)
    fluid, solid = one_over(columns_ref, 0, modes)
    sides = jnp.where(edge == 0, sides_ref[:, 0:2], sides_ref[:, 2:4])
    diagonal = pick(jnp.where(edge == 0, mask[rows[0]], mask[rows[1]]), fluid, solid)
    sweep = second_sweep(spectrum_ref[edge], edges_ref[edge], halo_ref[...], ones_ref[edge], sides, 0, diagonal)
    inverse_rows([sweep], cells, inverse_ref, outs[: count // 2], outs[count // 2 :])


def join_kernel(rows, cells, near, *refs):
    own_ref, blocks, out_ref = refs[0], refs[1 : 1 + rows * near], refs[-1]
    size = rows * cells + 8
    out_ref[:size, :] = own_ref[...]
    for d in range(near):
        base = (d + 1) * size
        out_ref[base + rows * cells : base + size, :] = jnp.zeros((8, out_ref.shape[1]), jnp.float32)
        for i in range(rows):
            block = blocks[d * rows + i]
            out_ref[base + i * cells : base + (i + 1) * cells, :] = block[:cells, :]
            at = base + rows * cells + 2 * i
            out_ref[at : at + 2, :] = block[cells : cells + 2, :]


def unpack_kernel(pieces, devices, row_count, cells, *refs):
    me = lax.axis_index("span")
    blocks, (out_ref, held, done) = refs[: len(pieces)], refs[-3:]
    pitch = held.shape[0] // cells
    own_lines = out_ref.shape[1] // lax.axis_size("span")
    some = cells // SPLIT
    edge_rows = {"near": paired_edge() * (row_count - 1), "far": (1 - paired_edge()) * (row_count - 1)}
    copies = []
    for part in range(SPLIT):
        for block, (d, base, rows, offset, tiles) in zip(blocks, pieces):
            for i, row in enumerate(rows):
                if row in edge_rows:
                    row = edge_rows[row]
                line = base + i * cells + part * some
                for tile in range(tiles):
                    at = part * some * pitch + devices.index(d) * own_lines + (offset + tile) * row_count + row
                    held[pl.ds(at, some, stride=pitch), :] = block[line : line + some, tile * LANES : (tile + 1) * LANES]
        for at, d in enumerate(devices):
            first = pl.multiple_of(jnp.bitwise_xor(me, d) * own_lines, own_lines)
            copies.append(
                pltpu.make_async_copy(
                    held.reshape(cells, pitch, LANES).at[pl.ds(part * some, some), pl.ds(at * own_lines, own_lines)],
                    out_ref.at[pl.ds(part * some, some), pl.ds(first, own_lines)],
                    done.at[part, at],
                )
            )
            copies[-1].start()
    for copy in copies:
        copy.wait()


def call(kernel, outs, *args, cost=LONG, earlier=()):
    shapes = [jax.ShapeDtypeStruct(shape, jnp.float32) for shape in outs]
    return pl.pallas_call(
        kernel,
        out_shape=shapes,
        in_specs=[VMEM] * len(args) + [ANY] * len(earlier),
        out_specs=[VMEM] * len(outs),
        compiler_params=PARAMS,
        cost_estimate=cost,
    )(*args, *earlier)


def swap(block, d):
    return lax.ppermute(block, "span", [(i, i ^ d) for i in range(lax.axis_size("span"))])


def local(pressure_source, solid_mask):
    count = lax.axis_size("span")
    half = count // 2
    plane_count = lax.axis_size("plane")
    cells, row_count, columns = pressure_source.shape
    width = columns // count
    tiles = width // LANES
    inner = tuple(range(1, row_count - 1))
    edges = (0, row_count - 1)
    near, far = range(1, half), range(half, count)
    *arrays, modes, rest = tables(cells * count, cells)
    forward, inverse, send, take, diagonals = map(jnp.asarray, arrays)

    lines = columns // LANES * row_count
    source = pressure_source.reshape(cells, row_count, columns // LANES, LANES).transpose(0, 2, 1, 3)
    source = source.reshape(cells, lines, LANES)
    scratch = [pltpu.VMEM((cells * (lines + 8), LANES), jnp.float32), pltpu.SemaphoreType.DMA((SPLIT,))]

    def pack(source, wanted, *earlier):
        jobs = [(at, 0, d, rows, 0, tiles) for at, (d, rows) in enumerate(wanted)]
        shapes = [(len(rows) * cells + 8, width) for _, rows in wanted]
        return pl.pallas_call(
            functools.partial(pack_kernel, jobs, row_count, cells, len(earlier)),
            out_shape=[jax.ShapeDtypeStruct(shape, jnp.float32) for shape in shapes],
            in_specs=[ANY] * (1 + len(earlier)),
            out_specs=[VMEM] * len(shapes),
            scratch_shapes=scratch,
            compiler_params=PARAMS,
            cost_estimate=LONG,
        )(source, *earlier)

    packed = pack(pltpu.with_memory_space_constraint(source, pltpu.HBM), [(d, edges) for d in range(1, count)])
    edge_blocks = [swap(block, d) for d, block in enumerate(packed, 1)]
    wanted = [(d, inner) for d in range(half + 1)] + [(0, edges)] + [(d, edges) for d in far]
    wanted += [(half + d, (row,)) for d in near for row in inner]
    packed = pack(source, wanted, packed[half - 1])
    edge_blocks = [packed[half + 1], *edge_blocks]
    inner_blocks = [packed[0]] + [swap(packed[d], d) for d in near]
    chip_edges = [packed[half + 2]] + [swap(packed[half + 2 + d], d) for d in near]
    relayed = packed[2 * half + 2 :]
    relayed = [swap(relayed[(d - 1) * len(inner) + i], d) for d in near for i in range(len(inner))]
    (message,) = call(
        functools.partial(join_kernel, len(inner), cells, half - 1),
        [(half * (len(inner) * cells + 8), width)],
        packed[half], *relayed, cost=SHORT, earlier=(edge_blocks[half],),
    )
    arrived = swap(message, half)

    length = len(inner) * cells
    (sent,) = call(
        functools.partial(send_kernel, inner, edges, rest, count, cells),
        [(len(inner) * (rest + 8), width)],
        *inner_blocks, *edge_blocks[:half], send, diagonals, solid_mask, cost=SHORT,
    )
    taken = swap(sent, half)
    (own,) = call(
        functools.partial(local_kernel, inner, edges, count, cells),
        [(half * length, width)],
        message, *chip_edges, forward, inverse, diagonals, solid_mask, cost=SHORT,
    )

    spectrum, edge_ones, paired, other, sides = call(
        functools.partial(edge_kernel, edges, count, cells),
        [(2, modes, width), (2, modes, width), (modes, width), (modes, width), (modes, 16)],
        *edge_blocks, forward, diagonals, solid_mask, earlier=(own,),
    )
    pairs = [[(i, i ^ 1) for i in range(plane_count)], [(i, ((i + 1) ^ 1) - 1) for i in range(plane_count)]]
    halos = [
        lax.ppermute(row, "plane", [(i, j) for i, j in pair if 0 <= j < plane_count])
        for row, pair in zip((paired, other), pairs)
    ]

    *made, ones = call(
        functools.partial(inner_kernel, inner, count, cells),
        [(length, width)] * half + [(2, modes, width)],
        *inner_blocks, arrived, forward, inverse, diagonals, solid_mask, edge_ones, cost=SHORT,
    )
    pieces = [(made[0], 0, 0, inner, 0, tiles)]
    pieces += [(swap(made[d], d), d, 0, inner, 0, tiles) for d in near]
    before = []
    for order, name in enumerate(("near", "far")):
        outs = call(
            functools.partial(rim_kernel, edges, order, count, cells),
            [(cells, width)] * count,
            spectrum, edge_ones, sides, halos[order], ones, inverse, diagonals, solid_mask,
            cost=LONG if order else SHORT, earlier=(*before, taken) if order else (),
        )
        before = (outs[-1],)
        pieces.append((outs[0], 0, 0, (name,), 0, tiles))
        pieces += [(swap(outs[d], d), d, 0, (name,), 0, tiles) for d in (*far, *near)]
        rim_got = pieces[-count + 1 :][0][0] if order == 0 else rim_got
    rebuilt = call(
        functools.partial(take_kernel, inner, count, cells), [(length, width)] * half, taken, own, take,
        cost=SHORT, earlier=(*before, rim_got),
    )
    pieces.append((rebuilt[0], half, 0, inner, 0, tiles))
    pieces += [(swap(rebuilt[d], d), half + d, 0, inner, 0, tiles) for d in near]

    result = None
    own_lines = tiles * row_count
    for devices in (range(count - 1), [count - 1]) if own_lines % 8 == 0 else (range(count),):
        chosen = [piece for piece in pieces if piece[1] in devices]
        previous = () if result is None else (result,)
        result = pl.pallas_call(
            functools.partial(unpack_kernel, [piece[1:] for piece in chosen], list(devices), row_count, cells),
            out_shape=jax.ShapeDtypeStruct((cells, lines, LANES), jnp.float32),
            in_specs=[VMEM] * len(chosen) + [ANY] * len(previous),
            out_specs=ANY,
            scratch_shapes=[
                pltpu.VMEM((cells * (len(devices) * own_lines + 8), LANES), jnp.float32),
                pltpu.SemaphoreType.DMA((SPLIT, len(devices))),
            ],
            input_output_aliases={len(chosen): 0} if previous else {},
            compiler_params=PARAMS,
            cost_estimate=SHORT if previous else LONG,
        )(*[piece[0] for piece in chosen], *previous)
    result = result.reshape(cells, columns // LANES, row_count, LANES).transpose(0, 2, 1, 3)
    return result.reshape(cells, row_count, columns)


def solution(mesh):
    placed = (P("span", "plane", None), P("plane", None))
    return jax.shard_map(
        local, mesh=mesh, in_specs=placed, out_specs=P("span", "plane", None), check_vma=False
    )
```

```python
import functools

import jax
import jax.numpy as jnp
import ml_dtypes
import numpy as np
from jax import lax
from jax.experimental import pallas as pl
from jax.experimental.pallas import tpu as pltpu
from jax.sharding import PartitionSpec as P

PENALTY = 12.0
LANES = 128
VMEM = pl.BlockSpec(memory_space=pltpu.VMEM)
ANY = pl.BlockSpec(memory_space=pl.ANY)
PARAMS = pltpu.CompilerParams(vmem_limit_bytes=24 * 1024 * 1024)
LONG = pl.CostEstimate(flops=0, bytes_accessed=200_000_000, transcendentals=0)
SHORT = pl.CostEstimate(flops=0, bytes_accessed=1024, transcendentals=0)
SPLIT = 4


def split(values):
    high = values.astype(ml_dtypes.bfloat16)
    low = (values - high.astype(np.float64)).astype(ml_dtypes.bfloat16)
    return np.concatenate([high, low, high], axis=-1)


def table_modes(length, wanted):
    modes = [(k, False) for k in range(length // 2 + 1) if wanted(k)]
    return modes + [(k, True) for k in range(1, length // 2) if wanted(k)]


def wave(length, points, k, sine):
    angles = (points * k % length) * (2.0 * np.pi / length)
    return np.sin(angles) if sine else np.cos(angles)


def fill(length, modes, forward, inverse, fluid, solid):
    points = np.arange(length // 2)
    for at, (k, sine) in enumerate(modes):
        forward[at] = wave(length, points, k, sine)
        inverse[:, at] = forward[at] * (1.0 if k in (0, length // 2) else 2.0) / length
        eigen = 2.0 - 2.0 * np.cos(2.0 * np.pi * k / length)
        fluid[at] = 1.0 / (4.0 + eigen)
        solid[at] = 1.0 / (4.0 + eigen + PENALTY)


def up_to(number, step):
    return -(-number // step) * step


def tables(length, cells):
    half = length // 2
    blocks = half // cells
    kept = [table_modes(length, lambda k: 3 * k <= length and k % 2 == parity) for parity in (0, 1)]
    padded = up_to(max(len(modes) for modes in kept), 16)
    left = table_modes(length, lambda k: 3 * k > length)
    rest = up_to(len(left), 16)
    columns = np.zeros((8, up_to(max(2 * padded, rest), LANES)))
    forward, inverse = np.zeros((2, padded, half)), np.zeros((2, half, padded))
    for parity, modes in enumerate(kept):
        part = slice(parity * padded, (parity + 1) * padded)
        fill(length, modes, forward[parity], inverse[parity], columns[0, part], columns[1, part])
    powers = 8
    send, take = np.zeros((rest + 6 * powers, half)), np.zeros((half, up_to(rest + powers, 16)))
    fill(length, left, send[:rest], take[:, :rest], columns[2, :rest], columns[3, :rest])
    take[:, : len(left)] *= [-1.0 if k % 2 == 0 else 1.0 for k, _ in left]
    ends = (np.arange(half), half - 1.0 - np.arange(half))
    for side in (0, 1):
        x, y = ends[side], ends[1 - side] + 1.0
        first = rest + 4 * side
        for solid, diagonal in enumerate((6.0, 6.0 + PENALTY)):
            rho = diagonal / 2.0 - np.sqrt(diagonal * diagonal / 4.0 - 1.0)
            at = first + 2 * solid
            take[:, at], take[:, at + 1] = rho**x, x * rho**x
            single = rho / (1.0 - rho**2) * rho**y
            double = rho**2 / (1.0 - rho**2) ** 2
            send[at + powers * solid] = single
            send[at + powers * (2 + solid)] = (double * (1.0 + rho**2) / (1.0 - rho**2) + double * y) * rho**y
            send[at + 1 + powers * (2 + solid)] = double * rho**y
            send[at + powers * 4] = single / PENALTY * (1.0 if solid == 0 else -1.0)
    forward = split(forward.reshape(2, padded, blocks, cells).transpose(0, 2, 1, 3))
    inverse = split(inverse.reshape(2, blocks, cells, padded))
    send = split(send.reshape(-1, blocks, cells).transpose(1, 0, 2))
    take = split(take.reshape(blocks, cells, -1))
    return forward, inverse, send, take, columns.astype(np.float32), 2 * padded, rest


def thirds(values, axis):
    high = values.astype(jnp.bfloat16)
    low = (values - high.astype(jnp.float32)).astype(jnp.bfloat16)
    return jnp.concatenate([high, high, low], axis=axis)


def pack_kernel(jobs, row_count, cells, earlier, x_ref, *refs):
    outs, (held, arrived) = refs[earlier:-2], refs[-2:]
    me = lax.axis_index("span")
    lines = x_ref.shape[1]
    all_tiles = lines // row_count
    own_tiles = all_tiles // lax.axis_size("span")
    pitch = held.shape[0] // cells
    some = cells // SPLIT
    copies = [
        pltpu.make_async_copy(
            x_ref.at[pl.ds(part * some, some)],
            held.reshape(cells, pitch, LANES).at[pl.ds(part * some, some), pl.ds(0, lines)],
            arrived.at[part],
        )
        for part in range(SPLIT)
    ]
    for copy in copies:
        copy.start()
    lane = lax.broadcasted_iota(jnp.int32, (some, LANES), 1)
    sides = []
    for part, copy in enumerate(copies):
        copy.wait()
        beside = jnp.zeros((some, LANES), jnp.float32)

        def line(tile, row):
            return held[pl.ds(part * some * pitch + tile * row_count + row, some, stride=pitch), :]

        for job, (out, base, d, rows, offset, tiles) in enumerate(jobs):
            first = jnp.bitwise_xor(me, d) * own_tiles + offset
            for i, row in enumerate(rows):
                at = base + i * cells + part * some
                for tile in range(tiles):
                    outs[out][at : at + some, tile * LANES : (tile + 1) * LANES] = line(first + tile, row)
                before = jnp.maximum(first - 1, 0)
                after = jnp.minimum(first + tiles, all_tiles - 1)
                for side, (tile, source) in enumerate(((before, LANES - 1), (after, 0))):
                    at = job * 8 + i * 2 + side
                    beside = jnp.where(lane == at, pltpu.roll(line(tile, row), (at - source) % LANES, 1), beside)
        sides.append(beside)
    if cells < LANES:
        sides.append(jnp.zeros((LANES - cells, LANES), jnp.float32))
    turned = jnp.concatenate(sides, axis=0).T
    for job, (out, base, _, rows, _, tiles) in enumerate(jobs):
        at = base + len(rows) * cells
        outs[out][at : at + 8, :LANES] = turned[job * 8 : (job + 1) * 8]
        if tiles > 1:
            outs[out][at : at + 8, LANES:] = jnp.zeros((8, (tiles - 1) * LANES), jnp.float32)


def place(d):
    half = lax.axis_size("span") // 2
    return jnp.bitwise_and(jnp.bitwise_xor(lax.axis_index("span"), d), half - 1)


def row_product(table, value):
    return jnp.dot(table, thirds(value, 0), preferred_element_type=jnp.float32)


def side_product(table, value):
    value = thirds(jnp.concatenate([value, jnp.zeros_like(value)], axis=0), 1)
    return lax.dot_general(table, value, (((1,), (1,)), ((), ())), preferred_element_type=jnp.float32)


def transform(rows, cells, near, far, forward_ref):
    def spectrum(lines, lanes, product):
        halves = []
        for parity in (0, 1):
            total = 0.0
            for d, block in enumerate(near):
                value = block[lines, lanes]
                if far:
                    other = far[d][lines, lanes]
                    value = value + other if parity == 0 else value - other
                total = total + product(forward_ref[parity, place(d)], value)
            halves.append(total)
        return jnp.concatenate(halves, axis=0)

    spectra = [spectrum(slice(i * cells, (i + 1) * cells), slice(None), row_product) for i in range(rows)]
    return spectra, spectrum(slice(rows * cells, rows * cells + 8), slice(0, cells), side_product)


def inverse_rows(sweeps, cells, inverse_ref, near, far=()):
    padded = sweeps[0].shape[0] // 2
    for i, sweep in enumerate(sweeps):
        even = thirds(sweep[:padded], 0)
        odd = thirds(sweep[padded:], 0)
        for d, out in enumerate(near):
            first = jnp.dot(inverse_ref[0, place(d)], even, preferred_element_type=jnp.float32)
            second = jnp.dot(inverse_ref[1, place(d)], odd, preferred_element_type=jnp.float32)
            out[i * cells : (i + 1) * cells, :] = first + second
            if far:
                far[d][i * cells : (i + 1) * cells, :] = first - second


def second_sweep(spectrum, one, above, below, sides, at, inverse_diagonal):
    width = one.shape[1]
    lane = lax.broadcasted_iota(jnp.int32, one.shape, 1)
    left = jnp.where(lane == 0, sides[:, at : at + 1], pltpu.roll(one, 1, 1))
    right = jnp.where(lane == width - 1, sides[:, at + 1 : at + 2], pltpu.roll(one, width - 1, 1))
    return (spectrum + above + below + left + right) * inverse_diagonal


def masks(mask_ref, rows, d, width):
    start = pl.multiple_of(jnp.bitwise_xor(lax.axis_index("span"), d) * width, LANES)
    last = mask_ref.shape[1] - LANES
    before = mask_ref[:, pl.ds(pl.multiple_of(jnp.maximum(start - LANES, 0), LANES), LANES)][:, LANES - 1 :]
    after = mask_ref[:, pl.ds(pl.multiple_of(jnp.minimum(start + width, last), LANES), LANES)][:, :1]
    before = jnp.where(start == 0, 2, before)
    after = jnp.where(start + width == mask_ref.shape[1], 2, after)
    lane = lax.broadcasted_iota(jnp.int32, (1, 16), 1)
    kinds = jnp.full((1, 16), 2, jnp.int32)
    for i, row in enumerate(rows):
        kinds = jnp.where(lane == 2 * i, before[row : row + 1], kinds)
        kinds = jnp.where(lane == 2 * i + 1, after[row : row + 1], kinds)
    return [mask_ref[row : row + 1, pl.ds(start, width)] for row in range(mask_ref.shape[0])], kinds


def pick(kind, fluid, solid):
    return jnp.where(kind == 0, fluid, jnp.where(kind == 1, solid, 0.0))


def one_over(columns_ref, first, modes):
    turned = columns_ref[...].T
    return turned[:modes, first : first + 1], turned[:modes, first + 1 : first + 2]


def paired_edge():
    return lax.rem(lax.axis_index("plane") + 1, 2)


def edge_kernel(rows, count, cells, *refs):
    near, far = refs[: count // 2], refs[count // 2 : count]
    forward_ref, columns_ref, mask_ref = refs[count : count + 3]
    spectrum_ref, ones_ref, paired_ref, other_ref, sides_ref = refs[-5:]
    spectra, sides = transform(len(rows), cells, near, far, forward_ref)
    modes, width = spectra[0].shape
    mask, kinds = masks(mask_ref, rows, 0, width)
    fluid, solid = one_over(columns_ref, 0, modes)
    ones = [spectrum * pick(mask[row], fluid, solid) for spectrum, row in zip(spectra, rows)]
    for i in (0, 1):
        spectrum_ref[i] = spectra[i]
        ones_ref[i] = ones[i]
    last = paired_edge() == 1
    paired_ref[...] = jnp.where(last, ones[1], ones[0])
    other_ref[...] = jnp.where(last, ones[0], ones[1])
    sides_ref[...] = sides * pick(kinds, fluid, solid)


def inner_sweeps(spectra, sides, rows, mask, kinds, fluid, solid, edges):
    diagonals = [pick(mask[row], fluid, solid) for row in rows]
    ones = [spectrum * diagonal for spectrum, diagonal in zip(spectra, diagonals)]
    around = [edges[0], *ones, edges[1]]
    sides = sides * pick(kinds, fluid, solid)
    return ones, [
        second_sweep(spectra[i], ones[i], around[i], around[i + 2], sides, 2 * i, diagonals[i])
        for i in range(len(rows))
    ]


def inner_kernel(rows, count, cells, *refs):
    half = count // 2
    far_ref, forward_ref, inverse_ref, columns_ref, mask_ref, edges_ref = refs[half : half + 6]
    outs, ones_ref = refs[-1 - half : -1], refs[-1]
    size = len(rows) * cells + 8
    far = [far_ref.at[e * size : (e + 1) * size] for e in range(half)]
    spectra, sides = transform(len(rows), cells, refs[:half], far, forward_ref)
    modes, width = spectra[0].shape
    mask, kinds = masks(mask_ref, rows, 0, width)
    fluid, solid = one_over(columns_ref, 0, modes)
    ones, sweeps = inner_sweeps(spectra, sides, rows, mask, kinds, fluid, solid, (edges_ref[0], edges_ref[1]))
    ones_ref[0] = ones[0]
    ones_ref[1] = ones[-1]
    inverse_rows(sweeps, cells, inverse_ref, outs)


def local_kernel(rows, edge_rows, count, cells, *refs):
    half = count // 2
    message_ref, edges = refs[0], refs[1 : 1 + half]
    forward_ref, inverse_ref, columns_ref, mask_ref = refs[1 + half : 5 + half]
    out_ref = refs[-1]
    size = len(rows) * cells + 8
    near = [message_ref.at[d * size : (d + 1) * size] for d in range(half)]
    spectra, sides = transform(len(rows), cells, near, (), forward_ref)
    edge_spectra, _ = transform(len(edge_rows), cells, edges, (), forward_ref)
    modes, width = spectra[0].shape
    mask, kinds = masks(mask_ref, rows, half, width)
    fluid, solid = one_over(columns_ref, 0, modes)
    around = [spectrum * pick(mask[row], fluid, solid) for spectrum, row in zip(edge_spectra, edge_rows)]
    _, sweeps = inner_sweeps(spectra, sides, rows, mask, kinds, fluid, solid, around)
    size = len(rows) * cells
    inverse_rows(sweeps, cells, inverse_ref, [out_ref.at[d * size : (d + 1) * size] for d in range(half)])


def send_kernel(rows, edge_rows, rest, count, cells, *refs):
    half = count // 2
    inner, edges = refs[:half], refs[half : 2 * half]
    send_ref, columns_ref, mask_ref, out_ref = refs[2 * half :]

    def product(blocks, lines, lanes, kind):
        return sum(kind(send_ref[place(d)], block[lines, lanes]) for d, block in enumerate(blocks))

    def whole(blocks, i):
        return product(blocks, slice(i * cells, (i + 1) * cells), slice(None), row_product)

    spectra = [whole(inner, i) for i in range(len(rows))]
    around = [whole(edges, i) for i in range(len(edge_rows))]
    sides = product(inner, slice(len(rows) * cells, len(rows) * cells + 8), slice(0, cells), side_product)
    mask, kinds = masks(mask_ref, rows, 0, inner[0].shape[1])
    fluid, solid = one_over(columns_ref, 2, rest)
    outer = [values[:rest] * pick(mask[row], fluid, solid) for values, row in zip(around, edge_rows)]
    _, sweeps = inner_sweeps([v[:rest] for v in spectra], sides[:rest], rows, mask, kinds, fluid, solid, outer)

    def power(values, at):
        return values[rest + 8 * at : rest + 8 * at + 8]

    numbers = []
    for target in (0, 1):

        def beside(values, kind):
            same, cross = power(values, 2 + target), power(values, 4)
            return pick(kind, same, cross) if target == 0 else pick(kind, cross, same)

        own = [beside(values, mask[row]) for values, row in zip(spectra, rows)]
        edge = [beside(values, mask[row]) for values, row in zip(around, edge_rows)]
        column = [edge[0], *own, edge[1]]
        outside = beside(sides, kinds)
        numbers.append(
            [
                second_sweep(power(spectra[i], target), own[i], column[i], column[i + 2], outside, 2 * i, 1.0)
                for i in range(len(rows))
            ]
        )
    for i, row in enumerate(rows):
        base = i * (rest + 8)
        out_ref[base : base + rest, :] = sweeps[i]
        out_ref[base + rest : base + rest + 8, :] = jnp.where(mask[row] == 0, numbers[0][i], numbers[1][i])


def take_kernel(rows, count, cells, *refs):
    half = count // 2
    message_ref, local_ref, take_ref = refs[:3]
    outs = refs[-half:]
    lines = message_ref.shape[0] // len(rows)
    short = take_ref.shape[2] // 3 - lines
    for i in range(len(rows)):
        values = message_ref[i * lines : (i + 1) * lines, :]
        if short:
            values = jnp.concatenate([values, jnp.zeros((short, values.shape[1]), jnp.float32)], axis=0)
        values = thirds(values, 0)
        for d, out in enumerate(outs):
            base = (d * len(rows) + i) * cells
            out[i * cells : (i + 1) * cells, :] = local_ref[base : base + cells, :] + jnp.dot(
                take_ref[place(d)], values, preferred_element_type=jnp.float32
            )


def rim_kernel(rows, order, count, cells, *refs):
    spectrum_ref, edges_ref, sides_ref, halo_ref, ones_ref, inverse_ref, columns_ref, mask_ref = refs[:8]
    outs = refs[-count:]
    _, modes, width = edges_ref.shape
    edge = paired_edge() if order == 0 else 1 - paired_edge()
    mask, _ = masks(mask_ref, rows, 0, width)
    fluid, solid = one_over(columns_ref, 0, modes)
    sides = jnp.where(edge == 0, sides_ref[:, 0:2], sides_ref[:, 2:4])
    diagonal = pick(jnp.where(edge == 0, mask[rows[0]], mask[rows[1]]), fluid, solid)
    sweep = second_sweep(spectrum_ref[edge], edges_ref[edge], halo_ref[...], ones_ref[edge], sides, 0, diagonal)
    inverse_rows([sweep], cells, inverse_ref, outs[: count // 2], outs[count // 2 :])


def join_kernel(rows, cells, near, *refs):
    own_ref, blocks, out_ref = refs[0], refs[1 : 1 + rows * near], refs[-1]
    size = own_ref.shape[0]
    out_ref[:size, :] = own_ref[...]
    for d in range(near):
        base = (d + 1) * size
        out_ref[base + rows * cells : base + size, :] = jnp.zeros((8, out_ref.shape[1]), jnp.float32)
        for i in range(rows):
            block = blocks[d * rows + i]
            out_ref[base + i * cells : base + (i + 1) * cells, :] = block[:cells, :]
            at = base + rows * cells + 2 * i
            out_ref[at : at + 2, :] = block[cells : cells + 2, :]


def unpack_kernel(pieces, devices, row_count, cells, *refs):
    me = lax.axis_index("span")
    blocks, (out_ref, held, done) = refs[: len(pieces)], refs[-3:]
    pitch = held.shape[0] // cells
    own_lines = out_ref.shape[1] // lax.axis_size("span")
    some = cells // SPLIT
    edge_rows = {"near": paired_edge() * (row_count - 1), "far": (1 - paired_edge()) * (row_count - 1)}
    copies = []
    for part in range(SPLIT):
        for block, (d, base, rows, offset, tiles) in zip(blocks, pieces):
            for i, row in enumerate(rows):
                if row in edge_rows:
                    row = edge_rows[row]
                line = base + i * cells + part * some
                for tile in range(tiles):
                    at = part * some * pitch + devices.index(d) * own_lines + (offset + tile) * row_count + row
                    held[pl.ds(at, some, stride=pitch), :] = block[line : line + some, tile * LANES : (tile + 1) * LANES]
        for at, d in enumerate(devices):
            first = pl.multiple_of(jnp.bitwise_xor(me, d) * own_lines, own_lines)
            copies.append(
                pltpu.make_async_copy(
                    held.reshape(cells, pitch, LANES).at[pl.ds(part * some, some), pl.ds(at * own_lines, own_lines)],
                    out_ref.at[pl.ds(part * some, some), pl.ds(first, own_lines)],
                    done.at[part, at],
                )
            )
            copies[-1].start()
    for copy in copies:
        copy.wait()


def call(kernel, outs, *args, cost=LONG, earlier=()):
    shapes = [jax.ShapeDtypeStruct(shape, jnp.float32) for shape in outs]
    return pl.pallas_call(
        kernel,
        out_shape=shapes,
        in_specs=[VMEM] * len(args) + [ANY] * len(earlier),
        out_specs=[VMEM] * len(outs),
        compiler_params=PARAMS,
        cost_estimate=cost,
    )(*args, *earlier)


def swap(block, d):
    return lax.ppermute(block, "span", [(i, i ^ d) for i in range(lax.axis_size("span"))])


def local(pressure_source, solid_mask):
    count = lax.axis_size("span")
    half = count // 2
    plane_count = lax.axis_size("plane")
    cells, row_count, columns = pressure_source.shape
    width = columns // count
    tiles = width // LANES
    inner = tuple(range(1, row_count - 1))
    edges = (0, row_count - 1)
    near, far = range(1, half), range(half, count)
    *arrays, modes, rest = tables(cells * count, cells)
    forward, inverse, send, take, diagonals = map(jnp.asarray, arrays)

    lines = columns // LANES * row_count
    source = pressure_source.reshape(cells, row_count, columns // LANES, LANES).transpose(0, 2, 1, 3)
    source = source.reshape(cells, lines, LANES)
    scratch = [pltpu.VMEM((cells * (lines + 8), LANES), jnp.float32), pltpu.SemaphoreType.DMA((SPLIT,))]

    def pack(source, wanted, *earlier):
        jobs = [(at, 0, d, rows, 0, tiles) for at, (d, rows) in enumerate(wanted)]
        shapes = [(len(rows) * cells + 8, width) for _, rows in wanted]
        return pl.pallas_call(
            functools.partial(pack_kernel, jobs, row_count, cells, len(earlier)),
            out_shape=[jax.ShapeDtypeStruct(shape, jnp.float32) for shape in shapes],
            in_specs=[ANY] * (1 + len(earlier)),
            out_specs=[VMEM] * len(shapes),
            scratch_shapes=scratch,
            compiler_params=PARAMS,
            cost_estimate=LONG,
        )(source, *earlier)

    packed = pack(pltpu.with_memory_space_constraint(source, pltpu.HBM), [(d, edges) for d in range(1, count)])
    edge_blocks = [swap(block, d) for d, block in enumerate(packed, 1)]
    wanted = [(d, inner) for d in range(half + 1)] + [(0, edges)] + [(d, edges) for d in far]
    wanted += [(half + d, (row,)) for d in near for row in inner]
    packed = pack(source, wanted, packed[half - 1])
    edge_blocks = [packed[half + 1], *edge_blocks]
    inner_blocks = [packed[0]] + [swap(packed[d], d) for d in near]
    chip_edges = [packed[half + 2]] + [swap(packed[half + 2 + d], d) for d in near]
    relayed = packed[2 * half + 2 :]
    relayed = [swap(relayed[(d - 1) * len(inner) + i], d) for d in near for i in range(len(inner))]
    (message,) = call(
        functools.partial(join_kernel, len(inner), cells, half - 1),
        [(half * (len(inner) * cells + 8), width)],
        packed[half], *relayed, cost=SHORT, earlier=(edge_blocks[half],),
    )
    arrived = swap(message, half)

    length = len(inner) * cells
    (sent,) = call(
        functools.partial(send_kernel, inner, edges, rest, count, cells),
        [(len(inner) * (rest + 8), width)],
        *inner_blocks, *edge_blocks[:half], send, diagonals, solid_mask, cost=SHORT,
    )
    taken = swap(sent, half)
    (own,) = call(
        functools.partial(local_kernel, inner, edges, count, cells),
        [(half * length, width)],
        message, *chip_edges, forward, inverse, diagonals, solid_mask, cost=SHORT,
    )

    spectrum, edge_ones, paired, other, sides = call(
        functools.partial(edge_kernel, edges, count, cells),
        [(2, modes, width), (2, modes, width), (modes, width), (modes, width), (modes, 16)],
        *edge_blocks, forward, diagonals, solid_mask,
    )
    pairs = [[(i, i ^ 1) for i in range(plane_count)], [(i, ((i + 1) ^ 1) - 1) for i in range(plane_count)]]
    pairs = [[(i, j) for i, j in pair if 0 <= j < plane_count] for pair in pairs]
    halos = [lax.ppermute(paired, "plane", pairs[0])]
    (other,) = call(
        functools.partial(join_kernel, 0, 0, 0), [(modes, width)], other, cost=SHORT, earlier=(own,)
    )
    halos.append(lax.ppermute(other, "plane", pairs[1]))

    *made, ones = call(
        functools.partial(inner_kernel, inner, count, cells),
        [(length, width)] * half + [(2, modes, width)],
        *inner_blocks, arrived, forward, inverse, diagonals, solid_mask, edge_ones, cost=SHORT, earlier=(own,),
    )
    pieces = [(made[0], 0, 0, inner, 0, tiles)]
    made_got = [swap(made[d], d) for d in near]
    pieces += [(block, d, 0, inner, 0, tiles) for d, block in zip(near, made_got)]
    rim_got, earlier = [], []
    for order, name in enumerate(("near", "far")):
        outs = call(
            functools.partial(rim_kernel, edges, order, count, cells),
            [(cells, width)] * count,
            spectrum, edge_ones, sides, halos[order], ones, inverse, diagonals, solid_mask,
            cost=LONG if order else SHORT, earlier=earlier,
        )
        pieces.append((outs[0], 0, 0, (name,), 0, tiles))
        rim_got.append([swap(outs[d], d) for d in (*far, *near)])
        pieces += [(block, d, 0, (name,), 0, tiles) for d, block in zip((*far, *near), rim_got[order])]
        earlier = [outs[-1], taken]
    rebuilt = call(
        functools.partial(take_kernel, inner, count, cells), [(length, width)] * half, taken, own, take,
        cost=SHORT, earlier=[outs[-1], *rim_got[0][:half]],
    )
    pieces.append((rebuilt[0], half, 0, inner, 0, tiles))
    pieces += [(swap(rebuilt[d], d), half + d, 0, inner, 0, tiles) for d in near]

    result = None
    own_lines = tiles * row_count
    for devices in (range(count - 1), [count - 1]) if own_lines % 8 == 0 else (range(count),):
        chosen = [piece for piece in pieces if piece[1] in devices]
        previous = () if result is None else (result,)
        result = pl.pallas_call(
            functools.partial(unpack_kernel, [piece[1:] for piece in chosen], list(devices), row_count, cells),
            out_shape=jax.ShapeDtypeStruct((cells, lines, LANES), jnp.float32),
            in_specs=[VMEM] * len(chosen) + [ANY] * len(previous),
            out_specs=ANY,
            scratch_shapes=[
                pltpu.VMEM((cells * (len(devices) * own_lines + 8), LANES), jnp.float32),
                pltpu.SemaphoreType.DMA((SPLIT, len(devices))),
            ],
            input_output_aliases={len(chosen): 0} if previous else {},
            compiler_params=PARAMS,
            cost_estimate=SHORT if previous else LONG,
        )(*[piece[0] for piece in chosen], *previous)
    result = result.reshape(cells, columns // LANES, row_count, LANES).transpose(0, 2, 1, 3)
    return result.reshape(cells, row_count, columns)


def solution(mesh):
    placed = (P("span", "plane", None), P("plane", None))
    return jax.shard_map(
        local, mesh=mesh, in_specs=placed, out_specs=P("span", "plane", None), check_vma=False
    )
```

```python
import functools

import jax
import jax.numpy as jnp
import ml_dtypes
import numpy as np
from jax import lax
from jax.experimental import pallas as pl
from jax.experimental.pallas import tpu as pltpu
from jax.sharding import PartitionSpec as P

PENALTY = 12.0
LANES = 128
VMEM = pl.BlockSpec(memory_space=pltpu.VMEM)
ANY = pl.BlockSpec(memory_space=pl.ANY)
PARAMS = pltpu.CompilerParams(vmem_limit_bytes=24 * 1024 * 1024)
LONG = pl.CostEstimate(flops=0, bytes_accessed=200_000_000, transcendentals=0)
SHORT = pl.CostEstimate(flops=0, bytes_accessed=1024, transcendentals=0)
SPLIT = 4


def split(values):
    high = values.astype(ml_dtypes.bfloat16)
    low = (values - high.astype(np.float64)).astype(ml_dtypes.bfloat16)
    return np.concatenate([high, low, high], axis=-1)


def table_modes(length, wanted):
    modes = [(k, False) for k in range(length // 2 + 1) if wanted(k)]
    return modes + [(k, True) for k in range(1, length // 2) if wanted(k)]


def wave(length, points, k, sine):
    angles = (points * k % length) * (2.0 * np.pi / length)
    return np.sin(angles) if sine else np.cos(angles)


def fill(length, modes, forward, inverse, fluid, solid):
    points = np.arange(length // 2)
    for at, (k, sine) in enumerate(modes):
        forward[at] = wave(length, points, k, sine)
        inverse[:, at] = forward[at] * (1.0 if k in (0, length // 2) else 2.0) / length
        eigen = 2.0 - 2.0 * np.cos(2.0 * np.pi * k / length)
        fluid[at] = 1.0 / (4.0 + eigen)
        solid[at] = 1.0 / (4.0 + eigen + PENALTY)


def up_to(number, step):
    return -(-number // step) * step


def tables(length, cells):
    half = length // 2
    blocks = half // cells
    kept = [table_modes(length, lambda k: 3 * k <= length and k % 2 == parity) for parity in (0, 1)]
    padded = up_to(max(len(modes) for modes in kept), 16)
    left = table_modes(length, lambda k: 3 * k > length)
    rest = up_to(len(left), 16)
    columns = np.zeros((8, up_to(max(2 * padded, rest), LANES)))
    forward, inverse = np.zeros((2, padded, half)), np.zeros((2, half, padded))
    for parity, modes in enumerate(kept):
        part = slice(parity * padded, (parity + 1) * padded)
        fill(length, modes, forward[parity], inverse[parity], columns[0, part], columns[1, part])
    powers = 8
    send, take = np.zeros((rest + 6 * powers, half)), np.zeros((half, up_to(rest + powers, 16)))
    fill(length, left, send[:rest], take[:, :rest], columns[2, :rest], columns[3, :rest])
    take[:, : len(left)] *= [-1.0 if k % 2 == 0 else 1.0 for k, _ in left]
    ends = (np.arange(half), half - 1.0 - np.arange(half))
    for side in (0, 1):
        x, y = ends[side], ends[1 - side] + 1.0
        first = rest + 4 * side
        for solid, diagonal in enumerate((6.0, 6.0 + PENALTY)):
            rho = diagonal / 2.0 - np.sqrt(diagonal * diagonal / 4.0 - 1.0)
            at = first + 2 * solid
            take[:, at], take[:, at + 1] = rho**x, x * rho**x
            single = rho / (1.0 - rho**2) * rho**y
            double = rho**2 / (1.0 - rho**2) ** 2
            send[at + powers * solid] = single
            send[at + powers * (2 + solid)] = (double * (1.0 + rho**2) / (1.0 - rho**2) + double * y) * rho**y
            send[at + 1 + powers * (2 + solid)] = double * rho**y
            send[at + powers * 4] = single / PENALTY * (1.0 if solid == 0 else -1.0)
    forward = split(forward.reshape(2, padded, blocks, cells).transpose(0, 2, 1, 3))
    inverse = split(inverse.reshape(2, blocks, cells, padded))
    send = split(send.reshape(-1, blocks, cells).transpose(1, 0, 2))
    take = split(take.reshape(blocks, cells, -1))
    return forward, inverse, send, take, columns.astype(np.float32), 2 * padded, rest


def thirds(values, axis):
    high = values.astype(jnp.bfloat16)
    low = (values - high.astype(jnp.float32)).astype(jnp.bfloat16)
    return jnp.concatenate([high, high, low], axis=axis)


def pack_kernel(jobs, row_count, cells, earlier, x_ref, *refs):
    outs, (held, arrived) = refs[earlier:-2], refs[-2:]
    me = lax.axis_index("span")
    lines = x_ref.shape[1]
    all_tiles = lines // row_count
    own_tiles = all_tiles // lax.axis_size("span")
    pitch = held.shape[0] // cells
    some = cells // SPLIT
    copies = [
        pltpu.make_async_copy(
            x_ref.at[pl.ds(part * some, some)],
            held.reshape(cells, pitch, LANES).at[pl.ds(part * some, some), pl.ds(0, lines)],
            arrived.at[part],
        )
        for part in range(SPLIT)
    ]
    for copy in copies:
        copy.start()
    lane = lax.broadcasted_iota(jnp.int32, (some, LANES), 1)
    sides = []
    for part, copy in enumerate(copies):
        copy.wait()
        beside = jnp.zeros((some, LANES), jnp.float32)

        def line(tile, row):
            return held[pl.ds(part * some * pitch + tile * row_count + row, some, stride=pitch), :]

        for job, (out, base, d, rows, offset, tiles) in enumerate(jobs):
            first = jnp.bitwise_xor(me, d) * own_tiles + offset
            for i, row in enumerate(rows):
                at = base + i * cells + part * some
                for tile in range(tiles):
                    outs[out][at : at + some, tile * LANES : (tile + 1) * LANES] = line(first + tile, row)
                before = jnp.maximum(first - 1, 0)
                after = jnp.minimum(first + tiles, all_tiles - 1)
                for side, (tile, source) in enumerate(((before, LANES - 1), (after, 0))):
                    at = job * 8 + i * 2 + side
                    beside = jnp.where(lane == at, pltpu.roll(line(tile, row), (at - source) % LANES, 1), beside)
        sides.append(beside)
    if cells < LANES:
        sides.append(jnp.zeros((LANES - cells, LANES), jnp.float32))
    turned = jnp.concatenate(sides, axis=0).T
    for job, (out, base, _, rows, _, tiles) in enumerate(jobs):
        at = base + len(rows) * cells
        outs[out][at : at + 8, :LANES] = turned[job * 8 : (job + 1) * 8]
        if tiles > 1:
            outs[out][at : at + 8, LANES:] = jnp.zeros((8, (tiles - 1) * LANES), jnp.float32)


def place(d):
    half = lax.axis_size("span") // 2
    return jnp.bitwise_and(jnp.bitwise_xor(lax.axis_index("span"), d), half - 1)


def row_product(table, value):
    return jnp.dot(table, thirds(value, 0), preferred_element_type=jnp.float32)


def side_product(table, value):
    value = thirds(jnp.concatenate([value, jnp.zeros_like(value)], axis=0), 1)
    return lax.dot_general(table, value, (((1,), (1,)), ((), ())), preferred_element_type=jnp.float32)


def transform(rows, cells, near, far, forward_ref):
    def spectrum(lines, lanes, product):
        halves = []
        for parity in (0, 1):
            total = 0.0
            for d, block in enumerate(near):
                value = block[lines, lanes]
                if far:
                    other = far[d][lines, lanes]
                    value = value + other if parity == 0 else value - other
                total = total + product(forward_ref[parity, place(d)], value)
            halves.append(total)
        return jnp.concatenate(halves, axis=0)

    spectra = [spectrum(slice(i * cells, (i + 1) * cells), slice(None), row_product) for i in range(rows)]
    return spectra, spectrum(slice(rows * cells, rows * cells + 8), slice(0, cells), side_product)


def inverse_rows(sweeps, cells, inverse_ref, near, far=()):
    padded = sweeps[0].shape[0] // 2
    for i, sweep in enumerate(sweeps):
        even = thirds(sweep[:padded], 0)
        odd = thirds(sweep[padded:], 0)
        for d, out in enumerate(near):
            first = jnp.dot(inverse_ref[0, place(d)], even, preferred_element_type=jnp.float32)
            second = jnp.dot(inverse_ref[1, place(d)], odd, preferred_element_type=jnp.float32)
            out[i * cells : (i + 1) * cells, :] = first + second
            if far:
                far[d][i * cells : (i + 1) * cells, :] = first - second


def second_sweep(spectrum, one, above, below, sides, at, inverse_diagonal):
    width = one.shape[1]
    lane = lax.broadcasted_iota(jnp.int32, one.shape, 1)
    left = jnp.where(lane == 0, sides[:, at : at + 1], pltpu.roll(one, 1, 1))
    right = jnp.where(lane == width - 1, sides[:, at + 1 : at + 2], pltpu.roll(one, width - 1, 1))
    return (spectrum + above + below + left + right) * inverse_diagonal


def masks(mask_ref, rows, d, width):
    start = pl.multiple_of(jnp.bitwise_xor(lax.axis_index("span"), d) * width, LANES)
    last = mask_ref.shape[1] - LANES
    before = mask_ref[:, pl.ds(pl.multiple_of(jnp.maximum(start - LANES, 0), LANES), LANES)][:, LANES - 1 :]
    after = mask_ref[:, pl.ds(pl.multiple_of(jnp.minimum(start + width, last), LANES), LANES)][:, :1]
    before = jnp.where(start == 0, 2, before)
    after = jnp.where(start + width == mask_ref.shape[1], 2, after)
    lane = lax.broadcasted_iota(jnp.int32, (1, 16), 1)
    kinds = jnp.full((1, 16), 2, jnp.int32)
    for i, row in enumerate(rows):
        kinds = jnp.where(lane == 2 * i, before[row : row + 1], kinds)
        kinds = jnp.where(lane == 2 * i + 1, after[row : row + 1], kinds)
    return [mask_ref[row : row + 1, pl.ds(start, width)] for row in range(mask_ref.shape[0])], kinds


def pick(kind, fluid, solid):
    return jnp.where(kind == 0, fluid, jnp.where(kind == 1, solid, 0.0))


def one_over(columns_ref, first, modes):
    turned = columns_ref[...].T
    return turned[:modes, first : first + 1], turned[:modes, first + 1 : first + 2]


def paired_edge():
    return lax.rem(lax.axis_index("plane") + 1, 2)


def edge_kernel(rows, count, cells, *refs):
    near, far = refs[: count // 2], refs[count // 2 : count]
    forward_ref, columns_ref, mask_ref = refs[count : count + 3]
    spectrum_ref, ones_ref, paired_ref, other_ref, sides_ref = refs[-5:]
    spectra, sides = transform(len(rows), cells, near, far, forward_ref)
    modes, width = spectra[0].shape
    mask, kinds = masks(mask_ref, rows, 0, width)
    fluid, solid = one_over(columns_ref, 0, modes)
    ones = [spectrum * pick(mask[row], fluid, solid) for spectrum, row in zip(spectra, rows)]
    for i in (0, 1):
        spectrum_ref[i] = spectra[i]
        ones_ref[i] = ones[i]
    last = paired_edge() == 1
    paired_ref[...] = jnp.where(last, ones[1], ones[0])
    other_ref[...] = jnp.where(last, ones[0], ones[1])
    sides_ref[...] = sides * pick(kinds, fluid, solid)


def inner_sweeps(spectra, sides, rows, mask, kinds, fluid, solid, edges):
    diagonals = [pick(mask[row], fluid, solid) for row in rows]
    ones = [spectrum * diagonal for spectrum, diagonal in zip(spectra, diagonals)]
    around = [edges[0], *ones, edges[1]]
    sides = sides * pick(kinds, fluid, solid)
    return ones, [
        second_sweep(spectra[i], ones[i], around[i], around[i + 2], sides, 2 * i, diagonals[i])
        for i in range(len(rows))
    ]


def inner_kernel(rows, count, cells, *refs):
    half = count // 2
    far_ref, forward_ref, inverse_ref, columns_ref, mask_ref, edges_ref = refs[half : half + 6]
    outs, ones_ref = refs[-1 - half : -1], refs[-1]
    size = len(rows) * cells + 8
    far = [far_ref.at[e * size : (e + 1) * size] for e in range(half)]
    spectra, sides = transform(len(rows), cells, refs[:half], far, forward_ref)
    modes, width = spectra[0].shape
    mask, kinds = masks(mask_ref, rows, 0, width)
    fluid, solid = one_over(columns_ref, 0, modes)
    ones, sweeps = inner_sweeps(spectra, sides, rows, mask, kinds, fluid, solid, (edges_ref[0], edges_ref[1]))
    ones_ref[0] = ones[0]
    ones_ref[1] = ones[-1]
    inverse_rows(sweeps, cells, inverse_ref, outs)


def local_kernel(rows, edge_rows, count, cells, *refs):
    half = count // 2
    message_ref, edges = refs[0], refs[1 : 1 + half]
    forward_ref, inverse_ref, columns_ref, mask_ref = refs[1 + half : 5 + half]
    out_ref = refs[-1]
    size = len(rows) * cells + 8
    near = [message_ref.at[d * size : (d + 1) * size] for d in range(half)]
    spectra, sides = transform(len(rows), cells, near, (), forward_ref)
    edge_spectra, _ = transform(len(edge_rows), cells, edges, (), forward_ref)
    modes, width = spectra[0].shape
    mask, kinds = masks(mask_ref, rows, half, width)
    fluid, solid = one_over(columns_ref, 0, modes)
    around = [spectrum * pick(mask[row], fluid, solid) for spectrum, row in zip(edge_spectra, edge_rows)]
    _, sweeps = inner_sweeps(spectra, sides, rows, mask, kinds, fluid, solid, around)
    size = len(rows) * cells
    inverse_rows(sweeps, cells, inverse_ref, [out_ref.at[d * size : (d + 1) * size] for d in range(half)])


def send_kernel(rows, edge_rows, rest, count, cells, *refs):
    half = count // 2
    inner, edges = refs[:half], refs[half : 2 * half]
    send_ref, columns_ref, mask_ref, out_ref = refs[2 * half :]

    def product(blocks, lines, lanes, kind):
        return sum(kind(send_ref[place(d)], block[lines, lanes]) for d, block in enumerate(blocks))

    def whole(blocks, i):
        return product(blocks, slice(i * cells, (i + 1) * cells), slice(None), row_product)

    spectra = [whole(inner, i) for i in range(len(rows))]
    around = [whole(edges, i) for i in range(len(edge_rows))]
    sides = product(inner, slice(len(rows) * cells, len(rows) * cells + 8), slice(0, cells), side_product)
    mask, kinds = masks(mask_ref, rows, 0, inner[0].shape[1])
    fluid, solid = one_over(columns_ref, 2, rest)
    outer = [values[:rest] * pick(mask[row], fluid, solid) for values, row in zip(around, edge_rows)]
    _, sweeps = inner_sweeps([v[:rest] for v in spectra], sides[:rest], rows, mask, kinds, fluid, solid, outer)

    def power(values, at):
        return values[rest + 8 * at : rest + 8 * at + 8]

    numbers = []
    for target in (0, 1):

        def beside(values, kind):
            same, cross = power(values, 2 + target), power(values, 4)
            return pick(kind, same, cross) if target == 0 else pick(kind, cross, same)

        own = [beside(values, mask[row]) for values, row in zip(spectra, rows)]
        edge = [beside(values, mask[row]) for values, row in zip(around, edge_rows)]
        column = [edge[0], *own, edge[1]]
        outside = beside(sides, kinds)
        numbers.append(
            [
                second_sweep(power(spectra[i], target), own[i], column[i], column[i + 2], outside, 2 * i, 1.0)
                for i in range(len(rows))
            ]
        )
    for i, row in enumerate(rows):
        base = i * (rest + 8)
        out_ref[base : base + rest, :] = sweeps[i]
        out_ref[base + rest : base + rest + 8, :] = jnp.where(mask[row] == 0, numbers[0][i], numbers[1][i])


def take_kernel(rows, count, cells, *refs):
    half = count // 2
    message_ref, local_ref, take_ref = refs[:3]
    outs = refs[-1 - (half - 1) * len(rows) :]
    lines = message_ref.shape[0] // len(rows)
    short = take_ref.shape[2] // 3 - lines
    for i in range(len(rows)):
        values = message_ref[i * lines : (i + 1) * lines, :]
        if short:
            values = jnp.concatenate([values, jnp.zeros((short, values.shape[1]), jnp.float32)], axis=0)
        values = thirds(values, 0)
        for d in range(half):
            base = (d * len(rows) + i) * cells
            value = local_ref[base : base + cells, :] + jnp.dot(
                take_ref[place(d)], values, preferred_element_type=jnp.float32
            )
            if d == 0:
                outs[0][i * cells : (i + 1) * cells, :] = value
            else:
                outs[1 + (d - 1) * len(rows) + i][...] = value


def rim_kernel(rows, order, count, cells, *refs):
    spectrum_ref, edges_ref, sides_ref, halo_ref, ones_ref, inverse_ref, columns_ref, mask_ref = refs[:8]
    outs = refs[-count:]
    _, modes, width = edges_ref.shape
    edge = paired_edge() if order == 0 else 1 - paired_edge()
    mask, _ = masks(mask_ref, rows, 0, width)
    fluid, solid = one_over(columns_ref, 0, modes)
    sides = jnp.where(edge == 0, sides_ref[:, 0:2], sides_ref[:, 2:4])
    diagonal = pick(jnp.where(edge == 0, mask[rows[0]], mask[rows[1]]), fluid, solid)
    sweep = second_sweep(spectrum_ref[edge], edges_ref[edge], halo_ref[...], ones_ref[edge], sides, 0, diagonal)
    inverse_rows([sweep], cells, inverse_ref, outs[: count // 2], outs[count // 2 :])
    if order == 1:
        for d in range(1, count // 2):
            outs[d][cells:, :] = refs[8 + d - 1][...]
    for out in outs[count // 2 :]:
        out[cells:, :] = jnp.zeros((out.shape[0] - cells, width), jnp.float32)


def join_kernel(rows, cells, near, *refs):
    own_ref, blocks, out_ref = refs[0], refs[1 : 1 + rows * near], refs[-1]
    size = own_ref.shape[0]
    out_ref[:size, :] = own_ref[...]
    for d in range(near):
        base = (d + 1) * size
        out_ref[base + rows * cells : base + size, :] = jnp.zeros((8, out_ref.shape[1]), jnp.float32)
        for i in range(rows):
            block = blocks[d * rows + i]
            out_ref[base + i * cells : base + (i + 1) * cells, :] = block[:cells, :]
            at = base + rows * cells + 2 * i
            out_ref[at : at + 2, :] = block[cells : cells + 2, :]


def unpack_kernel(pieces, devices, row_count, cells, *refs):
    me = lax.axis_index("span")
    blocks, (out_ref, held, done) = refs[: len(pieces)], refs[-3:]
    pitch = held.shape[0] // cells
    own_lines = out_ref.shape[1] // lax.axis_size("span")
    some = cells // SPLIT
    edge_rows = {"near": paired_edge() * (row_count - 1), "far": (1 - paired_edge()) * (row_count - 1)}
    copies = []
    for part in range(SPLIT):
        for block, (d, base, rows, offset, tiles) in zip(blocks, pieces):
            for i, row in enumerate(rows):
                if row in edge_rows:
                    row = edge_rows[row]
                line = base + i * cells + part * some
                for tile in range(tiles):
                    at = part * some * pitch + devices.index(d) * own_lines + (offset + tile) * row_count + row
                    held[pl.ds(at, some, stride=pitch), :] = block[line : line + some, tile * LANES : (tile + 1) * LANES]
        for at, d in enumerate(devices):
            first = pl.multiple_of(jnp.bitwise_xor(me, d) * own_lines, own_lines)
            copies.append(
                pltpu.make_async_copy(
                    held.reshape(cells, pitch, LANES).at[pl.ds(part * some, some), pl.ds(at * own_lines, own_lines)],
                    out_ref.at[pl.ds(part * some, some), pl.ds(first, own_lines)],
                    done.at[part, at],
                )
            )
            copies[-1].start()
    for copy in copies:
        copy.wait()


def call(kernel, outs, *args, cost=LONG, earlier=()):
    shapes = [jax.ShapeDtypeStruct(shape, jnp.float32) for shape in outs]
    return pl.pallas_call(
        kernel,
        out_shape=shapes,
        in_specs=[VMEM] * len(args) + [ANY] * len(earlier),
        out_specs=[VMEM] * len(outs),
        compiler_params=PARAMS,
        cost_estimate=cost,
    )(*args, *earlier)


def swap(block, d):
    return lax.ppermute(block, "span", [(i, i ^ d) for i in range(lax.axis_size("span"))])


def local(pressure_source, solid_mask):
    count = lax.axis_size("span")
    half = count // 2
    plane_count = lax.axis_size("plane")
    cells, row_count, columns = pressure_source.shape
    width = columns // count
    tiles = width // LANES
    inner = tuple(range(1, row_count - 1))
    edges = (0, row_count - 1)
    near, far = range(1, half), range(half, count)
    *arrays, modes, rest = tables(cells * count, cells)
    forward, inverse, send, take, diagonals = map(jnp.asarray, arrays)

    lines = columns // LANES * row_count
    source = pressure_source.reshape(cells, row_count, columns // LANES, LANES).transpose(0, 2, 1, 3)
    source = source.reshape(cells, lines, LANES)
    scratch = [pltpu.VMEM((cells * (lines + 8), LANES), jnp.float32), pltpu.SemaphoreType.DMA((SPLIT,))]

    def pack(source, wanted, *earlier):
        jobs = [(at, 0, d, rows, 0, tiles) for at, (d, rows) in enumerate(wanted)]
        shapes = [(len(rows) * cells + 8, width) for _, rows in wanted]
        return pl.pallas_call(
            functools.partial(pack_kernel, jobs, row_count, cells, len(earlier)),
            out_shape=[jax.ShapeDtypeStruct(shape, jnp.float32) for shape in shapes],
            in_specs=[ANY] * (1 + len(earlier)),
            out_specs=[VMEM] * len(shapes),
            scratch_shapes=scratch,
            compiler_params=PARAMS,
            cost_estimate=LONG,
        )(source, *earlier)

    packed = pack(pltpu.with_memory_space_constraint(source, pltpu.HBM), [(d, edges) for d in range(1, count)])
    edge_blocks = [swap(block, d) for d, block in enumerate(packed, 1)]
    wanted = [(d, inner) for d in range(half + 1)] + [(0, edges)] + [(d, edges) for d in far]
    wanted += [(half + d, (row,)) for d in near for row in inner]
    packed = pack(source, wanted, packed[half - 1])
    edge_blocks = [packed[half + 1], *edge_blocks]
    inner_blocks = [packed[0]] + [swap(packed[d], d) for d in near]
    chip_edges = [packed[half + 2]] + [swap(packed[half + 2 + d], d) for d in near]
    relayed = packed[2 * half + 2 :]
    relayed = [swap(relayed[(d - 1) * len(inner) + i], d) for d in near for i in range(len(inner))]
    (message,) = call(
        functools.partial(join_kernel, len(inner), cells, half - 1),
        [(half * (len(inner) * cells + 8), width)],
        packed[half], *relayed, cost=SHORT, earlier=(edge_blocks[half],),
    )
    arrived = swap(message, half)

    length = len(inner) * cells
    (sent,) = call(
        functools.partial(send_kernel, inner, edges, rest, count, cells),
        [(len(inner) * (rest + 8), width)],
        *inner_blocks, *edge_blocks[:half], send, diagonals, solid_mask, cost=SHORT,
    )
    taken = swap(sent, half)
    (own,) = call(
        functools.partial(local_kernel, inner, edges, count, cells),
        [(half * length, width)],
        message, *chip_edges, forward, inverse, diagonals, solid_mask, cost=SHORT,
    )

    spectrum, edge_ones, paired, other, sides = call(
        functools.partial(edge_kernel, edges, count, cells),
        [(2, modes, width), (2, modes, width), (modes, width), (modes, width), (modes, 16)],
        *edge_blocks, forward, diagonals, solid_mask,
    )
    pairs = [[(i, i ^ 1) for i in range(plane_count)], [(i, ((i + 1) ^ 1) - 1) for i in range(plane_count)]]
    pairs = [[(i, j) for i, j in pair if 0 <= j < plane_count] for pair in pairs]
    halos = [lax.ppermute(paired, "plane", pairs[0])]
    *made, ones = call(
        functools.partial(inner_kernel, inner, count, cells),
        [(length, width)] * half + [(2, modes, width)],
        *inner_blocks, arrived, forward, inverse, diagonals, solid_mask, edge_ones, cost=SHORT, earlier=(own,),
    )
    (other,) = call(
        functools.partial(join_kernel, 0, 0, 0), [(modes, width)], other, cost=SHORT, earlier=(halos[0], ones)
    )
    halos.append(lax.ppermute(other, "plane", pairs[1]))

    pieces = [(made[0], 0, 0, inner, 0, tiles)]
    made_got = [swap(made[d], d) for d in near]
    pieces += [(block, d, 0, inner, 0, tiles) for d, block in zip(near, made_got)]
    rim_got, near_rim, earlier = [], [], []
    for order, name in enumerate(("near", "far")):
        outs = call(
            functools.partial(rim_kernel, edges, order, count, cells),
            [(cells, width)] + [((order + 1) * cells, width)] * (half - 1) + [(cells + 8, width)] * half,
            spectrum, edge_ones, sides, halos[order], ones, inverse, diagonals, solid_mask, *near_rim,
            cost=LONG if order else SHORT, earlier=earlier,
        )
        near_rim = outs[1:half]
        pieces.append((outs[0], 0, 0, (name,), 0, tiles))
        rim_got.append([swap(outs[d], d) for d in far])
        pieces += [(block, d, 0, (name,), 0, tiles) for d, block in zip(far, rim_got[order])]
        earlier = [outs[-1], taken]
    pieces += [(swap(near_rim[d - 1], d), d, 0, ("far", "near"), 0, tiles) for d in near]
    rebuilt = call(
        functools.partial(take_kernel, inner, count, cells),
        [(length, width)] + [(cells, width)] * ((half - 1) * len(inner)),
        taken, own, take,
        cost=SHORT, earlier=[outs[-1], *rim_got[0], *made_got],
    )
    pieces.append((rebuilt[0], half, 0, inner, 0, tiles))
    for d in near:
        for i, row in enumerate(inner):
            pieces.append((swap(rebuilt[1 + (d - 1) * len(inner) + i], d), half + d, 0, (row,), 0, tiles))

    result = None
    own_lines = tiles * row_count
    for devices in (range(count - 1), [count - 1]) if own_lines % 8 == 0 else (range(count),):
        chosen = [piece for piece in pieces if piece[1] in devices]
        previous = () if result is None else (result,)
        result = pl.pallas_call(
            functools.partial(unpack_kernel, [piece[1:] for piece in chosen], list(devices), row_count, cells),
            out_shape=jax.ShapeDtypeStruct((cells, lines, LANES), jnp.float32),
            in_specs=[VMEM] * len(chosen) + [ANY] * len(previous),
            out_specs=ANY,
            scratch_shapes=[
                pltpu.VMEM((cells * (len(devices) * own_lines + 8), LANES), jnp.float32),
                pltpu.SemaphoreType.DMA((SPLIT, len(devices))),
            ],
            input_output_aliases={len(chosen): 0} if previous else {},
            compiler_params=PARAMS,
            cost_estimate=SHORT if previous else LONG,
        )(*[piece[0] for piece in chosen], *previous)
    result = result.reshape(cells, columns // LANES, row_count, LANES).transpose(0, 2, 1, 3)
    return result.reshape(cells, row_count, columns)


def solution(mesh):
    placed = (P("span", "plane", None), P("plane", None))
    return jax.shard_map(
        local, mesh=mesh, in_specs=placed, out_specs=P("span", "plane", None), check_vma=False
    )
```

```python
import functools

import jax
import jax.numpy as jnp
import ml_dtypes
import numpy as np
from jax import lax
from jax.experimental import pallas as pl
from jax.experimental.pallas import tpu as pltpu
from jax.sharding import PartitionSpec as P

PENALTY = 12.0
LANES = 128
VMEM = pl.BlockSpec(memory_space=pltpu.VMEM)
ANY = pl.BlockSpec(memory_space=pl.ANY)
PARAMS = pltpu.CompilerParams(vmem_limit_bytes=24 * 1024 * 1024)
LONG = pl.CostEstimate(flops=0, bytes_accessed=200_000_000, transcendentals=0)
SHORT = pl.CostEstimate(flops=0, bytes_accessed=1024, transcendentals=0)
SPLIT = 4


def split(values):
    high = values.astype(ml_dtypes.bfloat16)
    low = (values - high.astype(np.float64)).astype(ml_dtypes.bfloat16)
    return np.concatenate([high, low, high], axis=-1)


def table_modes(length, wanted):
    modes = [(k, False) for k in range(length // 2 + 1) if wanted(k)]
    return modes + [(k, True) for k in range(1, length // 2) if wanted(k)]


def wave(length, points, k, sine):
    angles = (points * k % length) * (2.0 * np.pi / length)
    return np.sin(angles) if sine else np.cos(angles)


def fill(length, modes, forward, inverse, fluid, solid):
    points = np.arange(length // 2)
    for at, (k, sine) in enumerate(modes):
        forward[at] = wave(length, points, k, sine)
        inverse[:, at] = forward[at] * (1.0 if k in (0, length // 2) else 2.0) / length
        eigen = 2.0 - 2.0 * np.cos(2.0 * np.pi * k / length)
        fluid[at] = 1.0 / (4.0 + eigen)
        solid[at] = 1.0 / (4.0 + eigen + PENALTY)


def up_to(number, step):
    return -(-number // step) * step


def tables(length, cells):
    half = length // 2
    blocks = half // cells
    kept = [table_modes(length, lambda k: 3 * k <= length and k % 2 == parity) for parity in (0, 1)]
    padded = up_to(max(len(modes) for modes in kept), 16)
    left = table_modes(length, lambda k: 3 * k > length)
    rest = up_to(len(left), 16)
    columns = np.zeros((8, up_to(max(2 * padded, rest), LANES)))
    forward, inverse = np.zeros((2, padded, half)), np.zeros((2, half, padded))
    for parity, modes in enumerate(kept):
        part = slice(parity * padded, (parity + 1) * padded)
        fill(length, modes, forward[parity], inverse[parity], columns[0, part], columns[1, part])
    powers = 8
    send, take = np.zeros((rest + 6 * powers, half)), np.zeros((half, up_to(rest + powers, 16)))
    fill(length, left, send[:rest], take[:, :rest], columns[2, :rest], columns[3, :rest])
    take[:, : len(left)] *= [-1.0 if k % 2 == 0 else 1.0 for k, _ in left]
    ends = (np.arange(half), half - 1.0 - np.arange(half))
    for side in (0, 1):
        x, y = ends[side], ends[1 - side] + 1.0
        first = rest + 4 * side
        for solid, diagonal in enumerate((6.0, 6.0 + PENALTY)):
            rho = diagonal / 2.0 - np.sqrt(diagonal * diagonal / 4.0 - 1.0)
            at = first + 2 * solid
            take[:, at], take[:, at + 1] = rho**x, x * rho**x
            single = rho / (1.0 - rho**2) * rho**y
            double = rho**2 / (1.0 - rho**2) ** 2
            send[at + powers * solid] = single
            send[at + powers * (2 + solid)] = (double * (1.0 + rho**2) / (1.0 - rho**2) + double * y) * rho**y
            send[at + 1 + powers * (2 + solid)] = double * rho**y
            send[at + powers * 4] = single / PENALTY * (1.0 if solid == 0 else -1.0)
    forward = split(forward.reshape(2, padded, blocks, cells).transpose(0, 2, 1, 3))
    inverse = split(inverse.reshape(2, blocks, cells, padded))
    send = split(send.reshape(-1, blocks, cells).transpose(1, 0, 2))
    take = split(take.reshape(blocks, cells, -1))
    return forward, inverse, send, take, columns.astype(np.float32), 2 * padded, rest


def thirds(values, axis):
    high = values.astype(jnp.bfloat16)
    low = (values - high.astype(jnp.float32)).astype(jnp.bfloat16)
    return jnp.concatenate([high, high, low], axis=axis)


def pack_kernel(jobs, row_count, cells, earlier, x_ref, *refs):
    outs, (held, arrived) = refs[earlier:-2], refs[-2:]
    me = lax.axis_index("span")
    lines = x_ref.shape[1]
    all_tiles = lines // row_count
    own_tiles = all_tiles // lax.axis_size("span")
    pitch = held.shape[0] // cells
    some = cells // SPLIT
    copies = [
        pltpu.make_async_copy(
            x_ref.at[pl.ds(part * some, some)],
            held.reshape(cells, pitch, LANES).at[pl.ds(part * some, some), pl.ds(0, lines)],
            arrived.at[part],
        )
        for part in range(SPLIT)
    ]
    for copy in copies:
        copy.start()
    lane = lax.broadcasted_iota(jnp.int32, (some, LANES), 1)
    sides = []
    for part, copy in enumerate(copies):
        copy.wait()
        beside = jnp.zeros((some, LANES), jnp.float32)

        def line(tile, row):
            return held[pl.ds(part * some * pitch + tile * row_count + row, some, stride=pitch), :]

        for job, (out, base, d, rows, offset, tiles) in enumerate(jobs):
            first = jnp.bitwise_xor(me, d) * own_tiles + offset
            for i, row in enumerate(rows):
                at = base + i * cells + part * some
                for tile in range(tiles):
                    outs[out][at : at + some, tile * LANES : (tile + 1) * LANES] = line(first + tile, row)
                before = jnp.maximum(first - 1, 0)
                after = jnp.minimum(first + tiles, all_tiles - 1)
                for side, (tile, source) in enumerate(((before, LANES - 1), (after, 0))):
                    at = job * 8 + i * 2 + side
                    beside = jnp.where(lane == at, pltpu.roll(line(tile, row), (at - source) % LANES, 1), beside)
        sides.append(beside)
    if cells < LANES:
        sides.append(jnp.zeros((LANES - cells, LANES), jnp.float32))
    turned = jnp.concatenate(sides, axis=0).T
    for job, (out, base, _, rows, _, tiles) in enumerate(jobs):
        at = base + len(rows) * cells
        outs[out][at : at + 8, :LANES] = turned[job * 8 : (job + 1) * 8]
        if tiles > 1:
            outs[out][at : at + 8, LANES:] = jnp.zeros((8, (tiles - 1) * LANES), jnp.float32)


def place(d):
    half = lax.axis_size("span") // 2
    return jnp.bitwise_and(jnp.bitwise_xor(lax.axis_index("span"), d), half - 1)


def row_product(table, value):
    return jnp.dot(table, thirds(value, 0), preferred_element_type=jnp.float32)


def side_product(table, value):
    value = thirds(jnp.concatenate([value, jnp.zeros_like(value)], axis=0), 1)
    return lax.dot_general(table, value, (((1,), (1,)), ((), ())), preferred_element_type=jnp.float32)


def transform(rows, cells, near, far, forward_ref):
    def spectrum(lines, lanes, product):
        halves = []
        for parity in (0, 1):
            total = 0.0
            for d, block in enumerate(near):
                value = block[lines, lanes]
                if far:
                    other = far[d][lines, lanes]
                    value = value + other if parity == 0 else value - other
                total = total + product(forward_ref[parity, place(d)], value)
            halves.append(total)
        return jnp.concatenate(halves, axis=0)

    spectra = [spectrum(slice(i * cells, (i + 1) * cells), slice(None), row_product) for i in range(rows)]
    return spectra, spectrum(slice(rows * cells, rows * cells + 8), slice(0, cells), side_product)


def inverse_rows(sweeps, cells, inverse_ref, near, far=()):
    padded = sweeps[0].shape[0] // 2
    for i, sweep in enumerate(sweeps):
        even = thirds(sweep[:padded], 0)
        odd = thirds(sweep[padded:], 0)
        for d, out in enumerate(near):
            first = jnp.dot(inverse_ref[0, place(d)], even, preferred_element_type=jnp.float32)
            second = jnp.dot(inverse_ref[1, place(d)], odd, preferred_element_type=jnp.float32)
            out[i * cells : (i + 1) * cells, :] = first + second
            if far:
                far[d][i * cells : (i + 1) * cells, :] = first - second


def second_sweep(spectrum, one, above, below, sides, at, inverse_diagonal):
    width = one.shape[1]
    lane = lax.broadcasted_iota(jnp.int32, one.shape, 1)
    left = jnp.where(lane == 0, sides[:, at : at + 1], pltpu.roll(one, 1, 1))
    right = jnp.where(lane == width - 1, sides[:, at + 1 : at + 2], pltpu.roll(one, width - 1, 1))
    return (spectrum + above + below + left + right) * inverse_diagonal


def masks(mask_ref, rows, d, width):
    start = pl.multiple_of(jnp.bitwise_xor(lax.axis_index("span"), d) * width, LANES)
    last = mask_ref.shape[1] - LANES
    before = mask_ref[:, pl.ds(pl.multiple_of(jnp.maximum(start - LANES, 0), LANES), LANES)][:, LANES - 1 :]
    after = mask_ref[:, pl.ds(pl.multiple_of(jnp.minimum(start + width, last), LANES), LANES)][:, :1]
    before = jnp.where(start == 0, 2, before)
    after = jnp.where(start + width == mask_ref.shape[1], 2, after)
    lane = lax.broadcasted_iota(jnp.int32, (1, 16), 1)
    kinds = jnp.full((1, 16), 2, jnp.int32)
    for i, row in enumerate(rows):
        kinds = jnp.where(lane == 2 * i, before[row : row + 1], kinds)
        kinds = jnp.where(lane == 2 * i + 1, after[row : row + 1], kinds)
    return [mask_ref[row : row + 1, pl.ds(start, width)] for row in range(mask_ref.shape[0])], kinds


def pick(kind, fluid, solid):
    return jnp.where(kind == 0, fluid, jnp.where(kind == 1, solid, 0.0))


def one_over(columns_ref, first, modes):
    turned = columns_ref[...].T
    return turned[:modes, first : first + 1], turned[:modes, first + 1 : first + 2]


def paired_edge():
    return lax.rem(lax.axis_index("plane") + 1, 2)


def edge_kernel(rows, count, cells, *refs):
    near, far = refs[: count // 2], refs[count // 2 : count]
    forward_ref, columns_ref, mask_ref = refs[count : count + 3]
    spectrum_ref, ones_ref, paired_ref, other_ref, sides_ref = refs[-5:]
    spectra, sides = transform(len(rows), cells, near, far, forward_ref)
    modes, width = spectra[0].shape
    mask, kinds = masks(mask_ref, rows, 0, width)
    fluid, solid = one_over(columns_ref, 0, modes)
    ones = [spectrum * pick(mask[row], fluid, solid) for spectrum, row in zip(spectra, rows)]
    for i in (0, 1):
        spectrum_ref[i] = spectra[i]
        ones_ref[i] = ones[i]
    last = paired_edge() == 1
    paired_ref[...] = jnp.where(last, ones[1], ones[0])
    other_ref[...] = jnp.where(last, ones[0], ones[1])
    sides_ref[...] = sides * pick(kinds, fluid, solid)


def inner_sweeps(spectra, sides, rows, mask, kinds, fluid, solid, edges):
    diagonals = [pick(mask[row], fluid, solid) for row in rows]
    ones = [spectrum * diagonal for spectrum, diagonal in zip(spectra, diagonals)]
    around = [edges[0], *ones, edges[1]]
    sides = sides * pick(kinds, fluid, solid)
    return ones, [
        second_sweep(spectra[i], ones[i], around[i], around[i + 2], sides, 2 * i, diagonals[i])
        for i in range(len(rows))
    ]


def inner_kernel(rows, count, cells, *refs):
    half = count // 2
    far_ref, forward_ref, inverse_ref, columns_ref, mask_ref, edges_ref = refs[half : half + 6]
    outs, ones_ref = refs[-1 - half : -1], refs[-1]
    size = len(rows) * cells + 8
    far = [far_ref.at[e * size : (e + 1) * size] for e in range(half)]
    spectra, sides = transform(len(rows), cells, refs[:half], far, forward_ref)
    modes, width = spectra[0].shape
    mask, kinds = masks(mask_ref, rows, 0, width)
    fluid, solid = one_over(columns_ref, 0, modes)
    ones, sweeps = inner_sweeps(spectra, sides, rows, mask, kinds, fluid, solid, (edges_ref[0], edges_ref[1]))
    ones_ref[0] = ones[0]
    ones_ref[1] = ones[-1]
    inverse_rows(sweeps, cells, inverse_ref, outs)
    for out in outs[1:]:
        out[len(rows) * cells :, :] = jnp.zeros((out.shape[0] - len(rows) * cells, width), jnp.float32)


def local_kernel(rows, edge_rows, count, cells, *refs):
    half = count // 2
    message_ref, edges = refs[0], refs[1 : 1 + half]
    forward_ref, inverse_ref, columns_ref, mask_ref = refs[1 + half : 5 + half]
    out_ref = refs[-1]
    size = len(rows) * cells + 8
    near = [message_ref.at[d * size : (d + 1) * size] for d in range(half)]
    spectra, sides = transform(len(rows), cells, near, (), forward_ref)
    edge_spectra, _ = transform(len(edge_rows), cells, edges, (), forward_ref)
    modes, width = spectra[0].shape
    mask, kinds = masks(mask_ref, rows, half, width)
    fluid, solid = one_over(columns_ref, 0, modes)
    around = [spectrum * pick(mask[row], fluid, solid) for spectrum, row in zip(edge_spectra, edge_rows)]
    _, sweeps = inner_sweeps(spectra, sides, rows, mask, kinds, fluid, solid, around)
    size = len(rows) * cells
    inverse_rows(sweeps, cells, inverse_ref, [out_ref.at[d * size : (d + 1) * size] for d in range(half)])


def send_kernel(rows, edge_rows, rest, count, cells, *refs):
    half = count // 2
    inner, edges = refs[:half], refs[half : 2 * half]
    send_ref, columns_ref, mask_ref = refs[2 * half : 2 * half + 3]
    out_ref = refs[-1]

    def product(blocks, lines, lanes, kind):
        return sum(kind(send_ref[place(d)], block[lines, lanes]) for d, block in enumerate(blocks))

    def whole(blocks, i):
        return product(blocks, slice(i * cells, (i + 1) * cells), slice(None), row_product)

    spectra = [whole(inner, i) for i in range(len(rows))]
    around = [whole(edges, i) for i in range(len(edge_rows))]
    sides = product(inner, slice(len(rows) * cells, len(rows) * cells + 8), slice(0, cells), side_product)
    mask, kinds = masks(mask_ref, rows, 0, inner[0].shape[1])
    fluid, solid = one_over(columns_ref, 2, rest)
    outer = [values[:rest] * pick(mask[row], fluid, solid) for values, row in zip(around, edge_rows)]
    _, sweeps = inner_sweeps([v[:rest] for v in spectra], sides[:rest], rows, mask, kinds, fluid, solid, outer)

    def power(values, at):
        return values[rest + 8 * at : rest + 8 * at + 8]

    numbers = []
    for target in (0, 1):

        def beside(values, kind):
            same, cross = power(values, 2 + target), power(values, 4)
            return pick(kind, same, cross) if target == 0 else pick(kind, cross, same)

        own = [beside(values, mask[row]) for values, row in zip(spectra, rows)]
        edge = [beside(values, mask[row]) for values, row in zip(around, edge_rows)]
        column = [edge[0], *own, edge[1]]
        outside = beside(sides, kinds)
        numbers.append(
            [
                second_sweep(power(spectra[i], target), own[i], column[i], column[i + 2], outside, 2 * i, 1.0)
                for i in range(len(rows))
            ]
        )
    for i, row in enumerate(rows):
        base = i * (rest + 8)
        out_ref[base : base + rest, :] = sweeps[i]
        out_ref[base + rest : base + rest + 8, :] = jnp.where(mask[row] == 0, numbers[0][i], numbers[1][i])


def take_kernel(rows, count, cells, *refs):
    half = count // 2
    message_ref, local_ref, take_ref = refs[:3]
    outs = refs[-1 - (half - 1) * len(rows) :]
    lines = message_ref.shape[0] // len(rows)
    short = take_ref.shape[2] // 3 - lines
    for i in range(len(rows)):
        values = message_ref[i * lines : (i + 1) * lines, :]
        if short:
            values = jnp.concatenate([values, jnp.zeros((short, values.shape[1]), jnp.float32)], axis=0)
        values = thirds(values, 0)
        for d in range(half):
            base = (d * len(rows) + i) * cells
            value = local_ref[base : base + cells, :] + jnp.dot(
                take_ref[place(d)], values, preferred_element_type=jnp.float32
            )
            if d == 0:
                outs[0][i * cells : (i + 1) * cells, :] = value
            else:
                outs[1 + (d - 1) * len(rows) + i][...] = value


def rim_kernel(rows, order, count, cells, *refs):
    spectrum_ref, edges_ref, sides_ref, halo_ref, ones_ref, inverse_ref, columns_ref, mask_ref = refs[:8]
    outs = refs[-count:]
    _, modes, width = edges_ref.shape
    edge = paired_edge() if order == 0 else 1 - paired_edge()
    mask, _ = masks(mask_ref, rows, 0, width)
    fluid, solid = one_over(columns_ref, 0, modes)
    sides = jnp.where(edge == 0, sides_ref[:, 0:2], sides_ref[:, 2:4])
    diagonal = pick(jnp.where(edge == 0, mask[rows[0]], mask[rows[1]]), fluid, solid)
    sweep = second_sweep(spectrum_ref[edge], edges_ref[edge], halo_ref[...], ones_ref[edge], sides, 0, diagonal)
    inverse_rows([sweep], cells, inverse_ref, outs[: count // 2], outs[count // 2 :])
    if order == 1:
        for d in range(1, count // 2):
            outs[d][cells:, :] = refs[8 + d - 1][...]
    for out in outs[count // 2 :]:
        out[cells:, :] = jnp.zeros((out.shape[0] - cells, width), jnp.float32)


def join_kernel(rows, cells, near, *refs):
    own_ref, blocks, out_ref = refs[0], refs[1 : 1 + rows * near], refs[-1]
    size = own_ref.shape[0]
    out_ref[:size, :] = own_ref[...]
    for d in range(near):
        base = (d + 1) * size
        out_ref[base + rows * cells : base + size, :] = jnp.zeros((8, out_ref.shape[1]), jnp.float32)
        for i in range(rows):
            block = blocks[d * rows + i]
            out_ref[base + i * cells : base + (i + 1) * cells, :] = block[:cells, :]
            at = base + rows * cells + 2 * i
            out_ref[at : at + 2, :] = block[cells : cells + 2, :]


def unpack_kernel(pieces, devices, row_count, cells, *refs):
    me = lax.axis_index("span")
    blocks, (out_ref, held, done) = refs[: len(pieces)], refs[-3:]
    pitch = held.shape[0] // cells
    own_lines = out_ref.shape[1] // lax.axis_size("span")
    some = cells // SPLIT
    edge_rows = {"near": paired_edge() * (row_count - 1), "far": (1 - paired_edge()) * (row_count - 1)}
    copies = []
    for part in range(SPLIT):
        for block, (d, base, rows, offset, tiles) in zip(blocks, pieces):
            for i, row in enumerate(rows):
                if row in edge_rows:
                    row = edge_rows[row]
                line = base + i * cells + part * some
                for tile in range(tiles):
                    at = part * some * pitch + devices.index(d) * own_lines + (offset + tile) * row_count + row
                    held[pl.ds(at, some, stride=pitch), :] = block[line : line + some, tile * LANES : (tile + 1) * LANES]
        for at, d in enumerate(devices):
            first = pl.multiple_of(jnp.bitwise_xor(me, d) * own_lines, own_lines)
            copies.append(
                pltpu.make_async_copy(
                    held.reshape(cells, pitch, LANES).at[pl.ds(part * some, some), pl.ds(at * own_lines, own_lines)],
                    out_ref.at[pl.ds(part * some, some), pl.ds(first, own_lines)],
                    done.at[part, at],
                )
            )
            copies[-1].start()
    for copy in copies:
        copy.wait()


def call(kernel, outs, *args, cost=LONG, earlier=()):
    shapes = [jax.ShapeDtypeStruct(shape, jnp.float32) for shape in outs]
    return pl.pallas_call(
        kernel,
        out_shape=shapes,
        in_specs=[VMEM] * len(args) + [ANY] * len(earlier),
        out_specs=[VMEM] * len(outs),
        compiler_params=PARAMS,
        cost_estimate=cost,
    )(*args, *earlier)


def swap(block, d):
    return lax.ppermute(block, "span", [(i, i ^ d) for i in range(lax.axis_size("span"))])


def local(pressure_source, solid_mask):
    count = lax.axis_size("span")
    half = count // 2
    plane_count = lax.axis_size("plane")
    cells, row_count, columns = pressure_source.shape
    width = columns // count
    tiles = width // LANES
    inner = tuple(range(1, row_count - 1))
    edges = (0, row_count - 1)
    near, far = range(1, half), range(half, count)
    *arrays, modes, rest = tables(cells * count, cells)
    forward, inverse, send, take, diagonals = map(jnp.asarray, arrays)

    lines = columns // LANES * row_count
    source = pressure_source.reshape(cells, row_count, columns // LANES, LANES).transpose(0, 2, 1, 3)
    source = source.reshape(cells, lines, LANES)
    scratch = [pltpu.VMEM((cells * (lines + 8), LANES), jnp.float32), pltpu.SemaphoreType.DMA((SPLIT,))]

    def pack(source, wanted, *earlier):
        jobs = [(at, 0, d, rows, 0, tiles) for at, (d, rows) in enumerate(wanted)]
        shapes = [(len(rows) * cells + 8, width) for _, rows in wanted]
        return pl.pallas_call(
            functools.partial(pack_kernel, jobs, row_count, cells, len(earlier)),
            out_shape=[jax.ShapeDtypeStruct(shape, jnp.float32) for shape in shapes],
            in_specs=[ANY] * (1 + len(earlier)),
            out_specs=[VMEM] * len(shapes),
            scratch_shapes=scratch,
            compiler_params=PARAMS,
            cost_estimate=LONG,
        )(source, *earlier)

    packed = pack(pltpu.with_memory_space_constraint(source, pltpu.HBM), [(d, edges) for d in range(1, count)])
    edge_blocks = [swap(block, d) for d, block in enumerate(packed, 1)]
    wanted = [(d, inner) for d in range(half + 1)] + [(0, edges)] + [(d, edges) for d in far]
    wanted += [(half + d, (row,)) for d in near for row in inner]
    packed = pack(source, wanted, packed[half - 1])
    edge_blocks = [packed[half + 1], *edge_blocks]
    inner_blocks = [packed[0]] + [swap(packed[d], d) for d in near]
    chip_edges = [packed[half + 2]] + [swap(packed[half + 2 + d], d) for d in near]
    relayed = packed[2 * half + 2 :]
    relayed = [swap(relayed[(d - 1) * len(inner) + i], d) for d in near for i in range(len(inner))]
    (message,) = call(
        functools.partial(join_kernel, len(inner), cells, half - 1),
        [(half * (len(inner) * cells + 8), width)],
        packed[half], *relayed, cost=SHORT, earlier=(edge_blocks[half],),
    )
    arrived = swap(message, half)

    length = len(inner) * cells
    (own,) = call(
        functools.partial(local_kernel, inner, edges, count, cells),
        [(half * length, width)],
        message, *chip_edges, forward, inverse, diagonals, solid_mask, cost=SHORT,
    )

    (sent,) = call(
        functools.partial(send_kernel, inner, edges, rest, count, cells),
        [(len(inner) * (rest + 8), width)],
        *inner_blocks, *edge_blocks[:half], send, diagonals, solid_mask, cost=SHORT, earlier=(own,),
    )
    taken = swap(sent, half)

    spectrum, edge_ones, paired, other, sides = call(
        functools.partial(edge_kernel, edges, count, cells),
        [(2, modes, width), (2, modes, width), (modes, width), (modes, width), (modes, 16)],
        *edge_blocks, forward, diagonals, solid_mask,
    )
    pairs = [[(i, i ^ 1) for i in range(plane_count)], [(i, ((i + 1) ^ 1) - 1) for i in range(plane_count)]]
    pairs = [[(i, j) for i, j in pair if 0 <= j < plane_count] for pair in pairs]
    halos = [lax.ppermute(paired, "plane", pairs[0])]
    *made, ones = call(
        functools.partial(inner_kernel, inner, count, cells),
        [(length, width)] + [(length + cells, width)] * (half - 1) + [(2, modes, width)],
        *inner_blocks, arrived, forward, inverse, diagonals, solid_mask, edge_ones, cost=SHORT, earlier=(own,),
    )
    (other,) = call(
        functools.partial(join_kernel, 0, 0, 0), [(modes, width)], other, cost=SHORT, earlier=(halos[0],)
    )
    halos.append(lax.ppermute(other, "plane", pairs[1]))

    pieces = [(made[0], 0, 0, inner, 0, tiles)]
    made_got = [swap(made[d], d) for d in near]
    pieces += [(block, d, 0, inner, 0, tiles) for d, block in zip(near, made_got)]
    rim_got, near_rim, earlier = [], [], []
    for order, name in enumerate(("near", "far")):
        outs = call(
            functools.partial(rim_kernel, edges, order, count, cells),
            [(cells, width)] + [((order + 1) * cells, width)] * (half - 1) + [(cells + 8, width)] * half,
            spectrum, edge_ones, sides, halos[order], ones, inverse, diagonals, solid_mask, *near_rim,
            cost=LONG if order else SHORT, earlier=earlier,
        )
        near_rim = outs[1:half]
        pieces.append((outs[0], 0, 0, (name,), 0, tiles))
        rim_got.append([swap(outs[d], d) for d in far])
        pieces += [(block, d, 0, (name,), 0, tiles) for d, block in zip(far, rim_got[order])]
        earlier = [outs[-1], taken]
    pieces += [(swap(near_rim[d - 1], d), d, 0, ("far", "near"), 0, tiles) for d in near]
    rebuilt = call(
        functools.partial(take_kernel, inner, count, cells),
        [(length, width)] + [(cells, width)] * ((half - 1) * len(inner)),
        taken, own, take,
        cost=SHORT, earlier=[outs[-1], *rim_got[0], *made_got],
    )
    pieces.append((rebuilt[0], half, 0, inner, 0, tiles))
    for d in near:
        for i, row in enumerate(inner):
            pieces.append((swap(rebuilt[1 + (d - 1) * len(inner) + i], d), half + d, 0, (row,), 0, tiles))

    result = None
    own_lines = tiles * row_count
    for devices in (range(count - 1), [count - 1]) if own_lines % 8 == 0 else (range(count),):
        chosen = [piece for piece in pieces if piece[1] in devices]
        previous = () if result is None else (result,)
        result = pl.pallas_call(
            functools.partial(unpack_kernel, [piece[1:] for piece in chosen], list(devices), row_count, cells),
            out_shape=jax.ShapeDtypeStruct((cells, lines, LANES), jnp.float32),
            in_specs=[VMEM] * len(chosen) + [ANY] * len(previous),
            out_specs=ANY,
            scratch_shapes=[
                pltpu.VMEM((cells * (len(devices) * own_lines + 8), LANES), jnp.float32),
                pltpu.SemaphoreType.DMA((SPLIT, len(devices))),
            ],
            input_output_aliases={len(chosen): 0} if previous else {},
            compiler_params=PARAMS,
            cost_estimate=SHORT if previous else LONG,
        )(*[piece[0] for piece in chosen], *previous)
    result = result.reshape(cells, columns // LANES, row_count, LANES).transpose(0, 2, 1, 3)
    return result.reshape(cells, row_count, columns)


def solution(mesh):
    placed = (P("span", "plane", None), P("plane", None))
    return jax.shard_map(
        local, mesh=mesh, in_specs=placed, out_specs=P("span", "plane", None), check_vma=False
    )
```

```python
import functools

import jax
import jax.numpy as jnp
import ml_dtypes
import numpy as np
from jax import lax
from jax.experimental import pallas as pl
from jax.experimental.pallas import tpu as pltpu
from jax.sharding import PartitionSpec as P

PENALTY = 12.0
LANES = 128
VMEM = pl.BlockSpec(memory_space=pltpu.VMEM)
ANY = pl.BlockSpec(memory_space=pl.ANY)
PARAMS = pltpu.CompilerParams(vmem_limit_bytes=24 * 1024 * 1024)
LONG = pl.CostEstimate(flops=0, bytes_accessed=200_000_000, transcendentals=0)
SHORT = pl.CostEstimate(flops=0, bytes_accessed=1024, transcendentals=0)
SPLIT = 4


def split(values):
    high = values.astype(ml_dtypes.bfloat16)
    low = (values - high.astype(np.float64)).astype(ml_dtypes.bfloat16)
    return np.concatenate([high, low, high], axis=-1)


def table_modes(length, wanted):
    modes = [(k, False) for k in range(length // 2 + 1) if wanted(k)]
    return modes + [(k, True) for k in range(1, length // 2) if wanted(k)]


def wave(length, points, k, sine):
    angles = (points * k % length) * (2.0 * np.pi / length)
    return np.sin(angles) if sine else np.cos(angles)


def fill(length, modes, forward, inverse, fluid, solid):
    points = np.arange(length // 2)
    for at, (k, sine) in enumerate(modes):
        forward[at] = wave(length, points, k, sine)
        inverse[:, at] = forward[at] * (1.0 if k in (0, length // 2) else 2.0) / length
        eigen = 2.0 - 2.0 * np.cos(2.0 * np.pi * k / length)
        fluid[at] = 1.0 / (4.0 + eigen)
        solid[at] = 1.0 / (4.0 + eigen + PENALTY)


def up_to(number, step):
    return -(-number // step) * step


def tables(length, cells):
    half = length // 2
    blocks = half // cells
    kept = [table_modes(length, lambda k: 3 * k <= length and k % 2 == parity) for parity in (0, 1)]
    padded = up_to(max(len(modes) for modes in kept), 16)
    left = table_modes(length, lambda k: 3 * k > length)
    rest = up_to(len(left), 16)
    columns = np.zeros((8, up_to(max(2 * padded, rest), LANES)))
    forward, inverse = np.zeros((2, padded, half)), np.zeros((2, half, padded))
    for parity, modes in enumerate(kept):
        part = slice(parity * padded, (parity + 1) * padded)
        fill(length, modes, forward[parity], inverse[parity], columns[0, part], columns[1, part])
    powers = 8
    send, take = np.zeros((rest + 6 * powers, half)), np.zeros((half, up_to(rest + powers, 16)))
    fill(length, left, send[:rest], take[:, :rest], columns[2, :rest], columns[3, :rest])
    take[:, : len(left)] *= [-1.0 if k % 2 == 0 else 1.0 for k, _ in left]
    ends = (np.arange(half), half - 1.0 - np.arange(half))
    for side in (0, 1):
        x, y = ends[side], ends[1 - side] + 1.0
        first = rest + 4 * side
        for solid, diagonal in enumerate((6.0, 6.0 + PENALTY)):
            rho = diagonal / 2.0 - np.sqrt(diagonal * diagonal / 4.0 - 1.0)
            at = first + 2 * solid
            take[:, at], take[:, at + 1] = rho**x, x * rho**x
            single = rho / (1.0 - rho**2) * rho**y
            double = rho**2 / (1.0 - rho**2) ** 2
            send[at + powers * solid] = single
            send[at + powers * (2 + solid)] = (double * (1.0 + rho**2) / (1.0 - rho**2) + double * y) * rho**y
            send[at + 1 + powers * (2 + solid)] = double * rho**y
            send[at + powers * 4] = single / PENALTY * (1.0 if solid == 0 else -1.0)
    forward = split(forward.reshape(2, padded, blocks, cells).transpose(0, 2, 1, 3))
    inverse = split(inverse.reshape(2, blocks, cells, padded))
    send = split(send.reshape(-1, blocks, cells).transpose(1, 0, 2))
    take = split(take.reshape(blocks, cells, -1))
    return forward, inverse, send, take, columns.astype(np.float32), 2 * padded, rest


def thirds(values, axis):
    high = values.astype(jnp.bfloat16)
    low = (values - high.astype(jnp.float32)).astype(jnp.bfloat16)
    return jnp.concatenate([high, high, low], axis=axis)


def pack_kernel(jobs, row_count, cells, earlier, x_ref, *refs):
    outs, (held, arrived) = refs[earlier:-2], refs[-2:]
    me = lax.axis_index("span")
    lines = x_ref.shape[1]
    all_tiles = lines // row_count
    own_tiles = all_tiles // lax.axis_size("span")
    pitch = held.shape[0] // cells
    some = cells // SPLIT
    copies = [
        pltpu.make_async_copy(
            x_ref.at[pl.ds(part * some, some)],
            held.reshape(cells, pitch, LANES).at[pl.ds(part * some, some), pl.ds(0, lines)],
            arrived.at[part],
        )
        for part in range(SPLIT)
    ]
    for copy in copies:
        copy.start()
    lane = lax.broadcasted_iota(jnp.int32, (some, LANES), 1)
    sides = []
    for part, copy in enumerate(copies):
        copy.wait()
        beside = jnp.zeros((some, LANES), jnp.float32)

        def line(tile, row):
            return held[pl.ds(part * some * pitch + tile * row_count + row, some, stride=pitch), :]

        for job, (out, base, d, rows, offset, tiles) in enumerate(jobs):
            first = jnp.bitwise_xor(me, d) * own_tiles + offset
            for i, row in enumerate(rows):
                at = base + i * cells + part * some
                for tile in range(tiles):
                    outs[out][at : at + some, tile * LANES : (tile + 1) * LANES] = line(first + tile, row)
                before = jnp.maximum(first - 1, 0)
                after = jnp.minimum(first + tiles, all_tiles - 1)
                for side, (tile, source) in enumerate(((before, LANES - 1), (after, 0))):
                    at = job * 8 + i * 2 + side
                    beside = jnp.where(lane == at, pltpu.roll(line(tile, row), (at - source) % LANES, 1), beside)
        sides.append(beside)
    if cells < LANES:
        sides.append(jnp.zeros((LANES - cells, LANES), jnp.float32))
    turned = jnp.concatenate(sides, axis=0).T
    for job, (out, base, _, rows, _, tiles) in enumerate(jobs):
        at = base + len(rows) * cells
        outs[out][at : at + 8, :LANES] = turned[job * 8 : (job + 1) * 8]
        if tiles > 1:
            outs[out][at : at + 8, LANES:] = jnp.zeros((8, (tiles - 1) * LANES), jnp.float32)


def place(d):
    half = lax.axis_size("span") // 2
    return jnp.bitwise_and(jnp.bitwise_xor(lax.axis_index("span"), d), half - 1)


def row_product(table, value):
    return jnp.dot(table, thirds(value, 0), preferred_element_type=jnp.float32)


def side_product(table, value):
    value = thirds(jnp.concatenate([value, jnp.zeros_like(value)], axis=0), 1)
    return lax.dot_general(table, value, (((1,), (1,)), ((), ())), preferred_element_type=jnp.float32)


def transform(rows, cells, near, far, forward_ref):
    def spectrum(lines, lanes, product):
        halves = []
        for parity in (0, 1):
            total = 0.0
            for d, block in enumerate(near):
                value = block[lines, lanes]
                if far:
                    other = far[d][lines, lanes]
                    value = value + other if parity == 0 else value - other
                total = total + product(forward_ref[parity, place(d)], value)
            halves.append(total)
        return jnp.concatenate(halves, axis=0)

    spectra = [spectrum(slice(i * cells, (i + 1) * cells), slice(None), row_product) for i in range(rows)]
    return spectra, spectrum(slice(rows * cells, rows * cells + 8), slice(0, cells), side_product)


def inverse_rows(sweeps, cells, inverse_ref, near, far=()):
    padded = sweeps[0].shape[0] // 2
    for i, sweep in enumerate(sweeps):
        even = thirds(sweep[:padded], 0)
        odd = thirds(sweep[padded:], 0)
        for d, out in enumerate(near):
            first = jnp.dot(inverse_ref[0, place(d)], even, preferred_element_type=jnp.float32)
            second = jnp.dot(inverse_ref[1, place(d)], odd, preferred_element_type=jnp.float32)
            out[i * cells : (i + 1) * cells, :] = first + second
            if far:
                far[d][i * cells : (i + 1) * cells, :] = first - second


def second_sweep(spectrum, one, above, below, sides, at, inverse_diagonal):
    width = one.shape[1]
    lane = lax.broadcasted_iota(jnp.int32, one.shape, 1)
    left = jnp.where(lane == 0, sides[:, at : at + 1], pltpu.roll(one, 1, 1))
    right = jnp.where(lane == width - 1, sides[:, at + 1 : at + 2], pltpu.roll(one, width - 1, 1))
    return (spectrum + above + below + left + right) * inverse_diagonal


def masks(mask_ref, rows, d, width):
    start = pl.multiple_of(jnp.bitwise_xor(lax.axis_index("span"), d) * width, LANES)
    last = mask_ref.shape[1] - LANES
    before = mask_ref[:, pl.ds(pl.multiple_of(jnp.maximum(start - LANES, 0), LANES), LANES)][:, LANES - 1 :]
    after = mask_ref[:, pl.ds(pl.multiple_of(jnp.minimum(start + width, last), LANES), LANES)][:, :1]
    before = jnp.where(start == 0, 2, before)
    after = jnp.where(start + width == mask_ref.shape[1], 2, after)
    lane = lax.broadcasted_iota(jnp.int32, (1, 16), 1)
    kinds = jnp.full((1, 16), 2, jnp.int32)
    for i, row in enumerate(rows):
        kinds = jnp.where(lane == 2 * i, before[row : row + 1], kinds)
        kinds = jnp.where(lane == 2 * i + 1, after[row : row + 1], kinds)
    return [mask_ref[row : row + 1, pl.ds(start, width)] for row in range(mask_ref.shape[0])], kinds


def pick(kind, fluid, solid):
    return jnp.where(kind == 0, fluid, jnp.where(kind == 1, solid, 0.0))


def one_over(columns_ref, first, modes):
    turned = columns_ref[...].T
    return turned[:modes, first : first + 1], turned[:modes, first + 1 : first + 2]


def paired_edge():
    return lax.rem(lax.axis_index("plane") + 1, 2)


def edge_kernel(rows, count, cells, *refs):
    near, far = refs[: count // 2], refs[count // 2 : count]
    forward_ref, columns_ref, mask_ref = refs[count : count + 3]
    spectrum_ref, ones_ref, paired_ref, other_ref, sides_ref = refs[-5:]
    spectra, sides = transform(len(rows), cells, near, far, forward_ref)
    modes, width = spectra[0].shape
    mask, kinds = masks(mask_ref, rows, 0, width)
    fluid, solid = one_over(columns_ref, 0, modes)
    ones = [spectrum * pick(mask[row], fluid, solid) for spectrum, row in zip(spectra, rows)]
    for i in (0, 1):
        spectrum_ref[i] = spectra[i]
        ones_ref[i] = ones[i]
    last = paired_edge() == 1
    paired_ref[:modes, :] = jnp.where(last, ones[1], ones[0])
    paired_ref[modes:, :] = jnp.zeros((paired_ref.shape[0] - modes, width), jnp.float32)
    other_ref[...] = jnp.where(last, ones[0], ones[1])
    sides_ref[...] = sides * pick(kinds, fluid, solid)


def inner_sweeps(spectra, sides, rows, mask, kinds, fluid, solid, edges):
    diagonals = [pick(mask[row], fluid, solid) for row in rows]
    ones = [spectrum * diagonal for spectrum, diagonal in zip(spectra, diagonals)]
    around = [edges[0], *ones, edges[1]]
    sides = sides * pick(kinds, fluid, solid)
    return ones, [
        second_sweep(spectra[i], ones[i], around[i], around[i + 2], sides, 2 * i, diagonals[i])
        for i in range(len(rows))
    ]


def inner_kernel(rows, count, cells, *refs):
    half = count // 2
    far_ref, forward_ref, inverse_ref, columns_ref, mask_ref, edges_ref = refs[half : half + 6]
    outs, ones_ref = refs[-1 - half : -1], refs[-1]
    size = len(rows) * cells + 8
    far = [far_ref.at[e * size : (e + 1) * size] for e in range(half)]
    spectra, sides = transform(len(rows), cells, refs[:half], far, forward_ref)
    modes, width = spectra[0].shape
    mask, kinds = masks(mask_ref, rows, 0, width)
    fluid, solid = one_over(columns_ref, 0, modes)
    ones, sweeps = inner_sweeps(spectra, sides, rows, mask, kinds, fluid, solid, (edges_ref[0], edges_ref[1]))
    ones_ref[0] = ones[0]
    ones_ref[1] = ones[-1]
    inverse_rows(sweeps, cells, inverse_ref, outs)


def local_kernel(rows, edge_rows, count, cells, *refs):
    half = count // 2
    message_ref, edges = refs[0], refs[1 : 1 + half]
    forward_ref, inverse_ref, columns_ref, mask_ref = refs[1 + half : 5 + half]
    out_ref = refs[-1]
    size = len(rows) * cells + 8
    near = [message_ref.at[d * size : (d + 1) * size] for d in range(half)]
    spectra, sides = transform(len(rows), cells, near, (), forward_ref)
    edge_spectra, _ = transform(len(edge_rows), cells, edges, (), forward_ref)
    modes, width = spectra[0].shape
    mask, kinds = masks(mask_ref, rows, half, width)
    fluid, solid = one_over(columns_ref, 0, modes)
    around = [spectrum * pick(mask[row], fluid, solid) for spectrum, row in zip(edge_spectra, edge_rows)]
    _, sweeps = inner_sweeps(spectra, sides, rows, mask, kinds, fluid, solid, around)
    size = len(rows) * cells
    inverse_rows(sweeps, cells, inverse_ref, [out_ref.at[d * size : (d + 1) * size] for d in range(half)])


def send_kernel(rows, edge_rows, rest, count, cells, *refs):
    half = count // 2
    inner, edges = refs[:half], refs[half : 2 * half]
    send_ref, columns_ref, mask_ref = refs[2 * half : 2 * half + 3]
    out_ref = refs[-1]

    def product(blocks, lines, lanes, kind):
        return sum(kind(send_ref[place(d)], block[lines, lanes]) for d, block in enumerate(blocks))

    def whole(blocks, i):
        return product(blocks, slice(i * cells, (i + 1) * cells), slice(None), row_product)

    spectra = [whole(inner, i) for i in range(len(rows))]
    around = [whole(edges, i) for i in range(len(edge_rows))]
    sides = product(inner, slice(len(rows) * cells, len(rows) * cells + 8), slice(0, cells), side_product)
    mask, kinds = masks(mask_ref, rows, 0, inner[0].shape[1])
    fluid, solid = one_over(columns_ref, 2, rest)
    outer = [values[:rest] * pick(mask[row], fluid, solid) for values, row in zip(around, edge_rows)]
    _, sweeps = inner_sweeps([v[:rest] for v in spectra], sides[:rest], rows, mask, kinds, fluid, solid, outer)

    def power(values, at):
        return values[rest + 8 * at : rest + 8 * at + 8]

    numbers = []
    for target in (0, 1):

        def beside(values, kind):
            same, cross = power(values, 2 + target), power(values, 4)
            return pick(kind, same, cross) if target == 0 else pick(kind, cross, same)

        own = [beside(values, mask[row]) for values, row in zip(spectra, rows)]
        edge = [beside(values, mask[row]) for values, row in zip(around, edge_rows)]
        column = [edge[0], *own, edge[1]]
        outside = beside(sides, kinds)
        numbers.append(
            [
                second_sweep(power(spectra[i], target), own[i], column[i], column[i + 2], outside, 2 * i, 1.0)
                for i in range(len(rows))
            ]
        )
    for i, row in enumerate(rows):
        base = i * (rest + 8)
        out_ref[base : base + rest, :] = sweeps[i]
        out_ref[base + rest : base + rest + 8, :] = jnp.where(mask[row] == 0, numbers[0][i], numbers[1][i])


def take_kernel(rows, count, cells, *refs):
    half = count // 2
    message_ref, local_ref, take_ref = refs[:3]
    outs = refs[-1 - (half - 1) * len(rows) :]
    lines = message_ref.shape[0] // len(rows)
    short = take_ref.shape[2] // 3 - lines
    for i in range(len(rows)):
        values = message_ref[i * lines : (i + 1) * lines, :]
        if short:
            values = jnp.concatenate([values, jnp.zeros((short, values.shape[1]), jnp.float32)], axis=0)
        values = thirds(values, 0)
        for d in range(half):
            base = (d * len(rows) + i) * cells
            value = local_ref[base : base + cells, :] + jnp.dot(
                take_ref[place(d)], values, preferred_element_type=jnp.float32
            )
            if d == 0:
                outs[0][i * cells : (i + 1) * cells, :] = value
            else:
                outs[1 + (d - 1) * len(rows) + i][...] = value


def rim_kernel(rows, order, count, cells, *refs):
    spectrum_ref, edges_ref, sides_ref, halo_ref, ones_ref, inverse_ref, columns_ref, mask_ref = refs[:8]
    outs = refs[-count:]
    _, modes, width = edges_ref.shape
    edge = 1 - paired_edge() if order == 0 else paired_edge()
    mask, _ = masks(mask_ref, rows, 0, width)
    fluid, solid = one_over(columns_ref, 0, modes)
    sides = jnp.where(edge == 0, sides_ref[:, 0:2], sides_ref[:, 2:4])
    diagonal = pick(jnp.where(edge == 0, mask[rows[0]], mask[rows[1]]), fluid, solid)
    sweep = second_sweep(spectrum_ref[edge], edges_ref[edge], halo_ref[:modes, :], ones_ref[edge], sides, 0, diagonal)
    inverse_rows([sweep], cells, inverse_ref, outs[: count // 2], outs[count // 2 :])
    if order == 1:
        for d in range(1, count // 2):
            outs[d][cells:, :] = refs[8 + d - 1][...]
    for out in outs[count // 2 :]:
        out[cells:, :] = jnp.zeros((out.shape[0] - cells, width), jnp.float32)


def join_kernel(rows, cells, near, *refs):
    own_ref, blocks, out_ref = refs[0], refs[1 : 1 + rows * near], refs[-1]
    size = rows * cells + 8
    out_ref[:size, :] = own_ref[...]
    for d in range(near):
        base = (d + 1) * size
        out_ref[base + rows * cells : base + size, :] = jnp.zeros((8, out_ref.shape[1]), jnp.float32)
        for i in range(rows):
            block = blocks[d * rows + i]
            out_ref[base + i * cells : base + (i + 1) * cells, :] = block[:cells, :]
            at = base + rows * cells + 2 * i
            out_ref[at : at + 2, :] = block[cells : cells + 2, :]


def copy_kernel(number, *refs):
    for ref, out in zip(refs[:number], refs[-number:]):
        out[...] = ref[...]


def unpack_kernel(pieces, devices, row_count, cells, *refs):
    me = lax.axis_index("span")
    blocks, (out_ref, held, done) = refs[: len(pieces)], refs[-3:]
    pitch = held.shape[0] // cells
    own_lines = out_ref.shape[1] // lax.axis_size("span")
    some = cells // SPLIT
    edge_rows = {"near": paired_edge() * (row_count - 1), "far": (1 - paired_edge()) * (row_count - 1)}
    copies = []
    for part in range(SPLIT):
        for block, (d, base, rows, offset, tiles) in zip(blocks, pieces):
            for i, row in enumerate(rows):
                if row in edge_rows:
                    row = edge_rows[row]
                line = base + i * cells + part * some
                for tile in range(tiles):
                    at = part * some * pitch + devices.index(d) * own_lines + (offset + tile) * row_count + row
                    held[pl.ds(at, some, stride=pitch), :] = block[line : line + some, tile * LANES : (tile + 1) * LANES]
        for at, d in enumerate(devices):
            first = pl.multiple_of(jnp.bitwise_xor(me, d) * own_lines, own_lines)
            copies.append(
                pltpu.make_async_copy(
                    held.reshape(cells, pitch, LANES).at[pl.ds(part * some, some), pl.ds(at * own_lines, own_lines)],
                    out_ref.at[pl.ds(part * some, some), pl.ds(first, own_lines)],
                    done.at[part, at],
                )
            )
            copies[-1].start()
    for copy in copies:
        copy.wait()


def call(kernel, outs, *args, cost=LONG, earlier=()):
    shapes = [jax.ShapeDtypeStruct(shape, jnp.float32) for shape in outs]
    return pl.pallas_call(
        kernel,
        out_shape=shapes,
        in_specs=[VMEM] * len(args) + [ANY] * len(earlier),
        out_specs=[VMEM] * len(outs),
        compiler_params=PARAMS,
        cost_estimate=cost,
    )(*args, *earlier)


def swap(block, d):
    return lax.ppermute(block, "span", [(i, i ^ d) for i in range(lax.axis_size("span"))])


def local(pressure_source, solid_mask):
    count = lax.axis_size("span")
    half = count // 2
    plane_count = lax.axis_size("plane")
    cells, row_count, columns = pressure_source.shape
    width = columns // count
    tiles = width // LANES
    inner = tuple(range(1, row_count - 1))
    edges = (0, row_count - 1)
    near, far = range(1, half), range(half, count)
    *arrays, modes, rest = tables(cells * count, cells)
    forward, inverse, send, take, diagonals = map(jnp.asarray, arrays)

    lines = columns // LANES * row_count
    source = pressure_source.reshape(cells, row_count, columns // LANES, LANES).transpose(0, 2, 1, 3)
    source = source.reshape(cells, lines, LANES)
    scratch = [pltpu.VMEM((cells * (lines + 8), LANES), jnp.float32), pltpu.SemaphoreType.DMA((SPLIT,))]

    def pack(source, wanted, *earlier):
        jobs = [(at, 0, d, rows, 0, tiles) for at, (d, rows) in enumerate(wanted)]
        shapes = [(len(rows) * cells + 8, width) for _, rows in wanted]
        return pl.pallas_call(
            functools.partial(pack_kernel, jobs, row_count, cells, len(earlier)),
            out_shape=[jax.ShapeDtypeStruct(shape, jnp.float32) for shape in shapes],
            in_specs=[ANY] * (1 + len(earlier)),
            out_specs=[VMEM] * len(shapes),
            scratch_shapes=scratch,
            compiler_params=PARAMS,
            cost_estimate=LONG,
        )(source, *earlier)

    packed = pack(pltpu.with_memory_space_constraint(source, pltpu.HBM), [(d, edges) for d in range(1, count)])
    edge_blocks = [swap(block, d) for d, block in enumerate(packed, 1)]
    wanted = [(d, inner) for d in range(half + 1)] + [(0, edges)] + [(d, edges) for d in far]
    wanted += [(half + d, (row,)) for d in near for row in inner]
    packed = pack(source, wanted, packed[half - 1])
    edge_blocks = [packed[half + 1], *edge_blocks]
    relayed = packed[2 * half + 2 :]
    relayed = [swap(relayed[(d - 1) * len(inner) + i], d) for d in near for i in range(len(inner))]
    size = len(inner) * cells + 8
    (message,) = call(
        functools.partial(join_kernel, len(inner), cells, half - 1),
        [(half * size, width)],
        packed[half], *relayed, cost=SHORT, earlier=(edge_blocks[half],),
    )
    arrived = swap(message, half)

    spectrum, edge_ones, paired, other, sides = call(
        functools.partial(edge_kernel, edges, count, cells),
        [(2, modes, width), (2, modes, width), (modes + 16, width), (modes, width), (modes, 16)],
        *edge_blocks, forward, diagonals, solid_mask,
    )
    later = [packed[d] for d in near] + [packed[half + 2 + d] for d in near]
    if later:
        later = call(
            functools.partial(copy_kernel, len(later)), [block.shape for block in later], *later,
            cost=SHORT, earlier=(sides,),
        )
    inner_blocks = [packed[0]] + [swap(later[d - 1], d) for d in near]
    chip_edges = [packed[half + 2]] + [swap(later[half + d - 2], d) for d in near]

    length = len(inner) * cells
    (own,) = call(
        functools.partial(local_kernel, inner, edges, count, cells),
        [(half * length, width)],
        message, *chip_edges, forward, inverse, diagonals, solid_mask, cost=SHORT,
    )

    (sent,) = call(
        functools.partial(send_kernel, inner, edges, rest, count, cells),
        [(len(inner) * (rest + 8), width)],
        *inner_blocks, *edge_blocks[:half], send, diagonals, solid_mask, cost=SHORT, earlier=(own,),
    )
    taken = swap(sent, half)

    pairs = [[(i, i ^ 1) for i in range(plane_count)], [(i, ((i + 1) ^ 1) - 1) for i in range(plane_count)]]
    pairs = [[(i, j) for i, j in pair if 0 <= j < plane_count] for pair in pairs]
    halos = [lax.ppermute(row, "plane", pair) for row, pair in zip((paired, other), pairs)]
    *made, ones = call(
        functools.partial(inner_kernel, inner, count, cells),
        [(length, width)] * half + [(2, modes, width)],
        *inner_blocks, arrived, forward, inverse, diagonals, solid_mask, edge_ones, cost=SHORT, earlier=(own,),
    )
    pieces = [(made[0], 0, 0, inner, 0, tiles)]
    made_got = [swap(made[d], d) for d in near]
    pieces += [(block, d, 0, inner, 0, tiles) for d, block in zip(near, made_got)]
    rim_got, near_rim, earlier = [], [], []
    for order, name in enumerate(("far", "near")):
        outs = call(
            functools.partial(rim_kernel, edges, order, count, cells),
            [(cells, width)] + [((order + 1) * cells, width)] * (half - 1) + [(cells + 8, width)] * half,
            spectrum, edge_ones, sides, halos[1 - order], ones, inverse, diagonals, solid_mask, *near_rim,
            cost=LONG if order else SHORT, earlier=earlier,
        )
        near_rim = outs[1:half]
        pieces.append((outs[0], 0, 0, (name,), 0, tiles))
        rim_got.append([swap(outs[d], d) for d in far])
        pieces += [(block, d, 0, (name,), 0, tiles) for d, block in zip(far, rim_got[order])]
        earlier = [outs[-1]]
    pieces += [(swap(near_rim[d - 1], d), d, 0, ("near", "far"), 0, tiles) for d in near]
    rebuilt = call(
        functools.partial(take_kernel, inner, count, cells),
        [(length, width)] + [(cells, width)] * ((half - 1) * len(inner)),
        taken, own, take,
        cost=SHORT, earlier=[outs[-1], *rim_got[0], *made_got],
    )
    pieces.append((rebuilt[0], half, 0, inner, 0, tiles))
    for d in near:
        for i, row in enumerate(inner):
            pieces.append((swap(rebuilt[1 + (d - 1) * len(inner) + i], d), half + d, 0, (row,), 0, tiles))

    result = None
    own_lines = tiles * row_count
    for devices in (range(count - 1), [count - 1]) if own_lines % 8 == 0 else (range(count),):
        chosen = [piece for piece in pieces if piece[1] in devices]
        previous = () if result is None else (result,)
        result = pl.pallas_call(
            functools.partial(unpack_kernel, [piece[1:] for piece in chosen], list(devices), row_count, cells),
            out_shape=jax.ShapeDtypeStruct((cells, lines, LANES), jnp.float32),
            in_specs=[VMEM] * len(chosen) + [ANY] * len(previous),
            out_specs=ANY,
            scratch_shapes=[
                pltpu.VMEM((cells * (len(devices) * own_lines + 8), LANES), jnp.float32),
                pltpu.SemaphoreType.DMA((SPLIT, len(devices))),
            ],
            input_output_aliases={len(chosen): 0} if previous else {},
            compiler_params=PARAMS,
            cost_estimate=SHORT if previous else LONG,
        )(*[piece[0] for piece in chosen], *previous)
    result = result.reshape(cells, columns // LANES, row_count, LANES).transpose(0, 2, 1, 3)
    return result.reshape(cells, row_count, columns)


def solution(mesh):
    placed = (P("span", "plane", None), P("plane", None))
    return jax.shard_map(
        local, mesh=mesh, in_specs=placed, out_specs=P("span", "plane", None), check_vma=False
    )
```

```python
import functools

import jax
import jax.numpy as jnp
import ml_dtypes
import numpy as np
from jax import lax
from jax.experimental import pallas as pl
from jax.experimental.pallas import tpu as pltpu
from jax.sharding import PartitionSpec as P

PENALTY = 12.0
LANES = 128
VMEM = pl.BlockSpec(memory_space=pltpu.VMEM)
ANY = pl.BlockSpec(memory_space=pl.ANY)
PARAMS = pltpu.CompilerParams(vmem_limit_bytes=24 * 1024 * 1024)
LONG = pl.CostEstimate(flops=0, bytes_accessed=200_000_000, transcendentals=0)
SHORT = pl.CostEstimate(flops=0, bytes_accessed=1024, transcendentals=0)
SPLIT = 4


def split(values):
    high = values.astype(ml_dtypes.bfloat16)
    low = (values - high.astype(np.float64)).astype(ml_dtypes.bfloat16)
    return np.concatenate([high, low, high], axis=-1)


def table_modes(length, wanted):
    modes = [(k, False) for k in range(length // 2 + 1) if wanted(k)]
    return modes + [(k, True) for k in range(1, length // 2) if wanted(k)]


def wave(length, points, k, sine):
    angles = (points * k % length) * (2.0 * np.pi / length)
    return np.sin(angles) if sine else np.cos(angles)


def fill(length, modes, forward, inverse, fluid, solid):
    points = np.arange(length // 2)
    for at, (k, sine) in enumerate(modes):
        forward[at] = wave(length, points, k, sine)
        inverse[:, at] = forward[at] * (1.0 if k in (0, length // 2) else 2.0) / length
        eigen = 2.0 - 2.0 * np.cos(2.0 * np.pi * k / length)
        fluid[at] = 1.0 / (4.0 + eigen)
        solid[at] = 1.0 / (4.0 + eigen + PENALTY)


def up_to(number, step):
    return -(-number // step) * step


def tables(length, cells):
    half = length // 2
    blocks = half // cells
    kept = [table_modes(length, lambda k: 3 * k <= length and k % 2 == parity) for parity in (0, 1)]
    padded = up_to(max(len(modes) for modes in kept), 16)
    left = table_modes(length, lambda k: 3 * k > length)
    rest = up_to(len(left), 16)
    columns = np.zeros((8, up_to(max(2 * padded, rest), LANES)))
    forward, inverse = np.zeros((2, padded, half)), np.zeros((2, half, padded))
    for parity, modes in enumerate(kept):
        part = slice(parity * padded, (parity + 1) * padded)
        fill(length, modes, forward[parity], inverse[parity], columns[0, part], columns[1, part])
    powers = 8
    send, take = np.zeros((rest + 6 * powers, half)), np.zeros((half, up_to(rest + powers, 16)))
    fill(length, left, send[:rest], take[:, :rest], columns[2, :rest], columns[3, :rest])
    take[:, : len(left)] *= [-1.0 if k % 2 == 0 else 1.0 for k, _ in left]
    ends = (np.arange(half), half - 1.0 - np.arange(half))
    for side in (0, 1):
        x, y = ends[side], ends[1 - side] + 1.0
        first = rest + 4 * side
        for solid, diagonal in enumerate((6.0, 6.0 + PENALTY)):
            rho = diagonal / 2.0 - np.sqrt(diagonal * diagonal / 4.0 - 1.0)
            at = first + 2 * solid
            take[:, at], take[:, at + 1] = rho**x, x * rho**x
            single = rho / (1.0 - rho**2) * rho**y
            double = rho**2 / (1.0 - rho**2) ** 2
            send[at + powers * solid] = single
            send[at + powers * (2 + solid)] = (double * (1.0 + rho**2) / (1.0 - rho**2) + double * y) * rho**y
            send[at + 1 + powers * (2 + solid)] = double * rho**y
            send[at + powers * 4] = single / PENALTY * (1.0 if solid == 0 else -1.0)
    forward = split(forward.reshape(2, padded, blocks, cells).transpose(0, 2, 1, 3))
    inverse = split(inverse.reshape(2, blocks, cells, padded))
    send = split(send.reshape(-1, blocks, cells).transpose(1, 0, 2))
    take = split(take.reshape(blocks, cells, -1))
    return forward, inverse, send, take, columns.astype(np.float32), 2 * padded, rest


def thirds(values, axis):
    high = values.astype(jnp.bfloat16)
    low = (values - high.astype(jnp.float32)).astype(jnp.bfloat16)
    return jnp.concatenate([high, high, low], axis=axis)


def pack_kernel(jobs, row_count, cells, earlier, x_ref, *refs):
    outs, (held, arrived) = refs[earlier:-2], refs[-2:]
    me = lax.axis_index("span")
    lines = x_ref.shape[1]
    all_tiles = lines // row_count
    own_tiles = all_tiles // lax.axis_size("span")
    pitch = held.shape[0] // cells
    some = cells // SPLIT
    copies = [
        pltpu.make_async_copy(
            x_ref.at[pl.ds(part * some, some)],
            held.reshape(cells, pitch, LANES).at[pl.ds(part * some, some), pl.ds(0, lines)],
            arrived.at[part],
        )
        for part in range(SPLIT)
    ]
    for copy in copies:
        copy.start()
    lane = lax.broadcasted_iota(jnp.int32, (some, LANES), 1)
    sides = []
    for part, copy in enumerate(copies):
        copy.wait()
        beside = jnp.zeros((some, LANES), jnp.float32)

        def line(tile, row):
            return held[pl.ds(part * some * pitch + tile * row_count + row, some, stride=pitch), :]

        for job, (out, base, d, rows, offset, tiles, more) in enumerate(jobs):
            first = jnp.bitwise_xor(me, d) * own_tiles + offset
            for i, row in enumerate(rows):
                at = base + i * cells + part * some
                for tile in range(tiles):
                    outs[out][at : at + some, tile * LANES : (tile + 1) * LANES] = line(first + tile, row)
            before = jnp.maximum(first - 1, 0)
            after = jnp.minimum(first + tiles, all_tiles - 1)
            for i, row in enumerate(rows + more if more else ()):
                for side, (tile, source) in enumerate(((before, LANES - 1), (after, 0))):
                    at = job * 8 + i * 2 + side
                    beside = jnp.where(lane == at, pltpu.roll(line(tile, row), (at - source) % LANES, 1), beside)
        sides.append(beside)
    if cells < LANES:
        sides.append(jnp.zeros((LANES - cells, LANES), jnp.float32))
    turned = jnp.concatenate(sides, axis=0).T
    for job, (out, base, _, rows, _, tiles, more) in enumerate(jobs):
        if not more:
            continue
        at = base + len(rows) * cells
        outs[out][at : at + 8, :LANES] = turned[job * 8 : (job + 1) * 8]
        if tiles > 1:
            outs[out][at : at + 8, LANES:] = jnp.zeros((8, (tiles - 1) * LANES), jnp.float32)


def place(d):
    half = lax.axis_size("span") // 2
    return jnp.bitwise_and(jnp.bitwise_xor(lax.axis_index("span"), d), half - 1)


def row_product(table, value):
    return jnp.dot(table, thirds(value, 0), preferred_element_type=jnp.float32)


def side_product(table, value):
    value = thirds(jnp.concatenate([value, jnp.zeros_like(value)], axis=0), 1)
    return lax.dot_general(table, value, (((1,), (1,)), ((), ())), preferred_element_type=jnp.float32)


def transform(rows, cells, near, far, forward_ref, beside=False):
    def spectrum(lines, lanes, product):
        halves = []
        for parity in (0, 1):
            total = 0.0
            for d, block in enumerate(near):
                value = block[lines, lanes]
                if far:
                    other = far[d][lines, lanes]
                    value = value + other if parity == 0 else value - other
                total = total + product(forward_ref[parity, place(d)], value)
            halves.append(total)
        return jnp.concatenate(halves, axis=0)

    if beside:
        return spectrum(slice(rows * cells, rows * cells + 8), slice(0, cells), side_product)
    return [spectrum(slice(i * cells, (i + 1) * cells), slice(None), row_product) for i in range(rows)]


def inverse_rows(sweeps, cells, inverse_ref, near, far=()):
    padded = sweeps[0].shape[0] // 2
    for i, sweep in enumerate(sweeps):
        even = thirds(sweep[:padded], 0)
        odd = thirds(sweep[padded:], 0)
        for d, out in enumerate(near):
            first = jnp.dot(inverse_ref[0, place(d)], even, preferred_element_type=jnp.float32)
            second = jnp.dot(inverse_ref[1, place(d)], odd, preferred_element_type=jnp.float32)
            out[i * cells : (i + 1) * cells, :] = first + second
            if far:
                far[d][i * cells : (i + 1) * cells, :] = first - second


def second_sweep(spectrum, one, above, below, sides, at, inverse_diagonal):
    width = one.shape[1]
    lane = lax.broadcasted_iota(jnp.int32, one.shape, 1)
    left = jnp.where(lane == 0, sides[:, at : at + 1], pltpu.roll(one, 1, 1))
    right = jnp.where(lane == width - 1, sides[:, at + 1 : at + 2], pltpu.roll(one, width - 1, 1))
    return (spectrum + above + below + left + right) * inverse_diagonal


def masks(mask_ref, d, width):
    count = mask_ref.shape[0]
    start = pl.multiple_of(jnp.bitwise_xor(lax.axis_index("span"), d) * width, LANES)
    last = mask_ref.shape[1] - LANES
    before = mask_ref[:, pl.ds(pl.multiple_of(jnp.maximum(start - LANES, 0), LANES), LANES)][:, LANES - 1 :]
    after = mask_ref[:, pl.ds(pl.multiple_of(jnp.minimum(start + width, last), LANES), LANES)][:, :1]
    before = jnp.where(start == 0, 2, before)
    after = jnp.where(start + width == mask_ref.shape[1], 2, after)
    lane = lax.broadcasted_iota(jnp.int32, (1, 16), 1)
    kinds = jnp.full((1, 16), 2, jnp.int32)
    for i, row in enumerate((0, count - 1, *range(1, count - 1))):
        kinds = jnp.where(lane == 2 * i, before[row : row + 1], kinds)
        kinds = jnp.where(lane == 2 * i + 1, after[row : row + 1], kinds)
    return [mask_ref[row : row + 1, pl.ds(start, width)] for row in range(mask_ref.shape[0])], kinds


def pick(kind, fluid, solid):
    return jnp.where(kind == 0, fluid, jnp.where(kind == 1, solid, 0.0))


def one_over(columns_ref, first, modes):
    turned = columns_ref[...].T
    return turned[:modes, first : first + 1], turned[:modes, first + 1 : first + 2]


def paired_edge():
    return lax.rem(lax.axis_index("plane") + 1, 2)


def edge_kernel(rows, count, cells, *refs):
    near, far = refs[: count // 2], refs[count // 2 : count]
    forward_ref, columns_ref, mask_ref = refs[count : count + 3]
    spectrum_ref, ones_ref, paired_ref, other_ref, sides_ref = refs[-5:]
    spectra = transform(len(rows), cells, near, far, forward_ref)
    sides = transform(len(rows), cells, near, far, forward_ref, beside=True)
    modes, width = spectra[0].shape
    mask, kinds = masks(mask_ref, 0, width)
    fluid, solid = one_over(columns_ref, 0, modes)
    ones = [spectrum * pick(mask[row], fluid, solid) for spectrum, row in zip(spectra, rows)]
    for i in (0, 1):
        spectrum_ref[i] = spectra[i]
        ones_ref[i] = ones[i]
    last = paired_edge() == 1
    paired_ref[:modes, :] = jnp.where(last, ones[1], ones[0])
    paired_ref[modes:, :] = jnp.zeros((paired_ref.shape[0] - modes, width), jnp.float32)
    other_ref[...] = jnp.where(last, ones[0], ones[1])
    sides_ref[...] = sides * pick(kinds, fluid, solid)


def inner_sweeps(spectra, sides, rows, mask, fluid, solid, edges):
    diagonals = [pick(mask[row], fluid, solid) for row in rows]
    ones = [spectrum * diagonal for spectrum, diagonal in zip(spectra, diagonals)]
    around = [edges[0], *ones, edges[1]]
    return ones, [
        second_sweep(spectra[i], ones[i], around[i], around[i + 2], sides, 4 + 2 * i, diagonals[i])
        for i in range(len(rows))
    ]


def inner_kernel(rows, count, cells, *refs):
    half = count // 2
    far_ref, forward_ref, inverse_ref, columns_ref, mask_ref, edges_ref, sides_ref = refs[half : half + 7]
    outs, ones_ref = refs[-1 - half : -1], refs[-1]
    size = len(rows) * cells
    far = [far_ref.at[e * size : (e + 1) * size] for e in range(half)]
    spectra = transform(len(rows), cells, refs[:half], far, forward_ref)
    modes, width = spectra[0].shape
    mask, _ = masks(mask_ref, 0, width)
    fluid, solid = one_over(columns_ref, 0, modes)
    ones, sweeps = inner_sweeps(spectra, sides_ref[...], rows, mask, fluid, solid, (edges_ref[0], edges_ref[1]))
    ones_ref[0] = ones[0]
    ones_ref[1] = ones[-1]
    inverse_rows(sweeps, cells, inverse_ref, outs)


def local_kernel(rows, edge_rows, count, cells, *refs):
    half = count // 2
    message_ref, edges = refs[0], refs[1 : 1 + half]
    forward_ref, inverse_ref, columns_ref, mask_ref = refs[1 + half : 5 + half]
    out_ref = refs[-1]
    size = len(rows) * cells
    near = [message_ref.at[d * size : (d + 1) * size] for d in range(half)]
    spectra = transform(len(rows), cells, near, (), forward_ref)
    edge_spectra = transform(len(edge_rows), cells, edges, (), forward_ref)
    sides = transform(len(edge_rows), cells, edges, (), forward_ref, beside=True)
    modes, width = spectra[0].shape
    mask, kinds = masks(mask_ref, half, width)
    fluid, solid = one_over(columns_ref, 0, modes)
    around = [spectrum * pick(mask[row], fluid, solid) for spectrum, row in zip(edge_spectra, edge_rows)]
    sides = sides * pick(kinds, fluid, solid)
    _, sweeps = inner_sweeps(spectra, sides, rows, mask, fluid, solid, around)
    inverse_rows(sweeps, cells, inverse_ref, [out_ref.at[d * size : (d + 1) * size] for d in range(half)])


def send_kernel(rows, edge_rows, rest, count, cells, *refs):
    half = count // 2
    inner, edges = refs[:half], refs[half : 2 * half]
    send_ref, columns_ref, mask_ref = refs[2 * half : 2 * half + 3]
    out_ref = refs[-1]

    def product(blocks, lines, lanes, kind):
        return sum(kind(send_ref[place(d)], block[lines, lanes]) for d, block in enumerate(blocks))

    def whole(blocks, i):
        return product(blocks, slice(i * cells, (i + 1) * cells), slice(None), row_product)

    spectra = [whole(inner, i) for i in range(len(rows))]
    around = [whole(edges, i) for i in range(len(edge_rows))]
    lines = len(edge_rows) * cells
    sides = product(edges, slice(lines, lines + 8), slice(0, cells), side_product)
    mask, kinds = masks(mask_ref, 0, inner[0].shape[1])
    fluid, solid = one_over(columns_ref, 2, rest)
    outer = [values[:rest] * pick(mask[row], fluid, solid) for values, row in zip(around, edge_rows)]
    outside = sides[:rest] * pick(kinds, fluid, solid)
    _, sweeps = inner_sweeps([v[:rest] for v in spectra], outside, rows, mask, fluid, solid, outer)

    def power(values, at):
        return values[rest + 8 * at : rest + 8 * at + 8]

    numbers = []
    for target in (0, 1):

        def beside(values, kind):
            same, cross = power(values, 2 + target), power(values, 4)
            return pick(kind, same, cross) if target == 0 else pick(kind, cross, same)

        own = [beside(values, mask[row]) for values, row in zip(spectra, rows)]
        edge = [beside(values, mask[row]) for values, row in zip(around, edge_rows)]
        column = [edge[0], *own, edge[1]]
        outside = beside(sides, kinds)
        numbers.append(
            [
                second_sweep(power(spectra[i], target), own[i], column[i], column[i + 2], outside, 4 + 2 * i, 1.0)
                for i in range(len(rows))
            ]
        )
    for i, row in enumerate(rows):
        base = i * (rest + 8)
        out_ref[base : base + rest, :] = sweeps[i]
        out_ref[base + rest : base + rest + 8, :] = jnp.where(mask[row] == 0, numbers[0][i], numbers[1][i])


def take_kernel(rows, count, cells, *refs):
    half = count // 2
    message_ref, local_ref, take_ref = refs[:3]
    outs = refs[-1 - (half - 1) * len(rows) :]
    lines = message_ref.shape[0] // len(rows)
    short = take_ref.shape[2] // 3 - lines
    for i in range(len(rows)):
        values = message_ref[i * lines : (i + 1) * lines, :]
        if short:
            values = jnp.concatenate([values, jnp.zeros((short, values.shape[1]), jnp.float32)], axis=0)
        values = thirds(values, 0)
        for d in range(half):
            base = (d * len(rows) + i) * cells
            value = local_ref[base : base + cells, :] + jnp.dot(
                take_ref[place(d)], values, preferred_element_type=jnp.float32
            )
            if d == 0:
                outs[0][i * cells : (i + 1) * cells, :] = value
            else:
                outs[1 + (d - 1) * len(rows) + i][...] = value


def rim_kernel(rows, order, count, cells, *refs):
    spectrum_ref, edges_ref, sides_ref, halo_ref, ones_ref, inverse_ref, columns_ref, mask_ref = refs[:8]
    outs = refs[-count:]
    _, modes, width = edges_ref.shape
    edge = 1 - paired_edge() if order == 0 else paired_edge()
    mask, _ = masks(mask_ref, 0, width)
    fluid, solid = one_over(columns_ref, 0, modes)
    sides = jnp.where(edge == 0, sides_ref[:, 0:2], sides_ref[:, 2:4])
    diagonal = pick(jnp.where(edge == 0, mask[rows[0]], mask[rows[1]]), fluid, solid)
    sweep = second_sweep(spectrum_ref[edge], edges_ref[edge], halo_ref[:modes, :], ones_ref[edge], sides, 0, diagonal)
    inverse_rows([sweep], cells, inverse_ref, outs[: count // 2], outs[count // 2 :])
    if order == 1:
        for d in range(1, count // 2):
            outs[d][cells:, :] = refs[8 + d - 1][...]
    for out in outs[count // 2 :]:
        if out.shape[0] > cells:
            out[cells:, :] = jnp.zeros((out.shape[0] - cells, width), jnp.float32)


def join_kernel(number, *refs):
    at = 0
    for ref in refs[:number]:
        refs[-1][at : at + ref.shape[0], :] = ref[...]
        at += ref.shape[0]


def copy_kernel(number, *refs):
    for ref, out in zip(refs[:number], refs[-number:]):
        out[...] = ref[...]


def unpack_kernel(pieces, devices, row_count, cells, *refs):
    me = lax.axis_index("span")
    blocks, (out_ref, held, done) = refs[: len(pieces)], refs[-3:]
    pitch = held.shape[0] // cells
    lines = out_ref.shape[1]
    own_lines = lines // lax.axis_size("span")
    whole = len(devices) > 1
    some = cells // SPLIT
    edge_rows = {"near": paired_edge() * (row_count - 1), "far": (1 - paired_edge()) * (row_count - 1)}

    def first_line(d):
        return pl.multiple_of(jnp.bitwise_xor(me, d) * own_lines, own_lines)

    copies = []
    for part in range(SPLIT):
        for block, (d, base, rows, offset, tiles) in zip(blocks, pieces):
            for i, row in enumerate(rows):
                if row in edge_rows:
                    row = edge_rows[row]
                line = base + i * cells + part * some
                for tile in range(tiles):
                    at = part * some * pitch + (first_line(d) if whole else 0) + (offset + tile) * row_count + row
                    held[pl.ds(at, some, stride=pitch), :] = block[line : line + some, tile * LANES : (tile + 1) * LANES]
        if whole:
            for d in set(range(lax.axis_size("span"))) - set(devices):
                for line in range(own_lines):
                    at = part * some * pitch + first_line(d) + line
                    held[pl.ds(at, some, stride=pitch), :] = jnp.zeros((some, LANES), jnp.float32)
        wanted = pl.ds(0, lines) if whole else pl.ds(first_line(devices[0]), own_lines)
        copies.append(
            pltpu.make_async_copy(
                held.reshape(cells, pitch, LANES).at[pl.ds(part * some, some), pl.ds(0, lines if whole else own_lines)],
                out_ref.at[pl.ds(part * some, some), wanted],
                done.at[part],
            )
        )
        copies[-1].start()
    for copy in copies:
        copy.wait()


def call(kernel, outs, *args, cost=LONG, earlier=()):
    shapes = [jax.ShapeDtypeStruct(shape, jnp.float32) for shape in outs]
    return pl.pallas_call(
        kernel,
        out_shape=shapes,
        in_specs=[VMEM] * len(args) + [ANY] * len(earlier),
        out_specs=[VMEM] * len(outs),
        compiler_params=PARAMS,
        cost_estimate=cost,
    )(*args, *earlier)


def swap(block, d):
    return lax.ppermute(block, "span", [(i, i ^ d) for i in range(lax.axis_size("span"))])


def local(pressure_source, solid_mask):
    count = lax.axis_size("span")
    half = count // 2
    plane_count = lax.axis_size("plane")
    cells, row_count, columns = pressure_source.shape
    width = columns // count
    tiles = width // LANES
    inner = tuple(range(1, row_count - 1))
    edges = (0, row_count - 1)
    near, far = range(1, half), range(half, count)
    *arrays, modes, rest = tables(cells * count, cells)
    forward, inverse, send, take, diagonals = map(jnp.asarray, arrays)

    lines = columns // LANES * row_count
    source = pressure_source.reshape(cells, row_count, columns // LANES, LANES).transpose(0, 2, 1, 3)
    source = source.reshape(cells, lines, LANES)
    scratch = [pltpu.VMEM((cells * (lines + 8), LANES), jnp.float32), pltpu.SemaphoreType.DMA((SPLIT,))]

    def pack(source, wanted, *earlier):
        jobs = [(at, 0, d, rows, 0, tiles, inner if rows == edges else ()) for at, (d, rows) in enumerate(wanted)]
        shapes = [(len(rows) * cells + (8 if rows == edges else 0), width) for _, rows in wanted]
        return pl.pallas_call(
            functools.partial(pack_kernel, jobs, row_count, cells, len(earlier)),
            out_shape=[jax.ShapeDtypeStruct(shape, jnp.float32) for shape in shapes],
            in_specs=[ANY] * (1 + len(earlier)),
            out_specs=[VMEM] * len(shapes),
            scratch_shapes=scratch,
            compiler_params=PARAMS,
            cost_estimate=LONG,
        )(source, *earlier)

    packed = pack(pltpu.with_memory_space_constraint(source, pltpu.HBM), [(d, edges) for d in range(1, count)])
    edge_blocks = [swap(block, d) for d, block in enumerate(packed, 1)]
    wanted = [(d, inner) for d in range(half + 1)] + [(0, edges)] + [(d, edges) for d in far]
    wanted += [(half + d, (row,)) for d in near for row in inner]
    packed = pack(source, wanted, packed[half - 1])
    edge_blocks = [packed[half + 1], *edge_blocks]
    relayed = packed[2 * half + 2 :]
    relayed = [swap(relayed[(d - 1) * len(inner) + i], d) for d in near for i in range(len(inner))]
    (message,) = call(
        functools.partial(join_kernel, 1 + len(relayed)),
        [(half * len(inner) * cells, width)],
        packed[half], *relayed, cost=SHORT, earlier=(edge_blocks[half],),
    )
    arrived = swap(message, half)

    spectrum, edge_ones, paired, other, sides = call(
        functools.partial(edge_kernel, edges, count, cells),
        [(2, modes, width), (2, modes, width), (modes + 16, width), (modes, width), (modes, 16)],
        *edge_blocks, forward, diagonals, solid_mask,
    )
    later = [packed[d] for d in near] + [packed[half + 2 + d] for d in near]
    if later:
        later = call(
            functools.partial(copy_kernel, len(later)), [block.shape for block in later], *later,
            cost=SHORT, earlier=(sides,),
        )
    inner_blocks = [packed[0]] + [swap(later[d - 1], d) for d in near]
    chip_edges = [packed[half + 2]] + [swap(later[half + d - 2], d) for d in near]

    length = len(inner) * cells
    (own,) = call(
        functools.partial(local_kernel, inner, edges, count, cells),
        [(half * length, width)],
        message, *chip_edges, forward, inverse, diagonals, solid_mask, cost=SHORT,
    )

    (sent,) = call(
        functools.partial(send_kernel, inner, edges, rest, count, cells),
        [(len(inner) * (rest + 8), width)],
        *inner_blocks, *edge_blocks[:half], send, diagonals, solid_mask, cost=SHORT, earlier=(own,),
    )
    taken = swap(sent, half)

    pairs = [[(i, i ^ 1) for i in range(plane_count)], [(i, ((i + 1) ^ 1) - 1) for i in range(plane_count)]]
    pairs = [[(i, j) for i, j in pair if 0 <= j < plane_count] for pair in pairs]
    halos = [lax.ppermute(row, "plane", pair) for row, pair in zip((paired, other), pairs)]
    *made, ones = call(
        functools.partial(inner_kernel, inner, count, cells),
        [(length, width)] * half + [(2, modes, width)],
        *inner_blocks, arrived, forward, inverse, diagonals, solid_mask, edge_ones, sides,
        cost=SHORT, earlier=(own,),
    )
    pieces = [(made[0], 0, 0, inner, 0, tiles)]
    made_got = [swap(made[d], d) for d in near]
    pieces += [(block, d, 0, inner, 0, tiles) for d, block in zip(near, made_got)]
    rim_got, near_rim, earlier = [], [], []
    for order, name in enumerate(("far", "near")):
        outs = call(
            functools.partial(rim_kernel, edges, order, count, cells),
            [(cells, width)] + [((order + 1) * cells, width)] * (half - 1) + [(cells + 8 * (1 - order), width)] * half,
            spectrum, edge_ones, sides, halos[1 - order], ones, inverse, diagonals, solid_mask, *near_rim,
            cost=LONG if order else SHORT, earlier=earlier,
        )
        near_rim = outs[1:half]
        pieces.append((outs[0], 0, 0, (name,), 0, tiles))
        rim_got.append([swap(outs[d], d) for d in far])
        pieces += [(block, d, 0, (name,), 0, tiles) for d, block in zip(far, rim_got[order])]
        earlier = [outs[-1]]
    pieces += [(swap(near_rim[d - 1], d), d, 0, ("near", "far"), 0, tiles) for d in near]
    rebuilt = call(
        functools.partial(take_kernel, inner, count, cells),
        [(length, width)] + [(cells, width)] * ((half - 1) * len(inner)),
        taken, own, take,
        cost=SHORT, earlier=[outs[-1], *rim_got[0], *made_got],
    )
    pieces.append((rebuilt[0], half, 0, inner, 0, tiles))
    for d in near:
        for i, row in enumerate(inner):
            pieces.append((swap(rebuilt[1 + (d - 1) * len(inner) + i], d), half + d, 0, (row,), 0, tiles))

    result = None
    own_lines = tiles * row_count
    for devices in (range(count - 1), [count - 1]) if own_lines % 8 == 0 else (range(count),):
        chosen = [piece for piece in pieces if piece[1] in devices]
        previous = () if result is None else (result,)
        result = pl.pallas_call(
            functools.partial(unpack_kernel, [piece[1:] for piece in chosen], list(devices), row_count, cells),
            out_shape=jax.ShapeDtypeStruct((cells, lines, LANES), jnp.float32),
            in_specs=[VMEM] * len(chosen) + [ANY] * len(previous),
            out_specs=ANY,
            scratch_shapes=[
                pltpu.VMEM((cells * ((lines if len(devices) > 1 else own_lines) + 8), LANES), jnp.float32),
                pltpu.SemaphoreType.DMA((SPLIT,)),
            ],
            input_output_aliases={len(chosen): 0} if previous else {},
            compiler_params=PARAMS,
            cost_estimate=SHORT if previous else LONG,
        )(*[piece[0] for piece in chosen], *previous)
    result = result.reshape(cells, columns // LANES, row_count, LANES).transpose(0, 2, 1, 3)
    return result.reshape(cells, row_count, columns)


def solution(mesh):
    placed = (P("span", "plane", None), P("plane", None))
    return jax.shard_map(
        local, mesh=mesh, in_specs=placed, out_specs=P("span", "plane", None), check_vma=False
    )
```

```python
import functools

import jax
import jax.numpy as jnp
import ml_dtypes
import numpy as np
from jax import lax
from jax.experimental import pallas as pl
from jax.experimental.pallas import tpu as pltpu
from jax.sharding import PartitionSpec as P

PENALTY = 12.0
LANES = 128
VMEM = pl.BlockSpec(memory_space=pltpu.VMEM)
ANY = pl.BlockSpec(memory_space=pl.ANY)
PARAMS = pltpu.CompilerParams(vmem_limit_bytes=24 * 1024 * 1024)
LONG = pl.CostEstimate(flops=0, bytes_accessed=200_000_000, transcendentals=0)
SHORT = pl.CostEstimate(flops=0, bytes_accessed=1024, transcendentals=0)
SPLIT = 4


def split(values):
    high = values.astype(ml_dtypes.bfloat16)
    low = (values - high.astype(np.float64)).astype(ml_dtypes.bfloat16)
    return np.concatenate([high, low, high], axis=-1)


def table_modes(length, wanted):
    modes = [(k, False) for k in range(length // 2 + 1) if wanted(k)]
    return modes + [(k, True) for k in range(1, length // 2) if wanted(k)]


def wave(length, points, k, sine):
    angles = (points * k % length) * (2.0 * np.pi / length)
    return np.sin(angles) if sine else np.cos(angles)


def fill(length, modes, forward, inverse, fluid, solid):
    points = np.arange(length // 2)
    for at, (k, sine) in enumerate(modes):
        forward[at] = wave(length, points, k, sine)
        inverse[:, at] = forward[at] * (1.0 if k in (0, length // 2) else 2.0) / length
        eigen = 2.0 - 2.0 * np.cos(2.0 * np.pi * k / length)
        fluid[at] = 1.0 / (4.0 + eigen)
        solid[at] = 1.0 / (4.0 + eigen + PENALTY)


def up_to(number, step):
    return -(-number // step) * step


def tables(length, cells):
    half = length // 2
    blocks = half // cells
    kept = [table_modes(length, lambda k: 3 * k <= length and k % 2 == parity) for parity in (0, 1)]
    padded = up_to(max(len(modes) for modes in kept), 16)
    left = table_modes(length, lambda k: 3 * k > length)
    rest = up_to(len(left), 16)
    columns = np.zeros((8, up_to(max(2 * padded, rest), LANES)))
    forward, inverse = np.zeros((2, padded, half)), np.zeros((2, half, padded))
    for parity, modes in enumerate(kept):
        part = slice(parity * padded, (parity + 1) * padded)
        fill(length, modes, forward[parity], inverse[parity], columns[0, part], columns[1, part])
    powers = 8
    send, take = np.zeros((rest + 6 * powers, half)), np.zeros((half, up_to(rest + powers, 16)))
    fill(length, left, send[:rest], take[:, :rest], columns[2, :rest], columns[3, :rest])
    take[:, : len(left)] *= [-1.0 if k % 2 == 0 else 1.0 for k, _ in left]
    ends = (np.arange(half), half - 1.0 - np.arange(half))
    for side in (0, 1):
        x, y = ends[side], ends[1 - side] + 1.0
        first = rest + 4 * side
        for solid, diagonal in enumerate((6.0, 6.0 + PENALTY)):
            rho = diagonal / 2.0 - np.sqrt(diagonal * diagonal / 4.0 - 1.0)
            at = first + 2 * solid
            take[:, at], take[:, at + 1] = rho**x, x * rho**x
            single = rho / (1.0 - rho**2) * rho**y
            double = rho**2 / (1.0 - rho**2) ** 2
            send[at + powers * solid] = single
            send[at + powers * (2 + solid)] = (double * (1.0 + rho**2) / (1.0 - rho**2) + double * y) * rho**y
            send[at + 1 + powers * (2 + solid)] = double * rho**y
            send[at + powers * 4] = single / PENALTY * (1.0 if solid == 0 else -1.0)
    forward = split(forward.reshape(2, padded, blocks, cells).transpose(0, 2, 1, 3))
    inverse = split(inverse.reshape(2, blocks, cells, padded))
    send = split(send.reshape(-1, blocks, cells).transpose(1, 0, 2))
    take = split(take.reshape(blocks, cells, -1))
    return forward, inverse, send, take, columns.astype(np.float32), 2 * padded, rest


def thirds(values, axis):
    high = values.astype(jnp.bfloat16)
    low = (values - high.astype(jnp.float32)).astype(jnp.bfloat16)
    return jnp.concatenate([high, high, low], axis=axis)


def pack_kernel(jobs, row_count, cells, earlier, x_ref, *refs):
    outs, (held, arrived) = refs[earlier:-2], refs[-2:]
    me = lax.axis_index("span")
    lines = x_ref.shape[1]
    all_tiles = lines // row_count
    own_tiles = all_tiles // lax.axis_size("span")
    pitch = held.shape[0] // cells
    some = cells // SPLIT
    copies = [
        pltpu.make_async_copy(
            x_ref.at[pl.ds(part * some, some)],
            held.reshape(cells, pitch, LANES).at[pl.ds(part * some, some), pl.ds(0, lines)],
            arrived.at[part],
        )
        for part in range(SPLIT)
    ]
    for copy in copies:
        copy.start()
    lane = lax.broadcasted_iota(jnp.int32, (some, LANES), 1)
    sides = []
    for part, copy in enumerate(copies):
        copy.wait()
        beside = jnp.zeros((some, LANES), jnp.float32)

        def line(tile, row):
            return held[pl.ds(part * some * pitch + tile * row_count + row, some, stride=pitch), :]

        for job, (out, base, d, rows, offset, tiles, more) in enumerate(jobs):
            first = jnp.bitwise_xor(me, d) * own_tiles + offset
            for i, row in enumerate(rows):
                at = base + i * cells + part * some
                for tile in range(tiles):
                    outs[out][at : at + some, tile * LANES : (tile + 1) * LANES] = line(first + tile, row)
            before = jnp.maximum(first - 1, 0)
            after = jnp.minimum(first + tiles, all_tiles - 1)
            for i, row in enumerate(rows + more if more else ()):
                for side, (tile, source) in enumerate(((before, LANES - 1), (after, 0))):
                    at = job * 8 + i * 2 + side
                    beside = jnp.where(lane == at, pltpu.roll(line(tile, row), (at - source) % LANES, 1), beside)
        sides.append(beside)
    if cells < LANES:
        sides.append(jnp.zeros((LANES - cells, LANES), jnp.float32))
    turned = jnp.concatenate(sides, axis=0).T
    for job, (out, base, _, rows, _, tiles, more) in enumerate(jobs):
        if not more:
            continue
        at = base + len(rows) * cells
        outs[out][at : at + 8, :LANES] = turned[job * 8 : (job + 1) * 8]
        if tiles > 1:
            outs[out][at : at + 8, LANES:] = jnp.zeros((8, (tiles - 1) * LANES), jnp.float32)


def place(d):
    half = lax.axis_size("span") // 2
    return jnp.bitwise_and(jnp.bitwise_xor(lax.axis_index("span"), d), half - 1)


def row_product(table, value):
    return jnp.dot(table, thirds(value, 0), preferred_element_type=jnp.float32)


def side_product(table, value):
    value = thirds(jnp.concatenate([value, jnp.zeros_like(value)], axis=0), 1)
    return lax.dot_general(table, value, (((1,), (1,)), ((), ())), preferred_element_type=jnp.float32)


def transform(rows, cells, near, far, forward_ref, beside=False):
    def spectrum(lines, lanes, product):
        halves = []
        for parity in (0, 1):
            total = 0.0
            for d, block in enumerate(near):
                value = block[lines, lanes]
                if far:
                    other = far[d][lines, lanes]
                    value = value + other if parity == 0 else value - other
                total = total + product(forward_ref[parity, place(d)], value)
            halves.append(total)
        return jnp.concatenate(halves, axis=0)

    if beside:
        return spectrum(slice(rows * cells, rows * cells + 8), slice(0, cells), side_product)
    return [spectrum(slice(i * cells, (i + 1) * cells), slice(None), row_product) for i in range(rows)]


def inverse_rows(sweeps, cells, inverse_ref, near, far=()):
    padded = sweeps[0].shape[0] // 2
    for i, sweep in enumerate(sweeps):
        even = thirds(sweep[:padded], 0)
        odd = thirds(sweep[padded:], 0)
        for d, out in enumerate(near):
            first = jnp.dot(inverse_ref[0, place(d)], even, preferred_element_type=jnp.float32)
            second = jnp.dot(inverse_ref[1, place(d)], odd, preferred_element_type=jnp.float32)
            out[i * cells : (i + 1) * cells, :] = first + second
            if far:
                far[d][i * cells : (i + 1) * cells, :] = first - second


def second_sweep(spectrum, one, above, below, sides, at, inverse_diagonal):
    width = one.shape[1]
    lane = lax.broadcasted_iota(jnp.int32, one.shape, 1)
    left = jnp.where(lane == 0, sides[:, at : at + 1], pltpu.roll(one, 1, 1))
    right = jnp.where(lane == width - 1, sides[:, at + 1 : at + 2], pltpu.roll(one, width - 1, 1))
    return (spectrum + above + below + left + right) * inverse_diagonal


def masks(mask_ref, d, width):
    count = mask_ref.shape[0]
    start = pl.multiple_of(jnp.bitwise_xor(lax.axis_index("span"), d) * width, LANES)
    last = mask_ref.shape[1] - LANES
    before = mask_ref[:, pl.ds(pl.multiple_of(jnp.maximum(start - LANES, 0), LANES), LANES)][:, LANES - 1 :]
    after = mask_ref[:, pl.ds(pl.multiple_of(jnp.minimum(start + width, last), LANES), LANES)][:, :1]
    before = jnp.where(start == 0, 2, before)
    after = jnp.where(start + width == mask_ref.shape[1], 2, after)
    lane = lax.broadcasted_iota(jnp.int32, (1, 16), 1)
    kinds = jnp.full((1, 16), 2, jnp.int32)
    for i, row in enumerate((0, count - 1, *range(1, count - 1))):
        kinds = jnp.where(lane == 2 * i, before[row : row + 1], kinds)
        kinds = jnp.where(lane == 2 * i + 1, after[row : row + 1], kinds)
    return [mask_ref[row : row + 1, pl.ds(start, width)] for row in range(mask_ref.shape[0])], kinds


def pick(kind, fluid, solid):
    return jnp.where(kind == 0, fluid, jnp.where(kind == 1, solid, 0.0))


def one_over(columns_ref, first, modes):
    turned = columns_ref[...].T
    return turned[:modes, first : first + 1], turned[:modes, first + 1 : first + 2]


def paired_edge():
    return lax.rem(lax.axis_index("plane") + 1, 2)


def edge_kernel(rows, count, cells, *refs):
    near, far = refs[: count // 2], refs[count // 2 : count]
    forward_ref, columns_ref, mask_ref = refs[count : count + 3]
    spectrum_ref, ones_ref, paired_ref, other_ref, sides_ref = refs[-5:]
    spectra = transform(len(rows), cells, near, far, forward_ref)
    sides = transform(len(rows), cells, near, far, forward_ref, beside=True)
    modes, width = spectra[0].shape
    mask, kinds = masks(mask_ref, 0, width)
    fluid, solid = one_over(columns_ref, 0, modes)
    ones = [spectrum * pick(mask[row], fluid, solid) for spectrum, row in zip(spectra, rows)]
    for i in (0, 1):
        spectrum_ref[i] = spectra[i]
        ones_ref[i] = ones[i]
    last = paired_edge() == 1
    paired_ref[:modes, :] = jnp.where(last, ones[1], ones[0])
    paired_ref[modes:, :] = jnp.zeros((paired_ref.shape[0] - modes, width), jnp.float32)
    other_ref[...] = jnp.where(last, ones[0], ones[1])
    sides_ref[...] = sides * pick(kinds, fluid, solid)


def inner_sweeps(spectra, sides, rows, mask, fluid, solid, edges):
    diagonals = [pick(mask[row], fluid, solid) for row in rows]
    ones = [spectrum * diagonal for spectrum, diagonal in zip(spectra, diagonals)]
    around = [edges[0], *ones, edges[1]]
    return ones, [
        second_sweep(spectra[i], ones[i], around[i], around[i + 2], sides, 4 + 2 * i, diagonals[i])
        for i in range(len(rows))
    ]


def inner_kernel(rows, count, cells, *refs):
    half = count // 2
    far_ref, forward_ref, inverse_ref, columns_ref, mask_ref, edges_ref, sides_ref = refs[half : half + 7]
    outs, ones_ref = refs[-1 - half : -1], refs[-1]
    size = len(rows) * cells
    far = [far_ref.at[e * size : (e + 1) * size] for e in range(half)]
    spectra = transform(len(rows), cells, refs[:half], far, forward_ref)
    modes, width = spectra[0].shape
    mask, _ = masks(mask_ref, 0, width)
    fluid, solid = one_over(columns_ref, 0, modes)
    ones, sweeps = inner_sweeps(spectra, sides_ref[...], rows, mask, fluid, solid, (edges_ref[0], edges_ref[1]))
    ones_ref[0] = ones[0]
    ones_ref[1] = ones[-1]
    inverse_rows(sweeps, cells, inverse_ref, outs)


def local_kernel(rows, edge_rows, count, cells, *refs):
    half = count // 2
    message_ref, edges = refs[0], refs[1 : 1 + half]
    forward_ref, inverse_ref, columns_ref, mask_ref = refs[1 + half : 5 + half]
    out_ref = refs[-1]
    size = len(rows) * cells
    near = [message_ref.at[d * size : (d + 1) * size] for d in range(half)]
    spectra = transform(len(rows), cells, near, (), forward_ref)
    edge_spectra = transform(len(edge_rows), cells, edges, (), forward_ref)
    sides = transform(len(edge_rows), cells, edges, (), forward_ref, beside=True)
    modes, width = spectra[0].shape
    mask, kinds = masks(mask_ref, half, width)
    fluid, solid = one_over(columns_ref, 0, modes)
    around = [spectrum * pick(mask[row], fluid, solid) for spectrum, row in zip(edge_spectra, edge_rows)]
    sides = sides * pick(kinds, fluid, solid)
    _, sweeps = inner_sweeps(spectra, sides, rows, mask, fluid, solid, around)
    inverse_rows(sweeps, cells, inverse_ref, [out_ref.at[d * size : (d + 1) * size] for d in range(half)])


def send_kernel(rows, edge_rows, rest, count, cells, *refs):
    half = count // 2
    inner, edges = refs[:half], refs[half : 2 * half]
    send_ref, columns_ref, mask_ref = refs[2 * half : 2 * half + 3]
    out_ref = refs[-1]

    def product(blocks, lines, lanes, kind):
        return sum(kind(send_ref[place(d)], block[lines, lanes]) for d, block in enumerate(blocks))

    def whole(blocks, i):
        return product(blocks, slice(i * cells, (i + 1) * cells), slice(None), row_product)

    spectra = [whole(inner, i) for i in range(len(rows))]
    around = [whole(edges, i) for i in range(len(edge_rows))]
    lines = len(edge_rows) * cells
    sides = product(edges, slice(lines, lines + 8), slice(0, cells), side_product)
    mask, kinds = masks(mask_ref, 0, inner[0].shape[1])
    fluid, solid = one_over(columns_ref, 2, rest)
    outer = [values[:rest] * pick(mask[row], fluid, solid) for values, row in zip(around, edge_rows)]
    outside = sides[:rest] * pick(kinds, fluid, solid)
    _, sweeps = inner_sweeps([v[:rest] for v in spectra], outside, rows, mask, fluid, solid, outer)

    def power(values, at):
        return values[rest + 8 * at : rest + 8 * at + 8]

    numbers = []
    for target in (0, 1):

        def beside(values, kind):
            same, cross = power(values, 2 + target), power(values, 4)
            return pick(kind, same, cross) if target == 0 else pick(kind, cross, same)

        own = [beside(values, mask[row]) for values, row in zip(spectra, rows)]
        edge = [beside(values, mask[row]) for values, row in zip(around, edge_rows)]
        column = [edge[0], *own, edge[1]]
        outside = beside(sides, kinds)
        numbers.append(
            [
                second_sweep(power(spectra[i], target), own[i], column[i], column[i + 2], outside, 4 + 2 * i, 1.0)
                for i in range(len(rows))
            ]
        )
    for i, row in enumerate(rows):
        base = i * (rest + 8)
        out_ref[base : base + rest, :] = sweeps[i]
        out_ref[base + rest : base + rest + 8, :] = jnp.where(mask[row] == 0, numbers[0][i], numbers[1][i])


def take_kernel(rows, count, cells, *refs):
    half = count // 2
    message_ref, local_ref, take_ref = refs[:3]
    outs = refs[-1 - (half - 1) * len(rows) :]
    lines = message_ref.shape[0] // len(rows)
    short = take_ref.shape[2] // 3 - lines
    for i in range(len(rows)):
        values = message_ref[i * lines : (i + 1) * lines, :]
        if short:
            values = jnp.concatenate([values, jnp.zeros((short, values.shape[1]), jnp.float32)], axis=0)
        values = thirds(values, 0)
        for d in range(half):
            base = (d * len(rows) + i) * cells
            value = local_ref[base : base + cells, :] + jnp.dot(
                take_ref[place(d)], values, preferred_element_type=jnp.float32
            )
            if d == 0:
                outs[0][i * cells : (i + 1) * cells, :] = value
            else:
                outs[1 + (d - 1) * len(rows) + i][...] = value


def rim_kernel(rows, order, count, cells, *refs):
    spectrum_ref, edges_ref, sides_ref, halo_ref, ones_ref, inverse_ref, columns_ref, mask_ref = refs[:8]
    outs = refs[-count:]
    _, modes, width = edges_ref.shape
    edge = 1 - paired_edge() if order == 0 else paired_edge()
    mask, _ = masks(mask_ref, 0, width)
    fluid, solid = one_over(columns_ref, 0, modes)
    sides = jnp.where(edge == 0, sides_ref[:, 0:2], sides_ref[:, 2:4])
    diagonal = pick(jnp.where(edge == 0, mask[rows[0]], mask[rows[1]]), fluid, solid)
    sweep = second_sweep(spectrum_ref[edge], edges_ref[edge], halo_ref[:modes, :], ones_ref[edge], sides, 0, diagonal)
    inverse_rows([sweep], cells, inverse_ref, outs[: count // 2], outs[count // 2 :])
    if order == 1:
        for d in range(1, count // 2):
            outs[d][cells:, :] = refs[8 + d - 1][...]
    for out in outs[count // 2 :]:
        if out.shape[0] > cells:
            out[cells:, :] = jnp.zeros((out.shape[0] - cells, width), jnp.float32)


def join_kernel(number, *refs):
    at = 0
    for ref in refs[:number]:
        refs[-1][at : at + ref.shape[0], :] = ref[...]
        at += ref.shape[0]


def copy_kernel(number, *refs):
    for ref, out in zip(refs[:number], refs[-number:]):
        out[...] = ref[...]


def unpack_kernel(pieces, row_count, cells, *refs):
    me = lax.axis_index("span")
    blocks, (out_ref, held, done) = refs[: len(pieces)], refs[-3:]
    pitch = held.shape[0] // cells
    count = lax.axis_size("span")
    own_lines = out_ref.shape[1] // count
    lines = own_lines * count // 2
    some = cells // SPLIT
    edge_rows = {"near": paired_edge() * (row_count - 1), "far": (1 - paired_edge()) * (row_count - 1)}
    chip = jnp.bitwise_xor(me, pieces[0][0]) // (count // 2)
    first = pl.multiple_of(chip * lines, lines)
    copies = []
    for part in range(SPLIT):
        for block, (d, base, rows, offset, tiles) in zip(blocks, pieces):
            for i, row in enumerate(rows):
                if row in edge_rows:
                    row = edge_rows[row]
                line = base + i * cells + part * some
                for tile in range(tiles):
                    at = part * some * pitch + place(d) * own_lines + (offset + tile) * row_count + row
                    held[pl.ds(at, some, stride=pitch), :] = block[line : line + some, tile * LANES : (tile + 1) * LANES]
        copies.append(
            pltpu.make_async_copy(
                held.reshape(cells, pitch, LANES).at[pl.ds(part * some, some), pl.ds(0, lines)],
                out_ref.at[pl.ds(part * some, some), pl.ds(first, lines)],
                done.at[part],
            )
        )
        copies[-1].start()
    for copy in copies:
        copy.wait()


def call(kernel, outs, *args, cost=LONG, earlier=()):
    shapes = [jax.ShapeDtypeStruct(shape, jnp.float32) for shape in outs]
    return pl.pallas_call(
        kernel,
        out_shape=shapes,
        in_specs=[VMEM] * len(args) + [ANY] * len(earlier),
        out_specs=[VMEM] * len(outs),
        compiler_params=PARAMS,
        cost_estimate=cost,
    )(*args, *earlier)


def swap(block, d):
    return lax.ppermute(block, "span", [(i, i ^ d) for i in range(lax.axis_size("span"))])


def local(pressure_source, solid_mask):
    count = lax.axis_size("span")
    half = count // 2
    plane_count = lax.axis_size("plane")
    cells, row_count, columns = pressure_source.shape
    width = columns // count
    tiles = width // LANES
    inner = tuple(range(1, row_count - 1))
    edges = (0, row_count - 1)
    near, far = range(1, half), range(half, count)
    *arrays, modes, rest = tables(cells * count, cells)
    forward, inverse, send, take, diagonals = map(jnp.asarray, arrays)

    lines = columns // LANES * row_count
    source = pressure_source.reshape(cells, row_count, columns // LANES, LANES).transpose(0, 2, 1, 3)
    source = source.reshape(cells, lines, LANES)
    scratch = [pltpu.VMEM((cells * (lines + 8), LANES), jnp.float32), pltpu.SemaphoreType.DMA((SPLIT,))]

    def pack(source, wanted, *earlier):
        jobs = [(at, 0, d, rows, 0, tiles, inner if rows == edges else ()) for at, (d, rows) in enumerate(wanted)]
        shapes = [(len(rows) * cells + (8 if rows == edges else 0), width) for _, rows in wanted]
        return pl.pallas_call(
            functools.partial(pack_kernel, jobs, row_count, cells, len(earlier)),
            out_shape=[jax.ShapeDtypeStruct(shape, jnp.float32) for shape in shapes],
            in_specs=[ANY] * (1 + len(earlier)),
            out_specs=[VMEM] * len(shapes),
            scratch_shapes=scratch,
            compiler_params=PARAMS,
            cost_estimate=LONG,
        )(source, *earlier)

    packed = pack(pltpu.with_memory_space_constraint(source, pltpu.HBM), [(d, edges) for d in range(1, count)])
    edge_blocks = [swap(block, d) for d, block in enumerate(packed, 1)]
    wanted = [(d, inner) for d in range(half + 1)] + [(0, edges)] + [(d, edges) for d in far]
    wanted += [(half + d, (row,)) for d in near for row in inner]
    packed = pack(source, wanted, packed[half - 1])
    edge_blocks = [packed[half + 1], *edge_blocks]
    relayed = packed[2 * half + 2 :]
    relayed = [swap(relayed[(d - 1) * len(inner) + i], d) for d in near for i in range(len(inner))]
    (message,) = call(
        functools.partial(join_kernel, 1 + len(relayed)),
        [(half * len(inner) * cells, width)],
        packed[half], *relayed, cost=SHORT, earlier=(edge_blocks[half],),
    )
    arrived = swap(message, half)

    spectrum, edge_ones, paired, other, sides = call(
        functools.partial(edge_kernel, edges, count, cells),
        [(2, modes, width), (2, modes, width), (modes + 16, width), (modes, width), (modes, 16)],
        *edge_blocks, forward, diagonals, solid_mask,
    )
    later = [packed[d] for d in near] + [packed[half + 2 + d] for d in near]
    if later:
        later = call(
            functools.partial(copy_kernel, len(later)), [block.shape for block in later], *later,
            cost=SHORT, earlier=(sides,),
        )
    inner_blocks = [packed[0]] + [swap(later[d - 1], d) for d in near]
    chip_edges = [packed[half + 2]] + [swap(later[half + d - 2], d) for d in near]

    length = len(inner) * cells
    (own,) = call(
        functools.partial(local_kernel, inner, edges, count, cells),
        [(half * length, width)],
        message, *chip_edges, forward, inverse, diagonals, solid_mask, cost=SHORT,
    )

    (sent,) = call(
        functools.partial(send_kernel, inner, edges, rest, count, cells),
        [(len(inner) * (rest + 8), width)],
        *inner_blocks, *edge_blocks[:half], send, diagonals, solid_mask, cost=SHORT, earlier=(own,),
    )
    taken = swap(sent, half)

    pairs = [[(i, i ^ 1) for i in range(plane_count)], [(i, ((i + 1) ^ 1) - 1) for i in range(plane_count)]]
    pairs = [[(i, j) for i, j in pair if 0 <= j < plane_count] for pair in pairs]
    halos = [lax.ppermute(row, "plane", pair) for row, pair in zip((paired, other), pairs)]
    *made, ones = call(
        functools.partial(inner_kernel, inner, count, cells),
        [(length, width)] * half + [(2, modes, width)],
        *inner_blocks, arrived, forward, inverse, diagonals, solid_mask, edge_ones, sides,
        cost=SHORT, earlier=(own,),
    )
    pieces = [(made[0], 0, 0, inner, 0, tiles)]
    made_got = [swap(made[d], d) for d in near]
    pieces += [(block, d, 0, inner, 0, tiles) for d, block in zip(near, made_got)]
    rim_got, near_rim, earlier = [], [], []
    for order, name in enumerate(("far", "near")):
        outs = call(
            functools.partial(rim_kernel, edges, order, count, cells),
            [(cells, width)] + [((order + 1) * cells, width)] * (half - 1) + [(cells + 8 * (1 - order), width)] * half,
            spectrum, edge_ones, sides, halos[1 - order], ones, inverse, diagonals, solid_mask, *near_rim,
            cost=LONG if order else SHORT, earlier=earlier,
        )
        near_rim = outs[1:half]
        pieces.append((outs[0], 0, 0, (name,), 0, tiles))
        rim_got.append([swap(outs[d], d) for d in far])
        pieces += [(block, d, 0, (name,), 0, tiles) for d, block in zip(far, rim_got[order])]
        earlier = [outs[-1]]
    pieces += [(swap(near_rim[d - 1], d), d, 0, ("near", "far"), 0, tiles) for d in near]
    rebuilt = call(
        functools.partial(take_kernel, inner, count, cells),
        [(length, width)] + [(cells, width)] * ((half - 1) * len(inner)),
        taken, own, take,
        cost=SHORT, earlier=[outs[-1], *rim_got[0], *made_got],
    )
    pieces.append((rebuilt[0], half, 0, inner, 0, tiles))
    for d in near:
        for i, row in enumerate(inner):
            pieces.append((swap(rebuilt[1 + (d - 1) * len(inner) + i], d), half + d, 0, (row,), 0, tiles))

    result = None
    for devices in (range(half), far):
        chosen = [piece for piece in pieces if piece[1] in devices]
        previous = () if result is None else (result,)
        result = pl.pallas_call(
            functools.partial(unpack_kernel, [piece[1:] for piece in chosen], row_count, cells),
            out_shape=jax.ShapeDtypeStruct((cells, lines, LANES), jnp.float32),
            in_specs=[VMEM] * len(chosen) + [ANY] * len(previous),
            out_specs=ANY,
            scratch_shapes=[
                pltpu.VMEM((cells * (lines // 2 + 8), LANES), jnp.float32),
                pltpu.SemaphoreType.DMA((SPLIT,)),
            ],
            input_output_aliases={len(chosen): 0} if previous else {},
            compiler_params=PARAMS,
            cost_estimate=SHORT if previous else LONG,
        )(*[piece[0] for piece in chosen], *previous)
    result = result.reshape(cells, columns // LANES, row_count, LANES).transpose(0, 2, 1, 3)
    return result.reshape(cells, row_count, columns)


def solution(mesh):
    placed = (P("span", "plane", None), P("plane", None))
    return jax.shard_map(
        local, mesh=mesh, in_specs=placed, out_specs=P("span", "plane", None), check_vma=False
    )
```

```python
import functools

import jax
import jax.numpy as jnp
import ml_dtypes
import numpy as np
from jax import lax
from jax.experimental import pallas as pl
from jax.experimental.pallas import tpu as pltpu
from jax.sharding import PartitionSpec as P

PENALTY = 12.0
LANES = 128
VMEM = pl.BlockSpec(memory_space=pltpu.VMEM)
ANY = pl.BlockSpec(memory_space=pl.ANY)
PARAMS = pltpu.CompilerParams(vmem_limit_bytes=24 * 1024 * 1024)
LONG = pl.CostEstimate(flops=0, bytes_accessed=200_000_000, transcendentals=0)
SHORT = pl.CostEstimate(flops=0, bytes_accessed=1024, transcendentals=0)
SPLIT = 4


def split(values):
    high = values.astype(ml_dtypes.bfloat16)
    low = (values - high.astype(np.float64)).astype(ml_dtypes.bfloat16)
    return np.concatenate([high, low, high], axis=-1)


def table_modes(length, wanted):
    modes = [(k, False) for k in range(length // 2 + 1) if wanted(k)]
    return modes + [(k, True) for k in range(1, length // 2) if wanted(k)]


def wave(length, points, k, sine):
    angles = (points * k % length) * (2.0 * np.pi / length)
    return np.sin(angles) if sine else np.cos(angles)


def fill(length, modes, forward, inverse, fluid, solid):
    points = np.arange(length // 2)
    for at, (k, sine) in enumerate(modes):
        forward[at] = wave(length, points, k, sine)
        inverse[:, at] = forward[at] * (1.0 if k in (0, length // 2) else 2.0) / length
        eigen = 2.0 - 2.0 * np.cos(2.0 * np.pi * k / length)
        fluid[at] = 1.0 / (4.0 + eigen)
        solid[at] = 1.0 / (4.0 + eigen + PENALTY)


def up_to(number, step):
    return -(-number // step) * step


def tables(length, cells):
    half = length // 2
    blocks = half // cells
    kept = [table_modes(length, lambda k: 3 * k <= length and k % 2 == parity) for parity in (0, 1)]
    padded = up_to(max(len(modes) for modes in kept), 16)
    left = table_modes(length, lambda k: 3 * k > length)
    rest = up_to(len(left), 16)
    columns = np.zeros((8, up_to(max(2 * padded, rest), LANES)))
    forward, inverse = np.zeros((2, padded, half)), np.zeros((2, half, padded))
    for parity, modes in enumerate(kept):
        part = slice(parity * padded, (parity + 1) * padded)
        fill(length, modes, forward[parity], inverse[parity], columns[0, part], columns[1, part])
    powers = 8
    send, take = np.zeros((rest + 6 * powers, half)), np.zeros((half, up_to(rest + powers, 16)))
    fill(length, left, send[:rest], take[:, :rest], columns[2, :rest], columns[3, :rest])
    take[:, : len(left)] *= [-1.0 if k % 2 == 0 else 1.0 for k, _ in left]
    ends = (np.arange(half), half - 1.0 - np.arange(half))
    for side in (0, 1):
        x, y = ends[side], ends[1 - side] + 1.0
        first = rest + 4 * side
        for solid, diagonal in enumerate((6.0, 6.0 + PENALTY)):
            rho = diagonal / 2.0 - np.sqrt(diagonal * diagonal / 4.0 - 1.0)
            at = first + 2 * solid
            take[:, at], take[:, at + 1] = rho**x, x * rho**x
            single = rho / (1.0 - rho**2) * rho**y
            double = rho**2 / (1.0 - rho**2) ** 2
            send[at + powers * solid] = single
            send[at + powers * (2 + solid)] = (double * (1.0 + rho**2) / (1.0 - rho**2) + double * y) * rho**y
            send[at + 1 + powers * (2 + solid)] = double * rho**y
            send[at + powers * 4] = single / PENALTY * (1.0 if solid == 0 else -1.0)
    forward = split(forward.reshape(2, padded, blocks, cells).transpose(0, 2, 1, 3))
    inverse = split(inverse.reshape(2, blocks, cells, padded))
    send = split(send.reshape(-1, blocks, cells).transpose(1, 0, 2))
    take = split(take.reshape(blocks, cells, -1))
    return forward, inverse, send, take, columns.astype(np.float32), 2 * padded, rest


def thirds(values, axis):
    high = values.astype(jnp.bfloat16)
    low = (values - high.astype(jnp.float32)).astype(jnp.bfloat16)
    return jnp.concatenate([high, high, low], axis=axis)


def pack_kernel(jobs, row_count, cells, earlier, x_ref, *refs):
    outs, (held, arrived) = refs[earlier:-2], refs[-2:]
    me = lax.axis_index("span")
    lines = x_ref.shape[1]
    all_tiles = lines // row_count
    own_tiles = all_tiles // lax.axis_size("span")
    pitch = held.shape[0] // cells
    some = cells // SPLIT
    copies = [
        pltpu.make_async_copy(
            x_ref.at[pl.ds(part * some, some)],
            held.reshape(cells, pitch, LANES).at[pl.ds(part * some, some), pl.ds(0, lines)],
            arrived.at[part],
        )
        for part in range(SPLIT)
    ]
    for copy in copies:
        copy.start()
    lane = lax.broadcasted_iota(jnp.int32, (some, LANES), 1)
    sides = []
    for part, copy in enumerate(copies):
        copy.wait()
        beside = jnp.zeros((some, LANES), jnp.float32)

        def line(tile, row):
            return held[pl.ds(part * some * pitch + tile * row_count + row, some, stride=pitch), :]

        for job, (out, base, d, rows, offset, tiles, more) in enumerate(jobs):
            first = jnp.bitwise_xor(me, d) * own_tiles + offset
            for i, row in enumerate(rows):
                at = base + i * cells + part * some
                for tile in range(tiles):
                    outs[out][at : at + some, tile * LANES : (tile + 1) * LANES] = line(first + tile, row)
            before = jnp.maximum(first - 1, 0)
            after = jnp.minimum(first + tiles, all_tiles - 1)
            for i, row in enumerate(rows + more if more else ()):
                for side, (tile, source) in enumerate(((before, LANES - 1), (after, 0))):
                    at = job * 8 + i * 2 + side
                    beside = jnp.where(lane == at, pltpu.roll(line(tile, row), (at - source) % LANES, 1), beside)
        sides.append(beside)
    if cells < LANES:
        sides.append(jnp.zeros((LANES - cells, LANES), jnp.float32))
    turned = jnp.concatenate(sides, axis=0).T
    for job, (out, base, _, rows, _, tiles, more) in enumerate(jobs):
        if not more:
            continue
        at = base + len(rows) * cells
        outs[out][at : at + 8, :LANES] = turned[job * 8 : (job + 1) * 8]
        if tiles > 1:
            outs[out][at : at + 8, LANES:] = jnp.zeros((8, (tiles - 1) * LANES), jnp.float32)


def place(d):
    half = lax.axis_size("span") // 2
    return jnp.bitwise_and(jnp.bitwise_xor(lax.axis_index("span"), d), half - 1)


def row_product(table, value):
    return jnp.dot(table, thirds(value, 0), preferred_element_type=jnp.float32)


def side_product(table, value):
    value = thirds(jnp.concatenate([value, jnp.zeros_like(value)], axis=0), 1)
    return lax.dot_general(table, value, (((1,), (1,)), ((), ())), preferred_element_type=jnp.float32)


def transform(rows, cells, near, far, forward_ref, beside=False):
    def spectrum(lines, lanes, product):
        halves = []
        for parity in (0, 1):
            total = 0.0
            for d, block in enumerate(near):
                value = block[lines, lanes]
                if far:
                    other = far[d][lines, lanes]
                    value = value + other if parity == 0 else value - other
                total = total + product(forward_ref[parity, place(d)], value)
            halves.append(total)
        return jnp.concatenate(halves, axis=0)

    if beside:
        return spectrum(slice(rows * cells, rows * cells + 8), slice(0, cells), side_product)
    return [spectrum(slice(i * cells, (i + 1) * cells), slice(None), row_product) for i in range(rows)]


def inverse_rows(sweeps, cells, inverse_ref, near, far=()):
    padded = sweeps[0].shape[0] // 2
    for i, sweep in enumerate(sweeps):
        even = thirds(sweep[:padded], 0)
        odd = thirds(sweep[padded:], 0)
        for d, out in enumerate(near):
            first = jnp.dot(inverse_ref[0, place(d)], even, preferred_element_type=jnp.float32)
            second = jnp.dot(inverse_ref[1, place(d)], odd, preferred_element_type=jnp.float32)
            out[i * cells : (i + 1) * cells, :] = first + second
            if far:
                far[d][i * cells : (i + 1) * cells, :] = first - second


def second_sweep(spectrum, one, above, below, sides, at, inverse_diagonal):
    width = one.shape[1]
    lane = lax.broadcasted_iota(jnp.int32, one.shape, 1)
    left = jnp.where(lane == 0, sides[:, at : at + 1], pltpu.roll(one, 1, 1))
    right = jnp.where(lane == width - 1, sides[:, at + 1 : at + 2], pltpu.roll(one, width - 1, 1))
    return (spectrum + above + below + left + right) * inverse_diagonal


def masks(mask_ref, d, width):
    count = mask_ref.shape[0]
    start = pl.multiple_of(jnp.bitwise_xor(lax.axis_index("span"), d) * width, LANES)
    last = mask_ref.shape[1] - LANES
    before = mask_ref[:, pl.ds(pl.multiple_of(jnp.maximum(start - LANES, 0), LANES), LANES)][:, LANES - 1 :]
    after = mask_ref[:, pl.ds(pl.multiple_of(jnp.minimum(start + width, last), LANES), LANES)][:, :1]
    before = jnp.where(start == 0, 2, before)
    after = jnp.where(start + width == mask_ref.shape[1], 2, after)
    lane = lax.broadcasted_iota(jnp.int32, (1, 16), 1)
    kinds = jnp.full((1, 16), 2, jnp.int32)
    for i, row in enumerate((0, count - 1, *range(1, count - 1))):
        kinds = jnp.where(lane == 2 * i, before[row : row + 1], kinds)
        kinds = jnp.where(lane == 2 * i + 1, after[row : row + 1], kinds)
    return [mask_ref[row : row + 1, pl.ds(start, width)] for row in range(mask_ref.shape[0])], kinds


def pick(kind, fluid, solid):
    return jnp.where(kind == 0, fluid, jnp.where(kind == 1, solid, 0.0))


def one_over(columns_ref, first, modes):
    turned = columns_ref[...].T
    return turned[:modes, first : first + 1], turned[:modes, first + 1 : first + 2]


def paired_edge():
    return lax.rem(lax.axis_index("plane") + 1, 2)


def edge_kernel(rows, count, cells, *refs):
    near, far = refs[: count // 2], refs[count // 2 : count]
    forward_ref, columns_ref, mask_ref = refs[count : count + 3]
    spectrum_ref, ones_ref, paired_ref, other_ref, sides_ref = refs[-5:]
    spectra = transform(len(rows), cells, near, far, forward_ref)
    sides = transform(len(rows), cells, near, far, forward_ref, beside=True)
    modes, width = spectra[0].shape
    mask, kinds = masks(mask_ref, 0, width)
    fluid, solid = one_over(columns_ref, 0, modes)
    ones = [spectrum * pick(mask[row], fluid, solid) for spectrum, row in zip(spectra, rows)]
    for i in (0, 1):
        spectrum_ref[i] = spectra[i]
        ones_ref[i] = ones[i]
    last = paired_edge() == 1
    paired_ref[:modes, :] = jnp.where(last, ones[1], ones[0])
    paired_ref[modes:, :] = jnp.zeros((paired_ref.shape[0] - modes, width), jnp.float32)
    other_ref[...] = jnp.where(last, ones[0], ones[1])
    sides_ref[...] = sides * pick(kinds, fluid, solid)


def inner_sweeps(spectra, sides, rows, mask, fluid, solid, edges):
    diagonals = [pick(mask[row], fluid, solid) for row in rows]
    ones = [spectrum * diagonal for spectrum, diagonal in zip(spectra, diagonals)]
    around = [edges[0], *ones, edges[1]]
    return ones, [
        second_sweep(spectra[i], ones[i], around[i], around[i + 2], sides, 4 + 2 * i, diagonals[i])
        for i in range(len(rows))
    ]


def inner_kernel(rows, count, cells, *refs):
    half = count // 2
    far_ref, forward_ref, inverse_ref, columns_ref, mask_ref, edges_ref, sides_ref = refs[half : half + 7]
    outs, ones_ref = refs[-1 - half : -1], refs[-1]
    size = len(rows) * cells
    far = [far_ref.at[e * size : (e + 1) * size] for e in range(half)]
    spectra = transform(len(rows), cells, refs[:half], far, forward_ref)
    modes, width = spectra[0].shape
    mask, _ = masks(mask_ref, 0, width)
    fluid, solid = one_over(columns_ref, 0, modes)
    ones, sweeps = inner_sweeps(spectra, sides_ref[...], rows, mask, fluid, solid, (edges_ref[0], edges_ref[1]))
    ones_ref[0] = ones[0]
    ones_ref[1] = ones[-1]
    inverse_rows(sweeps, cells, inverse_ref, outs)


def local_kernel(rows, edge_rows, count, cells, *refs):
    half = count // 2
    message_ref, edges = refs[0], refs[1 : 1 + half]
    forward_ref, inverse_ref, columns_ref, mask_ref = refs[1 + half : 5 + half]
    out_ref = refs[-1]
    size = len(rows) * cells
    near = [message_ref.at[d * size : (d + 1) * size] for d in range(half)]
    spectra = transform(len(rows), cells, near, (), forward_ref)
    edge_spectra = transform(len(edge_rows), cells, edges, (), forward_ref)
    sides = transform(len(edge_rows), cells, edges, (), forward_ref, beside=True)
    modes, width = spectra[0].shape
    mask, kinds = masks(mask_ref, half, width)
    fluid, solid = one_over(columns_ref, 0, modes)
    around = [spectrum * pick(mask[row], fluid, solid) for spectrum, row in zip(edge_spectra, edge_rows)]
    sides = sides * pick(kinds, fluid, solid)
    _, sweeps = inner_sweeps(spectra, sides, rows, mask, fluid, solid, around)
    inverse_rows(sweeps, cells, inverse_ref, [out_ref.at[d * size : (d + 1) * size] for d in range(half)])


def send_kernel(rows, edge_rows, rest, count, cells, *refs):
    half = count // 2
    inner, edges = refs[:half], refs[half : 2 * half]
    send_ref, columns_ref, mask_ref = refs[2 * half : 2 * half + 3]
    out_ref = refs[-1]

    def product(blocks, lines, lanes, kind):
        return sum(kind(send_ref[place(d)], block[lines, lanes]) for d, block in enumerate(blocks))

    def whole(blocks, i):
        return product(blocks, slice(i * cells, (i + 1) * cells), slice(None), row_product)

    spectra = [whole(inner, i) for i in range(len(rows))]
    around = [whole(edges, i) for i in range(len(edge_rows))]
    lines = len(edge_rows) * cells
    sides = product(edges, slice(lines, lines + 8), slice(0, cells), side_product)
    mask, kinds = masks(mask_ref, 0, inner[0].shape[1])
    fluid, solid = one_over(columns_ref, 2, rest)
    outer = [values[:rest] * pick(mask[row], fluid, solid) for values, row in zip(around, edge_rows)]
    outside = sides[:rest] * pick(kinds, fluid, solid)
    _, sweeps = inner_sweeps([v[:rest] for v in spectra], outside, rows, mask, fluid, solid, outer)

    def power(values, at):
        return values[rest + 8 * at : rest + 8 * at + 8]

    numbers = []
    for target in (0, 1):

        def beside(values, kind):
            same, cross = power(values, 2 + target), power(values, 4)
            return pick(kind, same, cross) if target == 0 else pick(kind, cross, same)

        own = [beside(values, mask[row]) for values, row in zip(spectra, rows)]
        edge = [beside(values, mask[row]) for values, row in zip(around, edge_rows)]
        column = [edge[0], *own, edge[1]]
        outside = beside(sides, kinds)
        numbers.append(
            [
                second_sweep(power(spectra[i], target), own[i], column[i], column[i + 2], outside, 4 + 2 * i, 1.0)
                for i in range(len(rows))
            ]
        )
    for i, row in enumerate(rows):
        base = i * (rest + 8)
        out_ref[base : base + rest, :] = sweeps[i]
        out_ref[base + rest : base + rest + 8, :] = jnp.where(mask[row] == 0, numbers[0][i], numbers[1][i])


def take_kernel(rows, count, cells, *refs):
    half = count // 2
    message_ref, local_ref, take_ref = refs[:3]
    outs = refs[-1 - (half - 1) * len(rows) :]
    lines = message_ref.shape[0] // len(rows)
    short = take_ref.shape[2] // 3 - lines
    for i in range(len(rows)):
        values = message_ref[i * lines : (i + 1) * lines, :]
        if short:
            values = jnp.concatenate([values, jnp.zeros((short, values.shape[1]), jnp.float32)], axis=0)
        values = thirds(values, 0)
        for d in range(half):
            base = (d * len(rows) + i) * cells
            value = local_ref[base : base + cells, :] + jnp.dot(
                take_ref[place(d)], values, preferred_element_type=jnp.float32
            )
            if d == 0:
                outs[0][i * cells : (i + 1) * cells, :] = value
            else:
                outs[1 + (d - 1) * len(rows) + i][...] = value


def rim_kernel(rows, order, count, cells, *refs):
    spectrum_ref, edges_ref, sides_ref, halo_ref, ones_ref, inverse_ref, columns_ref, mask_ref = refs[:8]
    outs = refs[-count:]
    _, modes, width = edges_ref.shape
    edge = 1 - paired_edge() if order == 0 else paired_edge()
    mask, _ = masks(mask_ref, 0, width)
    fluid, solid = one_over(columns_ref, 0, modes)
    sides = jnp.where(edge == 0, sides_ref[:, 0:2], sides_ref[:, 2:4])
    diagonal = pick(jnp.where(edge == 0, mask[rows[0]], mask[rows[1]]), fluid, solid)
    sweep = second_sweep(spectrum_ref[edge], edges_ref[edge], halo_ref[:modes, :], ones_ref[edge], sides, 0, diagonal)
    inverse_rows([sweep], cells, inverse_ref, outs[: count // 2], outs[count // 2 :])
    if order == 1:
        for d in range(1, count // 2):
            outs[d][cells:, :] = refs[8 + d - 1][...]
    for out in outs[count // 2 :]:
        if out.shape[0] > cells:
            out[cells:, :] = jnp.zeros((out.shape[0] - cells, width), jnp.float32)


def join_kernel(number, *refs):
    at = 0
    for ref in refs[:number]:
        refs[-1][at : at + ref.shape[0], :] = ref[...]
        at += ref.shape[0]


def copy_kernel(number, *refs):
    for ref, out in zip(refs[:number], refs[-number:]):
        out[...] = ref[...]


def unpack_kernel(pieces, row_count, cells, *refs):
    me = lax.axis_index("span")
    blocks, (out_ref, held, done) = refs[: len(pieces)], refs[-3:]
    pitch = held.shape[0] // cells
    count = lax.axis_size("span")
    own_lines = out_ref.shape[1] // count
    lines = own_lines * count // 2
    some = cells // SPLIT
    edge_rows = {"near": paired_edge() * (row_count - 1), "far": (1 - paired_edge()) * (row_count - 1)}
    chip = jnp.bitwise_xor(me, pieces[0][0]) // (count // 2)
    first = pl.multiple_of(chip * lines, lines)
    copies = []
    for part in range(SPLIT):
        for block, (d, base, rows, offset, tiles) in zip(blocks, pieces):
            for i, row in enumerate(rows):
                if row in edge_rows:
                    row = edge_rows[row]
                line = base + i * cells + part * some
                for tile in range(tiles):
                    at = part * some * pitch + place(d) * own_lines + (offset + tile) * row_count + row
                    held[pl.ds(at, some, stride=pitch), :] = block[line : line + some, tile * LANES : (tile + 1) * LANES]
        copies.append(
            pltpu.make_async_copy(
                held.reshape(cells, pitch, LANES).at[pl.ds(part * some, some), pl.ds(0, lines)],
                out_ref.at[pl.ds(part * some, some), pl.ds(first, lines)],
                done.at[part],
            )
        )
        copies[-1].start()
    for copy in copies:
        copy.wait()


def call(kernel, outs, *args, cost=LONG, earlier=()):
    shapes = [jax.ShapeDtypeStruct(shape, jnp.float32) for shape in outs]
    return pl.pallas_call(
        kernel,
        out_shape=shapes,
        in_specs=[VMEM] * len(args) + [ANY] * len(earlier),
        out_specs=[VMEM] * len(outs),
        compiler_params=PARAMS,
        cost_estimate=cost,
    )(*args, *earlier)


def swap(block, d):
    return lax.ppermute(block, "span", [(i, i ^ d) for i in range(lax.axis_size("span"))])


def local(pressure_source, solid_mask):
    count = lax.axis_size("span")
    half = count // 2
    plane_count = lax.axis_size("plane")
    cells, row_count, columns = pressure_source.shape
    width = columns // count
    tiles = width // LANES
    inner = tuple(range(1, row_count - 1))
    edges = (0, row_count - 1)
    near, far = range(1, half), range(half, count)
    *arrays, modes, rest = tables(cells * count, cells)
    forward, inverse, send, take, diagonals = map(jnp.asarray, arrays)

    lines = columns // LANES * row_count
    source = pressure_source.reshape(cells, row_count, columns // LANES, LANES).transpose(0, 2, 1, 3)
    source = source.reshape(cells, lines, LANES)
    scratch = [pltpu.VMEM((cells * (lines + 8), LANES), jnp.float32), pltpu.SemaphoreType.DMA((SPLIT,))]

    def pack(wanted, *earlier):
        jobs = [(at, 0, d, rows, 0, tiles, inner if rows == edges else ()) for at, (d, rows) in enumerate(wanted)]
        shapes = [(len(rows) * cells + (8 if rows == edges else 0), width) for _, rows in wanted]
        return pl.pallas_call(
            functools.partial(pack_kernel, jobs, row_count, cells, len(earlier)),
            out_shape=[jax.ShapeDtypeStruct(shape, jnp.float32) for shape in shapes],
            in_specs=[ANY] * (1 + len(earlier)),
            out_specs=[VMEM] * len(shapes),
            scratch_shapes=scratch,
            compiler_params=PARAMS,
            cost_estimate=LONG,
        )(pltpu.with_memory_space_constraint(source, pltpu.HBM), *earlier)

    packed = pack([(d, edges) for d in range(1, count)])
    edge_blocks = [swap(block, d) for d, block in enumerate(packed, 1)]
    wanted = [(d, inner) for d in range(half + 1)] + [(0, edges)] + [(d, edges) for d in far]
    wanted += [(half + d, (row,)) for d in near for row in inner]
    packed = pack(wanted, packed[half - 1])
    edge_blocks = [packed[half + 1], *edge_blocks]
    relayed = packed[2 * half + 2 :]
    relayed = [swap(relayed[(d - 1) * len(inner) + i], d) for d in near for i in range(len(inner))]
    (message,) = call(
        functools.partial(join_kernel, 1 + len(relayed)),
        [(half * len(inner) * cells, width)],
        packed[half], *relayed, cost=SHORT, earlier=(edge_blocks[half],),
    )
    arrived = swap(message, half)

    spectrum, edge_ones, paired, other, sides = call(
        functools.partial(edge_kernel, edges, count, cells),
        [(2, modes, width), (2, modes, width), (modes + 16, width), (modes, width), (modes, 16)],
        *edge_blocks, forward, diagonals, solid_mask,
    )
    later = [packed[d] for d in near] + [packed[half + 2 + d] for d in near]
    if later:
        later = call(
            functools.partial(copy_kernel, len(later)), [block.shape for block in later], *later,
            cost=SHORT, earlier=(sides,),
        )
    inner_blocks = [packed[0]] + [swap(later[d - 1], d) for d in near]
    chip_edges = [packed[half + 2]] + [swap(later[half + d - 2], d) for d in near]

    length = len(inner) * cells
    (own,) = call(
        functools.partial(local_kernel, inner, edges, count, cells),
        [(half * length, width)],
        message, *chip_edges, forward, inverse, diagonals, solid_mask, cost=SHORT,
    )

    (sent,) = call(
        functools.partial(send_kernel, inner, edges, rest, count, cells),
        [(len(inner) * (rest + 8), width)],
        *inner_blocks, *edge_blocks[:half], send, diagonals, solid_mask, cost=SHORT, earlier=(own,),
    )
    taken = swap(sent, half)

    pairs = [[(i, i ^ 1) for i in range(plane_count)], [(i, ((i + 1) ^ 1) - 1) for i in range(plane_count)]]
    pairs = [[(i, j) for i, j in pair if 0 <= j < plane_count] for pair in pairs]
    halos = [lax.ppermute(row, "plane", pair) for row, pair in zip((paired, other), pairs)]
    *made, ones = call(
        functools.partial(inner_kernel, inner, count, cells),
        [(length, width)] * half + [(2, modes, width)],
        *inner_blocks, arrived, forward, inverse, diagonals, solid_mask, edge_ones, sides,
        cost=SHORT, earlier=(own,),
    )
    pieces = [(made[0], 0, 0, inner, 0, tiles)]
    made_got = [swap(made[d], d) for d in near]
    pieces += [(block, d, 0, inner, 0, tiles) for d, block in zip(near, made_got)]
    rim_got, near_rim, earlier = [], [], []
    for order, name in enumerate(("far", "near")):
        outs = call(
            functools.partial(rim_kernel, edges, order, count, cells),
            [(cells, width)] + [((order + 1) * cells, width)] * (half - 1) + [(cells + 8 * (1 - order), width)] * half,
            spectrum, edge_ones, sides, halos[1 - order], ones, inverse, diagonals, solid_mask, *near_rim,
            cost=LONG if order else SHORT, earlier=earlier,
        )
        near_rim = outs[1:half]
        pieces.append((outs[0], 0, 0, (name,), 0, tiles))
        rim_got.append([swap(outs[d], d) for d in far])
        pieces += [(block, d, 0, (name,), 0, tiles) for d, block in zip(far, rim_got[order])]
        earlier = [outs[-1]]
    pieces += [(swap(near_rim[d - 1], d), d, 0, ("near", "far"), 0, tiles) for d in near]
    rebuilt = call(
        functools.partial(take_kernel, inner, count, cells),
        [(length, width)] + [(cells, width)] * ((half - 1) * len(inner)),
        taken, own, take,
        cost=SHORT, earlier=[outs[-1], *rim_got[0], *made_got],
    )
    pieces.append((rebuilt[0], half, 0, inner, 0, tiles))
    for d in near:
        for i, row in enumerate(inner):
            pieces.append((swap(rebuilt[1 + (d - 1) * len(inner) + i], d), half + d, 0, (row,), 0, tiles))

    result = None
    for devices in (range(half), far):
        chosen = [piece for piece in pieces if piece[1] in devices]
        previous = () if result is None else (result,)
        result = pl.pallas_call(
            functools.partial(unpack_kernel, [piece[1:] for piece in chosen], row_count, cells),
            out_shape=jax.ShapeDtypeStruct((cells, lines, LANES), jnp.float32),
            in_specs=[VMEM] * len(chosen) + [ANY] * len(previous),
            out_specs=ANY,
            scratch_shapes=[
                pltpu.VMEM((cells * (lines // 2 + 8), LANES), jnp.float32),
                pltpu.SemaphoreType.DMA((SPLIT,)),
            ],
            input_output_aliases={len(chosen): 0} if previous else {},
            compiler_params=PARAMS,
            cost_estimate=SHORT if previous else LONG,
        )(*[piece[0] for piece in chosen], *previous)
    result = result.reshape(cells, columns // LANES, row_count, LANES).transpose(0, 2, 1, 3)
    return result.reshape(cells, row_count, columns)


def solution(mesh):
    placed = (P("span", "plane", None), P("plane", None))
    return jax.shard_map(
        local, mesh=mesh, in_specs=placed, out_specs=P("span", "plane", None), check_vma=False
    )
```

```python
import functools

import jax
import jax.numpy as jnp
import ml_dtypes
import numpy as np
from jax import lax
from jax.experimental import pallas as pl
from jax.experimental.pallas import tpu as pltpu
from jax.sharding import PartitionSpec as P

PENALTY = 12.0
LANES = 128
VMEM = pl.BlockSpec(memory_space=pltpu.VMEM)
ANY = pl.BlockSpec(memory_space=pl.ANY)
PARAMS = pltpu.CompilerParams(vmem_limit_bytes=24 * 1024 * 1024)
LONG = pl.CostEstimate(flops=0, bytes_accessed=200_000_000, transcendentals=0)
SHORT = pl.CostEstimate(flops=0, bytes_accessed=1024, transcendentals=0)
SPLIT = 4


def split(values):
    high = values.astype(ml_dtypes.bfloat16)
    low = (values - high.astype(np.float64)).astype(ml_dtypes.bfloat16)
    return np.concatenate([high, low, high], axis=-1)


def table_modes(length, wanted):
    modes = [(k, False) for k in range(length // 2 + 1) if wanted(k)]
    return modes + [(k, True) for k in range(1, length // 2) if wanted(k)]


def wave(length, points, k, sine):
    angles = (points * k % length) * (2.0 * np.pi / length)
    return np.sin(angles) if sine else np.cos(angles)


def fill(length, modes, forward, inverse, fluid, solid):
    points = np.arange(length // 2)
    for at, (k, sine) in enumerate(modes):
        forward[at] = wave(length, points, k, sine)
        inverse[:, at] = forward[at] * (1.0 if k in (0, length // 2) else 2.0) / length
        eigen = 2.0 - 2.0 * np.cos(2.0 * np.pi * k / length)
        fluid[at] = 1.0 / (4.0 + eigen)
        solid[at] = 1.0 / (4.0 + eigen + PENALTY)


def up_to(number, step):
    return -(-number // step) * step


def tables(length, cells):
    half = length // 2
    blocks = half // cells
    kept = [table_modes(length, lambda k: 3 * k <= length and k % 2 == parity) for parity in (0, 1)]
    padded = up_to(max(len(modes) for modes in kept), 16)
    left = table_modes(length, lambda k: 3 * k > length)
    rest = up_to(len(left), 16)
    columns = np.zeros((8, up_to(max(2 * padded, rest), LANES)))
    forward, inverse = np.zeros((2, padded, half)), np.zeros((2, half, padded))
    for parity, modes in enumerate(kept):
        part = slice(parity * padded, (parity + 1) * padded)
        fill(length, modes, forward[parity], inverse[parity], columns[0, part], columns[1, part])
    powers = 8
    send, take = np.zeros((rest + 6 * powers, half)), np.zeros((half, up_to(rest + powers, 16)))
    fill(length, left, send[:rest], take[:, :rest], columns[2, :rest], columns[3, :rest])
    take[:, : len(left)] *= [-1.0 if k % 2 == 0 else 1.0 for k, _ in left]
    ends = (np.arange(half), half - 1.0 - np.arange(half))
    for side in (0, 1):
        x, y = ends[side], ends[1 - side] + 1.0
        first = rest + 4 * side
        for solid, diagonal in enumerate((6.0, 6.0 + PENALTY)):
            rho = diagonal / 2.0 - np.sqrt(diagonal * diagonal / 4.0 - 1.0)
            at = first + 2 * solid
            take[:, at], take[:, at + 1] = rho**x, x * rho**x
            single = rho / (1.0 - rho**2) * rho**y
            double = rho**2 / (1.0 - rho**2) ** 2
            send[at + powers * solid] = single
            send[at + powers * (2 + solid)] = (double * (1.0 + rho**2) / (1.0 - rho**2) + double * y) * rho**y
            send[at + 1 + powers * (2 + solid)] = double * rho**y
            send[at + powers * 4] = single / PENALTY * (1.0 if solid == 0 else -1.0)
    forward = split(forward.reshape(2, padded, blocks, cells).transpose(0, 2, 1, 3))
    inverse = split(inverse.reshape(2, blocks, cells, padded))
    send = split(send.reshape(-1, blocks, cells).transpose(1, 0, 2))
    take = split(take.reshape(blocks, cells, -1))
    return forward, inverse, send, take, columns.astype(np.float32), 2 * padded, rest


def thirds(values, axis):
    high = values.astype(jnp.bfloat16)
    low = (values - high.astype(jnp.float32)).astype(jnp.bfloat16)
    return jnp.concatenate([high, high, low], axis=axis)


def pack_kernel(jobs, row_count, cells, earlier, x_ref, *refs):
    outs, (held, arrived) = refs[earlier:-2], refs[-2:]
    me = lax.axis_index("span")
    lines = x_ref.shape[1]
    all_tiles = lines // row_count
    own_tiles = all_tiles // lax.axis_size("span")
    pitch = held.shape[0] // cells
    some = cells // SPLIT
    copies = [
        pltpu.make_async_copy(
            x_ref.at[pl.ds(part * some, some)],
            held.reshape(cells, pitch, LANES).at[pl.ds(part * some, some), pl.ds(0, lines)],
            arrived.at[part],
        )
        for part in range(SPLIT)
    ]
    for copy in copies:
        copy.start()
    lane = lax.broadcasted_iota(jnp.int32, (some, LANES), 1)
    sides = []
    for part, copy in enumerate(copies):
        copy.wait()
        beside = jnp.zeros((some, LANES), jnp.float32)

        def line(tile, row):
            return held[pl.ds(part * some * pitch + tile * row_count + row, some, stride=pitch), :]

        for job, (out, base, d, rows, offset, tiles, more) in enumerate(jobs):
            first = jnp.bitwise_xor(me, d) * own_tiles + offset
            for i, row in enumerate(rows):
                at = base + i * cells + part * some
                for tile in range(tiles):
                    outs[out][at : at + some, tile * LANES : (tile + 1) * LANES] = line(first + tile, row)
            before = jnp.maximum(first - 1, 0)
            after = jnp.minimum(first + tiles, all_tiles - 1)
            for i, row in enumerate(rows + more if more else ()):
                for side, (tile, source) in enumerate(((before, LANES - 1), (after, 0))):
                    at = job * 8 + i * 2 + side
                    beside = jnp.where(lane == at, pltpu.roll(line(tile, row), (at - source) % LANES, 1), beside)
        sides.append(beside)
    if cells < LANES:
        sides.append(jnp.zeros((LANES - cells, LANES), jnp.float32))
    turned = jnp.concatenate(sides, axis=0).T
    for job, (out, base, _, rows, _, tiles, more) in enumerate(jobs):
        if not more:
            continue
        at = base + len(rows) * cells
        outs[out][at : at + 8, :LANES] = turned[job * 8 : (job + 1) * 8]
        if tiles > 1:
            outs[out][at : at + 8, LANES:] = jnp.zeros((8, (tiles - 1) * LANES), jnp.float32)


def place(d):
    half = lax.axis_size("span") // 2
    return jnp.bitwise_and(jnp.bitwise_xor(lax.axis_index("span"), d), half - 1)


def row_product(table, value):
    return jnp.dot(table, thirds(value, 0), preferred_element_type=jnp.float32)


def side_product(table, value):
    value = thirds(jnp.concatenate([value, jnp.zeros_like(value)], axis=0), 1)
    return lax.dot_general(table, value, (((1,), (1,)), ((), ())), preferred_element_type=jnp.float32)


def transform(rows, cells, near, far, forward_ref, beside=False):
    def spectrum(lines, lanes, product):
        halves = []
        for parity in (0, 1):
            total = 0.0
            for d, block in enumerate(near):
                value = block[lines, lanes]
                if far:
                    other = far[d][lines, lanes]
                    value = value + other if parity == 0 else value - other
                total = total + product(forward_ref[parity, place(d)], value)
            halves.append(total)
        return jnp.concatenate(halves, axis=0)

    if beside:
        return spectrum(slice(rows * cells, rows * cells + 8), slice(0, cells), side_product)
    return [spectrum(slice(i * cells, (i + 1) * cells), slice(None), row_product) for i in range(rows)]


def inverse_rows(sweeps, cells, inverse_ref, near, far=()):
    padded = sweeps[0].shape[0] // 2
    for i, sweep in enumerate(sweeps):
        even = thirds(sweep[:padded], 0)
        odd = thirds(sweep[padded:], 0)
        for d, out in enumerate(near):
            first = jnp.dot(inverse_ref[0, place(d)], even, preferred_element_type=jnp.float32)
            second = jnp.dot(inverse_ref[1, place(d)], odd, preferred_element_type=jnp.float32)
            out[i * cells : (i + 1) * cells, :] = first + second
            if far:
                far[d][i * cells : (i + 1) * cells, :] = first - second


def second_sweep(spectrum, one, above, below, sides, at, inverse_diagonal):
    width = one.shape[1]
    lane = lax.broadcasted_iota(jnp.int32, one.shape, 1)
    left = jnp.where(lane == 0, sides[:, at : at + 1], pltpu.roll(one, 1, 1))
    right = jnp.where(lane == width - 1, sides[:, at + 1 : at + 2], pltpu.roll(one, width - 1, 1))
    return (spectrum + above + below + left + right) * inverse_diagonal


def masks(mask_ref, d, width):
    count = mask_ref.shape[0]
    start = pl.multiple_of(jnp.bitwise_xor(lax.axis_index("span"), d) * width, LANES)
    last = mask_ref.shape[1] - LANES
    before = mask_ref[:, pl.ds(pl.multiple_of(jnp.maximum(start - LANES, 0), LANES), LANES)][:, LANES - 1 :]
    after = mask_ref[:, pl.ds(pl.multiple_of(jnp.minimum(start + width, last), LANES), LANES)][:, :1]
    before = jnp.where(start == 0, 2, before)
    after = jnp.where(start + width == mask_ref.shape[1], 2, after)
    lane = lax.broadcasted_iota(jnp.int32, (1, 16), 1)
    kinds = jnp.full((1, 16), 2, jnp.int32)
    for i, row in enumerate((0, count - 1, *range(1, count - 1))):
        kinds = jnp.where(lane == 2 * i, before[row : row + 1], kinds)
        kinds = jnp.where(lane == 2 * i + 1, after[row : row + 1], kinds)
    return [mask_ref[row : row + 1, pl.ds(start, width)] for row in range(mask_ref.shape[0])], kinds


def pick(kind, fluid, solid):
    return jnp.where(kind == 0, fluid, jnp.where(kind == 1, solid, 0.0))


def one_over(columns_ref, first, modes):
    turned = columns_ref[...].T
    return turned[:modes, first : first + 1], turned[:modes, first + 1 : first + 2]


def paired_edge():
    return lax.rem(lax.axis_index("plane") + 1, 2)


def edge_kernel(rows, count, cells, *refs):
    near, far = refs[: count // 2], refs[count // 2 : count]
    forward_ref, columns_ref, mask_ref = refs[count : count + 3]
    spectrum_ref, ones_ref, paired_ref, other_ref, sides_ref = refs[-5:]
    spectra = transform(len(rows), cells, near, far, forward_ref)
    sides = transform(len(rows), cells, near, far, forward_ref, beside=True)
    modes, width = spectra[0].shape
    mask, kinds = masks(mask_ref, 0, width)
    fluid, solid = one_over(columns_ref, 0, modes)
    ones = [spectrum * pick(mask[row], fluid, solid) for spectrum, row in zip(spectra, rows)]
    for i in (0, 1):
        spectrum_ref[i] = spectra[i]
        ones_ref[i] = ones[i]
    last = paired_edge() == 1
    paired_ref[:modes, :] = jnp.where(last, ones[1], ones[0])
    paired_ref[modes:, :] = jnp.zeros((paired_ref.shape[0] - modes, width), jnp.float32)
    other_ref[...] = jnp.where(last, ones[0], ones[1])
    sides_ref[...] = sides * pick(kinds, fluid, solid)


def inner_sweeps(spectra, sides, rows, mask, fluid, solid, edges):
    diagonals = [pick(mask[row], fluid, solid) for row in rows]
    ones = [spectrum * diagonal for spectrum, diagonal in zip(spectra, diagonals)]
    around = [edges[0], *ones, edges[1]]
    return ones, [
        second_sweep(spectra[i], ones[i], around[i], around[i + 2], sides, 4 + 2 * i, diagonals[i])
        for i in range(len(rows))
    ]


def inner_kernel(rows, count, cells, *refs):
    half = count // 2
    far_ref, forward_ref, inverse_ref, columns_ref, mask_ref, edges_ref, sides_ref = refs[half : half + 7]
    outs, ones_ref = refs[-1 - half : -1], refs[-1]
    size = len(rows) * cells
    far = [far_ref.at[e * size : (e + 1) * size] for e in range(half)]
    spectra = transform(len(rows), cells, refs[:half], far, forward_ref)
    modes, width = spectra[0].shape
    mask, _ = masks(mask_ref, 0, width)
    fluid, solid = one_over(columns_ref, 0, modes)
    ones, sweeps = inner_sweeps(spectra, sides_ref[...], rows, mask, fluid, solid, (edges_ref[0], edges_ref[1]))
    ones_ref[0] = ones[0]
    ones_ref[1] = ones[-1]
    inverse_rows(sweeps, cells, inverse_ref, outs)


def local_kernel(rows, edge_rows, count, cells, *refs):
    half = count // 2
    message_ref, edges = refs[0], refs[1 : 1 + half]
    forward_ref, inverse_ref, columns_ref, mask_ref = refs[1 + half : 5 + half]
    out_ref = refs[-1]
    size = len(rows) * cells
    near = [message_ref.at[d * size : (d + 1) * size] for d in range(half)]
    spectra = transform(len(rows), cells, near, (), forward_ref)
    edge_spectra = transform(len(edge_rows), cells, edges, (), forward_ref)
    sides = transform(len(edge_rows), cells, edges, (), forward_ref, beside=True)
    modes, width = spectra[0].shape
    mask, kinds = masks(mask_ref, half, width)
    fluid, solid = one_over(columns_ref, 0, modes)
    around = [spectrum * pick(mask[row], fluid, solid) for spectrum, row in zip(edge_spectra, edge_rows)]
    sides = sides * pick(kinds, fluid, solid)
    _, sweeps = inner_sweeps(spectra, sides, rows, mask, fluid, solid, around)
    inverse_rows(sweeps, cells, inverse_ref, [out_ref.at[d * size : (d + 1) * size] for d in range(half)])


def send_kernel(rows, edge_rows, rest, count, cells, *refs):
    half = count // 2
    inner, edges = refs[:half], refs[half : 2 * half]
    send_ref, columns_ref, mask_ref = refs[2 * half : 2 * half + 3]
    out_ref = refs[-1]

    def product(blocks, lines, lanes, kind):
        return sum(kind(send_ref[place(d)], block[lines, lanes]) for d, block in enumerate(blocks))

    def whole(blocks, i):
        return product(blocks, slice(i * cells, (i + 1) * cells), slice(None), row_product)

    spectra = [whole(inner, i) for i in range(len(rows))]
    around = [whole(edges, i) for i in range(len(edge_rows))]
    lines = len(edge_rows) * cells
    sides = product(edges, slice(lines, lines + 8), slice(0, cells), side_product)
    mask, kinds = masks(mask_ref, 0, inner[0].shape[1])
    fluid, solid = one_over(columns_ref, 2, rest)
    outer = [values[:rest] * pick(mask[row], fluid, solid) for values, row in zip(around, edge_rows)]
    outside = sides[:rest] * pick(kinds, fluid, solid)
    _, sweeps = inner_sweeps([v[:rest] for v in spectra], outside, rows, mask, fluid, solid, outer)

    def power(values, at):
        return values[rest + 8 * at : rest + 8 * at + 8]

    numbers = []
    for target in (0, 1):

        def beside(values, kind):
            same, cross = power(values, 2 + target), power(values, 4)
            return pick(kind, same, cross) if target == 0 else pick(kind, cross, same)

        own = [beside(values, mask[row]) for values, row in zip(spectra, rows)]
        edge = [beside(values, mask[row]) for values, row in zip(around, edge_rows)]
        column = [edge[0], *own, edge[1]]
        outside = beside(sides, kinds)
        numbers.append(
            [
                second_sweep(power(spectra[i], target), own[i], column[i], column[i + 2], outside, 4 + 2 * i, 1.0)
                for i in range(len(rows))
            ]
        )
    for i, row in enumerate(rows):
        base = i * (rest + 8)
        out_ref[base : base + rest, :] = sweeps[i]
        out_ref[base + rest : base + rest + 8, :] = jnp.where(mask[row] == 0, numbers[0][i], numbers[1][i])


def take_kernel(rows, count, cells, *refs):
    half = count // 2
    message_ref, local_ref, take_ref = refs[:3]
    outs = refs[-1 - (half - 1) * len(rows) :]
    lines = message_ref.shape[0] // len(rows)
    short = take_ref.shape[2] // 3 - lines
    for i in range(len(rows)):
        values = message_ref[i * lines : (i + 1) * lines, :]
        if short:
            values = jnp.concatenate([values, jnp.zeros((short, values.shape[1]), jnp.float32)], axis=0)
        values = thirds(values, 0)
        for d in range(half):
            base = (d * len(rows) + i) * cells
            value = local_ref[base : base + cells, :] + jnp.dot(
                take_ref[place(d)], values, preferred_element_type=jnp.float32
            )
            if d == 0:
                outs[0][i * cells : (i + 1) * cells, :] = value
            else:
                outs[1 + (d - 1) * len(rows) + i][...] = value


def rim_kernel(rows, order, count, cells, *refs):
    spectrum_ref, edges_ref, sides_ref, halo_ref, ones_ref, inverse_ref, columns_ref, mask_ref = refs[:8]
    outs = refs[-count:]
    _, modes, width = edges_ref.shape
    edge = 1 - paired_edge() if order == 0 else paired_edge()
    mask, _ = masks(mask_ref, 0, width)
    fluid, solid = one_over(columns_ref, 0, modes)
    sides = jnp.where(edge == 0, sides_ref[:, 0:2], sides_ref[:, 2:4])
    diagonal = pick(jnp.where(edge == 0, mask[rows[0]], mask[rows[1]]), fluid, solid)
    sweep = second_sweep(spectrum_ref[edge], edges_ref[edge], halo_ref[:modes, :], ones_ref[edge], sides, 0, diagonal)
    inverse_rows([sweep], cells, inverse_ref, outs[: count // 2], outs[count // 2 :])
    if order == 1:
        for d in range(1, count // 2):
            outs[d][cells:, :] = refs[8 + d - 1][...]
    for out in outs[count // 2 :]:
        if out.shape[0] > cells:
            out[cells:, :] = jnp.zeros((out.shape[0] - cells, width), jnp.float32)


def join_kernel(number, *refs):
    at = 0
    for ref in refs[:number]:
        refs[-1][at : at + ref.shape[0], :] = ref[...]
        at += ref.shape[0]


def copy_kernel(number, *refs):
    for ref, out in zip(refs[:number], refs[-number:]):
        out[...] = ref[...]


def unpack_kernel(pieces, row_count, cells, *refs):
    me = lax.axis_index("span")
    blocks, (out_ref, held, done) = refs[: len(pieces)], refs[-3:]
    pitch = held.shape[0] // cells
    count = lax.axis_size("span")
    own_lines = out_ref.shape[1] // count
    lines = own_lines * count // 2
    some = cells // SPLIT
    edge_rows = {"near": paired_edge() * (row_count - 1), "far": (1 - paired_edge()) * (row_count - 1)}
    chip = jnp.bitwise_xor(me, pieces[0][0]) // (count // 2)
    first = pl.multiple_of(chip * lines, lines)
    copies = []
    for part in range(SPLIT):
        for block, (d, base, rows, offset, tiles) in zip(blocks, pieces):
            for i, row in enumerate(rows):
                if row in edge_rows:
                    row = edge_rows[row]
                line = base + i * cells + part * some
                for tile in range(tiles):
                    at = part * some * pitch + place(d) * own_lines + (offset + tile) * row_count + row
                    held[pl.ds(at, some, stride=pitch), :] = block[line : line + some, tile * LANES : (tile + 1) * LANES]
        copies.append(
            pltpu.make_async_copy(
                held.reshape(cells, pitch, LANES).at[pl.ds(part * some, some), pl.ds(0, lines)],
                out_ref.at[pl.ds(part * some, some), pl.ds(first, lines)],
                done.at[part],
            )
        )
        copies[-1].start()
    for copy in copies:
        copy.wait()


def call(kernel, outs, *args, cost=LONG, earlier=()):
    shapes = [jax.ShapeDtypeStruct(shape, jnp.float32) for shape in outs]
    return pl.pallas_call(
        kernel,
        out_shape=shapes,
        in_specs=[VMEM] * len(args) + [ANY] * len(earlier),
        out_specs=[VMEM] * len(outs),
        compiler_params=PARAMS,
        cost_estimate=cost,
    )(*args, *earlier)


def swap(block, d):
    return lax.ppermute(block, "span", [(i, i ^ d) for i in range(lax.axis_size("span"))])


def local(pressure_source, solid_mask):
    count = lax.axis_size("span")
    half = count // 2
    plane_count = lax.axis_size("plane")
    cells, row_count, columns = pressure_source.shape
    width = columns // count
    tiles = width // LANES
    inner = tuple(range(1, row_count - 1))
    edges = (0, row_count - 1)
    near, far = range(1, half), range(half, count)
    *arrays, modes, rest = tables(cells * count, cells)
    forward, inverse, send, take, diagonals = map(jnp.asarray, arrays)

    lines = columns // LANES * row_count
    source = pressure_source.reshape(cells, row_count, columns // LANES, LANES).transpose(0, 2, 1, 3)
    source = source.reshape(cells, lines, LANES)
    scratch = [pltpu.VMEM((cells * (lines + 8), LANES), jnp.float32), pltpu.SemaphoreType.DMA((SPLIT,))]

    def pack(wanted, *earlier):
        jobs = [(at, 0, d, rows, 0, tiles, inner if rows == edges else ()) for at, (d, rows) in enumerate(wanted)]
        shapes = [(len(rows) * cells + (8 if rows == edges else 0), width) for _, rows in wanted]
        return pl.pallas_call(
            functools.partial(pack_kernel, jobs, row_count, cells, len(earlier)),
            out_shape=[jax.ShapeDtypeStruct(shape, jnp.float32) for shape in shapes],
            in_specs=[ANY] * (1 + len(earlier)),
            out_specs=[VMEM] * len(shapes),
            scratch_shapes=scratch,
            compiler_params=PARAMS,
            cost_estimate=LONG,
        )(pltpu.with_memory_space_constraint(source, pltpu.HBM), *earlier)

    packed = pack([(d, edges) for d in range(1, count)])
    edge_blocks = [swap(block, d) for d, block in enumerate(packed, 1)]
    wanted = [(d, inner) for d in range(half + 1)] + [(0, edges)] + [(d, edges) for d in far]
    wanted += [(half + d, (row,)) for d in near for row in inner]
    packed = pack(wanted, packed[half - 1])
    edge_blocks = [packed[half + 1], *edge_blocks]
    relayed = packed[2 * half + 2 :]
    relayed = [swap(relayed[(d - 1) * len(inner) + i], d) for d in near for i in range(len(inner))]
    (message,) = call(
        functools.partial(join_kernel, 1 + len(relayed)),
        [(half * len(inner) * cells, width)],
        packed[half], *relayed, cost=SHORT, earlier=(edge_blocks[half],),
    )
    arrived = swap(message, half)

    spectrum, edge_ones, paired, other, sides = call(
        functools.partial(edge_kernel, edges, count, cells),
        [(2, modes, width), (2, modes, width), (modes + 16, width), (modes, width), (modes, 16)],
        *edge_blocks, forward, diagonals, solid_mask,
    )
    later = [packed[d] for d in near] + [packed[half + 2 + d] for d in near]
    if later:
        later = call(
            functools.partial(copy_kernel, len(later)), [block.shape for block in later], *later,
            cost=SHORT, earlier=(sides,),
        )
    inner_blocks = [packed[0]] + [swap(later[d - 1], d) for d in near]
    chip_edges = [packed[half + 2]] + [swap(later[half + d - 2], d) for d in near]

    length = len(inner) * cells
    (own,) = call(
        functools.partial(local_kernel, inner, edges, count, cells),
        [(half * length, width)],
        message, *chip_edges, forward, inverse, diagonals, solid_mask, cost=SHORT,
    )

    (sent,) = call(
        functools.partial(send_kernel, inner, edges, rest, count, cells),
        [(len(inner) * (rest + 8), width)],
        *inner_blocks, *edge_blocks[:half], send, diagonals, solid_mask, cost=SHORT,
    )
    taken = swap(sent, half)

    pairs = [[(i, i ^ 1) for i in range(plane_count)], [(i, ((i + 1) ^ 1) - 1) for i in range(plane_count)]]
    pairs = [[(i, j) for i, j in pair if 0 <= j < plane_count] for pair in pairs]
    halos = [lax.ppermute(row, "plane", pair) for row, pair in zip((paired, other), pairs)]
    *made, ones = call(
        functools.partial(inner_kernel, inner, count, cells),
        [(length, width)] * half + [(2, modes, width)],
        *inner_blocks, arrived, forward, inverse, diagonals, solid_mask, edge_ones, sides,
        cost=SHORT, earlier=(own,),
    )
    pieces = [(made[0], 0, 0, inner, 0, tiles)]
    made_got = [swap(made[d], d) for d in near]
    pieces += [(block, d, 0, inner, 0, tiles) for d, block in zip(near, made_got)]
    rim_got, near_rim, earlier = [], [], []
    for order, name in enumerate(("far", "near")):
        outs = call(
            functools.partial(rim_kernel, edges, order, count, cells),
            [(cells, width)] + [((order + 1) * cells, width)] * (half - 1) + [(cells + 8 * (1 - order), width)] * half,
            spectrum, edge_ones, sides, halos[1 - order], ones, inverse, diagonals, solid_mask, *near_rim,
            cost=LONG if order else SHORT, earlier=earlier,
        )
        near_rim = outs[1:half]
        pieces.append((outs[0], 0, 0, (name,), 0, tiles))
        rim_got.append([swap(outs[d], d) for d in far])
        pieces += [(block, d, 0, (name,), 0, tiles) for d, block in zip(far, rim_got[order])]
        earlier = [outs[-1]]
    pieces += [(swap(near_rim[d - 1], d), d, 0, ("near", "far"), 0, tiles) for d in near]
    rebuilt = call(
        functools.partial(take_kernel, inner, count, cells),
        [(length, width)] + [(cells, width)] * ((half - 1) * len(inner)),
        taken, own, take,
        cost=SHORT, earlier=[outs[-1], *rim_got[0], *made_got],
    )
    pieces.append((rebuilt[0], half, 0, inner, 0, tiles))
    for d in near:
        for i, row in enumerate(inner):
            pieces.append((swap(rebuilt[1 + (d - 1) * len(inner) + i], d), half + d, 0, (row,), 0, tiles))

    result = None
    for devices in (range(half), far):
        chosen = [piece for piece in pieces if piece[1] in devices]
        previous = () if result is None else (result,)
        result = pl.pallas_call(
            functools.partial(unpack_kernel, [piece[1:] for piece in chosen], row_count, cells),
            out_shape=jax.ShapeDtypeStruct((cells, lines, LANES), jnp.float32),
            in_specs=[VMEM] * len(chosen) + [ANY] * len(previous),
            out_specs=ANY,
            scratch_shapes=[
                pltpu.VMEM((cells * (lines // 2 + 8), LANES), jnp.float32),
                pltpu.SemaphoreType.DMA((SPLIT,)),
            ],
            input_output_aliases={len(chosen): 0} if previous else {},
            compiler_params=PARAMS,
            cost_estimate=SHORT if previous else LONG,
        )(*[piece[0] for piece in chosen], *previous)
    result = result.reshape(cells, columns // LANES, row_count, LANES).transpose(0, 2, 1, 3)
    return result.reshape(cells, row_count, columns)


def solution(mesh):
    placed = (P("span", "plane", None), P("plane", None))
    return jax.shard_map(
        local, mesh=mesh, in_specs=placed, out_specs=P("span", "plane", None), check_vma=False
    )
```

```python
import functools

import jax
import jax.numpy as jnp
import ml_dtypes
import numpy as np
from jax import lax
from jax.experimental import pallas as pl
from jax.experimental.pallas import tpu as pltpu
from jax.sharding import PartitionSpec as P

PENALTY = 12.0
LANES = 128
VMEM = pl.BlockSpec(memory_space=pltpu.VMEM)
ANY = pl.BlockSpec(memory_space=pl.ANY)
PARAMS = pltpu.CompilerParams(vmem_limit_bytes=24 * 1024 * 1024)
LONG = pl.CostEstimate(flops=0, bytes_accessed=200_000_000, transcendentals=0)
SHORT = pl.CostEstimate(flops=0, bytes_accessed=1024, transcendentals=0)
SPLIT = 8


def split(values):
    high = values.astype(ml_dtypes.bfloat16)
    low = (values - high.astype(np.float64)).astype(ml_dtypes.bfloat16)
    return np.concatenate([high, low, high], axis=-1)


def table_modes(length, wanted):
    modes = [(k, False) for k in range(length // 2 + 1) if wanted(k)]
    return modes + [(k, True) for k in range(1, length // 2) if wanted(k)]


def wave(length, points, k, sine):
    angles = (points * k % length) * (2.0 * np.pi / length)
    return np.sin(angles) if sine else np.cos(angles)


def fill(length, modes, forward, inverse, fluid, solid):
    points = np.arange(length // 2)
    for at, (k, sine) in enumerate(modes):
        forward[at] = wave(length, points, k, sine)
        inverse[:, at] = forward[at] * (1.0 if k in (0, length // 2) else 2.0) / length
        eigen = 2.0 - 2.0 * np.cos(2.0 * np.pi * k / length)
        fluid[at] = 1.0 / (4.0 + eigen)
        solid[at] = 1.0 / (4.0 + eigen + PENALTY)


def up_to(number, step):
    return -(-number // step) * step


def tables(length, cells):
    half = length // 2
    blocks = half // cells
    kept = [table_modes(length, lambda k: 3 * k <= length and k % 2 == parity) for parity in (0, 1)]
    padded = up_to(max(len(modes) for modes in kept), 16)
    left = table_modes(length, lambda k: 3 * k > length)
    rest = up_to(len(left), 16)
    columns = np.zeros((8, up_to(max(2 * padded, rest), LANES)))
    forward, inverse = np.zeros((2, padded, half)), np.zeros((2, half, padded))
    for parity, modes in enumerate(kept):
        part = slice(parity * padded, (parity + 1) * padded)
        fill(length, modes, forward[parity], inverse[parity], columns[0, part], columns[1, part])
    powers = 8
    send, take = np.zeros((rest + 6 * powers, half)), np.zeros((half, up_to(rest + powers, 16)))
    fill(length, left, send[:rest], take[:, :rest], columns[2, :rest], columns[3, :rest])
    take[:, : len(left)] *= [-1.0 if k % 2 == 0 else 1.0 for k, _ in left]
    ends = (np.arange(half), half - 1.0 - np.arange(half))
    for side in (0, 1):
        x, y = ends[side], ends[1 - side] + 1.0
        first = rest + 4 * side
        for solid, diagonal in enumerate((6.0, 6.0 + PENALTY)):
            rho = diagonal / 2.0 - np.sqrt(diagonal * diagonal / 4.0 - 1.0)
            at = first + 2 * solid
            take[:, at], take[:, at + 1] = rho**x, x * rho**x
            single = rho / (1.0 - rho**2) * rho**y
            double = rho**2 / (1.0 - rho**2) ** 2
            send[at + powers * solid] = single
            send[at + powers * (2 + solid)] = (double * (1.0 + rho**2) / (1.0 - rho**2) + double * y) * rho**y
            send[at + 1 + powers * (2 + solid)] = double * rho**y
            send[at + powers * 4] = single / PENALTY * (1.0 if solid == 0 else -1.0)
    forward = split(forward.reshape(2, padded, blocks, cells).transpose(0, 2, 1, 3))
    inverse = split(inverse.reshape(2, blocks, cells, padded))
    send = split(send.reshape(-1, blocks, cells).transpose(1, 0, 2))
    take = split(take.reshape(blocks, cells, -1))
    return forward, inverse, send, take, columns.astype(np.float32), 2 * padded, rest


def thirds(values, axis):
    high = values.astype(jnp.bfloat16)
    low = (values - high.astype(jnp.float32)).astype(jnp.bfloat16)
    return jnp.concatenate([high, high, low], axis=axis)


def pack_kernel(jobs, row_count, cells, earlier, x_ref, *refs):
    outs, (held, arrived) = refs[earlier:-2], refs[-2:]
    me = lax.axis_index("span")
    lines = x_ref.shape[1]
    all_tiles = lines // row_count
    own_tiles = all_tiles // lax.axis_size("span")
    pitch = held.shape[0] // cells
    some = cells // SPLIT
    copies = [
        pltpu.make_async_copy(
            x_ref.at[pl.ds(part * some, some)],
            held.reshape(cells, pitch, LANES).at[pl.ds(part * some, some), pl.ds(0, lines)],
            arrived.at[part],
        )
        for part in range(SPLIT)
    ]
    for copy in copies:
        copy.start()
    lane = lax.broadcasted_iota(jnp.int32, (some, LANES), 1)
    sides = []
    for part, copy in enumerate(copies):
        copy.wait()
        beside = jnp.zeros((some, LANES), jnp.float32)

        def line(tile, row):
            return held[pl.ds(part * some * pitch + tile * row_count + row, some, stride=pitch), :]

        for job, (out, base, d, rows, offset, tiles, more) in enumerate(jobs):
            first = jnp.bitwise_xor(me, d) * own_tiles + offset
            for i, row in enumerate(rows):
                at = base + i * cells + part * some
                for tile in range(tiles):
                    outs[out][at : at + some, tile * LANES : (tile + 1) * LANES] = line(first + tile, row)
            before = jnp.maximum(first - 1, 0)
            after = jnp.minimum(first + tiles, all_tiles - 1)
            for i, row in enumerate(rows + more if more else ()):
                for side, (tile, source) in enumerate(((before, LANES - 1), (after, 0))):
                    at = job * 8 + i * 2 + side
                    beside = jnp.where(lane == at, pltpu.roll(line(tile, row), (at - source) % LANES, 1), beside)
        sides.append(beside)
    if cells < LANES:
        sides.append(jnp.zeros((LANES - cells, LANES), jnp.float32))
    turned = jnp.concatenate(sides, axis=0).T
    for job, (out, base, _, rows, _, tiles, more) in enumerate(jobs):
        if not more:
            continue
        at = base + len(rows) * cells
        outs[out][at : at + 8, :LANES] = turned[job * 8 : (job + 1) * 8]
        if tiles > 1:
            outs[out][at : at + 8, LANES:] = jnp.zeros((8, (tiles - 1) * LANES), jnp.float32)


def place(d):
    half = lax.axis_size("span") // 2
    return jnp.bitwise_and(jnp.bitwise_xor(lax.axis_index("span"), d), half - 1)


def row_product(table, value):
    return jnp.dot(table, thirds(value, 0), preferred_element_type=jnp.float32)


def side_product(table, value):
    value = thirds(jnp.concatenate([value, jnp.zeros_like(value)], axis=0), 1)
    return lax.dot_general(table, value, (((1,), (1,)), ((), ())), preferred_element_type=jnp.float32)


def transform(rows, cells, near, far, forward_ref, beside=False):
    def spectrum(lines, lanes, product):
        halves = []
        for parity in (0, 1):
            total = 0.0
            for d, block in enumerate(near):
                value = block[lines, lanes]
                if far:
                    other = far[d][lines, lanes]
                    value = value + other if parity == 0 else value - other
                total = total + product(forward_ref[parity, place(d)], value)
            halves.append(total)
        return jnp.concatenate(halves, axis=0)

    if beside:
        return spectrum(slice(rows * cells, rows * cells + 8), slice(0, cells), side_product)
    return [spectrum(slice(i * cells, (i + 1) * cells), slice(None), row_product) for i in range(rows)]


def inverse_rows(sweeps, cells, inverse_ref, near, far=()):
    padded = sweeps[0].shape[0] // 2
    for i, sweep in enumerate(sweeps):
        even = thirds(sweep[:padded], 0)
        odd = thirds(sweep[padded:], 0)
        for d, out in enumerate(near):
            first = jnp.dot(inverse_ref[0, place(d)], even, preferred_element_type=jnp.float32)
            second = jnp.dot(inverse_ref[1, place(d)], odd, preferred_element_type=jnp.float32)
            out[i * cells : (i + 1) * cells, :] = first + second
            if far:
                far[d][i * cells : (i + 1) * cells, :] = first - second


def second_sweep(spectrum, one, above, below, sides, at, inverse_diagonal):
    width = one.shape[1]
    lane = lax.broadcasted_iota(jnp.int32, one.shape, 1)
    left = jnp.where(lane == 0, sides[:, at : at + 1], pltpu.roll(one, 1, 1))
    right = jnp.where(lane == width - 1, sides[:, at + 1 : at + 2], pltpu.roll(one, width - 1, 1))
    return (spectrum + above + below + left + right) * inverse_diagonal


def masks(mask_ref, d, width):
    count = mask_ref.shape[0]
    start = pl.multiple_of(jnp.bitwise_xor(lax.axis_index("span"), d) * width, LANES)
    last = mask_ref.shape[1] - LANES
    before = mask_ref[:, pl.ds(pl.multiple_of(jnp.maximum(start - LANES, 0), LANES), LANES)][:, LANES - 1 :]
    after = mask_ref[:, pl.ds(pl.multiple_of(jnp.minimum(start + width, last), LANES), LANES)][:, :1]
    before = jnp.where(start == 0, 2, before)
    after = jnp.where(start + width == mask_ref.shape[1], 2, after)
    lane = lax.broadcasted_iota(jnp.int32, (1, 16), 1)
    kinds = jnp.full((1, 16), 2, jnp.int32)
    for i, row in enumerate((0, count - 1, *range(1, count - 1))):
        kinds = jnp.where(lane == 2 * i, before[row : row + 1], kinds)
        kinds = jnp.where(lane == 2 * i + 1, after[row : row + 1], kinds)
    return [mask_ref[row : row + 1, pl.ds(start, width)] for row in range(mask_ref.shape[0])], kinds


def pick(kind, fluid, solid):
    return jnp.where(kind == 0, fluid, jnp.where(kind == 1, solid, 0.0))


def one_over(columns_ref, first, modes):
    turned = columns_ref[...].T
    return turned[:modes, first : first + 1], turned[:modes, first + 1 : first + 2]


def paired_edge():
    return lax.rem(lax.axis_index("plane") + 1, 2)


def edge_kernel(rows, count, cells, *refs):
    near, far = refs[: count // 2], refs[count // 2 : count]
    forward_ref, columns_ref, mask_ref = refs[count : count + 3]
    spectrum_ref, ones_ref, paired_ref, other_ref, sides_ref = refs[-5:]
    spectra = transform(len(rows), cells, near, far, forward_ref)
    sides = transform(len(rows), cells, near, far, forward_ref, beside=True)
    modes, width = spectra[0].shape
    mask, kinds = masks(mask_ref, 0, width)
    fluid, solid = one_over(columns_ref, 0, modes)
    ones = [spectrum * pick(mask[row], fluid, solid) for spectrum, row in zip(spectra, rows)]
    for i in (0, 1):
        spectrum_ref[i] = spectra[i]
        ones_ref[i] = ones[i]
    last = paired_edge() == 1
    paired_ref[:modes, :] = jnp.where(last, ones[1], ones[0])
    paired_ref[modes:, :] = jnp.zeros((paired_ref.shape[0] - modes, width), jnp.float32)
    other_ref[...] = jnp.where(last, ones[0], ones[1])
    sides_ref[...] = sides * pick(kinds, fluid, solid)


def inner_sweeps(spectra, sides, rows, mask, fluid, solid, edges):
    diagonals = [pick(mask[row], fluid, solid) for row in rows]
    ones = [spectrum * diagonal for spectrum, diagonal in zip(spectra, diagonals)]
    around = [edges[0], *ones, edges[1]]
    return ones, [
        second_sweep(spectra[i], ones[i], around[i], around[i + 2], sides, 4 + 2 * i, diagonals[i])
        for i in range(len(rows))
    ]


def inner_kernel(rows, count, cells, *refs):
    half = count // 2
    far_ref, forward_ref, inverse_ref, columns_ref, mask_ref, edges_ref, sides_ref = refs[half : half + 7]
    outs, ones_ref = refs[-1 - half : -1], refs[-1]
    size = len(rows) * cells
    far = [far_ref.at[e * size : (e + 1) * size] for e in range(half)]
    spectra = transform(len(rows), cells, refs[:half], far, forward_ref)
    modes, width = spectra[0].shape
    mask, _ = masks(mask_ref, 0, width)
    fluid, solid = one_over(columns_ref, 0, modes)
    ones, sweeps = inner_sweeps(spectra, sides_ref[...], rows, mask, fluid, solid, (edges_ref[0], edges_ref[1]))
    ones_ref[0] = ones[0]
    ones_ref[1] = ones[-1]
    inverse_rows(sweeps, cells, inverse_ref, outs)


def local_kernel(rows, edge_rows, count, cells, *refs):
    half = count // 2
    message_ref, edges = refs[0], refs[1 : 1 + half]
    forward_ref, inverse_ref, columns_ref, mask_ref = refs[1 + half : 5 + half]
    out_ref = refs[-1]
    size = len(rows) * cells
    near = [message_ref.at[d * size : (d + 1) * size] for d in range(half)]
    spectra = transform(len(rows), cells, near, (), forward_ref)
    edge_spectra = transform(len(edge_rows), cells, edges, (), forward_ref)
    sides = transform(len(edge_rows), cells, edges, (), forward_ref, beside=True)
    modes, width = spectra[0].shape
    mask, kinds = masks(mask_ref, half, width)
    fluid, solid = one_over(columns_ref, 0, modes)
    around = [spectrum * pick(mask[row], fluid, solid) for spectrum, row in zip(edge_spectra, edge_rows)]
    sides = sides * pick(kinds, fluid, solid)
    _, sweeps = inner_sweeps(spectra, sides, rows, mask, fluid, solid, around)
    inverse_rows(sweeps, cells, inverse_ref, [out_ref.at[d * size : (d + 1) * size] for d in range(half)])


def send_kernel(rows, edge_rows, rest, count, cells, *refs):
    half = count // 2
    inner, edges = refs[:half], refs[half : 2 * half]
    send_ref, columns_ref, mask_ref = refs[2 * half : 2 * half + 3]
    out_ref = refs[-1]

    def product(blocks, lines, lanes, kind):
        return sum(kind(send_ref[place(d)], block[lines, lanes]) for d, block in enumerate(blocks))

    def whole(blocks, i):
        return product(blocks, slice(i * cells, (i + 1) * cells), slice(None), row_product)

    spectra = [whole(inner, i) for i in range(len(rows))]
    around = [whole(edges, i) for i in range(len(edge_rows))]
    lines = len(edge_rows) * cells
    sides = product(edges, slice(lines, lines + 8), slice(0, cells), side_product)
    mask, kinds = masks(mask_ref, 0, inner[0].shape[1])
    fluid, solid = one_over(columns_ref, 2, rest)
    outer = [values[:rest] * pick(mask[row], fluid, solid) for values, row in zip(around, edge_rows)]
    outside = sides[:rest] * pick(kinds, fluid, solid)
    _, sweeps = inner_sweeps([v[:rest] for v in spectra], outside, rows, mask, fluid, solid, outer)

    def power(values, at):
        return values[rest + 8 * at : rest + 8 * at + 8]

    numbers = []
    for target in (0, 1):

        def beside(values, kind):
            same, cross = power(values, 2 + target), power(values, 4)
            return pick(kind, same, cross) if target == 0 else pick(kind, cross, same)

        own = [beside(values, mask[row]) for values, row in zip(spectra, rows)]
        edge = [beside(values, mask[row]) for values, row in zip(around, edge_rows)]
        column = [edge[0], *own, edge[1]]
        outside = beside(sides, kinds)
        numbers.append(
            [
                second_sweep(power(spectra[i], target), own[i], column[i], column[i + 2], outside, 4 + 2 * i, 1.0)
                for i in range(len(rows))
            ]
        )
    for i, row in enumerate(rows):
        base = i * (rest + 8)
        out_ref[base : base + rest, :] = sweeps[i]
        out_ref[base + rest : base + rest + 8, :] = jnp.where(mask[row] == 0, numbers[0][i], numbers[1][i])


def take_kernel(rows, count, cells, *refs):
    half = count // 2
    message_ref, local_ref, take_ref = refs[:3]
    outs = refs[-1 - (half - 1) * len(rows) :]
    lines = message_ref.shape[0] // len(rows)
    short = take_ref.shape[2] // 3 - lines
    for i in range(len(rows)):
        values = message_ref[i * lines : (i + 1) * lines, :]
        if short:
            values = jnp.concatenate([values, jnp.zeros((short, values.shape[1]), jnp.float32)], axis=0)
        values = thirds(values, 0)
        for d in range(half):
            base = (d * len(rows) + i) * cells
            value = local_ref[base : base + cells, :] + jnp.dot(
                take_ref[place(d)], values, preferred_element_type=jnp.float32
            )
            if d == 0:
                outs[0][i * cells : (i + 1) * cells, :] = value
            else:
                outs[1 + (d - 1) * len(rows) + i][...] = value


def rim_kernel(rows, order, count, cells, *refs):
    spectrum_ref, edges_ref, sides_ref, halo_ref, ones_ref, inverse_ref, columns_ref, mask_ref = refs[:8]
    outs = refs[-count:]
    _, modes, width = edges_ref.shape
    edge = 1 - paired_edge() if order == 0 else paired_edge()
    mask, _ = masks(mask_ref, 0, width)
    fluid, solid = one_over(columns_ref, 0, modes)
    sides = jnp.where(edge == 0, sides_ref[:, 0:2], sides_ref[:, 2:4])
    diagonal = pick(jnp.where(edge == 0, mask[rows[0]], mask[rows[1]]), fluid, solid)
    sweep = second_sweep(spectrum_ref[edge], edges_ref[edge], halo_ref[:modes, :], ones_ref[edge], sides, 0, diagonal)
    inverse_rows([sweep], cells, inverse_ref, outs[: count // 2], outs[count // 2 :])
    if order == 1:
        for d in range(1, count // 2):
            outs[d][cells:, :] = refs[8 + d - 1][...]
    for out in outs[count // 2 :]:
        if out.shape[0] > cells:
            out[cells:, :] = jnp.zeros((out.shape[0] - cells, width), jnp.float32)


def join_kernel(number, *refs):
    at = 0
    for ref in refs[:number]:
        refs[-1][at : at + ref.shape[0], :] = ref[...]
        at += ref.shape[0]


def copy_kernel(number, *refs):
    for ref, out in zip(refs[:number], refs[-number:]):
        out[...] = ref[...]


def unpack_kernel(pieces, row_count, cells, *refs):
    me = lax.axis_index("span")
    blocks, (out_ref, held, done) = refs[: len(pieces)], refs[-3:]
    pitch = held.shape[0] // cells
    count = lax.axis_size("span")
    own_lines = out_ref.shape[1] // count
    lines = own_lines * count // 2
    some = cells // SPLIT
    edge_rows = {"near": paired_edge() * (row_count - 1), "far": (1 - paired_edge()) * (row_count - 1)}
    chip = jnp.bitwise_xor(me, pieces[0][0]) // (count // 2)
    first = pl.multiple_of(chip * lines, lines)
    copies = []
    for part in range(SPLIT):
        for block, (d, base, rows, offset, tiles) in zip(blocks, pieces):
            for i, row in enumerate(rows):
                if row in edge_rows:
                    row = edge_rows[row]
                line = base + i * cells + part * some
                for tile in range(tiles):
                    at = part * some * pitch + place(d) * own_lines + (offset + tile) * row_count + row
                    held[pl.ds(at, some, stride=pitch), :] = block[line : line + some, tile * LANES : (tile + 1) * LANES]
        copies.append(
            pltpu.make_async_copy(
                held.reshape(cells, pitch, LANES).at[pl.ds(part * some, some), pl.ds(0, lines)],
                out_ref.at[pl.ds(part * some, some), pl.ds(first, lines)],
                done.at[part],
            )
        )
        copies[-1].start()
    for copy in copies:
        copy.wait()


def call(kernel, outs, *args, cost=LONG, earlier=()):
    shapes = [jax.ShapeDtypeStruct(shape, jnp.float32) for shape in outs]
    return pl.pallas_call(
        kernel,
        out_shape=shapes,
        in_specs=[VMEM] * len(args) + [ANY] * len(earlier),
        out_specs=[VMEM] * len(outs),
        compiler_params=PARAMS,
        cost_estimate=cost,
    )(*args, *earlier)


def swap(block, d):
    return lax.ppermute(block, "span", [(i, i ^ d) for i in range(lax.axis_size("span"))])


def local(pressure_source, solid_mask):
    count = lax.axis_size("span")
    half = count // 2
    plane_count = lax.axis_size("plane")
    cells, row_count, columns = pressure_source.shape
    width = columns // count
    tiles = width // LANES
    inner = tuple(range(1, row_count - 1))
    edges = (0, row_count - 1)
    near, far = range(1, half), range(half, count)
    *arrays, modes, rest = tables(cells * count, cells)
    forward, inverse, send, take, diagonals = map(jnp.asarray, arrays)

    lines = columns // LANES * row_count
    source = pressure_source.reshape(cells, row_count, columns // LANES, LANES).transpose(0, 2, 1, 3)
    source = source.reshape(cells, lines, LANES)
    scratch = [pltpu.VMEM((cells * (lines + 8), LANES), jnp.float32), pltpu.SemaphoreType.DMA((SPLIT,))]

    def pack(wanted, *earlier):
        jobs = [(at, 0, d, rows, 0, tiles, inner if rows == edges else ()) for at, (d, rows) in enumerate(wanted)]
        shapes = [(len(rows) * cells + (8 if rows == edges else 0), width) for _, rows in wanted]
        return pl.pallas_call(
            functools.partial(pack_kernel, jobs, row_count, cells, len(earlier)),
            out_shape=[jax.ShapeDtypeStruct(shape, jnp.float32) for shape in shapes],
            in_specs=[ANY] * (1 + len(earlier)),
            out_specs=[VMEM] * len(shapes),
            scratch_shapes=scratch,
            compiler_params=PARAMS,
            cost_estimate=LONG,
        )(pltpu.with_memory_space_constraint(source, pltpu.HBM), *earlier)

    packed = pack([(d, edges) for d in range(1, count)])
    edge_blocks = [swap(block, d) for d, block in enumerate(packed, 1)]
    wanted = [(d, inner) for d in range(half + 1)] + [(0, edges)] + [(d, edges) for d in far]
    wanted += [(half + d, (row,)) for d in near for row in inner]
    packed = pack(wanted, packed[half - 1])
    edge_blocks = [packed[half + 1], *edge_blocks]
    relayed = packed[2 * half + 2 :]
    relayed = [swap(relayed[(d - 1) * len(inner) + i], d) for d in near for i in range(len(inner))]
    (message,) = call(
        functools.partial(join_kernel, 1 + len(relayed)),
        [(half * len(inner) * cells, width)],
        packed[half], *relayed, cost=SHORT, earlier=(edge_blocks[half],),
    )
    arrived = swap(message, half)

    spectrum, edge_ones, paired, other, sides = call(
        functools.partial(edge_kernel, edges, count, cells),
        [(2, modes, width), (2, modes, width), (modes + 16, width), (modes, width), (modes, 16)],
        *edge_blocks, forward, diagonals, solid_mask,
    )
    later = [packed[d] for d in near] + [packed[half + 2 + d] for d in near]
    if later:
        later = call(
            functools.partial(copy_kernel, len(later)), [block.shape for block in later], *later,
            cost=SHORT, earlier=(sides,),
        )
    inner_blocks = [packed[0]] + [swap(later[d - 1], d) for d in near]
    chip_edges = [packed[half + 2]] + [swap(later[half + d - 2], d) for d in near]

    length = len(inner) * cells
    (own,) = call(
        functools.partial(local_kernel, inner, edges, count, cells),
        [(half * length, width)],
        message, *chip_edges, forward, inverse, diagonals, solid_mask, cost=SHORT,
    )

    (sent,) = call(
        functools.partial(send_kernel, inner, edges, rest, count, cells),
        [(len(inner) * (rest + 8), width)],
        *inner_blocks, *edge_blocks[:half], send, diagonals, solid_mask, cost=SHORT,
    )
    taken = swap(sent, half)

    pairs = [[(i, i ^ 1) for i in range(plane_count)], [(i, ((i + 1) ^ 1) - 1) for i in range(plane_count)]]
    pairs = [[(i, j) for i, j in pair if 0 <= j < plane_count] for pair in pairs]
    halos = [lax.ppermute(row, "plane", pair) for row, pair in zip((paired, other), pairs)]
    *made, ones = call(
        functools.partial(inner_kernel, inner, count, cells),
        [(length, width)] * half + [(2, modes, width)],
        *inner_blocks, arrived, forward, inverse, diagonals, solid_mask, edge_ones, sides,
        cost=SHORT, earlier=(own,),
    )
    pieces = [(made[0], 0, 0, inner, 0, tiles)]
    made_got = [swap(made[d], d) for d in near]
    pieces += [(block, d, 0, inner, 0, tiles) for d, block in zip(near, made_got)]
    rim_got, near_rim, earlier = [], [], []
    for order, name in enumerate(("far", "near")):
        outs = call(
            functools.partial(rim_kernel, edges, order, count, cells),
            [(cells, width)] + [((order + 1) * cells, width)] * (half - 1) + [(cells, width)] * (half - 1) + [(cells + 8 * (1 - order), width)],
            spectrum, edge_ones, sides, halos[1 - order], ones, inverse, diagonals, solid_mask, *near_rim,
            cost=LONG if order else SHORT, earlier=earlier,
        )
        near_rim = outs[1:half]
        pieces.append((outs[0], 0, 0, (name,), 0, tiles))
        rim_got.append([swap(outs[d], d) for d in far])
        pieces += [(block, d, 0, (name,), 0, tiles) for d, block in zip(far, rim_got[order])]
        earlier = [outs[-1]]
    pieces += [(swap(near_rim[d - 1], d), d, 0, ("near", "far"), 0, tiles) for d in near]
    rebuilt = call(
        functools.partial(take_kernel, inner, count, cells),
        [(length, width)] + [(cells, width)] * ((half - 1) * len(inner)),
        taken, own, take,
        cost=SHORT, earlier=[outs[-1], *rim_got[0], *made_got],
    )
    pieces.append((rebuilt[0], half, 0, inner, 0, tiles))
    for d in near:
        for i, row in enumerate(inner):
            pieces.append((swap(rebuilt[1 + (d - 1) * len(inner) + i], d), half + d, 0, (row,), 0, tiles))

    result = None
    for devices in (range(half), far):
        chosen = [piece for piece in pieces if piece[1] in devices]
        previous = () if result is None else (result,)
        result = pl.pallas_call(
            functools.partial(unpack_kernel, [piece[1:] for piece in chosen], row_count, cells),
            out_shape=jax.ShapeDtypeStruct((cells, lines, LANES), jnp.float32),
            in_specs=[VMEM] * len(chosen) + [ANY] * len(previous),
            out_specs=ANY,
            scratch_shapes=[
                pltpu.VMEM((cells * (lines // 2 + 8), LANES), jnp.float32),
                pltpu.SemaphoreType.DMA((SPLIT,)),
            ],
            input_output_aliases={len(chosen): 0} if previous else {},
            compiler_params=PARAMS,
            cost_estimate=SHORT if previous else LONG,
        )(*[piece[0] for piece in chosen], *previous)
    result = result.reshape(cells, columns // LANES, row_count, LANES).transpose(0, 2, 1, 3)
    return result.reshape(cells, row_count, columns)


def solution(mesh):
    placed = (P("span", "plane", None), P("plane", None))
    return jax.shard_map(
        local, mesh=mesh, in_specs=placed, out_specs=P("span", "plane", None), check_vma=False
    )
```

```python
import functools

import jax
import jax.numpy as jnp
import ml_dtypes
import numpy as np
from jax import lax
from jax.experimental import pallas as pl
from jax.experimental.pallas import tpu as pltpu
from jax.sharding import PartitionSpec as P

PENALTY = 12.0
LANES = 128
VMEM = pl.BlockSpec(memory_space=pltpu.VMEM)
ANY = pl.BlockSpec(memory_space=pl.ANY)
PARAMS = pltpu.CompilerParams(vmem_limit_bytes=24 * 1024 * 1024)
LONG = pl.CostEstimate(flops=0, bytes_accessed=200_000_000, transcendentals=0)
SHORT = pl.CostEstimate(flops=0, bytes_accessed=1024, transcendentals=0)
SPLIT = 4


def split(values):
    high = values.astype(ml_dtypes.bfloat16)
    low = (values - high.astype(np.float64)).astype(ml_dtypes.bfloat16)
    return np.concatenate([high, low, high], axis=-1)


def table_modes(length, wanted):
    modes = [(k, False) for k in range(length // 2 + 1) if wanted(k)]
    return modes + [(k, True) for k in range(1, length // 2) if wanted(k)]


def wave(length, points, k, sine):
    angles = (points * k % length) * (2.0 * np.pi / length)
    return np.sin(angles) if sine else np.cos(angles)


def fill(length, modes, forward, inverse, fluid, solid):
    points = np.arange(length // 2)
    for at, (k, sine) in enumerate(modes):
        forward[at] = wave(length, points, k, sine)
        inverse[:, at] = forward[at] * (1.0 if k in (0, length // 2) else 2.0) / length
        eigen = 2.0 - 2.0 * np.cos(2.0 * np.pi * k / length)
        fluid[at] = 1.0 / (4.0 + eigen)
        solid[at] = 1.0 / (4.0 + eigen + PENALTY)


def up_to(number, step):
    return -(-number // step) * step


def tables(length, cells):
    half = length // 2
    blocks = half // cells
    kept = [table_modes(length, lambda k: 3 * k <= length and k % 2 == parity) for parity in (0, 1)]
    padded = up_to(max(len(modes) for modes in kept), 16)
    left = table_modes(length, lambda k: 3 * k > length)
    rest = up_to(len(left), 16)
    columns = np.zeros((8, up_to(max(2 * padded, rest), LANES)))
    forward, inverse = np.zeros((2, padded, half)), np.zeros((2, half, padded))
    for parity, modes in enumerate(kept):
        part = slice(parity * padded, (parity + 1) * padded)
        fill(length, modes, forward[parity], inverse[parity], columns[0, part], columns[1, part])
    powers = 8
    send, take = np.zeros((rest + 6 * powers, half)), np.zeros((half, up_to(rest + powers, 16)))
    fill(length, left, send[:rest], take[:, :rest], columns[2, :rest], columns[3, :rest])
    take[:, : len(left)] *= [-1.0 if k % 2 == 0 else 1.0 for k, _ in left]
    ends = (np.arange(half), half - 1.0 - np.arange(half))
    for side in (0, 1):
        x, y = ends[side], ends[1 - side] + 1.0
        first = rest + 4 * side
        for solid, diagonal in enumerate((6.0, 6.0 + PENALTY)):
            rho = diagonal / 2.0 - np.sqrt(diagonal * diagonal / 4.0 - 1.0)
            at = first + 2 * solid
            take[:, at], take[:, at + 1] = rho**x, x * rho**x
            single = rho / (1.0 - rho**2) * rho**y
            double = rho**2 / (1.0 - rho**2) ** 2
            send[at + powers * solid] = single
            send[at + powers * (2 + solid)] = (double * (1.0 + rho**2) / (1.0 - rho**2) + double * y) * rho**y
            send[at + 1 + powers * (2 + solid)] = double * rho**y
            send[at + powers * 4] = single / PENALTY * (1.0 if solid == 0 else -1.0)
    forward = split(forward.reshape(2, padded, blocks, cells).transpose(0, 2, 1, 3))
    inverse = split(inverse.reshape(2, blocks, cells, padded))
    send = split(send.reshape(-1, blocks, cells).transpose(1, 0, 2))
    take = split(take.reshape(blocks, cells, -1))
    return forward, inverse, send, take, columns.astype(np.float32), 2 * padded, rest


def thirds(values, axis):
    high = values.astype(jnp.bfloat16)
    low = (values - high.astype(jnp.float32)).astype(jnp.bfloat16)
    return jnp.concatenate([high, high, low], axis=axis)


def pack_kernel(jobs, row_count, cells, earlier, x_ref, *refs):
    outs, (held, arrived) = refs[earlier:-2], refs[-2:]
    me = lax.axis_index("span")
    lines = x_ref.shape[1]
    all_tiles = lines // row_count
    own_tiles = all_tiles // lax.axis_size("span")
    pitch = held.shape[0] // cells
    some = cells // SPLIT
    copies = [
        pltpu.make_async_copy(
            x_ref.at[pl.ds(part * some, some)],
            held.reshape(cells, pitch, LANES).at[pl.ds(part * some, some), pl.ds(0, lines)],
            arrived.at[part],
        )
        for part in range(SPLIT)
    ]
    for copy in copies:
        copy.start()
    lane = lax.broadcasted_iota(jnp.int32, (some, LANES), 1)
    sides = []
    for part, copy in enumerate(copies):
        copy.wait()
        beside = jnp.zeros((some, LANES), jnp.float32)

        def line(tile, row):
            return held[pl.ds(part * some * pitch + tile * row_count + row, some, stride=pitch), :]

        for job, (out, base, d, rows, offset, tiles, more) in enumerate(jobs):
            first = jnp.bitwise_xor(me, d) * own_tiles + offset
            for i, row in enumerate(rows):
                at = base + i * cells + part * some
                for tile in range(tiles):
                    outs[out][at : at + some, tile * LANES : (tile + 1) * LANES] = line(first + tile, row)
            before = jnp.maximum(first - 1, 0)
            after = jnp.minimum(first + tiles, all_tiles - 1)
            for i, row in enumerate(rows + more if more else ()):
                for side, (tile, source) in enumerate(((before, LANES - 1), (after, 0))):
                    at = job * 8 + i * 2 + side
                    beside = jnp.where(lane == at, pltpu.roll(line(tile, row), (at - source) % LANES, 1), beside)
        sides.append(beside)
    if cells < LANES:
        sides.append(jnp.zeros((LANES - cells, LANES), jnp.float32))
    turned = jnp.concatenate(sides, axis=0).T
    for job, (out, base, _, rows, _, tiles, more) in enumerate(jobs):
        if not more:
            continue
        at = base + len(rows) * cells
        outs[out][at : at + 8, :LANES] = turned[job * 8 : (job + 1) * 8]
        if tiles > 1:
            outs[out][at : at + 8, LANES:] = jnp.zeros((8, (tiles - 1) * LANES), jnp.float32)


def place(d):
    half = lax.axis_size("span") // 2
    return jnp.bitwise_and(jnp.bitwise_xor(lax.axis_index("span"), d), half - 1)


def row_product(table, value):
    return jnp.dot(table, thirds(value, 0), preferred_element_type=jnp.float32)


def side_product(table, value):
    value = thirds(jnp.concatenate([value, jnp.zeros_like(value)], axis=0), 1)
    return lax.dot_general(table, value, (((1,), (1,)), ((), ())), preferred_element_type=jnp.float32)


def transform(rows, cells, near, far, forward_ref, beside=False):
    def spectrum(lines, lanes, product):
        halves = []
        for parity in (0, 1):
            total = 0.0
            for d, block in enumerate(near):
                value = block[lines, lanes]
                if far:
                    other = far[d][lines, lanes]
                    value = value + other if parity == 0 else value - other
                total = total + product(forward_ref[parity, place(d)], value)
            halves.append(total)
        return jnp.concatenate(halves, axis=0)

    if beside:
        return spectrum(slice(rows * cells, rows * cells + 8), slice(0, cells), side_product)
    return [spectrum(slice(i * cells, (i + 1) * cells), slice(None), row_product) for i in range(rows)]


def inverse_rows(sweeps, cells, inverse_ref, near, far=()):
    padded = sweeps[0].shape[0] // 2
    for i, sweep in enumerate(sweeps):
        even = thirds(sweep[:padded], 0)
        odd = thirds(sweep[padded:], 0)
        for d, out in enumerate(near):
            first = jnp.dot(inverse_ref[0, place(d)], even, preferred_element_type=jnp.float32)
            second = jnp.dot(inverse_ref[1, place(d)], odd, preferred_element_type=jnp.float32)
            out[i * cells : (i + 1) * cells, :] = first + second
            if far:
                far[d][i * cells : (i + 1) * cells, :] = first - second


def second_sweep(spectrum, one, above, below, sides, at, inverse_diagonal):
    width = one.shape[1]
    lane = lax.broadcasted_iota(jnp.int32, one.shape, 1)
    left = jnp.where(lane == 0, sides[:, at : at + 1], pltpu.roll(one, 1, 1))
    right = jnp.where(lane == width - 1, sides[:, at + 1 : at + 2], pltpu.roll(one, width - 1, 1))
    return (spectrum + above + below + left + right) * inverse_diagonal


def masks(mask_ref, d, width):
    count = mask_ref.shape[0]
    start = pl.multiple_of(jnp.bitwise_xor(lax.axis_index("span"), d) * width, LANES)
    last = mask_ref.shape[1] - LANES
    before = mask_ref[:, pl.ds(pl.multiple_of(jnp.maximum(start - LANES, 0), LANES), LANES)][:, LANES - 1 :]
    after = mask_ref[:, pl.ds(pl.multiple_of(jnp.minimum(start + width, last), LANES), LANES)][:, :1]
    before = jnp.where(start == 0, 2, before)
    after = jnp.where(start + width == mask_ref.shape[1], 2, after)
    lane = lax.broadcasted_iota(jnp.int32, (1, 16), 1)
    kinds = jnp.full((1, 16), 2, jnp.int32)
    for i, row in enumerate((0, count - 1, *range(1, count - 1))):
        kinds = jnp.where(lane == 2 * i, before[row : row + 1], kinds)
        kinds = jnp.where(lane == 2 * i + 1, after[row : row + 1], kinds)
    return [mask_ref[row : row + 1, pl.ds(start, width)] for row in range(mask_ref.shape[0])], kinds


def pick(kind, fluid, solid):
    return jnp.where(kind == 0, fluid, jnp.where(kind == 1, solid, 0.0))


def one_over(columns_ref, first, modes):
    turned = columns_ref[...].T
    return turned[:modes, first : first + 1], turned[:modes, first + 1 : first + 2]


def paired_edge():
    return lax.rem(lax.axis_index("plane") + 1, 2)


def edge_kernel(rows, count, cells, *refs):
    near, far = refs[: count // 2], refs[count // 2 : count]
    forward_ref, columns_ref, mask_ref = refs[count : count + 3]
    spectrum_ref, ones_ref, paired_ref, other_ref, sides_ref = refs[-5:]
    spectra = transform(len(rows), cells, near, far, forward_ref)
    sides = transform(len(rows), cells, near, far, forward_ref, beside=True)
    modes, width = spectra[0].shape
    mask, kinds = masks(mask_ref, 0, width)
    fluid, solid = one_over(columns_ref, 0, modes)
    ones = [spectrum * pick(mask[row], fluid, solid) for spectrum, row in zip(spectra, rows)]
    for i in (0, 1):
        spectrum_ref[i] = spectra[i]
        ones_ref[i] = ones[i]
    last = paired_edge() == 1
    paired_ref[:modes, :] = jnp.where(last, ones[1], ones[0])
    paired_ref[modes:, :] = jnp.zeros((paired_ref.shape[0] - modes, width), jnp.float32)
    other_ref[...] = jnp.where(last, ones[0], ones[1])
    sides_ref[...] = sides * pick(kinds, fluid, solid)


def inner_sweeps(spectra, sides, rows, mask, fluid, solid, edges):
    diagonals = [pick(mask[row], fluid, solid) for row in rows]
    ones = [spectrum * diagonal for spectrum, diagonal in zip(spectra, diagonals)]
    around = [edges[0], *ones, edges[1]]
    return ones, [
        second_sweep(spectra[i], ones[i], around[i], around[i + 2], sides, 4 + 2 * i, diagonals[i])
        for i in range(len(rows))
    ]


def inner_kernel(rows, count, cells, *refs):
    half = count // 2
    far_ref, forward_ref, inverse_ref, columns_ref, mask_ref, edges_ref, sides_ref = refs[half : half + 7]
    outs, ones_ref = refs[-1 - half : -1], refs[-1]
    size = len(rows) * cells
    far = [far_ref.at[e * size : (e + 1) * size] for e in range(half)]
    spectra = transform(len(rows), cells, refs[:half], far, forward_ref)
    modes, width = spectra[0].shape
    mask, _ = masks(mask_ref, 0, width)
    fluid, solid = one_over(columns_ref, 0, modes)
    ones, sweeps = inner_sweeps(spectra, sides_ref[...], rows, mask, fluid, solid, (edges_ref[0], edges_ref[1]))
    ones_ref[0] = ones[0]
    ones_ref[1] = ones[-1]
    inverse_rows(sweeps, cells, inverse_ref, outs)


def local_kernel(rows, edge_rows, count, cells, *refs):
    half = count // 2
    message_ref, edges = refs[0], refs[1 : 1 + half]
    forward_ref, inverse_ref, columns_ref, mask_ref = refs[1 + half : 5 + half]
    out_ref = refs[-1]
    size = len(rows) * cells
    near = [message_ref.at[d * size : (d + 1) * size] for d in range(half)]
    spectra = transform(len(rows), cells, near, (), forward_ref)
    edge_spectra = transform(len(edge_rows), cells, edges, (), forward_ref)
    sides = transform(len(edge_rows), cells, edges, (), forward_ref, beside=True)
    modes, width = spectra[0].shape
    mask, kinds = masks(mask_ref, half, width)
    fluid, solid = one_over(columns_ref, 0, modes)
    around = [spectrum * pick(mask[row], fluid, solid) for spectrum, row in zip(edge_spectra, edge_rows)]
    sides = sides * pick(kinds, fluid, solid)
    _, sweeps = inner_sweeps(spectra, sides, rows, mask, fluid, solid, around)
    inverse_rows(sweeps, cells, inverse_ref, [out_ref.at[d * size : (d + 1) * size] for d in range(half)])


def send_kernel(rows, edge_rows, rest, count, cells, *refs):
    half = count // 2
    inner, edges = refs[:half], refs[half : 2 * half]
    send_ref, columns_ref, mask_ref = refs[2 * half : 2 * half + 3]
    out_ref = refs[-1]

    def product(blocks, lines, lanes, kind):
        return sum(kind(send_ref[place(d)], block[lines, lanes]) for d, block in enumerate(blocks))

    def whole(blocks, i):
        return product(blocks, slice(i * cells, (i + 1) * cells), slice(None), row_product)

    spectra = [whole(inner, i) for i in range(len(rows))]
    around = [whole(edges, i) for i in range(len(edge_rows))]
    lines = len(edge_rows) * cells
    sides = product(edges, slice(lines, lines + 8), slice(0, cells), side_product)
    mask, kinds = masks(mask_ref, 0, inner[0].shape[1])
    fluid, solid = one_over(columns_ref, 2, rest)
    outer = [values[:rest] * pick(mask[row], fluid, solid) for values, row in zip(around, edge_rows)]
    outside = sides[:rest] * pick(kinds, fluid, solid)
    _, sweeps = inner_sweeps([v[:rest] for v in spectra], outside, rows, mask, fluid, solid, outer)

    def power(values, at):
        return values[rest + 8 * at : rest + 8 * at + 8]

    numbers = []
    for target in (0, 1):

        def beside(values, kind):
            same, cross = power(values, 2 + target), power(values, 4)
            return pick(kind, same, cross) if target == 0 else pick(kind, cross, same)

        own = [beside(values, mask[row]) for values, row in zip(spectra, rows)]
        edge = [beside(values, mask[row]) for values, row in zip(around, edge_rows)]
        column = [edge[0], *own, edge[1]]
        outside = beside(sides, kinds)
        numbers.append(
            [
                second_sweep(power(spectra[i], target), own[i], column[i], column[i + 2], outside, 4 + 2 * i, 1.0)
                for i in range(len(rows))
            ]
        )
    for i, row in enumerate(rows):
        base = i * (rest + 8)
        out_ref[base : base + rest, :] = sweeps[i]
        out_ref[base + rest : base + rest + 8, :] = jnp.where(mask[row] == 0, numbers[0][i], numbers[1][i])


def take_kernel(rows, count, cells, *refs):
    half = count // 2
    message_ref, local_ref, take_ref = refs[:3]
    outs = refs[-1 - (half - 1) * len(rows) :]
    lines = message_ref.shape[0] // len(rows)
    short = take_ref.shape[2] // 3 - lines
    for i in range(len(rows)):
        values = message_ref[i * lines : (i + 1) * lines, :]
        if short:
            values = jnp.concatenate([values, jnp.zeros((short, values.shape[1]), jnp.float32)], axis=0)
        values = thirds(values, 0)
        for d in range(half):
            base = (d * len(rows) + i) * cells
            value = local_ref[base : base + cells, :] + jnp.dot(
                take_ref[place(d)], values, preferred_element_type=jnp.float32
            )
            if d == 0:
                outs[0][i * cells : (i + 1) * cells, :] = value
            else:
                outs[1 + (d - 1) * len(rows) + i][...] = value


def rim_kernel(rows, order, count, cells, *refs):
    spectrum_ref, edges_ref, sides_ref, halo_ref, ones_ref, inverse_ref, columns_ref, mask_ref = refs[:8]
    outs = refs[-count:]
    _, modes, width = edges_ref.shape
    edge = 1 - paired_edge() if order == 0 else paired_edge()
    mask, _ = masks(mask_ref, 0, width)
    fluid, solid = one_over(columns_ref, 0, modes)
    sides = jnp.where(edge == 0, sides_ref[:, 0:2], sides_ref[:, 2:4])
    diagonal = pick(jnp.where(edge == 0, mask[rows[0]], mask[rows[1]]), fluid, solid)
    sweep = second_sweep(spectrum_ref[edge], edges_ref[edge], halo_ref[:modes, :], ones_ref[edge], sides, 0, diagonal)
    inverse_rows([sweep], cells, inverse_ref, outs[: count // 2], outs[count // 2 :])
    if order == 1:
        for d in range(1, count // 2):
            outs[d][cells:, :] = refs[8 + d - 1][...]
    for out in outs[count // 2 :]:
        if out.shape[0] > cells:
            out[cells:, :] = jnp.zeros((out.shape[0] - cells, width), jnp.float32)


def join_kernel(number, *refs):
    at = 0
    for ref in refs[:number]:
        refs[-1][at : at + ref.shape[0], :] = ref[...]
        at += ref.shape[0]


def copy_kernel(number, *refs):
    for ref, out in zip(refs[:number], refs[-number:]):
        out[...] = ref[...]


def unpack_kernel(pieces, row_count, cells, *refs):
    me = lax.axis_index("span")
    blocks, (out_ref, held, done) = refs[: len(pieces)], refs[-3:]
    pitch = held.shape[0] // cells
    count = lax.axis_size("span")
    own_lines = out_ref.shape[1] // count
    lines = own_lines * count // 2
    some = cells // SPLIT
    edge_rows = {"near": paired_edge() * (row_count - 1), "far": (1 - paired_edge()) * (row_count - 1)}
    chip = jnp.bitwise_xor(me, pieces[0][0]) // (count // 2)
    first = pl.multiple_of(chip * lines, lines)
    copies = []
    for part in range(SPLIT):
        for block, (d, base, rows, offset, tiles) in zip(blocks, pieces):
            for i, row in enumerate(rows):
                if row in edge_rows:
                    row = edge_rows[row]
                line = base + i * cells + part * some
                for tile in range(tiles):
                    at = part * some * pitch + place(d) * own_lines + (offset + tile) * row_count + row
                    held[pl.ds(at, some, stride=pitch), :] = block[line : line + some, tile * LANES : (tile + 1) * LANES]
        copies.append(
            pltpu.make_async_copy(
                held.reshape(cells, pitch, LANES).at[pl.ds(part * some, some), pl.ds(0, lines)],
                out_ref.at[pl.ds(part * some, some), pl.ds(first, lines)],
                done.at[part],
            )
        )
        copies[-1].start()
    for copy in copies:
        copy.wait()


def call(kernel, outs, *args, cost=LONG, earlier=()):
    shapes = [jax.ShapeDtypeStruct(shape, jnp.float32) for shape in outs]
    return pl.pallas_call(
        kernel,
        out_shape=shapes,
        in_specs=[VMEM] * len(args) + [ANY] * len(earlier),
        out_specs=[VMEM] * len(outs),
        compiler_params=PARAMS,
        cost_estimate=cost,
    )(*args, *earlier)


def swap(block, d):
    return lax.ppermute(block, "span", [(i, i ^ d) for i in range(lax.axis_size("span"))])


def local(pressure_source, solid_mask):
    count = lax.axis_size("span")
    half = count // 2
    plane_count = lax.axis_size("plane")
    cells, row_count, columns = pressure_source.shape
    width = columns // count
    tiles = width // LANES
    inner = tuple(range(1, row_count - 1))
    edges = (0, row_count - 1)
    near, far = range(1, half), range(half, count)
    *arrays, modes, rest = tables(cells * count, cells)
    forward, inverse, send, take, diagonals = map(jnp.asarray, arrays)

    lines = columns // LANES * row_count
    source = pressure_source.reshape(cells, row_count, columns // LANES, LANES).transpose(0, 2, 1, 3)
    source = source.reshape(cells, lines, LANES)
    scratch = [pltpu.VMEM((cells * (lines + 8), LANES), jnp.float32), pltpu.SemaphoreType.DMA((SPLIT,))]

    def pack(wanted, *earlier):
        jobs = [(at, 0, d, rows, 0, tiles, inner if rows == edges else ()) for at, (d, rows) in enumerate(wanted)]
        shapes = [(len(rows) * cells + (8 if rows == edges else 0), width) for _, rows in wanted]
        return pl.pallas_call(
            functools.partial(pack_kernel, jobs, row_count, cells, len(earlier)),
            out_shape=[jax.ShapeDtypeStruct(shape, jnp.float32) for shape in shapes],
            in_specs=[ANY] * (1 + len(earlier)),
            out_specs=[VMEM] * len(shapes),
            scratch_shapes=scratch,
            compiler_params=PARAMS,
            cost_estimate=LONG,
        )(pltpu.with_memory_space_constraint(source, pltpu.HBM), *earlier)

    packed = pack([(d, edges) for d in range(1, count)])
    edge_blocks = [swap(block, d) for d, block in enumerate(packed, 1)]
    wanted = [(d, inner) for d in range(half + 1)] + [(0, edges)] + [(d, edges) for d in far]
    wanted += [(half + d, (row,)) for d in near for row in inner]
    packed = pack(wanted, packed[half - 1])
    edge_blocks = [packed[half + 1], *edge_blocks]
    relayed = packed[2 * half + 2 :]
    relayed = [swap(relayed[(d - 1) * len(inner) + i], d) for d in near for i in range(len(inner))]
    (message,) = call(
        functools.partial(join_kernel, 1 + len(relayed)),
        [(half * len(inner) * cells, width)],
        packed[half], *relayed, cost=SHORT, earlier=(edge_blocks[half],),
    )
    arrived = swap(message, half)

    spectrum, edge_ones, paired, other, sides = call(
        functools.partial(edge_kernel, edges, count, cells),
        [(2, modes, width), (2, modes, width), (modes + 16, width), (modes, width), (modes, 16)],
        *edge_blocks, forward, diagonals, solid_mask,
    )
    later = [packed[d] for d in near] + [packed[half + 2 + d] for d in near]
    if later:
        later = call(
            functools.partial(copy_kernel, len(later)), [block.shape for block in later], *later,
            cost=SHORT, earlier=(sides,),
        )
    inner_blocks = [packed[0]] + [swap(later[d - 1], d) for d in near]
    chip_edges = [packed[half + 2]] + [swap(later[half + d - 2], d) for d in near]

    length = len(inner) * cells
    (own,) = call(
        functools.partial(local_kernel, inner, edges, count, cells),
        [(half * length, width)],
        message, *chip_edges, forward, inverse, diagonals, solid_mask, cost=SHORT,
    )

    (sent,) = call(
        functools.partial(send_kernel, inner, edges, rest, count, cells),
        [(len(inner) * (rest + 8), width)],
        *inner_blocks, *edge_blocks[:half], send, diagonals, solid_mask, cost=SHORT,
    )
    taken = swap(sent, half)

    pairs = [[(i, i ^ 1) for i in range(plane_count)], [(i, ((i + 1) ^ 1) - 1) for i in range(plane_count)]]
    pairs = [[(i, j) for i, j in pair if 0 <= j < plane_count] for pair in pairs]
    halos = [lax.ppermute(row, "plane", pair) for row, pair in zip((paired, other), pairs)]
    *made, ones = call(
        functools.partial(inner_kernel, inner, count, cells),
        [(length, width)] * half + [(2, modes, width)],
        *inner_blocks, arrived, forward, inverse, diagonals, solid_mask, edge_ones, sides,
        cost=SHORT, earlier=(own,),
    )
    pieces = [(made[0], 0, 0, inner, 0, tiles)]
    made_got = [swap(made[d], d) for d in near]
    pieces += [(block, d, 0, inner, 0, tiles) for d, block in zip(near, made_got)]
    rim_got, near_rim, earlier = [], [], []
    for order, name in enumerate(("far", "near")):
        outs = call(
            functools.partial(rim_kernel, edges, order, count, cells),
            [(cells, width)] + [((order + 1) * cells, width)] * (half - 1) + [(cells, width)] * (half - 1) + [(cells + 8 * (1 - order), width)],
            spectrum, edge_ones, sides, halos[1 - order], ones, inverse, diagonals, solid_mask, *near_rim,
            cost=LONG if order else SHORT, earlier=earlier,
        )
        near_rim = outs[1:half]
        pieces.append((outs[0], 0, 0, (name,), 0, tiles))
        rim_got.append([swap(outs[d], d) for d in far])
        pieces += [(block, d, 0, (name,), 0, tiles) for d, block in zip(far, rim_got[order])]
        earlier = [outs[-1]]
    pieces += [(swap(near_rim[d - 1], d), d, 0, ("near", "far"), 0, tiles) for d in near]
    rebuilt = call(
        functools.partial(take_kernel, inner, count, cells),
        [(length, width)] + [(cells, width)] * ((half - 1) * len(inner)),
        taken, own, take,
        cost=SHORT, earlier=[outs[-1], *rim_got[0], *made_got],
    )
    pieces.append((rebuilt[0], half, 0, inner, 0, tiles))
    for d in near:
        for i, row in enumerate(inner):
            pieces.append((swap(rebuilt[1 + (d - 1) * len(inner) + i], d), half + d, 0, (row,), 0, tiles))

    result = None
    for devices in (range(half), far):
        chosen = [piece for piece in pieces if piece[1] in devices]
        previous = () if result is None else (result,)
        result = pl.pallas_call(
            functools.partial(unpack_kernel, [piece[1:] for piece in chosen], row_count, cells),
            out_shape=jax.ShapeDtypeStruct((cells, lines, LANES), jnp.float32),
            in_specs=[VMEM] * len(chosen) + [ANY] * len(previous),
            out_specs=ANY,
            scratch_shapes=[
                pltpu.VMEM((cells * (lines // 2 + 8), LANES), jnp.float32),
                pltpu.SemaphoreType.DMA((SPLIT,)),
            ],
            input_output_aliases={len(chosen): 0} if previous else {},
            compiler_params=PARAMS,
            cost_estimate=SHORT if previous else LONG,
        )(*[piece[0] for piece in chosen], *previous)
    result = result.reshape(cells, columns // LANES, row_count, LANES).transpose(0, 2, 1, 3)
    return result.reshape(cells, row_count, columns)


def solution(mesh):
    placed = (P("span", "plane", None), P("plane", None))
    return jax.shard_map(
        local, mesh=mesh, in_specs=placed, out_specs=P("span", "plane", None), check_vma=False
    )
```
